32 devices in a mesh: row: 4 (over z), col: 8 (over y, x, core).
Axes of the slice: x: 2, y: 2, z: 4, core: 2. Of those that a mesh axis runs over, the one named last changes fastest.
Arguments:
- front: float32 [16384, 16384], P('row', 'col')
- tiles: float32 [4096, 128, 128], P(('row', 'col')), may hold values from -0.375 to 0.375
- tile_block: int32 [2, 4096], replicated, may hold values from 0 to 127, as said below
- valid_rows: int32 [4096], P(('row', 'col')), may hold values from 64 to 128
Outputs:
- factored: float32 [16384, 16384], P('row', 'col')
The draws below stay inside these ranges and needn't reach their ends.
Inputs may be any that keep to these rules, and one draw needn't show every extreme that they name: tile_block[0, t] and tile_block[1, t] give the block row and block column, in blocks of 128, that tile t is added to. The 128 tiles of each device (tiles laid in order over row+col) go to blocks held by exactly 16 different devices, 8 tiles to each.
All inputs are finite; a program needn't handle non-finite values.
Results may differ from the reference program's by a relative error of at most 0.0001.
Values sent between devices are 32-bit elements; how exact they have to be, the bound alone decides.
No kernel may reach another device: no remote copies, remote signals or barrier semaphores. Data moves between devices by JAX's collectives and lax.ppermute only.
A program may use at most 192 MiB of HBM per device.

```python
import jax
import jax.numpy as jnp
from jax import lax

F = 16384
NB = 128
PANELS = 2
BS = 128
TILE_DEV = 128
TILES = 4096
CAP = 8
ROW_BLOCKS = 32
COL_BLOCKS = 16
N_ROW = 4
N_COL = 8


def draw_front(key, part):
    total = PANELS * NB
    first_key, second_key, third_key = jax.random.split(key, 3)
    values = jax.random.normal(first_key, (F, F), jnp.float32)
    rows_index = jnp.arange(F)[:, None]
    cols_index = jnp.arange(F)[None, :]
    leading = (rows_index < total) & (cols_index < total)
    coupling = (rows_index >= total) & (cols_index < total)
    spread = jnp.where(leading, 0.3, jnp.where(coupling, 0.25, 8.0 / F ** 0.5))
    lead_pivots = jax.random.uniform(second_key, (F,), jnp.float32, 24.0, 30.0)
    rest_pivots = jax.random.uniform(third_key, (F,), jnp.float32, 4.0, 8.0)
    pivots = jnp.where(jnp.arange(F) < total, lead_pivots, rest_pivots)
    return jnp.where(rows_index == cols_index, pivots[None, :], values * spread)


def choose_targets(key_one):
    return jax.random.permutation(key_one, N_ROW * N_COL)[:TILE_DEV // CAP]


def shuffle_tiles(key_one):
    return jax.random.permutation(key_one, TILE_DEV)


def draw_tile_block(key, part):
    device_count = N_ROW * N_COL
    keys = jax.random.split(key, 4)
    chosen = jax.vmap(choose_targets)(jax.random.split(keys[0], device_count))
    shuffled = jax.vmap(shuffle_tiles)(jax.random.split(keys[1], device_count))
    target = jnp.take_along_axis(chosen, shuffled // CAP, axis=1)
    inner_row = jax.random.randint(keys[2], (device_count, TILE_DEV), 0, ROW_BLOCKS)
    inner_col = jax.random.randint(keys[3], (device_count, TILE_DEV), 0, COL_BLOCKS)
    block_row = target // N_COL * ROW_BLOCKS + inner_row
    block_col = target % N_COL * COL_BLOCKS + inner_col
    return jnp.stack([block_row.reshape(-1), block_col.reshape(-1)]).astype(jnp.int32)


def touch_ends(entries, key, low, largest):
    index_at = [jax.random.randint(jax.random.fold_in(key, axis), (), 0, length) for axis, length in enumerate(entries.shape)]
    widest = entries.shape.index(max(entries.shape))
    neighbour = index_at[:widest] + [(index_at[widest] + 1) % entries.shape[widest]] + index_at[widest + 1:]
    return entries.at[tuple(index_at)].set(low).at[tuple(neighbour)].set(largest)


def block_scale(own_key, dims, shards, smallest, high):
    gain = 1.0
    for axis_at, blocks in shards:
        heights = jax.random.uniform(jax.random.fold_in(jax.random.fold_in(own_key, 6), axis_at), (blocks,), jnp.float32, smallest / len(shards), high / len(shards))
        gain = gain * jnp.repeat(jnp.exp(heights), dims[axis_at] // blocks).reshape((-1,) + (1,) * (len(dims) - 1 - axis_at))
    return gain


def noise(own_key, dims, scale, limit, cuts=(), kind=jnp.bfloat16):
    drawn = jax.random.normal(own_key, dims, jnp.float32) * scale
    if len(cuts) > 0:
        drawn = block_scale(own_key, dims, cuts, -0.22, 0.18) * drawn
    return jnp.clip(drawn, min=-limit, max=limit).astype(kind)


def setup_inputs(seed: int = 0) -> dict:
    key_of = jax.random.split(jax.random.key(seed), 5)
    front = draw_front(jax.random.fold_in(key_of[4], 71), 0)
    tiles = noise(key_of[1], (TILES, BS, BS), (8.0 / (F ** 0.5)), 0.375, ((0, 32),), jnp.float32)
    tile_block = draw_tile_block(jax.random.fold_in(key_of[4], 71), 0)
    valid_rows = touch_ends(jax.random.randint(key_of[3], (TILES,), BS // 2, BS + 1), jax.random.fold_in(key_of[3], 1), BS // 2, BS).astype(jnp.int32)
    return {"front": front, "tiles": tiles, "tile_block": tile_block, "valid_rows": valid_rows}


precise = lax.Precision.HIGHEST

def reference(front, tiles, tile_block, valid_rows):
    blocks_side = F // BS
    keeping = jnp.arange(BS)[None, :, None] < valid_rows[:, None, None]
    masked = jnp.where(keeping, tiles, jnp.zeros_like(tiles))
    blocks = front.reshape(blocks_side, BS, blocks_side, BS)
    blocks = blocks.at[tile_block[0], :, tile_block[1], :].add(masked)
    current = blocks.reshape(F, F)
    total = PANELS * NB
    factors = []
    for number in range(PANELS):
        offset = number * NB
        ending = offset + NB
        diagonal = current[offset:ending, offset:ending]
        symmetric = jnp.tril(diagonal) + jnp.tril(diagonal, -1).T
        lower = jnp.linalg.cholesky(symmetric)
        solved = jax.scipy.linalg.solve_triangular(lower, current[ending:, offset:ending].T, lower=True).T
        column = jnp.concatenate([jnp.zeros((offset, NB), current.dtype), lower, solved], 0)
        factors.append(column)
        change = jnp.dot(solved.astype(jnp.float32), solved.T.astype(jnp.float32), precision=precise, preferred_element_type=jnp.float32)
        current = current.at[ending:, ending:].set(current[ending:, ending:] - change)
    panel_factor = jnp.concatenate(factors, 1)
    result = current.at[:, :total].set(panel_factor)
    result = result.at[:total, total:].set(panel_factor[total:].T)
    return result
```

```python
import functools

import jax
import jax.numpy as jnp
from jax import lax
from jax.experimental import pallas as pl
from jax.experimental.pallas import tpu as pltpu
from jax.sharding import PartitionSpec as P

NB = 128
PANELS = 2
TOTAL = NB * PANELS
MIB = 1 << 20


precise = lax.Precision.HIGHEST


def dot_nt(a, b, precision=precise):
    return lax.dot_general(
        a, b, (((1,), (1,)), ((), ())), precision=precision, preferred_element_type=jnp.float32
    )


def pack_kernel(slot_ref, valid_ref, tiles_ref, out_ref, buf, sem_in, sem_out):
    count, side = tiles_ref.shape[0], tiles_ref.shape[1]

    def fetch(t):
        return pltpu.make_async_copy(tiles_ref.at[t], buf.at[t], sem_in.at[t])

    def store(t):
        return pltpu.make_async_copy(buf.at[t], out_ref.at[jnp.maximum(slot_ref[t], 0)], sem_out.at[t])

    def each(act):
        @pl.loop(0, count)
        def _(t):
            @pl.when(slot_ref[t] >= 0)
            def _():
                act(t)

    def mask(t):
        fetch(t).wait()
        rows = lax.broadcasted_iota(jnp.int32, (side, side), 0)
        buf[t] = jnp.where(rows < valid_ref[t], buf[t], 0.0)
        store(t).start()

    each(lambda t: fetch(t).start())
    each(mask)
    each(lambda t: store(t).wait())


def pack(tiles, slots, valid, n_slots):
    count, side = tiles.shape[0], tiles.shape[1]
    smem = pl.BlockSpec(memory_space=pltpu.SMEM)
    return pl.pallas_call(
        pack_kernel,
        out_shape=jax.ShapeDtypeStruct((n_slots, side, side), jnp.float32),
        in_specs=[smem, smem, pl.BlockSpec(memory_space=pl.ANY)],
        out_specs=pl.BlockSpec(memory_space=pl.ANY),
        scratch_shapes=[
            pltpu.VMEM((count, side, side), jnp.float32),
            pltpu.SemaphoreType.DMA((count,)),
            pltpu.SemaphoreType.DMA((count,)),
        ],
        compiler_params=pltpu.CompilerParams(vmem_limit_bytes=24 * MIB),
    )(slots, valid, tiles)


def panel_kernel(code_ref, first_ref, front_ref, arrived_ref, out_ref):
    side = arrived_ref.shape[1]

    @pl.when(first_ref[0] == 1)
    def _():
        out_ref[...] = front_ref[...]

    @pl.when(first_ref[0] == 0)
    def _():
        out_ref[...] = jnp.zeros_like(out_ref)

    @pl.loop(0, arrived_ref.shape[0])
    def _(k):
        code = code_ref[k]
        for part in range(PANELS):

            @pl.when((code >= 0) & (code % PANELS == part))
            def _():
                rows = pl.ds(pl.multiple_of(code // PANELS * side, side), side)
                out_ref[rows, part * side : (part + 1) * side] += arrived_ref[k]


def raw_panel(front, arrived, codes, first):
    row_len = front.shape[0]
    smem = pl.BlockSpec(memory_space=pltpu.SMEM)
    return pl.pallas_call(
        panel_kernel,
        grid=(1,),
        out_shape=jax.ShapeDtypeStruct((row_len, TOTAL), jnp.float32),
        in_specs=[
            smem,
            smem,
            pl.BlockSpec((row_len, TOTAL), lambda i: (0, 0)),
            pl.BlockSpec(arrived.shape, lambda i: (0, 0, 0)),
        ],
        out_specs=pl.BlockSpec((row_len, TOTAL), lambda i: (0, 0)),
        compiler_params=pltpu.CompilerParams(vmem_limit_bytes=40 * MIB),
    )(codes, first, front, arrived)


def split(value):
    high = value.astype(jnp.bfloat16)
    low = (value - high.astype(jnp.float32)).astype(jnp.bfloat16)
    return high, low


def rows_kernel(raw_ref, inverse_ref, out_ref, high_ref, low_ref):
    solved = dot_nt(raw_ref[...], inverse_ref[...])
    out_ref[...] = solved
    high_ref[...], low_ref[...] = split(solved)


def solve_rows(raw, inverse):
    length = raw.shape[0]
    step = min(512, length)
    block = pl.BlockSpec((step, TOTAL), lambda i: (i, 0))
    return pl.pallas_call(
        rows_kernel,
        grid=(length // step,),
        out_shape=[
            jax.ShapeDtypeStruct((length, TOTAL), jnp.float32),
            jax.ShapeDtypeStruct((length, TOTAL), jnp.bfloat16),
            jax.ShapeDtypeStruct((length, TOTAL), jnp.bfloat16),
        ],
        in_specs=[block, pl.BlockSpec((TOTAL, TOTAL), lambda i: (0, 0))],
        out_specs=[block, block, block],
        compiler_params=pltpu.CompilerParams(vmem_limit_bytes=24 * MIB),
    )(raw, inverse)


def cols_kernel(raw_ref, inverse_ref, out_ref, high_ref, low_ref):
    solved = dot_nt(inverse_ref[...], raw_ref[...])
    out_ref[...] = solved
    high_ref[...], low_ref[...] = split(solved)


def solve_cols(raw, inverse):
    length = raw.shape[0]
    step = min(512, length)
    block = pl.BlockSpec((TOTAL, step), lambda i: (0, i))
    return pl.pallas_call(
        cols_kernel,
        grid=(length // step,),
        out_shape=[
            jax.ShapeDtypeStruct((TOTAL, length), jnp.float32),
            jax.ShapeDtypeStruct((TOTAL, length), jnp.bfloat16),
            jax.ShapeDtypeStruct((TOTAL, length), jnp.bfloat16),
        ],
        in_specs=[
            pl.BlockSpec((step, TOTAL), lambda i: (i, 0)),
            pl.BlockSpec((TOTAL, TOTAL), lambda i: (0, 0)),
        ],
        out_specs=[block, block, block],
        compiler_params=pltpu.CompilerParams(vmem_limit_bytes=24 * MIB),
    )(raw, inverse)


def final_kernel(
    cols_blocks, code_ref, place_ref, front_ref, rows_ref, rows_high, rows_low, cols_ref, cols_high,
    cols_low, lower_ref, arrived_ref, out_ref, cursor
):
    step = pl.program_id(0)
    sources, capacity = code_ref.shape
    height, width = front_ref.shape
    side = arrived_ref.shape[1]
    per_step = height // side

    @pl.when(step == 0)
    def _():
        for s in range(sources):
            cursor[s] = 0

    chunk = min(512, width)
    for start in range(0, width, chunk):
        at = slice(start, start + chunk)
        change = jnp.dot(rows_high[...], cols_high[:, at], preferred_element_type=jnp.float32)
        change += jnp.dot(rows_high[...], cols_low[:, at], preferred_element_type=jnp.float32)
        change += jnp.dot(rows_low[...], cols_high[:, at], preferred_element_type=jnp.float32)
        out_ref[:, at] = front_ref[:, at] - change

    edge = (step + 1) * per_step * cols_blocks

    @pl.loop(0, sources)
    def _(s):
        def more(k):
            code = code_ref[s, jnp.minimum(k, capacity - 1)]
            return (k < capacity) & (code >= 0) & (code < edge)

        def add(k):
            code = code_ref[s, k]
            block_row = code // cols_blocks - step * per_step
            block_col = code % cols_blocks
            rows = pl.ds(pl.multiple_of(block_row * side, side), side)
            columns = pl.ds(pl.multiple_of(block_col * side, side), side)
            out_ref[rows, columns] += arrived_ref[s * capacity + k]
            return k + 1

        cursor[s] = lax.while_loop(more, add, cursor[s])

    top = (place_ref[0] == 0) & (step == 0)

    @pl.when(top)
    def _():
        out_ref[...] = cols_ref[...]

    @pl.when(place_ref[1] == 0)
    def _():
        out_ref[:, :TOTAL] = jnp.where(top, lower_ref[...], rows_ref[...])


def finish(front, rows, cols, lower, arrived, codes, place, cols_blocks):
    row_len, col_len = front.shape
    height = TOTAL
    smem = pl.BlockSpec(memory_space=pltpu.SMEM)
    block = pl.BlockSpec((height, TOTAL), lambda i: (i, 0))
    wide = pl.BlockSpec((height, col_len), lambda i: (i, 0))
    whole = pl.BlockSpec((TOTAL, col_len), lambda i: (0, 0))
    return pl.pallas_call(
        functools.partial(final_kernel, cols_blocks),
        grid=(row_len // height,),
        out_shape=jax.ShapeDtypeStruct((row_len, col_len), jnp.float32),
        in_specs=[
            smem, smem, wide, block, block, block, whole, whole, whole,
            pl.BlockSpec((TOTAL, TOTAL), lambda i: (0, 0)),
            pl.BlockSpec(memory_space=pltpu.VMEM),
        ],
        out_specs=wide,
        scratch_shapes=[pltpu.SMEM((codes.shape[0],), jnp.int32)],
        compiler_params=pltpu.CompilerParams(vmem_limit_bytes=56 * MIB),
    )(codes, place, front, *rows, *cols, lower, arrived)


def factor(diagonal):
    def lower_of(block):
        return jnp.linalg.cholesky(jnp.tril(block) + jnp.tril(block, -1).T)

    def inverse_of(block):
        return jax.scipy.linalg.solve_triangular(block, jnp.eye(NB, dtype=jnp.float32), lower=True)

    first = lower_of(diagonal[:NB, :NB])
    first_inverse = inverse_of(first)
    below = dot_nt(diagonal[NB:, :NB], first_inverse)
    second = lower_of(diagonal[NB:, NB:] - dot_nt(below, below))
    second_inverse = inverse_of(second)
    corner = -jnp.dot(second_inverse, jnp.dot(below, first_inverse, precision=precise), precision=precise)
    zero = jnp.zeros((NB, NB), jnp.float32)
    return jnp.block([[first, zero], [below, second]]), jnp.block([[first_inverse, zero], [corner, second_inverse]])


def body(front, tiles, tile_block, valid_rows):
    row_len, col_len = front.shape
    row_count = lax.axis_size("row")
    col_count = lax.axis_size("col")
    device_count = row_count * col_count
    per_device = tiles.shape[0]
    side = tiles.shape[1]
    capacity = 2 * per_device // device_count
    rows_blocks = row_len // side
    cols_blocks = col_len // side
    row_now = lax.axis_index("row")
    col_now = lax.axis_index("col")
    device_now = row_now * col_count + col_now

    block_row = tile_block[0].reshape(device_count, per_device)
    block_col = tile_block[1].reshape(device_count, per_device)
    target_row = block_row // rows_blocks
    target = target_row * col_count + block_col // cols_blocks
    code = block_row % rows_blocks * cols_blocks + block_col % cols_blocks
    position = lax.broadcasted_iota(jnp.int32, target.shape, 1)
    place = jnp.stack([row_now, col_now]).astype(jnp.int32)

    def own(values):
        return lax.dynamic_index_in_dim(values, device_now, 0, keepdims=False)

    in_panel = block_col < PANELS
    panel_key = jnp.where(in_panel, target_row, -1)
    panel_rank = jnp.sum(
        (panel_key[:, :, None] == panel_key[:, None, :]) & (position[:, None, :] < position[:, :, None]),
        axis=2,
    )
    ahead = (own(target_row) - row_now) % row_count
    panel_slot = jnp.where(own(in_panel), ahead * capacity + own(panel_rank), -1)
    panel_out = pack(tiles, panel_slot, valid_rows, row_count * capacity)
    panel_in = [panel_out[:capacity]]
    for shift in range(1, row_count):
        sending = panel_out[shift * capacity : (shift + 1) * capacity]
        turn = [(r, (r + shift) % row_count) for r in range(row_count)]
        panel_in.append(lax.ppermute(sending, "row", turn))
    same_col = lax.dynamic_index_in_dim(
        jnp.stack([panel_key, panel_rank, code]).reshape(3, row_count, col_count, per_device),
        col_now, 2, keepdims=False,
    )
    slots = jnp.arange(capacity)
    fits = (same_col[0] == row_now)[:, :, None] & (same_col[1][:, :, None] == slots)
    panel_code = same_col[2] // cols_blocks * PANELS + same_col[2] % cols_blocks
    panel_codes = jnp.sum(jnp.where(fits, panel_code[:, :, None] + 1, 0), axis=1) - 1
    by_shift = (row_now - jnp.arange(row_count)) % row_count
    panel_codes = jnp.take(panel_codes, by_shift, axis=0).reshape(-1)

    order = (target * rows_blocks * cols_blocks + code) * per_device + position
    ranking = jnp.sum(
        (target[:, :, None] == target[:, None, :]) & (order[:, None, :] < order[:, :, None]), axis=2
    )
    slot = own(target) * capacity + own(ranking)
    here = (target == device_now)[:, :, None] & (ranking[:, :, None] == slots)
    codes = jnp.sum(jnp.where(here, code[:, :, None] + 1, 0), axis=1) - 1
    outgoing = pack(tiles, slot, valid_rows, device_count * capacity)
    arrived = lax.all_to_all(
        outgoing.reshape(device_count, capacity, side, side), ("row", "col"), 0, 0, tiled=True
    ).reshape(device_count * capacity, side, side)

    first = (col_now == 0).astype(jnp.int32).reshape(1)
    partial = raw_panel(front, jnp.concatenate(panel_in, 0), panel_codes, first)
    raw_rows = lax.psum(partial, "col")
    slice_start = col_now * col_len % row_len
    slice_root = col_now * col_len // row_len
    picked = lax.dynamic_slice_in_dim(raw_rows, slice_start, col_len, 0)
    raw_cols = lax.psum(jnp.where(row_now == slice_root, picked, 0.0), "row")
    diagonal = jnp.where(row_now == 0, raw_rows[:TOTAL], jnp.eye(TOTAL, dtype=jnp.float32))
    lower, inverse = factor(diagonal)
    inverse = lax.psum(jnp.where(row_now == 0, inverse, 0.0), "row")
    rows = solve_rows(raw_rows, inverse)
    cols = solve_cols(raw_cols, inverse)
    return finish(front, rows, cols, lower, arrived, codes, place, cols_blocks)


def solution(mesh):
    placed = (P("row", "col"), P(("row", "col"), None, None), P(), P(("row", "col")))
    return jax.shard_map(
        body, mesh=mesh, in_specs=placed, out_specs=P("row", "col"), check_vma=False
    )
```

```python
import functools

import jax
import jax.numpy as jnp
from jax import lax
from jax.experimental import pallas as pl
from jax.experimental.pallas import tpu as pltpu
from jax.sharding import PartitionSpec as P

NB = 128
PANELS = 2
TOTAL = NB * PANELS
MIB = 1 << 20


precise = lax.Precision.HIGHEST


def dot_nt(a, b, precision=precise):
    return lax.dot_general(
        a, b, (((1,), (1,)), ((), ())), precision=precision, preferred_element_type=jnp.float32
    )


def pack_kernel(slot_ref, valid_ref, tiles_ref, out_ref, buf, sem):
    count, side = tiles_ref.shape[0], tiles_ref.shape[1]
    half = side // 2

    def store(t):
        return pltpu.make_async_copy(buf.at[t], out_ref.at[jnp.maximum(slot_ref[t], 0)], sem.at[t])

    def each(act):
        @pl.loop(0, count)
        def _(t):
            @pl.when(slot_ref[t] >= 0)
            def _():
                act(t)

    def mask(t):
        rows = lax.broadcasted_iota(jnp.int32, (half, side), 0) + half
        buf[t, :half] = tiles_ref[t, :half]
        buf[t, half:] = jnp.where(rows < valid_ref[t], tiles_ref[t, half:], 0.0)
        store(t).start()

    each(mask)
    each(lambda t: store(t).wait())


def pack(tiles, slots, valid, n_slots):
    count, side = tiles.shape[0], tiles.shape[1]
    smem = pl.BlockSpec(memory_space=pltpu.SMEM)
    return pl.pallas_call(
        pack_kernel,
        out_shape=jax.ShapeDtypeStruct((n_slots, side, side), jnp.float32),
        in_specs=[smem, smem, pl.BlockSpec(memory_space=pltpu.VMEM)],
        out_specs=pl.BlockSpec(memory_space=pl.ANY),
        scratch_shapes=[
            pltpu.VMEM((count, side, side), jnp.float32),
            pltpu.SemaphoreType.DMA((count,)),
        ],
        compiler_params=pltpu.CompilerParams(vmem_limit_bytes=24 * MIB),
    )(slots, valid, tiles)


def panel_kernel(code_ref, first_ref, front_ref, arrived_ref, out_ref):
    side = arrived_ref.shape[1]

    @pl.when(first_ref[0] == 1)
    def _():
        out_ref[...] = front_ref[...]

    @pl.when(first_ref[0] == 0)
    def _():
        out_ref[...] = jnp.zeros_like(out_ref)

    @pl.loop(0, arrived_ref.shape[0])
    def _(k):
        code = code_ref[k]
        for part in range(PANELS):

            @pl.when((code >= 0) & (code % PANELS == part))
            def _():
                rows = pl.ds(pl.multiple_of(code // PANELS * side, side), side)
                out_ref[rows, part * side : (part + 1) * side] += arrived_ref[k]


def raw_panel(front, arrived, codes, first):
    row_len = front.shape[0]
    smem = pl.BlockSpec(memory_space=pltpu.SMEM)
    return pl.pallas_call(
        panel_kernel,
        grid=(1,),
        out_shape=jax.ShapeDtypeStruct((row_len, TOTAL), jnp.float32),
        in_specs=[
            smem,
            smem,
            pl.BlockSpec((row_len, TOTAL), lambda i: (0, 0)),
            pl.BlockSpec(arrived.shape, lambda i: (0, 0, 0)),
        ],
        out_specs=pl.BlockSpec((row_len, TOTAL), lambda i: (0, 0)),
        compiler_params=pltpu.CompilerParams(vmem_limit_bytes=40 * MIB),
    )(codes, first, front, arrived)


def split(value):
    high = value.astype(jnp.bfloat16)
    low = (value - high.astype(jnp.float32)).astype(jnp.bfloat16)
    return high, low


def rows_kernel(raw_ref, inverse_ref, out_ref, high_ref, low_ref):
    solved = dot_nt(raw_ref[...], inverse_ref[...])
    out_ref[...] = solved
    high_ref[...], low_ref[...] = split(solved)


def solve_rows(raw, inverse):
    length = raw.shape[0]
    step = min(512, length)
    block = pl.BlockSpec((step, TOTAL), lambda i: (i, 0))
    return pl.pallas_call(
        rows_kernel,
        grid=(length // step,),
        out_shape=[
            jax.ShapeDtypeStruct((length, TOTAL), jnp.float32),
            jax.ShapeDtypeStruct((length, TOTAL), jnp.bfloat16),
            jax.ShapeDtypeStruct((length, TOTAL), jnp.bfloat16),
        ],
        in_specs=[block, pl.BlockSpec((TOTAL, TOTAL), lambda i: (0, 0))],
        out_specs=[block, block, block],
        compiler_params=pltpu.CompilerParams(vmem_limit_bytes=24 * MIB),
    )(raw, inverse)


def cols_kernel(raw_ref, inverse_ref, out_ref, high_ref, low_ref):
    solved = dot_nt(inverse_ref[...], raw_ref[...])
    out_ref[...] = solved
    high_ref[...], low_ref[...] = split(solved)


def solve_cols(raw, inverse):
    length = raw.shape[0]
    step = min(512, length)
    block = pl.BlockSpec((TOTAL, step), lambda i: (0, i))
    return pl.pallas_call(
        cols_kernel,
        grid=(length // step,),
        out_shape=[
            jax.ShapeDtypeStruct((TOTAL, length), jnp.float32),
            jax.ShapeDtypeStruct((TOTAL, length), jnp.bfloat16),
            jax.ShapeDtypeStruct((TOTAL, length), jnp.bfloat16),
        ],
        in_specs=[
            pl.BlockSpec((step, TOTAL), lambda i: (i, 0)),
            pl.BlockSpec((TOTAL, TOTAL), lambda i: (0, 0)),
        ],
        out_specs=[block, block, block],
        compiler_params=pltpu.CompilerParams(vmem_limit_bytes=24 * MIB),
    )(raw, inverse)


def final_kernel(
    cols_blocks, code_ref, place_ref, front_ref, rows_ref, rows_high, rows_low, cols_ref, cols_high,
    cols_low, lower_ref, arrived_ref, out_ref, cursor
):
    step = pl.program_id(0)
    sources, capacity = code_ref.shape
    height, width = front_ref.shape
    side = arrived_ref.shape[1]
    per_step = height // side

    @pl.when(step == 0)
    def _():
        for s in range(sources):
            cursor[s] = 0

    chunk = min(512, width)
    for start in range(0, width, chunk):
        at = slice(start, start + chunk)
        change = jnp.dot(rows_high[...], cols_high[:, at], preferred_element_type=jnp.float32)
        change += jnp.dot(rows_high[...], cols_low[:, at], preferred_element_type=jnp.float32)
        change += jnp.dot(rows_low[...], cols_high[:, at], preferred_element_type=jnp.float32)
        out_ref[:, at] = front_ref[:, at] - change

    edge = (step + 1) * per_step * cols_blocks

    @pl.loop(0, sources)
    def _(s):
        def more(k):
            code = code_ref[s, jnp.minimum(k, capacity - 1)]
            return (k < capacity) & (code >= 0) & (code < edge)

        def add(k):
            code = code_ref[s, k]
            block_row = code // cols_blocks - step * per_step
            block_col = code % cols_blocks
            rows = pl.ds(pl.multiple_of(block_row * side, side), side)
            columns = pl.ds(pl.multiple_of(block_col * side, side), side)
            out_ref[rows, columns] += arrived_ref[s * capacity + k]
            return k + 1

        cursor[s] = lax.while_loop(more, add, cursor[s])

    top = (place_ref[0] == 0) & (step == 0)

    @pl.when(top)
    def _():
        out_ref[...] = cols_ref[...]

    @pl.when(place_ref[1] == 0)
    def _():
        out_ref[:, :TOTAL] = jnp.where(top, lower_ref[...], rows_ref[...])


def finish(front, rows, cols, lower, arrived, codes, place, cols_blocks):
    row_len, col_len = front.shape
    height = TOTAL
    smem = pl.BlockSpec(memory_space=pltpu.SMEM)
    block = pl.BlockSpec((height, TOTAL), lambda i: (i, 0))
    wide = pl.BlockSpec((height, col_len), lambda i: (i, 0))
    whole = pl.BlockSpec((TOTAL, col_len), lambda i: (0, 0))
    return pl.pallas_call(
        functools.partial(final_kernel, cols_blocks),
        grid=(row_len // height,),
        out_shape=jax.ShapeDtypeStruct((row_len, col_len), jnp.float32),
        in_specs=[
            smem, smem, wide, block, block, block, whole, whole, whole,
            pl.BlockSpec((TOTAL, TOTAL), lambda i: (0, 0)),
            pl.BlockSpec(memory_space=pltpu.VMEM),
        ],
        out_specs=wide,
        scratch_shapes=[pltpu.SMEM((codes.shape[0],), jnp.int32)],
        compiler_params=pltpu.CompilerParams(vmem_limit_bytes=56 * MIB),
    )(codes, place, front, *rows, *cols, lower, arrived)


def factor(diagonal):
    def lower_of(block):
        return jnp.linalg.cholesky(jnp.tril(block) + jnp.tril(block, -1).T)

    def inverse_of(block):
        return jax.scipy.linalg.solve_triangular(block, jnp.eye(NB, dtype=jnp.float32), lower=True)

    first = lower_of(diagonal[:NB, :NB])
    first_inverse = inverse_of(first)
    below = dot_nt(diagonal[NB:, :NB], first_inverse)
    second = lower_of(diagonal[NB:, NB:] - dot_nt(below, below))
    second_inverse = inverse_of(second)
    corner = -jnp.dot(second_inverse, jnp.dot(below, first_inverse, precision=precise), precision=precise)
    zero = jnp.zeros((NB, NB), jnp.float32)
    return jnp.block([[first, zero], [below, second]]), jnp.block([[first_inverse, zero], [corner, second_inverse]])


def body(front, tiles, tile_block, valid_rows):
    row_len, col_len = front.shape
    row_count = lax.axis_size("row")
    col_count = lax.axis_size("col")
    device_count = row_count * col_count
    per_device = tiles.shape[0]
    side = tiles.shape[1]
    capacity = 2 * per_device // device_count
    rows_blocks = row_len // side
    cols_blocks = col_len // side
    row_now = lax.axis_index("row")
    col_now = lax.axis_index("col")
    device_now = row_now * col_count + col_now

    block_row = tile_block[0].reshape(device_count, per_device)
    block_col = tile_block[1].reshape(device_count, per_device)
    target_row = block_row // rows_blocks
    target = target_row * col_count + block_col // cols_blocks
    code = block_row % rows_blocks * cols_blocks + block_col % cols_blocks
    position = lax.broadcasted_iota(jnp.int32, target.shape, 1)
    place = jnp.stack([row_now, col_now]).astype(jnp.int32)

    def own(values):
        return lax.dynamic_index_in_dim(values, device_now, 0, keepdims=False)

    in_panel = block_col < PANELS
    panel_key = jnp.where(in_panel, target_row, -1)
    panel_rank = jnp.sum(
        (panel_key[:, :, None] == panel_key[:, None, :]) & (position[:, None, :] < position[:, :, None]),
        axis=2,
    )
    ahead = (own(target_row) - row_now) % row_count
    panel_slot = jnp.where(own(in_panel), ahead * capacity + own(panel_rank), -1)
    panel_out = pack(tiles, panel_slot, valid_rows, row_count * capacity)
    panel_in = [panel_out[:capacity]]
    for shift in range(1, row_count):
        sending = panel_out[shift * capacity : (shift + 1) * capacity]
        turn = [(r, (r + shift) % row_count) for r in range(row_count)]
        panel_in.append(lax.ppermute(sending, "row", turn))
    same_col = lax.dynamic_index_in_dim(
        jnp.stack([panel_key, panel_rank, code]).reshape(3, row_count, col_count, per_device),
        col_now, 2, keepdims=False,
    )
    slots = jnp.arange(capacity)
    fits = (same_col[0] == row_now)[:, :, None] & (same_col[1][:, :, None] == slots)
    panel_code = same_col[2] // cols_blocks * PANELS + same_col[2] % cols_blocks
    panel_codes = jnp.sum(jnp.where(fits, panel_code[:, :, None] + 1, 0), axis=1) - 1
    by_shift = (row_now - jnp.arange(row_count)) % row_count
    panel_codes = jnp.take(panel_codes, by_shift, axis=0).reshape(-1)

    order = (target * rows_blocks * cols_blocks + code) * per_device + position
    ranking = jnp.sum(
        (target[:, :, None] == target[:, None, :]) & (order[:, None, :] < order[:, :, None]), axis=2
    )
    slot = own(target) * capacity + own(ranking)
    here = (target == device_now)[:, :, None] & (ranking[:, :, None] == slots)
    codes = jnp.sum(jnp.where(here, code[:, :, None] + 1, 0), axis=1) - 1
    outgoing = pack(tiles, slot, valid_rows, device_count * capacity)
    outgoing, *panel_in = lax.optimization_barrier((outgoing, *panel_in))
    arrived = lax.all_to_all(
        outgoing.reshape(device_count, capacity, side, side), ("row", "col"), 0, 0, tiled=True
    ).reshape(device_count * capacity, side, side)

    first = (col_now == 0).astype(jnp.int32).reshape(1)
    partial = raw_panel(front, jnp.concatenate(panel_in, 0), panel_codes, first)
    raw_rows = lax.psum(partial, "col")
    slice_start = col_now * col_len % row_len
    slice_root = col_now * col_len // row_len
    picked = lax.dynamic_slice_in_dim(raw_rows, slice_start, col_len, 0)
    raw_cols = lax.psum(jnp.where(row_now == slice_root, picked, 0.0), "row")
    diagonal = jnp.where(row_now == 0, raw_rows[:TOTAL], jnp.eye(TOTAL, dtype=jnp.float32))
    lower, inverse = factor(diagonal)
    inverse = lax.psum(jnp.where(row_now == 0, inverse, 0.0), "row")
    rows = solve_rows(raw_rows, inverse)
    cols = solve_cols(raw_cols, inverse)
    return finish(front, rows, cols, lower, arrived, codes, place, cols_blocks)


def solution(mesh):
    placed = (P("row", "col"), P(("row", "col"), None, None), P(), P(("row", "col")))
    return jax.shard_map(
        body, mesh=mesh, in_specs=placed, out_specs=P("row", "col"), check_vma=False
    )
```

```python
import functools

import jax
import jax.numpy as jnp
from jax import lax
from jax.experimental import pallas as pl
from jax.experimental.pallas import tpu as pltpu
from jax.sharding import PartitionSpec as P

NB = 128
PANELS = 2
TOTAL = NB * PANELS
MIB = 1 << 20
UNIT = 8


precise = lax.Precision.HIGHEST


def dot_nt(a, b, precision=precise):
    return lax.dot_general(
        a, b, (((1,), (1,)), ((), ())), precision=precision, preferred_element_type=jnp.float32
    )


def pack_kernel(slot_ref, valid_ref, tiles_ref, out_ref, buf, sem):
    count, side = tiles_ref.shape[0], tiles_ref.shape[1]
    half = side // 2

    def store(t):
        return pltpu.make_async_copy(buf.at[t], out_ref.at[jnp.maximum(slot_ref[t], 0)], sem.at[t])

    def each(act):
        @pl.loop(0, count)
        def _(t):
            @pl.when(slot_ref[t] >= 0)
            def _():
                act(t)

    def mask(t):
        rows = lax.broadcasted_iota(jnp.int32, (half, side), 0) + half
        buf[t, :half] = tiles_ref[t, :half]
        buf[t, half:] = jnp.where(rows < valid_ref[t], tiles_ref[t, half:], 0.0)
        store(t).start()

    each(mask)
    each(lambda t: store(t).wait())


def pack(tiles, slots, valid, n_slots):
    count, side = tiles.shape[0], tiles.shape[1]
    smem = pl.BlockSpec(memory_space=pltpu.SMEM)
    return pl.pallas_call(
        pack_kernel,
        out_shape=jax.ShapeDtypeStruct((n_slots, side, side), jnp.float32),
        in_specs=[smem, smem, pl.BlockSpec(memory_space=pltpu.VMEM)],
        out_specs=pl.BlockSpec(memory_space=pl.ANY),
        scratch_shapes=[
            pltpu.VMEM((count, side, side), jnp.float32),
            pltpu.SemaphoreType.DMA((count,)),
        ],
        compiler_params=pltpu.CompilerParams(vmem_limit_bytes=24 * MIB),
    )(slots, valid, tiles)


def spread_kernel(
    width, stride, meta_ref, empty_ref, count_ref, tiles_ref, out_ref, code_ref, stage, sem
):
    count, units = tiles_ref.shape[0], tiles_ref.shape[1]
    devices, length = code_ref.shape

    @pl.loop(0, devices)
    def _(d):
        for k in range(length):
            code_ref[d, k] = -1

    @pl.loop(0, count)
    def _(i):
        tile, target, base = meta_ref[0, i], meta_ref[1, i], meta_ref[2, i]
        filled, code, valid = meta_ref[3, i], meta_ref[4, i], meta_ref[5, i]
        shape = tiles_ref.shape[1:]
        rows = lax.broadcasted_iota(jnp.int32, shape, 0) * shape[1]
        rows += lax.broadcasted_iota(jnp.int32, shape, 1)
        stage[target, pl.ds(base, units)] = jnp.where(rows < valid, tiles_ref[tile], 0.0)
        for u in range(units):
            code_ref[target, base + u] = jnp.where(u < filled, code + u * stride, -1)

    for half in range(2):
        first = 0 if half == 0 else count_ref[0]
        last = count_ref[0] if half == 0 else count
        free = count_ref[1 + half]

        def each_tile(i, carry):
            target, base, filled = meta_ref[1, i], meta_ref[2, i], meta_ref[3, i]

            def each_unit(q, carry):
                at, depth = carry
                relay = empty_ref[half, at]
                place = jnp.minimum(depth, width - 1)
                stage[relay, place] = stage[target, q]
                code_ref[relay, place] = code_ref[target, q]
                wrap = at + 1 >= free
                return jnp.where(wrap, 0, at + 1), jnp.where(wrap, depth + 1, depth)

            return lax.fori_loop(jnp.maximum(base, width), base + filled, each_unit, carry)

        lax.fori_loop(first, last, each_tile, (jnp.int32(0), jnp.int32(0)))

    copy = pltpu.make_async_copy(stage.at[:, pl.ds(0, width)], out_ref, sem)
    copy.start()
    copy.wait()


def spread(tiles, meta, empties, counts, devices, width, length, stride):
    count, side = tiles.shape[0], tiles.shape[1]
    units = side // UNIT
    smem = pl.BlockSpec(memory_space=pltpu.SMEM)
    return pl.pallas_call(
        functools.partial(spread_kernel, width, stride),
        out_shape=[
            jax.ShapeDtypeStruct((devices, width, UNIT, side), jnp.float32),
            jax.ShapeDtypeStruct((devices, length), jnp.int32),
        ],
        in_specs=[smem, smem, smem, pl.BlockSpec(memory_space=pltpu.VMEM)],
        out_specs=[pl.BlockSpec(memory_space=pl.ANY), smem],
        scratch_shapes=[
            pltpu.VMEM((devices, length, UNIT, side), jnp.float32),
            pltpu.SemaphoreType.DMA,
        ],
        compiler_params=pltpu.CompilerParams(vmem_limit_bytes=40 * MIB),
    )(meta, empties, counts, tiles.reshape(count, units, UNIT, side))


def relay_kernel(slot_ref, arrived_ref, out_ref):
    devices, width = slot_ref.shape

    @pl.loop(0, devices)
    def _(s):
        def more(k):
            return (k < width) & (slot_ref[s, jnp.minimum(k, width - 1)] >= 0)

        def move(k):
            out_ref[slot_ref[s, k]] = arrived_ref[s, k]
            return k + 1

        lax.while_loop(more, move, jnp.int32(0))


def relay(slots, arrived, length):
    vmem = pl.BlockSpec(memory_space=pltpu.VMEM)
    return pl.pallas_call(
        relay_kernel,
        out_shape=jax.ShapeDtypeStruct((length,) + arrived.shape[2:], jnp.float32),
        in_specs=[pl.BlockSpec(memory_space=pltpu.SMEM), vmem],
        out_specs=vmem,
        compiler_params=pltpu.CompilerParams(vmem_limit_bytes=40 * MIB),
    )(slots, arrived)


def add_kernel(cols_blocks, code_ref, place_ref, partial_ref, arrived_ref, out_ref, cursor):
    step = pl.program_id(0)
    sources, capacity = code_ref.shape
    unit, side = arrived_ref.shape[2:]
    per_step = partial_ref.shape[0] // unit

    @pl.when(step == 0)
    def _():
        for s in range(sources):
            cursor[s] = 0

    out_ref[...] = partial_ref[...]
    edge = (step + 1) * per_step * cols_blocks

    @pl.loop(0, sources)
    def _(s):
        def more(k):
            code = code_ref[s, jnp.minimum(k, capacity - 1)]
            return (k < capacity) & (code >= 0) & (code < edge)

        def add(k):
            code = code_ref[s, k]
            unit_row = code // cols_blocks - step * per_step
            block_col = code % cols_blocks
            fixed = (place_ref[0] == 0) & (step == 0)
            fixed |= (place_ref[1] == 0) & (block_col < PANELS)

            @pl.when(jnp.logical_not(fixed))
            def _():
                rows = pl.ds(pl.multiple_of(unit_row * unit, unit), unit)
                columns = pl.ds(pl.multiple_of(block_col * side, side), side)
                out_ref[rows, columns] += arrived_ref[s, k]

            return k + 1

        cursor[s] = lax.while_loop(more, add, cursor[s])


def add_relayed(partial, arrived, codes, place, cols_blocks):
    row_len, col_len = partial.shape
    smem = pl.BlockSpec(memory_space=pltpu.SMEM)
    wide = pl.BlockSpec((TOTAL, col_len), lambda i: (i, 0))
    return pl.pallas_call(
        functools.partial(add_kernel, cols_blocks),
        grid=(row_len // TOTAL,),
        out_shape=jax.ShapeDtypeStruct((row_len, col_len), jnp.float32),
        in_specs=[smem, smem, wide, pl.BlockSpec(memory_space=pltpu.VMEM)],
        out_specs=wide,
        scratch_shapes=[pltpu.SMEM((codes.shape[0],), jnp.int32)],
        input_output_aliases={2: 0},
        compiler_params=pltpu.CompilerParams(vmem_limit_bytes=40 * MIB),
    )(codes, place, partial, arrived)


def panel_kernel(code_ref, first_ref, front_ref, arrived_ref, out_ref):
    side = arrived_ref.shape[1]

    @pl.when(first_ref[0] == 1)
    def _():
        out_ref[...] = front_ref[...]

    @pl.when(first_ref[0] == 0)
    def _():
        out_ref[...] = jnp.zeros_like(out_ref)

    @pl.loop(0, arrived_ref.shape[0])
    def _(k):
        code = code_ref[k]
        for part in range(PANELS):

            @pl.when((code >= 0) & (code % PANELS == part))
            def _():
                rows = pl.ds(pl.multiple_of(code // PANELS * side, side), side)
                out_ref[rows, part * side : (part + 1) * side] += arrived_ref[k]


def raw_panel(front, arrived, codes, first):
    row_len = front.shape[0]
    smem = pl.BlockSpec(memory_space=pltpu.SMEM)
    return pl.pallas_call(
        panel_kernel,
        grid=(1,),
        out_shape=jax.ShapeDtypeStruct((row_len, TOTAL), jnp.float32),
        in_specs=[
            smem,
            smem,
            pl.BlockSpec((row_len, TOTAL), lambda i: (0, 0)),
            pl.BlockSpec(arrived.shape, lambda i: (0, 0, 0)),
        ],
        out_specs=pl.BlockSpec((row_len, TOTAL), lambda i: (0, 0)),
        compiler_params=pltpu.CompilerParams(vmem_limit_bytes=40 * MIB),
    )(codes, first, front, arrived)


def split(value):
    high = value.astype(jnp.bfloat16)
    low = (value - high.astype(jnp.float32)).astype(jnp.bfloat16)
    return high, low


def rows_kernel(raw_ref, inverse_ref, out_ref, high_ref, low_ref):
    solved = dot_nt(raw_ref[...], inverse_ref[...])
    out_ref[...] = solved
    high_ref[...], low_ref[...] = split(solved)


def solve_rows(raw, inverse):
    length = raw.shape[0]
    step = min(512, length)
    block = pl.BlockSpec((step, TOTAL), lambda i: (i, 0))
    return pl.pallas_call(
        rows_kernel,
        grid=(length // step,),
        out_shape=[
            jax.ShapeDtypeStruct((length, TOTAL), jnp.float32),
            jax.ShapeDtypeStruct((length, TOTAL), jnp.bfloat16),
            jax.ShapeDtypeStruct((length, TOTAL), jnp.bfloat16),
        ],
        in_specs=[block, pl.BlockSpec((TOTAL, TOTAL), lambda i: (0, 0))],
        out_specs=[block, block, block],
        compiler_params=pltpu.CompilerParams(vmem_limit_bytes=24 * MIB),
    )(raw, inverse)


def cols_kernel(raw_ref, inverse_ref, out_ref, high_ref, low_ref):
    solved = dot_nt(inverse_ref[...], raw_ref[...])
    out_ref[...] = solved
    high_ref[...], low_ref[...] = split(solved)


def solve_cols(raw, inverse):
    length = raw.shape[0]
    step = min(512, length)
    block = pl.BlockSpec((TOTAL, step), lambda i: (0, i))
    return pl.pallas_call(
        cols_kernel,
        grid=(length // step,),
        out_shape=[
            jax.ShapeDtypeStruct((TOTAL, length), jnp.float32),
            jax.ShapeDtypeStruct((TOTAL, length), jnp.bfloat16),
            jax.ShapeDtypeStruct((TOTAL, length), jnp.bfloat16),
        ],
        in_specs=[
            pl.BlockSpec((step, TOTAL), lambda i: (i, 0)),
            pl.BlockSpec((TOTAL, TOTAL), lambda i: (0, 0)),
        ],
        out_specs=[block, block, block],
        compiler_params=pltpu.CompilerParams(vmem_limit_bytes=24 * MIB),
    )(raw, inverse)


def final_kernel(
    cols_blocks, code_ref, place_ref, front_ref, rows_ref, rows_high, rows_low, cols_ref, cols_high,
    cols_low, lower_ref, arrived_ref, out_ref, cursor
):
    step = pl.program_id(0)
    sources, capacity = code_ref.shape
    height, width = front_ref.shape
    unit, side = arrived_ref.shape[2:]
    per_step = height // unit

    @pl.when(step == 0)
    def _():
        for s in range(sources):
            cursor[s] = 0

    chunk = min(512, width)
    for start in range(0, width, chunk):
        at = slice(start, start + chunk)
        change = jnp.dot(rows_high[...], cols_high[:, at], preferred_element_type=jnp.float32)
        change += jnp.dot(rows_high[...], cols_low[:, at], preferred_element_type=jnp.float32)
        change += jnp.dot(rows_low[...], cols_high[:, at], preferred_element_type=jnp.float32)
        out_ref[:, at] = front_ref[:, at] - change

    edge = (step + 1) * per_step * cols_blocks

    @pl.loop(0, sources)
    def _(s):
        def more(k):
            code = code_ref[s, jnp.minimum(k, capacity - 1)]
            return (k < capacity) & (code >= 0) & (code < edge)

        def add(k):
            code = code_ref[s, k]
            unit_row = code // cols_blocks - step * per_step
            block_col = code % cols_blocks
            rows = pl.ds(pl.multiple_of(unit_row * unit, unit), unit)
            columns = pl.ds(pl.multiple_of(block_col * side, side), side)
            out_ref[rows, columns] += arrived_ref[s, k]
            return k + 1

        cursor[s] = lax.while_loop(more, add, cursor[s])

    top = (place_ref[0] == 0) & (step == 0)

    @pl.when(top)
    def _():
        out_ref[...] = cols_ref[...]

    @pl.when(place_ref[1] == 0)
    def _():
        out_ref[:, :TOTAL] = jnp.where(top, lower_ref[...], rows_ref[...])


def finish(front, rows, cols, lower, arrived, codes, place, cols_blocks):
    row_len, col_len = front.shape
    height = TOTAL
    smem = pl.BlockSpec(memory_space=pltpu.SMEM)
    block = pl.BlockSpec((height, TOTAL), lambda i: (i, 0))
    wide = pl.BlockSpec((height, col_len), lambda i: (i, 0))
    whole = pl.BlockSpec((TOTAL, col_len), lambda i: (0, 0))
    return pl.pallas_call(
        functools.partial(final_kernel, cols_blocks),
        grid=(row_len // height,),
        out_shape=jax.ShapeDtypeStruct((row_len, col_len), jnp.float32),
        in_specs=[
            smem, smem, wide, block, block, block, whole, whole, whole,
            pl.BlockSpec((TOTAL, TOTAL), lambda i: (0, 0)),
            pl.BlockSpec(memory_space=pltpu.VMEM),
        ],
        out_specs=wide,
        scratch_shapes=[pltpu.SMEM((codes.shape[0],), jnp.int32)],
        compiler_params=pltpu.CompilerParams(vmem_limit_bytes=56 * MIB),
    )(codes, place, front, *rows, *cols, lower, arrived)


def factor(diagonal):
    def lower_of(block):
        return jnp.linalg.cholesky(jnp.tril(block) + jnp.tril(block, -1).T)

    def inverse_of(block):
        return jax.scipy.linalg.solve_triangular(block, jnp.eye(NB, dtype=jnp.float32), lower=True)

    first = lower_of(diagonal[:NB, :NB])
    first_inverse = inverse_of(first)
    below = dot_nt(diagonal[NB:, :NB], first_inverse)
    second = lower_of(diagonal[NB:, NB:] - dot_nt(below, below))
    second_inverse = inverse_of(second)
    corner = -jnp.dot(second_inverse, jnp.dot(below, first_inverse, precision=precise), precision=precise)
    zero = jnp.zeros((NB, NB), jnp.float32)
    return jnp.block([[first, zero], [below, second]]), jnp.block([[first_inverse, zero], [corner, second_inverse]])


def body(front, tiles, tile_block, valid_rows):
    row_len, col_len = front.shape
    row_count = lax.axis_size("row")
    col_count = lax.axis_size("col")
    device_count = row_count * col_count
    per_device = tiles.shape[0]
    side = tiles.shape[1]
    capacity = 2 * per_device // device_count
    rows_blocks = row_len // side
    cols_blocks = col_len // side
    row_now = lax.axis_index("row")
    col_now = lax.axis_index("col")
    device_now = row_now * col_count + col_now

    block_row = tile_block[0].reshape(device_count, per_device)
    block_col = tile_block[1].reshape(device_count, per_device)
    target_row = block_row // rows_blocks
    target = target_row * col_count + block_col // cols_blocks
    code = block_row % rows_blocks * cols_blocks + block_col % cols_blocks
    position = lax.broadcasted_iota(jnp.int32, target.shape, 1)
    place = jnp.stack([row_now, col_now]).astype(jnp.int32)

    def own(values):
        return lax.dynamic_index_in_dim(values, device_now, 0, keepdims=False)

    in_panel = block_col < PANELS
    panel_key = jnp.where(in_panel, target_row, -1)
    panel_rank = jnp.sum(
        (panel_key[:, :, None] == panel_key[:, None, :]) & (position[:, None, :] < position[:, :, None]),
        axis=2,
    )
    ahead = (own(target_row) - row_now) % row_count
    panel_slot = jnp.where(own(in_panel), ahead * capacity + own(panel_rank), -1)
    panel_out = pack(tiles, panel_slot, valid_rows, row_count * capacity)
    panel_in = [panel_out[:capacity]]
    for shift in range(1, row_count):
        sending = panel_out[shift * capacity : (shift + 1) * capacity]
        turn = [(r, (r + shift) % row_count) for r in range(row_count)]
        panel_in.append(lax.ppermute(sending, "row", turn))
    same_col = lax.dynamic_index_in_dim(
        jnp.stack([panel_key, panel_rank, code]).reshape(3, row_count, col_count, per_device),
        col_now, 2, keepdims=False,
    )
    slots = jnp.arange(capacity)
    fits = (same_col[0] == row_now)[:, :, None] & (same_col[1][:, :, None] == slots)
    panel_code = same_col[2] // cols_blocks * PANELS + same_col[2] % cols_blocks
    panel_codes = jnp.sum(jnp.where(fits, panel_code[:, :, None] + 1, 0), axis=1) - 1
    by_shift = (row_now - jnp.arange(row_count)) % row_count
    panel_codes = jnp.take(panel_codes, by_shift, axis=0).reshape(-1)

    units = side // UNIT
    length = capacity * units
    width = length * 9 // 16
    pass_on = length * 3 // 8
    half_count = device_count // 2
    half_base = device_now // half_count * half_count
    unit_rows = rows_blocks * units
    local_codes = unit_rows * cols_blocks
    own_target, own_code = own(target), own(code)
    own_position = own(position)
    filled = (valid_rows + UNIT - 1) // UNIT
    key = (own_target * rows_blocks * cols_blocks + own_code) * per_device + own_position
    before = key[None, :] < key[:, None]
    together = own_target[None, :] == own_target[:, None]
    base = jnp.sum(jnp.where(before & together, filled[None, :], 0), axis=1)
    order = jnp.sum(before, axis=1)
    unit_code = (own_target * unit_rows + own_code // cols_blocks * units) * cols_blocks
    unit_code += own_code % cols_blocks
    meta = jnp.stack([own_position, own_target, base, filled, unit_code, valid_rows])
    meta = jnp.sum(
        jnp.where(order[None, :, None] == jnp.arange(per_device), meta[:, :, None], 0), axis=1
    )
    to_device = own_target[:, None] == jnp.arange(device_count)
    load = jnp.sum(jnp.where(to_device, filled[:, None], 0), axis=0).reshape(2, half_count)
    empty = load == 0
    empty_rank = jnp.cumsum(empty, axis=1) - 1
    device_ids = jnp.arange(device_count).reshape(2, half_count)
    listed = (empty[:, :, None]) & (empty_rank[:, :, None] == jnp.arange(half_count))
    empties = jnp.sum(jnp.where(listed, device_ids[:, :, None], 0), axis=1)
    free = jnp.sum(empty, axis=1)
    left = jnp.sum(jnp.maximum(load - width, 0), axis=1)
    failed = jnp.any(left > free * width)
    counts = jnp.concatenate([jnp.sum(own_target < half_count)[None], free]).astype(jnp.int32)
    outgoing, sent_codes = spread(
        tiles, meta.astype(jnp.int32), empties.astype(jnp.int32), counts,
        device_count, width, length, cols_blocks,
    )

    got = lax.all_to_all(sent_codes[:, :width], ("row", "col"), 0, 0, tiled=True)
    got_target = got // local_codes
    local = got % local_codes
    mine = (got >= 0) & (got_target == device_now)
    direct_codes = jnp.where(mine, local, -1)
    total_units = device_count * width
    passing = ((got >= 0) & (got_target != device_now)).reshape(-1)
    flat_key = jnp.where(passing, got.reshape(-1) * total_units + jnp.arange(total_units), -1)
    flat_target = jnp.where(passing, got_target.reshape(-1), -1)
    rank = jnp.sum(
        (flat_target[None, :] == flat_target[:, None]) & (flat_key[None, :] < flat_key[:, None]), axis=1
    )
    failed = failed | jnp.any(passing & (rank >= pass_on))
    relay_slot = jnp.where(
        passing & (rank < pass_on), (flat_target - half_base) * pass_on + rank, -1
    )
    picked = relay_slot[:, None] == jnp.arange(half_count * pass_on)
    relay_codes = jnp.sum(jnp.where(picked, local.reshape(-1)[:, None] + 1, 0), axis=0) - 1
    notes = jnp.zeros((2, half_count, pass_on + 1), jnp.int32)
    notes = lax.dynamic_update_slice(
        notes, relay_codes.reshape(1, half_count, pass_on).astype(jnp.int32), (device_now // half_count, 0, 0)
    )
    notes = notes.at[:, :, pass_on].set(failed.astype(jnp.int32))
    notes = lax.all_to_all(
        notes.reshape(device_count, pass_on + 1), ("row", "col"), 0, 0, tiled=True
    )
    too_full = jnp.any(notes[:, pass_on] != 0)
    relay_codes = lax.dynamic_slice_in_dim(notes, half_base, half_count, 0)[:, :pass_on]
    relay_slot = relay_slot.reshape(device_count, width)

    first = (col_now == 0).astype(jnp.int32).reshape(1)
    partial = raw_panel(front, jnp.concatenate(panel_in, 0), panel_codes, first)
    raw_rows = lax.psum(partial, "col")
    slice_start = col_now * col_len % row_len
    slice_root = col_now * col_len // row_len

    def chain(raw_rows):
        picked = lax.dynamic_slice_in_dim(raw_rows, slice_start, col_len, 0)
        raw_cols = lax.psum(jnp.where(row_now == slice_root, picked, 0.0), "row")
        diagonal = jnp.where(row_now == 0, raw_rows[:TOTAL], jnp.eye(TOTAL, dtype=jnp.float32))
        lower, inverse = factor(diagonal)
        inverse, raw_cols = lax.optimization_barrier((inverse, raw_cols))
        inverse = lax.psum(jnp.where(row_now == 0, inverse, 0.0), "row")
        return solve_rows(raw_rows, inverse), solve_cols(raw_cols, inverse), lower

    def relayed(front, tiles, valid_rows, outgoing, raw_rows):
        arrived = lax.all_to_all(outgoing, ("row", "col"), 0, 0, tiled=True)
        rows, cols, lower = chain(raw_rows)
        passed = relay(relay_slot, arrived, half_count * pass_on)
        halves = [list(range(half_count)), list(range(half_count, device_count))]
        passed = lax.all_to_all(
            passed.reshape(half_count, pass_on, UNIT, side), ("row", "col"), 0, 0,
            axis_index_groups=halves, tiled=True,
        )
        partial = finish(front, rows, cols, lower, arrived, direct_codes, place, cols_blocks)
        return add_relayed(partial, passed, relay_codes, place, cols_blocks)

    def padded(front, tiles, valid_rows, outgoing, raw_rows):
        order = (target * rows_blocks * cols_blocks + code) * per_device + position
        ranking = jnp.sum(
            (target[:, :, None] == target[:, None, :]) & (order[:, None, :] < order[:, :, None]), axis=2
        )
        slot = own(target) * capacity + own(ranking)
        here = (target == device_now)[:, :, None] & (ranking[:, :, None] == slots)
        codes = jnp.sum(jnp.where(here, code[:, :, None] + 1, 0), axis=1) - 1
        packed = pack(tiles, slot, valid_rows, device_count * capacity)
        arrived = lax.all_to_all(
            packed.reshape(device_count, capacity, side, side), ("row", "col"), 0, 0, tiled=True
        )
        rows, cols, lower = chain(raw_rows)
        return finish(front, rows, cols, lower, arrived, codes, place, cols_blocks)

    return lax.cond(too_full, padded, relayed, front, tiles, valid_rows, outgoing, raw_rows)


def solution(mesh):
    placed = (P("row", "col"), P(("row", "col"), None, None), P(), P(("row", "col")))
    return jax.shard_map(
        body, mesh=mesh, in_specs=placed, out_specs=P("row", "col"), check_vma=False
    )
```

```python
import functools

import jax
import jax.numpy as jnp
from jax import lax
from jax.experimental import pallas as pl
from jax.experimental.pallas import tpu as pltpu
from jax.sharding import PartitionSpec as P

NB = 128
PANELS = 2
TOTAL = NB * PANELS
MIB = 1 << 20
UNIT = 8


precise = lax.Precision.HIGHEST


def dot_nt(a, b, precision=precise):
    return lax.dot_general(
        a, b, (((1,), (1,)), ((), ())), precision=precision, preferred_element_type=jnp.float32
    )


def pack_kernel(slot_ref, valid_ref, tiles_ref, out_ref, buf, sem):
    count, side = tiles_ref.shape[0], tiles_ref.shape[1]
    half = side // 2

    def store(t):
        return pltpu.make_async_copy(buf.at[t], out_ref.at[jnp.maximum(slot_ref[t], 0)], sem.at[t])

    def each(act):
        @pl.loop(0, count)
        def _(t):
            @pl.when(slot_ref[t] >= 0)
            def _():
                act(t)

    def mask(t):
        rows = lax.broadcasted_iota(jnp.int32, (half, side), 0) + half
        buf[t, :half] = tiles_ref[t, :half]
        buf[t, half:] = jnp.where(rows < valid_ref[t], tiles_ref[t, half:], 0.0)
        store(t).start()

    each(mask)
    each(lambda t: store(t).wait())


def pack(tiles, slots, valid, n_slots):
    count, side = tiles.shape[0], tiles.shape[1]
    smem = pl.BlockSpec(memory_space=pltpu.SMEM)
    return pl.pallas_call(
        pack_kernel,
        out_shape=jax.ShapeDtypeStruct((n_slots, side, side), jnp.float32),
        in_specs=[smem, smem, pl.BlockSpec(memory_space=pltpu.VMEM)],
        out_specs=pl.BlockSpec(memory_space=pl.ANY),
        scratch_shapes=[
            pltpu.VMEM((count, side, side), jnp.float32),
            pltpu.SemaphoreType.DMA((count,)),
        ],
        compiler_params=pltpu.CompilerParams(vmem_limit_bytes=24 * MIB),
    )(slots, valid, tiles)


def spread_kernel(
    width, stride, meta_ref, empty_ref, count_ref, tiles_ref, out_ref, code_ref, stage, sem
):
    count, units = tiles_ref.shape[0], tiles_ref.shape[1]
    devices, length = code_ref.shape

    @pl.loop(0, devices)
    def _(d):
        for k in range(length):
            code_ref[d, k] = -1

    @pl.loop(0, count)
    def _(i):
        tile, target, base = meta_ref[0, i], meta_ref[1, i], meta_ref[2, i]
        filled, code, valid = meta_ref[3, i], meta_ref[4, i], meta_ref[5, i]
        shape = tiles_ref.shape[1:]
        rows = lax.broadcasted_iota(jnp.int32, shape, 0) * shape[1]
        rows += lax.broadcasted_iota(jnp.int32, shape, 1)
        stage[target, pl.ds(base, units)] = jnp.where(rows < valid, tiles_ref[tile], 0.0)
        for u in range(units):
            code_ref[target, base + u] = jnp.where(u < filled, code + u * stride, -1)

    for half in range(2):
        first = 0 if half == 0 else count_ref[0]
        last = count_ref[0] if half == 0 else count
        free = count_ref[1 + half]

        def each_tile(i, carry):
            target, base, filled = meta_ref[1, i], meta_ref[2, i], meta_ref[3, i]

            def each_unit(q, carry):
                at, depth = carry
                relay = empty_ref[half, at]
                place = jnp.minimum(depth, width - 1)
                stage[relay, place] = stage[target, q]
                code_ref[relay, place] = code_ref[target, q]
                wrap = at + 1 >= free
                return jnp.where(wrap, 0, at + 1), jnp.where(wrap, depth + 1, depth)

            return lax.fori_loop(jnp.maximum(base, width), base + filled, each_unit, carry)

        lax.fori_loop(first, last, each_tile, (jnp.int32(0), jnp.int32(0)))

    copy = pltpu.make_async_copy(stage.at[:, pl.ds(0, width)], out_ref, sem)
    copy.start()
    copy.wait()


def spread(tiles, meta, empties, counts, devices, width, length, stride):
    count, side = tiles.shape[0], tiles.shape[1]
    units = side // UNIT
    smem = pl.BlockSpec(memory_space=pltpu.SMEM)
    return pl.pallas_call(
        functools.partial(spread_kernel, width, stride),
        out_shape=[
            jax.ShapeDtypeStruct((devices, width, UNIT, side), jnp.float32),
            jax.ShapeDtypeStruct((devices, length), jnp.int32),
        ],
        in_specs=[smem, smem, smem, pl.BlockSpec(memory_space=pltpu.VMEM)],
        out_specs=[pl.BlockSpec(memory_space=pl.ANY), smem],
        scratch_shapes=[
            pltpu.VMEM((devices, length, UNIT, side), jnp.float32),
            pltpu.SemaphoreType.DMA,
        ],
        compiler_params=pltpu.CompilerParams(vmem_limit_bytes=40 * MIB),
    )(meta, empties, counts, tiles.reshape(count, units, UNIT, side))


def relay_kernel(slot_ref, arrived_ref, out_ref):
    devices, width = slot_ref.shape

    @pl.loop(0, devices)
    def _(s):
        def more(k):
            return (k < width) & (slot_ref[s, jnp.minimum(k, width - 1)] >= 0)

        def move(k):
            out_ref[slot_ref[s, k]] = arrived_ref[s, k]
            return k + 1

        lax.while_loop(more, move, jnp.int32(0))


def relay(slots, arrived, length):
    vmem = pl.BlockSpec(memory_space=pltpu.VMEM)
    return pl.pallas_call(
        relay_kernel,
        out_shape=jax.ShapeDtypeStruct((length,) + arrived.shape[2:], jnp.float32),
        in_specs=[pl.BlockSpec(memory_space=pltpu.SMEM), vmem],
        out_specs=vmem,
        compiler_params=pltpu.CompilerParams(vmem_limit_bytes=40 * MIB),
    )(slots, arrived)


def add_kernel(cols_blocks, code_ref, place_ref, partial_ref, arrived_ref, out_ref, cursor):
    step = pl.program_id(0)
    sources, capacity = code_ref.shape
    unit, side = arrived_ref.shape[2:]
    per_step = partial_ref.shape[0] // unit

    @pl.when(step == 0)
    def _():
        for s in range(sources):
            cursor[s] = 0

    out_ref[...] = partial_ref[...]
    edge = (step + 1) * per_step * cols_blocks

    @pl.loop(0, sources)
    def _(s):
        def more(k):
            code = code_ref[s, jnp.minimum(k, capacity - 1)]
            return (k < capacity) & (code >= 0) & (code < edge)

        def add(k):
            code = code_ref[s, k]
            unit_row = code // cols_blocks - step * per_step
            block_col = code % cols_blocks
            fixed = (place_ref[0] == 0) & (step == 0)
            fixed |= (place_ref[1] == 0) & (block_col < PANELS)

            @pl.when(jnp.logical_not(fixed))
            def _():
                rows = pl.ds(pl.multiple_of(unit_row * unit, unit), unit)
                columns = pl.ds(pl.multiple_of(block_col * side, side), side)
                out_ref[rows, columns] += arrived_ref[s, k]

            return k + 1

        cursor[s] = lax.while_loop(more, add, cursor[s])


def add_relayed(partial, arrived, codes, place, cols_blocks):
    row_len, col_len = partial.shape
    smem = pl.BlockSpec(memory_space=pltpu.SMEM)
    wide = pl.BlockSpec((TOTAL, col_len), lambda i: (i, 0))
    return pl.pallas_call(
        functools.partial(add_kernel, cols_blocks),
        grid=(row_len // TOTAL,),
        out_shape=jax.ShapeDtypeStruct((row_len, col_len), jnp.float32),
        in_specs=[smem, smem, wide, pl.BlockSpec(memory_space=pltpu.VMEM)],
        out_specs=wide,
        scratch_shapes=[pltpu.SMEM((codes.shape[0],), jnp.int32)],
        input_output_aliases={2: 0},
        compiler_params=pltpu.CompilerParams(vmem_limit_bytes=40 * MIB),
    )(codes, place, partial, arrived)


def panel_kernel(code_ref, first_ref, front_ref, arrived_ref, out_ref):
    side = arrived_ref.shape[1]

    @pl.when(first_ref[0] == 1)
    def _():
        out_ref[...] = front_ref[...]

    @pl.when(first_ref[0] == 0)
    def _():
        out_ref[...] = jnp.zeros_like(out_ref)

    @pl.loop(0, arrived_ref.shape[0])
    def _(k):
        code = code_ref[k]
        for part in range(PANELS):

            @pl.when((code >= 0) & (code % PANELS == part))
            def _():
                rows = pl.ds(pl.multiple_of(code // PANELS * side, side), side)
                out_ref[rows, part * side : (part + 1) * side] += arrived_ref[k]


def raw_panel(front, arrived, codes, first):
    row_len = front.shape[0]
    smem = pl.BlockSpec(memory_space=pltpu.SMEM)
    return pl.pallas_call(
        panel_kernel,
        grid=(1,),
        out_shape=jax.ShapeDtypeStruct((row_len, TOTAL), jnp.float32),
        in_specs=[
            smem,
            smem,
            pl.BlockSpec((row_len, TOTAL), lambda i: (0, 0)),
            pl.BlockSpec(arrived.shape, lambda i: (0, 0, 0)),
        ],
        out_specs=pl.BlockSpec((row_len, TOTAL), lambda i: (0, 0)),
        compiler_params=pltpu.CompilerParams(vmem_limit_bytes=40 * MIB),
    )(codes, first, front, arrived)


def split(value):
    high = value.astype(jnp.bfloat16)
    low = (value - high.astype(jnp.float32)).astype(jnp.bfloat16)
    return high, low


def rows_kernel(raw_ref, inverse_ref, out_ref, high_ref, low_ref):
    solved = dot_nt(raw_ref[...], inverse_ref[...])
    out_ref[...] = solved
    high_ref[...], low_ref[...] = split(solved)


def solve_rows(raw, inverse):
    length = raw.shape[0]
    step = min(512, length)
    block = pl.BlockSpec((step, TOTAL), lambda i: (i, 0))
    return pl.pallas_call(
        rows_kernel,
        grid=(length // step,),
        out_shape=[
            jax.ShapeDtypeStruct((length, TOTAL), jnp.float32),
            jax.ShapeDtypeStruct((length, TOTAL), jnp.bfloat16),
            jax.ShapeDtypeStruct((length, TOTAL), jnp.bfloat16),
        ],
        in_specs=[block, pl.BlockSpec((TOTAL, TOTAL), lambda i: (0, 0))],
        out_specs=[block, block, block],
        compiler_params=pltpu.CompilerParams(vmem_limit_bytes=24 * MIB),
    )(raw, inverse)


def cols_kernel(raw_ref, inverse_ref, out_ref, high_ref, low_ref):
    solved = dot_nt(inverse_ref[...], raw_ref[...])
    out_ref[...] = solved
    high_ref[...], low_ref[...] = split(solved)


def solve_cols(raw, inverse):
    length = raw.shape[0]
    step = min(512, length)
    block = pl.BlockSpec((TOTAL, step), lambda i: (0, i))
    return pl.pallas_call(
        cols_kernel,
        grid=(length // step,),
        out_shape=[
            jax.ShapeDtypeStruct((TOTAL, length), jnp.float32),
            jax.ShapeDtypeStruct((TOTAL, length), jnp.bfloat16),
            jax.ShapeDtypeStruct((TOTAL, length), jnp.bfloat16),
        ],
        in_specs=[
            pl.BlockSpec((step, TOTAL), lambda i: (i, 0)),
            pl.BlockSpec((TOTAL, TOTAL), lambda i: (0, 0)),
        ],
        out_specs=[block, block, block],
        compiler_params=pltpu.CompilerParams(vmem_limit_bytes=24 * MIB),
    )(raw, inverse)


def final_kernel(
    cols_blocks, code_ref, place_ref, front_ref, rows_ref, rows_high, rows_low, cols_ref, cols_high,
    cols_low, lower_ref, arrived_ref, out_ref, cursor
):
    step = pl.program_id(0)
    sources, capacity = code_ref.shape
    height, width = front_ref.shape
    unit, side = arrived_ref.shape[2:]
    per_step = height // unit

    @pl.when(step == 0)
    def _():
        for s in range(sources):
            cursor[s] = 0

    chunk = min(512, width)
    for start in range(0, width, chunk):
        at = slice(start, start + chunk)
        change = jnp.dot(rows_high[...], cols_high[:, at], preferred_element_type=jnp.float32)
        change += jnp.dot(rows_high[...], cols_low[:, at], preferred_element_type=jnp.float32)
        change += jnp.dot(rows_low[...], cols_high[:, at], preferred_element_type=jnp.float32)
        out_ref[:, at] = front_ref[:, at] - change

    edge = (step + 1) * per_step * cols_blocks

    @pl.loop(0, sources)
    def _(s):
        def more(k):
            code = code_ref[s, jnp.minimum(k, capacity - 1)]
            return (k < capacity) & (code >= 0) & (code < edge)

        def add(k):
            code = code_ref[s, k]
            unit_row = code // cols_blocks - step * per_step
            block_col = code % cols_blocks
            rows = pl.ds(pl.multiple_of(unit_row * unit, unit), unit)
            columns = pl.ds(pl.multiple_of(block_col * side, side), side)
            out_ref[rows, columns] += arrived_ref[s, k]
            return k + 1

        cursor[s] = lax.while_loop(more, add, cursor[s])

    top = (place_ref[0] == 0) & (step == 0)

    @pl.when(top)
    def _():
        out_ref[...] = cols_ref[...]

    @pl.when(place_ref[1] == 0)
    def _():
        out_ref[:, :TOTAL] = jnp.where(top, lower_ref[...], rows_ref[...])


def finish(front, rows, cols, lower, arrived, codes, place, cols_blocks):
    row_len, col_len = front.shape
    height = TOTAL
    smem = pl.BlockSpec(memory_space=pltpu.SMEM)
    block = pl.BlockSpec((height, TOTAL), lambda i: (i, 0))
    wide = pl.BlockSpec((height, col_len), lambda i: (i, 0))
    whole = pl.BlockSpec((TOTAL, col_len), lambda i: (0, 0))
    return pl.pallas_call(
        functools.partial(final_kernel, cols_blocks),
        grid=(row_len // height,),
        out_shape=jax.ShapeDtypeStruct((row_len, col_len), jnp.float32),
        in_specs=[
            smem, smem, wide, block, block, block, whole, whole, whole,
            pl.BlockSpec((TOTAL, TOTAL), lambda i: (0, 0)),
            pl.BlockSpec(memory_space=pltpu.VMEM),
        ],
        out_specs=wide,
        scratch_shapes=[pltpu.SMEM((codes.shape[0],), jnp.int32)],
        compiler_params=pltpu.CompilerParams(vmem_limit_bytes=56 * MIB),
    )(codes, place, front, *rows, *cols, lower, arrived)


def factor(diagonal):
    def lower_of(block):
        return jnp.linalg.cholesky(jnp.tril(block) + jnp.tril(block, -1).T)

    def inverse_of(block):
        return jax.scipy.linalg.solve_triangular(block, jnp.eye(NB, dtype=jnp.float32), lower=True)

    first = lower_of(diagonal[:NB, :NB])
    first_inverse = inverse_of(first)
    below = dot_nt(diagonal[NB:, :NB], first_inverse)
    second = lower_of(diagonal[NB:, NB:] - dot_nt(below, below))
    second_inverse = inverse_of(second)
    corner = -jnp.dot(second_inverse, jnp.dot(below, first_inverse, precision=precise), precision=precise)
    zero = jnp.zeros((NB, NB), jnp.float32)
    return jnp.block([[first, zero], [below, second]]), jnp.block([[first_inverse, zero], [corner, second_inverse]])


def body(front, tiles, tile_block, valid_rows):
    row_len, col_len = front.shape
    row_count = lax.axis_size("row")
    col_count = lax.axis_size("col")
    device_count = row_count * col_count
    per_device = tiles.shape[0]
    side = tiles.shape[1]
    capacity = 2 * per_device // device_count
    rows_blocks = row_len // side
    cols_blocks = col_len // side
    row_now = lax.axis_index("row")
    col_now = lax.axis_index("col")
    device_now = row_now * col_count + col_now

    block_row = tile_block[0].reshape(device_count, per_device)
    block_col = tile_block[1].reshape(device_count, per_device)
    target_row = block_row // rows_blocks
    target = target_row * col_count + block_col // cols_blocks
    code = block_row % rows_blocks * cols_blocks + block_col % cols_blocks
    position = lax.broadcasted_iota(jnp.int32, target.shape, 1)
    place = jnp.stack([row_now, col_now]).astype(jnp.int32)

    def own(values):
        return lax.dynamic_index_in_dim(values, device_now, 0, keepdims=False)

    in_panel = block_col < PANELS
    panel_key = jnp.where(in_panel, target_row, -1)
    panel_rank = jnp.sum(
        (panel_key[:, :, None] == panel_key[:, None, :]) & (position[:, None, :] < position[:, :, None]),
        axis=2,
    )
    ahead = (own(target_row) - row_now) % row_count
    panel_slot = jnp.where(own(in_panel), ahead * capacity + own(panel_rank), -1)
    panel_out = pack(tiles, panel_slot, valid_rows, row_count * capacity)
    panel_in = [panel_out[:capacity]]
    for shift in range(1, row_count):
        sending = panel_out[shift * capacity : (shift + 1) * capacity]
        turn = [(r, (r + shift) % row_count) for r in range(row_count)]
        panel_in.append(lax.ppermute(sending, "row", turn))
    same_col = lax.dynamic_index_in_dim(
        jnp.stack([panel_key, panel_rank, code]).reshape(3, row_count, col_count, per_device),
        col_now, 2, keepdims=False,
    )
    slots = jnp.arange(capacity)
    fits = (same_col[0] == row_now)[:, :, None] & (same_col[1][:, :, None] == slots)
    panel_code = same_col[2] // cols_blocks * PANELS + same_col[2] % cols_blocks
    panel_codes = jnp.sum(jnp.where(fits, panel_code[:, :, None] + 1, 0), axis=1) - 1
    by_shift = (row_now - jnp.arange(row_count)) % row_count
    panel_codes = jnp.take(panel_codes, by_shift, axis=0).reshape(-1)

    units = side // UNIT
    length = capacity * units
    width = length * 21 // 32
    pass_on = length * 3 // 8
    half_count = device_count // 2
    half_base = device_now // half_count * half_count
    unit_rows = rows_blocks * units
    local_codes = unit_rows * cols_blocks
    own_target, own_code = own(target), own(code)
    own_position = own(position)
    filled = (valid_rows + UNIT - 1) // UNIT
    key = (own_target * rows_blocks * cols_blocks + own_code) * per_device + own_position
    before = key[None, :] < key[:, None]
    together = own_target[None, :] == own_target[:, None]
    base = jnp.sum(jnp.where(before & together, filled[None, :], 0), axis=1)
    order = jnp.sum(before, axis=1)
    unit_code = (own_target * unit_rows + own_code // cols_blocks * units) * cols_blocks
    unit_code += own_code % cols_blocks
    meta = jnp.stack([own_position, own_target, base, filled, unit_code, valid_rows])
    meta = jnp.sum(
        jnp.where(order[None, :, None] == jnp.arange(per_device), meta[:, :, None], 0), axis=1
    )
    to_device = own_target[:, None] == jnp.arange(device_count)
    load = jnp.sum(jnp.where(to_device, filled[:, None], 0), axis=0).reshape(2, half_count)
    empty = load == 0
    empty_rank = jnp.cumsum(empty, axis=1) - 1
    device_ids = jnp.arange(device_count).reshape(2, half_count)
    listed = (empty[:, :, None]) & (empty_rank[:, :, None] == jnp.arange(half_count))
    empties = jnp.sum(jnp.where(listed, device_ids[:, :, None], 0), axis=1)
    free = jnp.sum(empty, axis=1)
    left = jnp.sum(jnp.maximum(load - width, 0), axis=1)
    failed = jnp.any(left > free * width)
    counts = jnp.concatenate([jnp.sum(own_target < half_count)[None], free]).astype(jnp.int32)
    outgoing, sent_codes = spread(
        tiles, meta.astype(jnp.int32), empties.astype(jnp.int32), counts,
        device_count, width, length, cols_blocks,
    )

    got = lax.all_to_all(sent_codes[:, :width], ("row", "col"), 0, 0, tiled=True)
    got_target = got // local_codes
    local = got % local_codes
    mine = (got >= 0) & (got_target == device_now)
    direct_codes = jnp.where(mine, local, -1)
    total_units = device_count * width
    passing = ((got >= 0) & (got_target != device_now)).reshape(-1)
    flat_key = jnp.where(passing, got.reshape(-1) * total_units + jnp.arange(total_units), -1)
    flat_target = jnp.where(passing, got_target.reshape(-1), -1)
    rank = jnp.sum(
        (flat_target[None, :] == flat_target[:, None]) & (flat_key[None, :] < flat_key[:, None]), axis=1
    )
    failed = failed | jnp.any(passing & (rank >= pass_on))
    relay_slot = jnp.where(
        passing & (rank < pass_on), (flat_target - half_base) * pass_on + rank, -1
    )
    picked = relay_slot[:, None] == jnp.arange(half_count * pass_on)
    relay_codes = jnp.sum(jnp.where(picked, local.reshape(-1)[:, None] + 1, 0), axis=0) - 1
    notes = jnp.zeros((2, half_count, pass_on + 1), jnp.int32)
    notes = lax.dynamic_update_slice(
        notes, relay_codes.reshape(1, half_count, pass_on).astype(jnp.int32), (device_now // half_count, 0, 0)
    )
    notes = notes.at[:, :, pass_on].set(failed.astype(jnp.int32))
    notes = lax.all_to_all(
        notes.reshape(device_count, pass_on + 1), ("row", "col"), 0, 0, tiled=True
    )
    too_full = jnp.any(notes[:, pass_on] != 0)
    relay_codes = lax.dynamic_slice_in_dim(notes, half_base, half_count, 0)[:, :pass_on]
    relay_slot = relay_slot.reshape(device_count, width)

    first = (col_now == 0).astype(jnp.int32).reshape(1)
    partial = raw_panel(front, jnp.concatenate(panel_in, 0), panel_codes, first)
    raw_rows = lax.psum(partial, "col")
    slice_start = col_now * col_len % row_len
    slice_root = col_now * col_len // row_len

    def chain(raw_rows):
        picked = lax.dynamic_slice_in_dim(raw_rows, slice_start, col_len, 0)
        raw_cols = lax.psum(jnp.where(row_now == slice_root, picked, 0.0), "row")
        diagonal = jnp.where(row_now == 0, raw_rows[:TOTAL], jnp.eye(TOTAL, dtype=jnp.float32))
        lower, inverse = factor(diagonal)
        inverse, raw_cols = lax.optimization_barrier((inverse, raw_cols))
        inverse = lax.psum(jnp.where(row_now == 0, inverse, 0.0), "row")
        return solve_rows(raw_rows, inverse), solve_cols(raw_cols, inverse), lower

    def relayed(front, tiles, valid_rows, outgoing, raw_rows):
        arrived = lax.all_to_all(outgoing, ("row", "col"), 0, 0, tiled=True)
        rows, cols, lower = chain(raw_rows)
        passed = relay(relay_slot, arrived, half_count * pass_on)
        halves = [list(range(half_count)), list(range(half_count, device_count))]
        passed = lax.all_to_all(
            passed.reshape(half_count, pass_on, UNIT, side), ("row", "col"), 0, 0,
            axis_index_groups=halves, tiled=True,
        )
        partial = finish(front, rows, cols, lower, arrived, direct_codes, place, cols_blocks)
        return add_relayed(partial, passed, relay_codes, place, cols_blocks)

    def padded(front, tiles, valid_rows, outgoing, raw_rows):
        order = (target * rows_blocks * cols_blocks + code) * per_device + position
        ranking = jnp.sum(
            (target[:, :, None] == target[:, None, :]) & (order[:, None, :] < order[:, :, None]), axis=2
        )
        slot = own(target) * capacity + own(ranking)
        here = (target == device_now)[:, :, None] & (ranking[:, :, None] == slots)
        codes = jnp.sum(jnp.where(here, code[:, :, None] + 1, 0), axis=1) - 1
        packed = pack(tiles, slot, valid_rows, device_count * capacity)
        arrived = lax.all_to_all(
            packed.reshape(device_count, capacity, side, side), ("row", "col"), 0, 0, tiled=True
        )
        rows, cols, lower = chain(raw_rows)
        return finish(front, rows, cols, lower, arrived, codes, place, cols_blocks)

    return lax.cond(too_full, padded, relayed, front, tiles, valid_rows, outgoing, raw_rows)


def solution(mesh):
    placed = (P("row", "col"), P(("row", "col"), None, None), P(), P(("row", "col")))
    return jax.shard_map(
        body, mesh=mesh, in_specs=placed, out_specs=P("row", "col"), check_vma=False
    )
```

```python
import functools

import jax
import jax.numpy as jnp
from jax import lax
from jax.experimental import pallas as pl
from jax.experimental.pallas import tpu as pltpu
from jax.sharding import PartitionSpec as P

NB = 128
PANELS = 2
TOTAL = NB * PANELS
MIB = 1 << 20
UNIT = 8


precise = lax.Precision.HIGHEST


def dot_nt(a, b, precision=precise):
    return lax.dot_general(
        a, b, (((1,), (1,)), ((), ())), precision=precision, preferred_element_type=jnp.float32
    )


def pack_kernel(slot_ref, valid_ref, tiles_ref, out_ref, buf, sem):
    count, side = tiles_ref.shape[0], tiles_ref.shape[1]
    half = side // 2

    def store(t):
        return pltpu.make_async_copy(buf.at[t], out_ref.at[jnp.maximum(slot_ref[t], 0)], sem.at[t])

    def each(act):
        @pl.loop(0, count)
        def _(t):
            @pl.when(slot_ref[t] >= 0)
            def _():
                act(t)

    def mask(t):
        rows = lax.broadcasted_iota(jnp.int32, (half, side), 0) + half
        buf[t, :half] = tiles_ref[t, :half]
        buf[t, half:] = jnp.where(rows < valid_ref[t], tiles_ref[t, half:], 0.0)
        store(t).start()

    each(mask)
    each(lambda t: store(t).wait())


def pack(tiles, slots, valid, n_slots):
    count, side = tiles.shape[0], tiles.shape[1]
    smem = pl.BlockSpec(memory_space=pltpu.SMEM)
    return pl.pallas_call(
        pack_kernel,
        out_shape=jax.ShapeDtypeStruct((n_slots, side, side), jnp.float32),
        in_specs=[smem, smem, pl.BlockSpec(memory_space=pltpu.VMEM)],
        out_specs=pl.BlockSpec(memory_space=pl.ANY),
        scratch_shapes=[
            pltpu.VMEM((count, side, side), jnp.float32),
            pltpu.SemaphoreType.DMA((count,)),
        ],
        compiler_params=pltpu.CompilerParams(vmem_limit_bytes=24 * MIB),
    )(slots, valid, tiles)


def spread_kernel(
    width, stride, meta_ref, empty_ref, count_ref, tiles_ref, out_ref, code_ref, stage, sem
):
    count, units = tiles_ref.shape[0], tiles_ref.shape[1]
    devices, length = code_ref.shape

    @pl.loop(0, devices)
    def _(d):
        for k in range(length):
            code_ref[d, k] = -1

    @pl.loop(0, count)
    def _(i):
        tile, target, base = meta_ref[0, i], meta_ref[1, i], meta_ref[2, i]
        filled, code, valid = meta_ref[3, i], meta_ref[4, i], meta_ref[5, i]
        shape = tiles_ref.shape[1:]
        rows = lax.broadcasted_iota(jnp.int32, shape, 0) * shape[1]
        rows += lax.broadcasted_iota(jnp.int32, shape, 1)
        stage[target, pl.ds(base, units)] = jnp.where(rows < valid, tiles_ref[tile], 0.0)
        for u in range(units):
            code_ref[target, base + u] = jnp.where(u < filled, code + u * stride, -1)

    for half in range(2):
        first = 0 if half == 0 else count_ref[0]
        last = count_ref[0] if half == 0 else count
        free = count_ref[1 + half]

        def each_tile(i, carry):
            target, base, filled = meta_ref[1, i], meta_ref[2, i], meta_ref[3, i]

            def each_unit(q, carry):
                at, depth = carry
                relay = empty_ref[half, at]
                place = jnp.minimum(depth, width - 1)
                stage[relay, place] = stage[target, q]
                code_ref[relay, place] = code_ref[target, q]
                wrap = at + 1 >= free
                return jnp.where(wrap, 0, at + 1), jnp.where(wrap, depth + 1, depth)

            return lax.fori_loop(jnp.maximum(base, width), base + filled, each_unit, carry)

        lax.fori_loop(first, last, each_tile, (jnp.int32(0), jnp.int32(0)))

    copy = pltpu.make_async_copy(stage.at[:, pl.ds(0, width)], out_ref, sem)
    copy.start()
    copy.wait()


def spread(tiles, meta, empties, counts, devices, width, length, stride):
    count, side = tiles.shape[0], tiles.shape[1]
    units = side // UNIT
    smem = pl.BlockSpec(memory_space=pltpu.SMEM)
    return pl.pallas_call(
        functools.partial(spread_kernel, width, stride),
        out_shape=[
            jax.ShapeDtypeStruct((devices, width, UNIT, side), jnp.float32),
            jax.ShapeDtypeStruct((devices, length), jnp.int32),
        ],
        in_specs=[smem, smem, smem, pl.BlockSpec(memory_space=pltpu.VMEM)],
        out_specs=[pl.BlockSpec(memory_space=pl.ANY), smem],
        scratch_shapes=[
            pltpu.VMEM((devices, length, UNIT, side), jnp.float32),
            pltpu.SemaphoreType.DMA,
        ],
        compiler_params=pltpu.CompilerParams(vmem_limit_bytes=40 * MIB),
    )(meta, empties, counts, tiles.reshape(count, units, UNIT, side))


def relay_kernel(slot_ref, arrived_ref, out_ref):
    devices, width = slot_ref.shape

    @pl.loop(0, devices)
    def _(s):
        def more(k):
            return (k < width) & (slot_ref[s, jnp.minimum(k, width - 1)] >= 0)

        def move(k):
            out_ref[slot_ref[s, k]] = arrived_ref[s, k]
            return k + 1

        lax.while_loop(more, move, jnp.int32(0))


def relay(slots, arrived, length):
    vmem = pl.BlockSpec(memory_space=pltpu.VMEM)
    return pl.pallas_call(
        relay_kernel,
        out_shape=jax.ShapeDtypeStruct((length,) + arrived.shape[2:], jnp.float32),
        in_specs=[pl.BlockSpec(memory_space=pltpu.SMEM), vmem],
        out_specs=vmem,
        compiler_params=pltpu.CompilerParams(vmem_limit_bytes=40 * MIB),
    )(slots, arrived)


def add_kernel(
    cols_blocks, block_ref, unit_ref, index_ref, count_ref, partial_ref, arrived_ref, out_ref, buf,
    group_start, sem_in, sem_out
):
    slots, side = buf.shape[0], buf.shape[1]
    unit = arrived_ref.shape[1]
    ahead = slots // 2
    count = count_ref[0]

    def listed(i, carry):
        groups, last = carry
        block = block_ref[i]
        fresh = block != last

        @pl.when(fresh)
        def _():
            group_start[groups] = i

        return jnp.where(fresh, groups + 1, groups), block

    groups, _ = lax.fori_loop(0, count, listed, (jnp.int32(0), jnp.int32(-1)))
    group_start[groups] = count

    def window(g):
        block = block_ref[group_start[g]]
        rows = pl.ds(pl.multiple_of(block // cols_blocks * side, side), side)
        columns = pl.ds(pl.multiple_of(block % cols_blocks * side, side), side)
        return out_ref.at[rows, columns]

    def fetch(g):
        at = g % slots
        return pltpu.make_async_copy(window(g), buf.at[at], sem_in.at[at])

    def store(g):
        at = g % slots
        return pltpu.make_async_copy(buf.at[at], window(g), sem_out.at[at])

    @pl.loop(0, jnp.minimum(groups, ahead))
    def _(g):
        fetch(g).start()

    @pl.loop(0, groups)
    def _(g):
        @pl.when(g + ahead < groups)
        def _():
            @pl.when(g >= ahead)
            def _():
                store(g - ahead).wait()

            fetch(g + ahead).start()

        fetch(g).wait()

        @pl.loop(group_start[g], group_start[g + 1])
        def _(i):
            rows = pl.ds(pl.multiple_of(unit_ref[i] * unit, unit), unit)
            buf[g % slots, rows] += arrived_ref[index_ref[i]]

        store(g).start()

    @pl.loop(jnp.maximum(groups - slots, 0), groups)
    def _(g):
        store(g).wait()


def add_relayed(partial, arrived, listing, cols_blocks):
    row_len, col_len = partial.shape
    unit, side = arrived.shape[1:]
    smem = pl.BlockSpec(memory_space=pltpu.SMEM)
    hbm = pl.BlockSpec(memory_space=pl.ANY)
    return pl.pallas_call(
        functools.partial(add_kernel, cols_blocks),
        out_shape=jax.ShapeDtypeStruct((row_len, col_len), jnp.float32),
        in_specs=[smem, smem, smem, smem, hbm, pl.BlockSpec(memory_space=pltpu.VMEM)],
        out_specs=hbm,
        scratch_shapes=[
            pltpu.VMEM((16, side, side), jnp.float32),
            pltpu.SMEM((arrived.shape[0] + 1,), jnp.int32),
            pltpu.SemaphoreType.DMA((16,)),
            pltpu.SemaphoreType.DMA((16,)),
        ],
        input_output_aliases={4: 0},
        compiler_params=pltpu.CompilerParams(vmem_limit_bytes=24 * MIB),
    )(*listing, partial, arrived)


def panel_kernel(code_ref, first_ref, front_ref, arrived_ref, out_ref):
    side = arrived_ref.shape[1]

    @pl.when(first_ref[0] == 1)
    def _():
        out_ref[...] = front_ref[...]

    @pl.when(first_ref[0] == 0)
    def _():
        out_ref[...] = jnp.zeros_like(out_ref)

    @pl.loop(0, arrived_ref.shape[0])
    def _(k):
        code = code_ref[k]
        for part in range(PANELS):

            @pl.when((code >= 0) & (code % PANELS == part))
            def _():
                rows = pl.ds(pl.multiple_of(code // PANELS * side, side), side)
                out_ref[rows, part * side : (part + 1) * side] += arrived_ref[k]


def raw_panel(front, arrived, codes, first):
    row_len = front.shape[0]
    smem = pl.BlockSpec(memory_space=pltpu.SMEM)
    return pl.pallas_call(
        panel_kernel,
        grid=(1,),
        out_shape=jax.ShapeDtypeStruct((row_len, TOTAL), jnp.float32),
        in_specs=[
            smem,
            smem,
            pl.BlockSpec((row_len, TOTAL), lambda i: (0, 0)),
            pl.BlockSpec(arrived.shape, lambda i: (0, 0, 0)),
        ],
        out_specs=pl.BlockSpec((row_len, TOTAL), lambda i: (0, 0)),
        compiler_params=pltpu.CompilerParams(vmem_limit_bytes=40 * MIB),
    )(codes, first, front, arrived)


def split(value):
    high = value.astype(jnp.bfloat16)
    low = (value - high.astype(jnp.float32)).astype(jnp.bfloat16)
    return high, low


def rows_kernel(raw_ref, inverse_ref, out_ref, parts_ref):
    solved = dot_nt(raw_ref[...], inverse_ref[...])
    out_ref[...] = solved
    high, low = split(solved)
    parts_ref[:, :TOTAL] = high
    parts_ref[:, TOTAL : 2 * TOTAL] = high
    parts_ref[:, 2 * TOTAL :] = low


def solve_rows(raw, inverse):
    length = raw.shape[0]
    step = min(512, length)
    block = pl.BlockSpec((step, TOTAL), lambda i: (i, 0))
    return pl.pallas_call(
        rows_kernel,
        grid=(length // step,),
        out_shape=[
            jax.ShapeDtypeStruct((length, TOTAL), jnp.float32),
            jax.ShapeDtypeStruct((length, 3 * TOTAL), jnp.bfloat16),
        ],
        in_specs=[block, pl.BlockSpec((TOTAL, TOTAL), lambda i: (0, 0))],
        out_specs=[block, pl.BlockSpec((step, 3 * TOTAL), lambda i: (i, 0))],
        compiler_params=pltpu.CompilerParams(vmem_limit_bytes=24 * MIB),
    )(raw, inverse)


def cols_kernel(raw_ref, inverse_ref, out_ref, parts_ref):
    solved = dot_nt(inverse_ref[...], raw_ref[...])
    out_ref[...] = solved
    high, low = split(solved)
    parts_ref[:TOTAL] = high
    parts_ref[TOTAL : 2 * TOTAL] = low
    parts_ref[2 * TOTAL :] = high


def solve_cols(raw, inverse):
    length = raw.shape[0]
    step = min(512, length)
    block = pl.BlockSpec((TOTAL, step), lambda i: (0, i))
    return pl.pallas_call(
        cols_kernel,
        grid=(length // step,),
        out_shape=[
            jax.ShapeDtypeStruct((TOTAL, length), jnp.float32),
            jax.ShapeDtypeStruct((3 * TOTAL, length), jnp.bfloat16),
        ],
        in_specs=[
            pl.BlockSpec((step, TOTAL), lambda i: (i, 0)),
            pl.BlockSpec((TOTAL, TOTAL), lambda i: (0, 0)),
        ],
        out_specs=[block, pl.BlockSpec((3 * TOTAL, step), lambda i: (0, i))],
        compiler_params=pltpu.CompilerParams(vmem_limit_bytes=24 * MIB),
    )(raw, inverse)


def final_kernel(
    cols_blocks, runs, code_ref, place_ref, front_ref, rows_ref, rows_parts, cols_ref, cols_parts,
    lower_ref, arrived_ref, out_ref, cursor
):
    step = pl.program_id(0)
    sources, capacity = code_ref.shape
    height, width = front_ref.shape
    unit, side = arrived_ref.shape[2:]
    per_step = height // unit

    @pl.when(step == 0)
    def _():
        for s in range(sources):
            cursor[s] = 0

    chunk = min(512, width)
    for start in range(0, width, chunk):
        at = slice(start, start + chunk)
        change = jnp.dot(rows_parts[...], cols_parts[:, at], preferred_element_type=jnp.float32)
        out_ref[:, at] = front_ref[:, at] - change

    edge = (step + 1) * per_step * cols_blocks

    @pl.loop(0, sources)
    def _(s):
        def more(k):
            code = code_ref[s, jnp.minimum(k, capacity - 1)]
            return (k < capacity) & (code >= 0) & (code < edge)

        def add(k):
            code = code_ref[s, k]
            unit_row = code // cols_blocks - step * per_step
            block_col = code % cols_blocks
            columns = pl.ds(pl.multiple_of(block_col * side, side), side)
            taken = jnp.int32(0)
            for run in runs:
                ending = code_ref[s, jnp.minimum(k + run - 1, capacity - 1)]
                whole = (k + run <= capacity) & (ending == code + (run - 1) * cols_blocks)
                use = whole & (ending < edge) & (taken == 0)

                @pl.when(use)
                def _():
                    rows = pl.ds(pl.multiple_of(unit_row * unit, unit), run * unit)
                    block = arrived_ref[s, pl.ds(k, run)]
                    out_ref[rows, columns] += block.reshape(run * unit, side)

                taken = jnp.where(use, run, taken)
            return k + taken

        cursor[s] = lax.while_loop(more, add, cursor[s])

    top = (place_ref[0] == 0) & (step == 0)

    @pl.when(top)
    def _():
        out_ref[...] = cols_ref[...]

    @pl.when(place_ref[1] == 0)
    def _():
        out_ref[:, :TOTAL] = jnp.where(top, lower_ref[...], rows_ref[...])


def finish(front, rows, cols, lower, arrived, codes, place, cols_blocks):
    row_len, col_len = front.shape
    height = TOTAL
    smem = pl.BlockSpec(memory_space=pltpu.SMEM)
    block = pl.BlockSpec((height, TOTAL), lambda i: (i, 0))
    parts = pl.BlockSpec((height, 3 * TOTAL), lambda i: (i, 0))
    wide = pl.BlockSpec((height, col_len), lambda i: (i, 0))
    whole = pl.BlockSpec((TOTAL, col_len), lambda i: (0, 0))
    whole_parts = pl.BlockSpec((3 * TOTAL, col_len), lambda i: (0, 0))
    runs = (8, 4, 1) if arrived.shape[2] == UNIT else (1,)
    return pl.pallas_call(
        functools.partial(final_kernel, cols_blocks, runs),
        grid=(row_len // height,),
        out_shape=jax.ShapeDtypeStruct((row_len, col_len), jnp.float32),
        in_specs=[
            smem, smem, wide, block, parts, whole, whole_parts,
            pl.BlockSpec((TOTAL, TOTAL), lambda i: (0, 0)),
            pl.BlockSpec(memory_space=pltpu.VMEM),
        ],
        out_specs=wide,
        scratch_shapes=[pltpu.SMEM((codes.shape[0],), jnp.int32)],
        compiler_params=pltpu.CompilerParams(vmem_limit_bytes=56 * MIB),
    )(codes, place, front, *rows, *cols, lower, arrived)


def factor(diagonal):
    def lower_of(block):
        return jnp.linalg.cholesky(jnp.tril(block) + jnp.tril(block, -1).T)

    def inverse_of(block):
        return jax.scipy.linalg.solve_triangular(block, jnp.eye(NB, dtype=jnp.float32), lower=True)

    first = lower_of(diagonal[:NB, :NB])
    first_inverse = inverse_of(first)
    below = dot_nt(diagonal[NB:, :NB], first_inverse)
    second = lower_of(diagonal[NB:, NB:] - dot_nt(below, below))
    second_inverse = inverse_of(second)
    corner = -jnp.dot(second_inverse, jnp.dot(below, first_inverse, precision=precise), precision=precise)
    zero = jnp.zeros((NB, NB), jnp.float32)
    return jnp.block([[first, zero], [below, second]]), jnp.block([[first_inverse, zero], [corner, second_inverse]])


def body(front, tiles, tile_block, valid_rows):
    row_len, col_len = front.shape
    row_count = lax.axis_size("row")
    col_count = lax.axis_size("col")
    device_count = row_count * col_count
    per_device = tiles.shape[0]
    side = tiles.shape[1]
    capacity = 2 * per_device // device_count
    rows_blocks = row_len // side
    cols_blocks = col_len // side
    row_now = lax.axis_index("row")
    col_now = lax.axis_index("col")
    device_now = row_now * col_count + col_now

    block_row = tile_block[0].reshape(device_count, per_device)
    block_col = tile_block[1].reshape(device_count, per_device)
    target_row = block_row // rows_blocks
    target = target_row * col_count + block_col // cols_blocks
    code = block_row % rows_blocks * cols_blocks + block_col % cols_blocks
    position = lax.broadcasted_iota(jnp.int32, target.shape, 1)
    place = jnp.stack([row_now, col_now]).astype(jnp.int32)

    def own(values):
        return lax.dynamic_index_in_dim(values, device_now, 0, keepdims=False)

    in_panel = block_col < PANELS
    panel_key = jnp.where(in_panel, target_row, -1)
    panel_rank = jnp.sum(
        (panel_key[:, :, None] == panel_key[:, None, :]) & (position[:, None, :] < position[:, :, None]),
        axis=2,
    )
    same_col = lax.dynamic_index_in_dim(
        jnp.stack([panel_key, panel_rank, code]).reshape(3, row_count, col_count, per_device),
        col_now, 2, keepdims=False,
    )

    def send_panel(tiles, valid_rows, depth):
        ahead = (own(target_row) - row_now) % row_count
        fits = own(in_panel) & (own(panel_rank) < depth)
        panel_slot = jnp.where(fits, ahead * depth + own(panel_rank), -1)
        panel_out = pack(tiles, panel_slot, valid_rows, row_count * depth)
        panel_in = [panel_out[:depth]]
        for shift in range(1, row_count):
            sending = panel_out[shift * depth : (shift + 1) * depth]
            turn = [(r, (r + shift) % row_count) for r in range(row_count)]
            panel_in.append(lax.ppermute(sending, "row", turn))
        return panel_in

    def sum_panel(front, panel_in, depth):
        fits = (same_col[0] == row_now)[:, :, None] & (same_col[1][:, :, None] == jnp.arange(depth))
        panel_code = same_col[2] // cols_blocks * PANELS + same_col[2] % cols_blocks
        panel_codes = jnp.sum(jnp.where(fits, panel_code[:, :, None] + 1, 0), axis=1) - 1
        by_shift = (row_now - jnp.arange(row_count)) % row_count
        panel_codes = jnp.take(panel_codes, by_shift, axis=0).reshape(-1)
        first = (col_now == 0).astype(jnp.int32).reshape(1)
        partial = raw_panel(front, jnp.concatenate(panel_in, 0), panel_codes, first)
        corner = jnp.where(row_now == 0, partial[:TOTAL], 0.0)
        diagonal = corner
        for other in range(1, row_count):
            diagonal += lax.ppermute(corner, "row", [(0, other)])
        return lax.psum((partial, diagonal), "col")

    panel_depth = (capacity * 5 + 7) // 8
    panel_in = send_panel(tiles, valid_rows, panel_depth)

    units = side // UNIT
    length = capacity * units
    width = length * 21 // 32
    pass_on = length * 3 // 8
    half_count = device_count // 2
    half_base = device_now // half_count * half_count
    unit_rows = rows_blocks * units
    local_codes = unit_rows * cols_blocks
    own_target, own_code = own(target), own(code)
    own_position = own(position)
    filled = (valid_rows + UNIT - 1) // UNIT
    key = (own_target * rows_blocks * cols_blocks + own_code) * per_device + own_position
    before = key[None, :] < key[:, None]
    together = own_target[None, :] == own_target[:, None]
    base = jnp.sum(jnp.where(before & together, filled[None, :], 0), axis=1)
    order = jnp.sum(before, axis=1)
    unit_code = (own_target * unit_rows + own_code // cols_blocks * units) * cols_blocks
    unit_code += own_code % cols_blocks
    meta = jnp.stack([own_position, own_target, base, filled, unit_code, valid_rows])
    meta = jnp.sum(
        jnp.where(order[None, :, None] == jnp.arange(per_device), meta[:, :, None], 0), axis=1
    )
    to_device = own_target[:, None] == jnp.arange(device_count)
    load = jnp.sum(jnp.where(to_device, filled[:, None], 0), axis=0).reshape(2, half_count)
    empty = load == 0
    empty_rank = jnp.cumsum(empty, axis=1) - 1
    device_ids = jnp.arange(device_count).reshape(2, half_count)
    listed = (empty[:, :, None]) & (empty_rank[:, :, None] == jnp.arange(half_count))
    empties = jnp.sum(jnp.where(listed, device_ids[:, :, None], 0), axis=1)
    free = jnp.sum(empty, axis=1)
    left = jnp.sum(jnp.maximum(load - width, 0), axis=1)
    failed = jnp.any(left > free * width) | jnp.any(own(in_panel) & (own(panel_rank) >= panel_depth))
    counts = jnp.concatenate([jnp.sum(own_target < half_count)[None], free]).astype(jnp.int32)
    outgoing, sent_codes = spread(
        tiles, meta.astype(jnp.int32), empties.astype(jnp.int32), counts,
        device_count, width, length, cols_blocks,
    )

    got = lax.all_to_all(sent_codes[:, :width], ("row", "col"), 0, 0, tiled=True)
    got_target = got // local_codes
    local = got % local_codes
    mine = (got >= 0) & (got_target == device_now)
    direct_codes = jnp.where(mine, local, -1)
    total_units = device_count * width
    passing = ((got >= 0) & (got_target != device_now)).reshape(-1)
    flat_key = jnp.where(passing, got.reshape(-1) * total_units + jnp.arange(total_units), -1)
    flat_target = jnp.where(passing, got_target.reshape(-1), -1)
    rank = jnp.sum(
        (flat_target[None, :] == flat_target[:, None]) & (flat_key[None, :] < flat_key[:, None]), axis=1
    )
    failed = failed | jnp.any(passing & (rank >= pass_on))
    relay_slot = jnp.where(
        passing & (rank < pass_on), (flat_target - half_base) * pass_on + rank, -1
    )
    picked = relay_slot[:, None] == jnp.arange(half_count * pass_on)
    relay_codes = jnp.sum(jnp.where(picked, local.reshape(-1)[:, None] + 1, 0), axis=0) - 1
    notes = jnp.zeros((2, half_count, pass_on + 1), jnp.int32)
    notes = lax.dynamic_update_slice(
        notes, relay_codes.reshape(1, half_count, pass_on).astype(jnp.int32), (device_now // half_count, 0, 0)
    )
    notes = notes.at[:, :, pass_on].set(failed.astype(jnp.int32))
    notes = lax.all_to_all(
        notes.reshape(device_count, pass_on + 1), ("row", "col"), 0, 0, tiled=True
    )
    too_full = jnp.any(notes[:, pass_on] != 0)
    relay_codes = lax.dynamic_slice_in_dim(notes, half_base, half_count, 0)[:, :pass_on]
    relay_slot = relay_slot.reshape(device_count, width)

    flat = relay_codes.reshape(-1)
    unit_row, relay_col = flat // cols_blocks, flat % cols_blocks
    wanted = (flat >= 0) & ((row_now > 0) | (unit_row >= TOTAL // UNIT))
    wanted &= (col_now > 0) | (relay_col >= PANELS)
    relay_block = unit_row // units * cols_blocks + relay_col
    relay_key = jnp.where(wanted, relay_block * units + unit_row % units, local_codes)
    relay_key = relay_key * flat.shape[0] + jnp.arange(flat.shape[0])
    relay_order = jnp.sum(relay_key[None, :] < relay_key[:, None], axis=1)
    listing = jnp.stack([relay_block, unit_row % units, jnp.arange(flat.shape[0])])
    at_order = relay_order[None, :, None] == jnp.arange(flat.shape[0])
    listing = jnp.sum(jnp.where(at_order, listing[:, :, None], 0), axis=1).astype(jnp.int32)
    listing = [*listing, jnp.sum(wanted).astype(jnp.int32).reshape(1)]

    raw_rows, diagonal = sum_panel(front, panel_in, panel_depth)
    slice_start = col_now * col_len % row_len
    slice_root = col_now * col_len // row_len

    def chain(raw_rows, diagonal):
        picked = lax.dynamic_slice_in_dim(raw_rows, slice_start, col_len, 0)
        raw_cols = lax.psum(jnp.where(row_now == slice_root, picked, 0.0), "row")
        lower, inverse = factor(diagonal)
        return solve_rows(raw_rows, inverse), solve_cols(raw_cols, inverse), lower

    def relayed(front, tiles, valid_rows, outgoing, raw_rows, diagonal):
        arrived = lax.all_to_all(outgoing, ("row", "col"), 0, 0, tiled=True)
        rows, cols, lower = chain(raw_rows, diagonal)
        arrived, rows, cols, lower = lax.optimization_barrier((arrived, rows, cols, lower))
        passed = relay(relay_slot, arrived, half_count * pass_on)
        halves = [list(range(half_count)), list(range(half_count, device_count))]
        passed = lax.all_to_all(
            passed.reshape(half_count, pass_on, UNIT, side), ("row", "col"), 0, 0,
            axis_index_groups=halves, tiled=True,
        )
        partial = finish(front, rows, cols, lower, arrived, direct_codes, place, cols_blocks)
        return add_relayed(partial, passed.reshape(-1, UNIT, side), listing, cols_blocks)

    def padded(front, tiles, valid_rows, outgoing, raw_rows, diagonal):
        raw_rows, diagonal = sum_panel(front, send_panel(tiles, valid_rows, capacity), capacity)
        order = (target * rows_blocks * cols_blocks + code) * per_device + position
        ranking = jnp.sum(
            (target[:, :, None] == target[:, None, :]) & (order[:, None, :] < order[:, :, None]), axis=2
        )
        slot = own(target) * capacity + own(ranking)
        here = (target == device_now)[:, :, None] & (ranking[:, :, None] == jnp.arange(capacity))
        codes = jnp.sum(jnp.where(here, code[:, :, None] + 1, 0), axis=1) - 1
        packed = pack(tiles, slot, valid_rows, device_count * capacity)
        arrived = lax.all_to_all(
            packed.reshape(device_count, capacity, side, side), ("row", "col"), 0, 0, tiled=True
        )
        rows, cols, lower = chain(raw_rows, diagonal)
        return finish(front, rows, cols, lower, arrived, codes, place, cols_blocks)

    return lax.cond(
        too_full, padded, relayed, front, tiles, valid_rows, outgoing, raw_rows, diagonal
    )


def solution(mesh):
    placed = (P("row", "col"), P(("row", "col"), None, None), P(), P(("row", "col")))
    return jax.shard_map(
        body, mesh=mesh, in_specs=placed, out_specs=P("row", "col"), check_vma=False
    )
```

```python
import functools

import jax
import jax.numpy as jnp
from jax import lax
from jax.experimental import pallas as pl
from jax.experimental.pallas import tpu as pltpu
from jax.sharding import PartitionSpec as P

NB = 128
PANELS = 2
TOTAL = NB * PANELS
MIB = 1 << 20
UNIT = 8


precise = lax.Precision.HIGHEST


def dot_nt(a, b, precision=precise):
    return lax.dot_general(
        a, b, (((1,), (1,)), ((), ())), precision=precision, preferred_element_type=jnp.float32
    )


def pack_kernel(slot_ref, valid_ref, tiles_ref, out_ref, buf, sem):
    count, side = tiles_ref.shape[0], tiles_ref.shape[1]
    half = side // 2

    def store(t):
        return pltpu.make_async_copy(buf.at[t], out_ref.at[jnp.maximum(slot_ref[t], 0)], sem.at[t])

    def each(act):
        @pl.loop(0, count)
        def _(t):
            @pl.when(slot_ref[t] >= 0)
            def _():
                act(t)

    def mask(t):
        rows = lax.broadcasted_iota(jnp.int32, (half, side), 0) + half
        buf[t, :half] = tiles_ref[t, :half]
        buf[t, half:] = jnp.where(rows < valid_ref[t], tiles_ref[t, half:], 0.0)
        store(t).start()

    each(mask)
    each(lambda t: store(t).wait())


def pack(tiles, slots, valid, n_slots):
    count, side = tiles.shape[0], tiles.shape[1]
    smem = pl.BlockSpec(memory_space=pltpu.SMEM)
    return pl.pallas_call(
        pack_kernel,
        out_shape=jax.ShapeDtypeStruct((n_slots, side, side), jnp.float32),
        in_specs=[smem, smem, pl.BlockSpec(memory_space=pltpu.VMEM)],
        out_specs=pl.BlockSpec(memory_space=pl.ANY),
        scratch_shapes=[
            pltpu.VMEM((count, side, side), jnp.float32),
            pltpu.SemaphoreType.DMA((count,)),
        ],
        compiler_params=pltpu.CompilerParams(vmem_limit_bytes=24 * MIB),
    )(slots, valid, tiles)


def spread_kernel(
    width, stride, meta_ref, empty_ref, count_ref, tiles_ref, out_ref, code_ref, stage, sem
):
    count, units = tiles_ref.shape[0], tiles_ref.shape[1]
    devices, length = code_ref.shape

    @pl.loop(0, devices)
    def _(d):
        for k in range(length):
            code_ref[d, k] = -1

    @pl.loop(0, count)
    def _(i):
        tile, target, base = meta_ref[0, i], meta_ref[1, i], meta_ref[2, i]
        filled, code, valid = meta_ref[3, i], meta_ref[4, i], meta_ref[5, i]
        shape = tiles_ref.shape[1:]
        rows = lax.broadcasted_iota(jnp.int32, shape, 0) * shape[1]
        rows += lax.broadcasted_iota(jnp.int32, shape, 1)
        stage[target, pl.ds(base, units)] = jnp.where(rows < valid, tiles_ref[tile], 0.0)
        for u in range(units):
            code_ref[target, base + u] = jnp.where(u < filled, code + u * stride, -1)

    for half in range(2):
        first = 0 if half == 0 else count_ref[0]
        last = count_ref[0] if half == 0 else count
        free = count_ref[1 + half]

        def each_tile(i, carry):
            target, base, filled = meta_ref[1, i], meta_ref[2, i], meta_ref[3, i]

            def each_unit(q, carry):
                at, depth = carry
                relay = empty_ref[half, at]
                place = jnp.minimum(depth, width - 1)
                stage[relay, place] = stage[target, q]
                code_ref[relay, place] = code_ref[target, q]
                wrap = at + 1 >= free
                return jnp.where(wrap, 0, at + 1), jnp.where(wrap, depth + 1, depth)

            return lax.fori_loop(jnp.maximum(base, width), base + filled, each_unit, carry)

        lax.fori_loop(first, last, each_tile, (jnp.int32(0), jnp.int32(0)))

    copy = pltpu.make_async_copy(stage.at[:, pl.ds(0, width)], out_ref, sem)
    copy.start()
    copy.wait()


def spread(tiles, meta, empties, counts, devices, width, length, stride):
    count, side = tiles.shape[0], tiles.shape[1]
    units = side // UNIT
    smem = pl.BlockSpec(memory_space=pltpu.SMEM)
    return pl.pallas_call(
        functools.partial(spread_kernel, width, stride),
        out_shape=[
            jax.ShapeDtypeStruct((devices, width, UNIT, side), jnp.float32),
            jax.ShapeDtypeStruct((devices, length), jnp.int32),
        ],
        in_specs=[smem, smem, smem, pl.BlockSpec(memory_space=pltpu.VMEM)],
        out_specs=[pl.BlockSpec(memory_space=pl.ANY), smem],
        scratch_shapes=[
            pltpu.VMEM((devices, length, UNIT, side), jnp.float32),
            pltpu.SemaphoreType.DMA,
        ],
        compiler_params=pltpu.CompilerParams(vmem_limit_bytes=40 * MIB),
    )(meta, empties, counts, tiles.reshape(count, units, UNIT, side))


def relay_kernel(slot_ref, arrived_ref, out_ref):
    devices, width = slot_ref.shape

    @pl.loop(0, devices)
    def _(s):
        def more(k):
            return (k < width) & (slot_ref[s, jnp.minimum(k, width - 1)] >= 0)

        def move(k):
            out_ref[slot_ref[s, k]] = arrived_ref[s, k]
            return k + 1

        lax.while_loop(more, move, jnp.int32(0))


def relay(slots, arrived, length):
    vmem = pl.BlockSpec(memory_space=pltpu.VMEM)
    return pl.pallas_call(
        relay_kernel,
        out_shape=jax.ShapeDtypeStruct((length,) + arrived.shape[2:], jnp.float32),
        in_specs=[pl.BlockSpec(memory_space=pltpu.SMEM), vmem],
        out_specs=vmem,
        compiler_params=pltpu.CompilerParams(vmem_limit_bytes=40 * MIB),
    )(slots, arrived)


def add_kernel(
    cols_blocks, block_ref, unit_ref, index_ref, count_ref, partial_ref, arrived_ref, out_ref, buf,
    group_start, sem_in, sem_out
):
    slots, side = buf.shape[0], buf.shape[1]
    unit = arrived_ref.shape[1]
    ahead = slots // 2
    count = count_ref[0]

    def listed(i, carry):
        groups, last = carry
        block = block_ref[i]
        fresh = block != last

        @pl.when(fresh)
        def _():
            group_start[groups] = i

        return jnp.where(fresh, groups + 1, groups), block

    groups, _ = lax.fori_loop(0, count, listed, (jnp.int32(0), jnp.int32(-1)))
    group_start[groups] = count

    def window(g):
        block = block_ref[group_start[g]]
        rows = pl.ds(pl.multiple_of(block // cols_blocks * side, side), side)
        columns = pl.ds(pl.multiple_of(block % cols_blocks * side, side), side)
        return out_ref.at[rows, columns]

    def fetch(g):
        at = g % slots
        return pltpu.make_async_copy(window(g), buf.at[at], sem_in.at[at])

    def store(g):
        at = g % slots
        return pltpu.make_async_copy(buf.at[at], window(g), sem_out.at[at])

    @pl.loop(0, jnp.minimum(groups, ahead))
    def _(g):
        fetch(g).start()

    @pl.loop(0, groups)
    def _(g):
        @pl.when(g + ahead < groups)
        def _():
            @pl.when(g >= ahead)
            def _():
                store(g - ahead).wait()

            fetch(g + ahead).start()

        fetch(g).wait()

        @pl.loop(group_start[g], group_start[g + 1])
        def _(i):
            rows = pl.ds(pl.multiple_of(unit_ref[i] * unit, unit), unit)
            buf[g % slots, rows] += arrived_ref[index_ref[i]]

        store(g).start()

    @pl.loop(jnp.maximum(groups - slots, 0), groups)
    def _(g):
        store(g).wait()


def add_relayed(partial, arrived, listing, cols_blocks):
    row_len, col_len = partial.shape
    unit, side = arrived.shape[1:]
    smem = pl.BlockSpec(memory_space=pltpu.SMEM)
    hbm = pl.BlockSpec(memory_space=pl.ANY)
    return pl.pallas_call(
        functools.partial(add_kernel, cols_blocks),
        out_shape=jax.ShapeDtypeStruct((row_len, col_len), jnp.float32),
        in_specs=[smem, smem, smem, smem, hbm, pl.BlockSpec(memory_space=pltpu.VMEM)],
        out_specs=hbm,
        scratch_shapes=[
            pltpu.VMEM((16, side, side), jnp.float32),
            pltpu.SMEM((arrived.shape[0] + 1,), jnp.int32),
            pltpu.SemaphoreType.DMA((16,)),
            pltpu.SemaphoreType.DMA((16,)),
        ],
        input_output_aliases={4: 0},
        compiler_params=pltpu.CompilerParams(vmem_limit_bytes=24 * MIB),
    )(*listing, partial, arrived)


def panel_kernel(code_ref, first_ref, front_ref, arrived_ref, out_ref):
    side = arrived_ref.shape[1]

    @pl.when(first_ref[0] == 1)
    def _():
        out_ref[...] = front_ref[...]

    @pl.when(first_ref[0] == 0)
    def _():
        out_ref[...] = jnp.zeros_like(out_ref)

    @pl.loop(0, arrived_ref.shape[0])
    def _(k):
        code = code_ref[k]
        for part in range(PANELS):

            @pl.when((code >= 0) & (code % PANELS == part))
            def _():
                rows = pl.ds(pl.multiple_of(code // PANELS * side, side), side)
                out_ref[rows, part * side : (part + 1) * side] += arrived_ref[k]


def raw_panel(front, arrived, codes, first):
    row_len = front.shape[0]
    smem = pl.BlockSpec(memory_space=pltpu.SMEM)
    return pl.pallas_call(
        panel_kernel,
        grid=(1,),
        out_shape=jax.ShapeDtypeStruct((row_len, TOTAL), jnp.float32),
        in_specs=[
            smem,
            smem,
            pl.BlockSpec((row_len, TOTAL), lambda i: (0, 0)),
            pl.BlockSpec(arrived.shape, lambda i: (0, 0, 0)),
        ],
        out_specs=pl.BlockSpec((row_len, TOTAL), lambda i: (0, 0)),
        compiler_params=pltpu.CompilerParams(vmem_limit_bytes=40 * MIB),
    )(codes, first, front, arrived)


def split(value):
    high = value.astype(jnp.bfloat16)
    low = (value - high.astype(jnp.float32)).astype(jnp.bfloat16)
    return high, low


def rows_kernel(raw_ref, inverse_ref, out_ref, parts_ref):
    solved = dot_nt(raw_ref[...], inverse_ref[...])
    out_ref[...] = solved
    high, low = split(solved)
    parts_ref[:, :TOTAL] = high
    parts_ref[:, TOTAL : 2 * TOTAL] = high
    parts_ref[:, 2 * TOTAL :] = low


def solve_rows(raw, inverse):
    length = raw.shape[0]
    step = min(512, length)
    block = pl.BlockSpec((step, TOTAL), lambda i: (i, 0))
    return pl.pallas_call(
        rows_kernel,
        grid=(length // step,),
        out_shape=[
            jax.ShapeDtypeStruct((length, TOTAL), jnp.float32),
            jax.ShapeDtypeStruct((length, 3 * TOTAL), jnp.bfloat16),
        ],
        in_specs=[block, pl.BlockSpec((TOTAL, TOTAL), lambda i: (0, 0))],
        out_specs=[block, pl.BlockSpec((step, 3 * TOTAL), lambda i: (i, 0))],
        compiler_params=pltpu.CompilerParams(vmem_limit_bytes=24 * MIB),
    )(raw, inverse)


def cols_kernel(raw_ref, inverse_ref, out_ref, parts_ref):
    solved = dot_nt(inverse_ref[...], raw_ref[...])
    out_ref[...] = solved
    high, low = split(solved)
    parts_ref[:TOTAL] = high
    parts_ref[TOTAL : 2 * TOTAL] = low
    parts_ref[2 * TOTAL :] = high


def solve_cols(raw, inverse):
    length = raw.shape[0]
    step = min(512, length)
    block = pl.BlockSpec((TOTAL, step), lambda i: (0, i))
    return pl.pallas_call(
        cols_kernel,
        grid=(length // step,),
        out_shape=[
            jax.ShapeDtypeStruct((TOTAL, length), jnp.float32),
            jax.ShapeDtypeStruct((3 * TOTAL, length), jnp.bfloat16),
        ],
        in_specs=[
            pl.BlockSpec((step, TOTAL), lambda i: (i, 0)),
            pl.BlockSpec((TOTAL, TOTAL), lambda i: (0, 0)),
        ],
        out_specs=[block, pl.BlockSpec((3 * TOTAL, step), lambda i: (0, i))],
        compiler_params=pltpu.CompilerParams(vmem_limit_bytes=24 * MIB),
    )(raw, inverse)


def final_kernel(
    cols_blocks, runs, code_ref, run_ref, place_ref, front_ref, rows_ref, rows_parts, cols_ref, cols_parts,
    lower_ref, arrived_ref, out_ref, cursor
):
    step = pl.program_id(0)
    sources, capacity = code_ref.shape
    height, width = front_ref.shape
    unit, side = arrived_ref.shape[2:]
    per_step = height // unit

    @pl.when(step == 0)
    def _():
        for s in range(sources):
            cursor[s] = 0

    chunk = min(512, width)
    for start in range(0, width, chunk):
        at = slice(start, start + chunk)
        change = jnp.dot(rows_parts[...], cols_parts[:, at], preferred_element_type=jnp.float32)
        out_ref[:, at] = front_ref[:, at] - change

    edge = (step + 1) * per_step * cols_blocks

    @pl.loop(0, sources)
    def _(s):
        def more(k):
            code = code_ref[s, jnp.minimum(k, capacity - 1)]
            return (k < capacity) & (code >= 0) & (code < edge)

        def add(k):
            code = code_ref[s, k]
            length = run_ref[s, k]
            unit_row = code // cols_blocks - step * per_step
            columns = pl.ds(pl.multiple_of(code % cols_blocks * side, side), side)
            for run in runs:
                skipped = length // (2 * run) * (2 * run)

                @pl.when(length // run % 2 == 1)
                def _():
                    rows = pl.ds(pl.multiple_of((unit_row + skipped) * unit, unit), run * unit)
                    block = arrived_ref[s, pl.ds(k + skipped, run)]
                    out_ref[rows, columns] += block.reshape(run * unit, side)

            return k + length

        cursor[s] = lax.while_loop(more, add, cursor[s])

    top = (place_ref[0] == 0) & (step == 0)

    @pl.when(top)
    def _():
        out_ref[...] = cols_ref[...]

    @pl.when(place_ref[1] == 0)
    def _():
        out_ref[:, :TOTAL] = jnp.where(top, lower_ref[...], rows_ref[...])


def finish(front, rows, cols, lower, arrived, codes, lengths, place, cols_blocks):
    row_len, col_len = front.shape
    height = TOTAL
    smem = pl.BlockSpec(memory_space=pltpu.SMEM)
    block = pl.BlockSpec((height, TOTAL), lambda i: (i, 0))
    parts = pl.BlockSpec((height, 3 * TOTAL), lambda i: (i, 0))
    wide = pl.BlockSpec((height, col_len), lambda i: (i, 0))
    whole = pl.BlockSpec((TOTAL, col_len), lambda i: (0, 0))
    whole_parts = pl.BlockSpec((3 * TOTAL, col_len), lambda i: (0, 0))
    runs = (16, 8, 4, 2, 1) if arrived.shape[2] == UNIT else (1,)
    return pl.pallas_call(
        functools.partial(final_kernel, cols_blocks, runs),
        grid=(row_len // height,),
        out_shape=jax.ShapeDtypeStruct((row_len, col_len), jnp.float32),
        in_specs=[
            smem, smem, smem, wide, block, parts, whole, whole_parts,
            pl.BlockSpec((TOTAL, TOTAL), lambda i: (0, 0)),
            pl.BlockSpec(memory_space=pltpu.VMEM),
        ],
        out_specs=wide,
        scratch_shapes=[pltpu.SMEM((codes.shape[0],), jnp.int32)],
        compiler_params=pltpu.CompilerParams(vmem_limit_bytes=56 * MIB),
    )(codes, lengths, place, front, *rows, *cols, lower, arrived)


def factor(diagonal):
    def lower_of(block):
        return jnp.linalg.cholesky(jnp.tril(block) + jnp.tril(block, -1).T)

    def inverse_of(block):
        return jax.scipy.linalg.solve_triangular(block, jnp.eye(NB, dtype=jnp.float32), lower=True)

    first = lower_of(diagonal[:NB, :NB])
    first_inverse = inverse_of(first)
    below = dot_nt(diagonal[NB:, :NB], first_inverse)
    second = lower_of(diagonal[NB:, NB:] - dot_nt(below, below))
    second_inverse = inverse_of(second)
    corner = -jnp.dot(second_inverse, jnp.dot(below, first_inverse, precision=precise), precision=precise)
    zero = jnp.zeros((NB, NB), jnp.float32)
    return jnp.block([[first, zero], [below, second]]), jnp.block([[first_inverse, zero], [corner, second_inverse]])


def body(front, tiles, tile_block, valid_rows):
    row_len, col_len = front.shape
    row_count = lax.axis_size("row")
    col_count = lax.axis_size("col")
    device_count = row_count * col_count
    per_device = tiles.shape[0]
    side = tiles.shape[1]
    capacity = 2 * per_device // device_count
    rows_blocks = row_len // side
    cols_blocks = col_len // side
    row_now = lax.axis_index("row")
    col_now = lax.axis_index("col")
    device_now = row_now * col_count + col_now

    block_row = tile_block[0].reshape(device_count, per_device)
    block_col = tile_block[1].reshape(device_count, per_device)
    target_row = block_row // rows_blocks
    target = target_row * col_count + block_col // cols_blocks
    code = block_row % rows_blocks * cols_blocks + block_col % cols_blocks
    position = lax.broadcasted_iota(jnp.int32, target.shape, 1)
    place = jnp.stack([row_now, col_now]).astype(jnp.int32)

    def own(values):
        return lax.dynamic_index_in_dim(values, device_now, 0, keepdims=False)

    in_panel = block_col < PANELS
    panel_key = jnp.where(in_panel, target_row, -1)
    panel_rank = jnp.sum(
        (panel_key[:, :, None] == panel_key[:, None, :]) & (position[:, None, :] < position[:, :, None]),
        axis=2,
    )
    same_col = lax.dynamic_index_in_dim(
        jnp.stack([panel_key, panel_rank, code]).reshape(3, row_count, col_count, per_device),
        col_now, 2, keepdims=False,
    )

    def send_panel(tiles, valid_rows, depth):
        ahead = (own(target_row) - row_now) % row_count
        fits = own(in_panel) & (own(panel_rank) < depth)
        panel_slot = jnp.where(fits, ahead * depth + own(panel_rank), -1)
        panel_out = pack(tiles, panel_slot, valid_rows, row_count * depth)
        panel_in = [panel_out[:depth]]
        for shift in range(1, row_count):
            sending = panel_out[shift * depth : (shift + 1) * depth]
            turn = [(r, (r + shift) % row_count) for r in range(row_count)]
            panel_in.append(lax.ppermute(sending, "row", turn))
        return panel_in

    def sum_panel(front, panel_in, depth):
        fits = (same_col[0] == row_now)[:, :, None] & (same_col[1][:, :, None] == jnp.arange(depth))
        panel_code = same_col[2] // cols_blocks * PANELS + same_col[2] % cols_blocks
        panel_codes = jnp.sum(jnp.where(fits, panel_code[:, :, None] + 1, 0), axis=1) - 1
        by_shift = (row_now - jnp.arange(row_count)) % row_count
        panel_codes = jnp.take(panel_codes, by_shift, axis=0).reshape(-1)
        first = (col_now == 0).astype(jnp.int32).reshape(1)
        return raw_panel(front, jnp.concatenate(panel_in, 0), panel_codes, first)

    def sum_corner(partial):
        corner = jnp.where(row_now == 0, partial[:TOTAL], 0.0)
        diagonal = corner
        for other in range(1, row_count):
            diagonal += lax.ppermute(corner, "row", [(0, other)])
        return diagonal

    panel_depth = (capacity * 5 + 7) // 8
    panel_in = send_panel(tiles, valid_rows, panel_depth)

    units = side // UNIT
    length = capacity * units
    width = length * 21 // 32
    pass_on = length * 3 // 8
    half_count = device_count // 2
    half_base = device_now // half_count * half_count
    unit_rows = rows_blocks * units
    local_codes = unit_rows * cols_blocks
    own_target, own_code = own(target), own(code)
    own_position = own(position)
    filled = (valid_rows + UNIT - 1) // UNIT
    key = (own_target * rows_blocks * cols_blocks + own_code) * per_device + own_position
    before = key[None, :] < key[:, None]
    together = own_target[None, :] == own_target[:, None]
    base = jnp.sum(jnp.where(before & together, filled[None, :], 0), axis=1)
    order = jnp.sum(before, axis=1)
    unit_code = (own_target * unit_rows + own_code // cols_blocks * units) * cols_blocks
    unit_code += own_code % cols_blocks
    meta = jnp.stack([own_position, own_target, base, filled, unit_code, valid_rows])
    meta = jnp.sum(
        jnp.where(order[None, :, None] == jnp.arange(per_device), meta[:, :, None], 0), axis=1
    )
    to_device = own_target[:, None] == jnp.arange(device_count)
    load = jnp.sum(jnp.where(to_device, filled[:, None], 0), axis=0).reshape(2, half_count)
    empty = load == 0
    empty_rank = jnp.cumsum(empty, axis=1) - 1
    device_ids = jnp.arange(device_count).reshape(2, half_count)
    listed = (empty[:, :, None]) & (empty_rank[:, :, None] == jnp.arange(half_count))
    empties = jnp.sum(jnp.where(listed, device_ids[:, :, None], 0), axis=1)
    free = jnp.sum(empty, axis=1)
    left = jnp.sum(jnp.maximum(load - width, 0), axis=1)
    failed = jnp.any(left > free * width) | jnp.any(own(in_panel) & (own(panel_rank) >= panel_depth))
    counts = jnp.concatenate([jnp.sum(own_target < half_count)[None], free]).astype(jnp.int32)
    outgoing, sent_codes = spread(
        tiles, meta.astype(jnp.int32), empties.astype(jnp.int32), counts,
        device_count, width, length, cols_blocks,
    )

    partial = sum_panel(front, panel_in, panel_depth)
    partial, sent_codes = lax.optimization_barrier((partial, sent_codes))
    diagonal = sum_corner(partial)
    got = lax.all_to_all(sent_codes[:, :width], ("row", "col"), 0, 0, tiled=True)
    got_target = got // local_codes
    local = got % local_codes
    mine = (got >= 0) & (got_target == device_now)
    direct_codes = jnp.where(mine, local, -1)
    steps = jnp.arange(width)
    opening = (local // cols_blocks % units == 0) | jnp.logical_not(mine)
    later = (steps[None, :] > steps[:, None]) & opening[:, None, :]
    direct_runs = jnp.min(jnp.where(later, steps, width), axis=2) - steps
    total_units = device_count * width
    passing = ((got >= 0) & (got_target != device_now)).reshape(-1)
    flat_key = jnp.where(passing, got.reshape(-1) * total_units + jnp.arange(total_units), -1)
    flat_target = jnp.where(passing, got_target.reshape(-1), -1)
    rank = jnp.sum(
        (flat_target[None, :] == flat_target[:, None]) & (flat_key[None, :] < flat_key[:, None]), axis=1
    )
    failed = failed | jnp.any(passing & (rank >= pass_on))
    relay_slot = jnp.where(
        passing & (rank < pass_on), (flat_target - half_base) * pass_on + rank, -1
    )
    picked = relay_slot[:, None] == jnp.arange(half_count * pass_on)
    relay_codes = jnp.sum(jnp.where(picked, local.reshape(-1)[:, None] + 1, 0), axis=0) - 1
    notes = jnp.zeros((2, half_count, pass_on + 1), jnp.int32)
    notes = lax.dynamic_update_slice(
        notes, relay_codes.reshape(1, half_count, pass_on).astype(jnp.int32), (device_now // half_count, 0, 0)
    )
    notes = notes.at[:, :, pass_on].set(failed.astype(jnp.int32))
    notes = lax.all_to_all(
        notes.reshape(device_count, pass_on + 1), ("row", "col"), 0, 0, tiled=True
    )
    too_full = jnp.any(notes[:, pass_on] != 0)
    relay_codes = lax.dynamic_slice_in_dim(notes, half_base, half_count, 0)[:, :pass_on]
    relay_slot = relay_slot.reshape(device_count, width)

    flat = relay_codes.reshape(-1)
    unit_row, relay_col = flat // cols_blocks, flat % cols_blocks
    wanted = (flat >= 0) & ((row_now > 0) | (unit_row >= TOTAL // UNIT))
    wanted &= (col_now > 0) | (relay_col >= PANELS)
    relay_block = unit_row // units * cols_blocks + relay_col
    relay_key = jnp.where(wanted, relay_block * units + unit_row % units, local_codes)
    relay_key = relay_key * flat.shape[0] + jnp.arange(flat.shape[0])
    relay_order = jnp.sum(relay_key[None, :] < relay_key[:, None], axis=1)
    listing = jnp.stack([relay_block, unit_row % units, jnp.arange(flat.shape[0])])
    at_order = relay_order[None, :, None] == jnp.arange(flat.shape[0])
    listing = jnp.sum(jnp.where(at_order, listing[:, :, None], 0), axis=1).astype(jnp.int32)
    listing = [*listing, jnp.sum(wanted).astype(jnp.int32).reshape(1)]

    outgoing, notes, diagonal, partial = lax.optimization_barrier((outgoing, notes, diagonal, partial))
    raw_rows, diagonal = lax.psum((partial, diagonal), "col")
    arrived = lax.all_to_all(outgoing, ("row", "col"), 0, 0, tiled=True)
    slice_start = col_now * col_len % row_len
    slice_root = col_now * col_len // row_len

    def chain(raw_rows, diagonal):
        picked = lax.dynamic_slice_in_dim(raw_rows, slice_start, col_len, 0)
        raw_cols = lax.psum(jnp.where(row_now == slice_root, picked, 0.0), "row")
        lower, inverse = factor(diagonal)
        return solve_rows(raw_rows, inverse), solve_cols(raw_cols, inverse), lower

    rows, cols, lower = chain(raw_rows, diagonal)
    arrived, rows, cols, lower = lax.optimization_barrier((arrived, rows, cols, lower))

    def relayed(front, tiles, valid_rows, arrived, rows, cols, lower):
        passed = relay(relay_slot, arrived, half_count * pass_on)
        halves = [list(range(half_count)), list(range(half_count, device_count))]
        passed = lax.all_to_all(
            passed.reshape(half_count, pass_on, UNIT, side), ("row", "col"), 0, 0,
            axis_index_groups=halves, tiled=True,
        )
        partial = finish(
            front, rows, cols, lower, arrived, direct_codes, direct_runs, place, cols_blocks
        )
        return add_relayed(partial, passed.reshape(-1, UNIT, side), listing, cols_blocks)

    def padded(front, tiles, valid_rows, arrived, rows, cols, lower):
        partial = sum_panel(front, send_panel(tiles, valid_rows, capacity), capacity)
        raw_rows, diagonal = lax.psum((partial, sum_corner(partial)), "col")
        order = (target * rows_blocks * cols_blocks + code) * per_device + position
        ranking = jnp.sum(
            (target[:, :, None] == target[:, None, :]) & (order[:, None, :] < order[:, :, None]), axis=2
        )
        slot = own(target) * capacity + own(ranking)
        here = (target == device_now)[:, :, None] & (ranking[:, :, None] == jnp.arange(capacity))
        codes = jnp.sum(jnp.where(here, code[:, :, None] + 1, 0), axis=1) - 1
        packed = pack(tiles, slot, valid_rows, device_count * capacity)
        arrived = lax.all_to_all(
            packed.reshape(device_count, capacity, side, side), ("row", "col"), 0, 0, tiled=True
        )
        rows, cols, lower = chain(raw_rows, diagonal)
        return finish(
            front, rows, cols, lower, arrived, codes, jnp.ones_like(codes), place, cols_blocks
        )

    return lax.cond(
        too_full, padded, relayed, front, tiles, valid_rows, arrived, rows, cols, lower
    )


def solution(mesh):
    placed = (P("row", "col"), P(("row", "col"), None, None), P(), P(("row", "col")))
    return jax.shard_map(
        body, mesh=mesh, in_specs=placed, out_specs=P("row", "col"), check_vma=False
    )
```

```python
import functools

import jax
import jax.numpy as jnp
from jax import lax
from jax.experimental import pallas as pl
from jax.experimental.pallas import tpu as pltpu
from jax.sharding import PartitionSpec as P

NB = 128
PANELS = 2
TOTAL = NB * PANELS
MIB = 1 << 20
UNIT = 8


precise = lax.Precision.HIGHEST


def dot_nt(a, b, precision=precise):
    return lax.dot_general(
        a, b, (((1,), (1,)), ((), ())), precision=precision, preferred_element_type=jnp.float32
    )


def pack_kernel(slot_ref, valid_ref, tiles_ref, out_ref, buf, sem_in, sem_out):
    count, side = tiles_ref.shape[0], tiles_ref.shape[1]

    def fetch(t):
        return pltpu.make_async_copy(tiles_ref.at[t], buf.at[t], sem_in.at[t])

    def store(t):
        return pltpu.make_async_copy(buf.at[t], out_ref.at[jnp.maximum(slot_ref[t], 0)], sem_out.at[t])

    def each(act):
        @pl.loop(0, count)
        def _(t):
            @pl.when(slot_ref[t] >= 0)
            def _():
                act(t)

    def mask(t):
        fetch(t).wait()
        rows = lax.broadcasted_iota(jnp.int32, (side, side), 0)
        buf[t] = jnp.where(rows < valid_ref[t], buf[t], 0.0)
        store(t).start()

    each(lambda t: fetch(t).start())
    each(mask)
    each(lambda t: store(t).wait())


def pack(tiles, slots, valid, n_slots):
    count, side = tiles.shape[0], tiles.shape[1]
    smem = pl.BlockSpec(memory_space=pltpu.SMEM)
    return pl.pallas_call(
        pack_kernel,
        out_shape=jax.ShapeDtypeStruct((n_slots, side, side), jnp.float32),
        in_specs=[smem, smem, pl.BlockSpec(memory_space=pl.ANY)],
        out_specs=pl.BlockSpec(memory_space=pl.ANY),
        scratch_shapes=[
            pltpu.VMEM((count, side, side), jnp.float32),
            pltpu.SemaphoreType.DMA((count,)),
            pltpu.SemaphoreType.DMA((count,)),
        ],
        compiler_params=pltpu.CompilerParams(vmem_limit_bytes=24 * MIB),
    )(slots, valid, tiles)


def spread_kernel(
    width, stride, meta_ref, empty_ref, count_ref, tiles_ref, out_ref, code_ref, stage, sem
):
    count, units = tiles_ref.shape[0], tiles_ref.shape[1]
    devices, length = code_ref.shape

    @pl.loop(0, devices)
    def _(d):
        for k in range(length):
            code_ref[d, k] = -1

    @pl.loop(0, count)
    def _(i):
        tile, target, base = meta_ref[0, i], meta_ref[1, i], meta_ref[2, i]
        filled, code, valid = meta_ref[3, i], meta_ref[4, i], meta_ref[5, i]
        shape = tiles_ref.shape[1:]
        rows = lax.broadcasted_iota(jnp.int32, shape, 0) * shape[1]
        rows += lax.broadcasted_iota(jnp.int32, shape, 1)
        stage[target, pl.ds(base, units)] = jnp.where(rows < valid, tiles_ref[tile], 0.0)
        for u in range(units):
            code_ref[target, base + u] = jnp.where(u < filled, code + u * stride, -1)

    for half in range(2):
        first = 0 if half == 0 else count_ref[0]
        last = count_ref[0] if half == 0 else count
        free = count_ref[1 + half]

        def each_tile(i, carry):
            target, base, filled = meta_ref[1, i], meta_ref[2, i], meta_ref[3, i]

            def each_unit(q, carry):
                at, depth = carry
                relay = empty_ref[half, at]
                place = jnp.minimum(depth, width - 1)
                stage[relay, place] = stage[target, q]
                code_ref[relay, place] = code_ref[target, q]
                wrap = at + 1 >= free
                return jnp.where(wrap, 0, at + 1), jnp.where(wrap, depth + 1, depth)

            return lax.fori_loop(jnp.maximum(base, width), base + filled, each_unit, carry)

        lax.fori_loop(first, last, each_tile, (jnp.int32(0), jnp.int32(0)))

    copy = pltpu.make_async_copy(stage.at[:, pl.ds(0, width)], out_ref, sem)
    copy.start()
    copy.wait()


def spread(tiles, meta, empties, counts, devices, width, length, stride):
    count, side = tiles.shape[0], tiles.shape[1]
    units = side // UNIT
    smem = pl.BlockSpec(memory_space=pltpu.SMEM)
    return pl.pallas_call(
        functools.partial(spread_kernel, width, stride),
        out_shape=[
            jax.ShapeDtypeStruct((devices, width, UNIT, side), jnp.float32),
            jax.ShapeDtypeStruct((devices, length), jnp.int32),
        ],
        in_specs=[smem, smem, smem, pl.BlockSpec(memory_space=pltpu.VMEM)],
        out_specs=[pl.BlockSpec(memory_space=pl.ANY), smem],
        scratch_shapes=[
            pltpu.VMEM((devices, length, UNIT, side), jnp.float32),
            pltpu.SemaphoreType.DMA,
        ],
        compiler_params=pltpu.CompilerParams(vmem_limit_bytes=40 * MIB),
    )(meta, empties, counts, tiles.reshape(count, units, UNIT, side))


def relay_kernel(slot_ref, arrived_ref, out_ref):
    devices, width = slot_ref.shape

    @pl.loop(0, devices)
    def _(s):
        def more(k):
            return (k < width) & (slot_ref[s, jnp.minimum(k, width - 1)] >= 0)

        def move(k):
            out_ref[slot_ref[s, k]] = arrived_ref[s, k]
            return k + 1

        lax.while_loop(more, move, jnp.int32(0))


def relay(slots, arrived, length):
    vmem = pl.BlockSpec(memory_space=pltpu.VMEM)
    return pl.pallas_call(
        relay_kernel,
        out_shape=jax.ShapeDtypeStruct((length,) + arrived.shape[2:], jnp.float32),
        in_specs=[pl.BlockSpec(memory_space=pltpu.SMEM), vmem],
        out_specs=vmem,
        compiler_params=pltpu.CompilerParams(vmem_limit_bytes=40 * MIB),
    )(slots, arrived)


def add_kernel(
    cols_blocks, block_ref, unit_ref, index_ref, count_ref, partial_ref, arrived_ref, out_ref, buf,
    group_start, sem_in, sem_out
):
    slots, side = buf.shape[0], buf.shape[1]
    unit = arrived_ref.shape[1]
    ahead = slots // 2
    count = count_ref[0]

    def listed(i, carry):
        groups, last = carry
        block = block_ref[i]
        fresh = block != last

        @pl.when(fresh)
        def _():
            group_start[groups] = i

        return jnp.where(fresh, groups + 1, groups), block

    groups, _ = lax.fori_loop(0, count, listed, (jnp.int32(0), jnp.int32(-1)))
    group_start[groups] = count

    def window(g):
        block = block_ref[group_start[g]]
        rows = pl.ds(pl.multiple_of(block // cols_blocks * side, side), side)
        columns = pl.ds(pl.multiple_of(block % cols_blocks * side, side), side)
        return out_ref.at[rows, columns]

    def fetch(g):
        at = g % slots
        return pltpu.make_async_copy(window(g), buf.at[at], sem_in.at[at])

    def store(g):
        at = g % slots
        return pltpu.make_async_copy(buf.at[at], window(g), sem_out.at[at])

    @pl.loop(0, jnp.minimum(groups, ahead))
    def _(g):
        fetch(g).start()

    @pl.loop(0, groups)
    def _(g):
        @pl.when(g + ahead < groups)
        def _():
            @pl.when(g >= ahead)
            def _():
                store(g - ahead).wait()

            fetch(g + ahead).start()

        fetch(g).wait()

        @pl.loop(group_start[g], group_start[g + 1])
        def _(i):
            rows = pl.ds(pl.multiple_of(unit_ref[i] * unit, unit), unit)
            buf[g % slots, rows] += arrived_ref[index_ref[i]]

        store(g).start()

    @pl.loop(jnp.maximum(groups - slots, 0), groups)
    def _(g):
        store(g).wait()


def add_relayed(partial, arrived, listing, cols_blocks):
    row_len, col_len = partial.shape
    unit, side = arrived.shape[1:]
    smem = pl.BlockSpec(memory_space=pltpu.SMEM)
    hbm = pl.BlockSpec(memory_space=pl.ANY)
    return pl.pallas_call(
        functools.partial(add_kernel, cols_blocks),
        out_shape=jax.ShapeDtypeStruct((row_len, col_len), jnp.float32),
        in_specs=[smem, smem, smem, smem, hbm, pl.BlockSpec(memory_space=pltpu.VMEM)],
        out_specs=hbm,
        scratch_shapes=[
            pltpu.VMEM((16, side, side), jnp.float32),
            pltpu.SMEM((arrived.shape[0] + 1,), jnp.int32),
            pltpu.SemaphoreType.DMA((16,)),
            pltpu.SemaphoreType.DMA((16,)),
        ],
        input_output_aliases={4: 0},
        compiler_params=pltpu.CompilerParams(vmem_limit_bytes=24 * MIB),
    )(*listing, partial, arrived)


def panel_kernel(code_ref, first_ref, front_ref, arrived_ref, out_ref):
    side = arrived_ref.shape[1]

    @pl.when(first_ref[0] == 1)
    def _():
        out_ref[...] = front_ref[...]

    @pl.when(first_ref[0] == 0)
    def _():
        out_ref[...] = jnp.zeros_like(out_ref)

    @pl.loop(0, arrived_ref.shape[0])
    def _(k):
        code = code_ref[k]
        for part in range(PANELS):

            @pl.when((code >= 0) & (code % PANELS == part))
            def _():
                rows = pl.ds(pl.multiple_of(code // PANELS * side, side), side)
                out_ref[rows, part * side : (part + 1) * side] += arrived_ref[k]


def raw_panel(front, arrived, codes, first):
    row_len = front.shape[0]
    smem = pl.BlockSpec(memory_space=pltpu.SMEM)
    return pl.pallas_call(
        panel_kernel,
        grid=(1,),
        out_shape=jax.ShapeDtypeStruct((row_len, TOTAL), jnp.float32),
        in_specs=[
            smem,
            smem,
            pl.BlockSpec((row_len, TOTAL), lambda i: (0, 0)),
            pl.BlockSpec(arrived.shape, lambda i: (0, 0, 0)),
        ],
        out_specs=pl.BlockSpec((row_len, TOTAL), lambda i: (0, 0)),
        compiler_params=pltpu.CompilerParams(vmem_limit_bytes=40 * MIB),
    )(codes, first, front, arrived)


def split(value):
    high = value.astype(jnp.bfloat16)
    low = (value - high.astype(jnp.float32)).astype(jnp.bfloat16)
    return high, low


def rows_kernel(raw_ref, inverse_ref, out_ref, parts_ref):
    solved = dot_nt(raw_ref[...], inverse_ref[...])
    out_ref[...] = solved
    high, low = split(solved)
    parts_ref[:, :TOTAL] = high
    parts_ref[:, TOTAL : 2 * TOTAL] = high
    parts_ref[:, 2 * TOTAL :] = low


def solve_rows(raw, inverse):
    length = raw.shape[0]
    step = min(512, length)
    block = pl.BlockSpec((step, TOTAL), lambda i: (i, 0))
    return pl.pallas_call(
        rows_kernel,
        grid=(length // step,),
        out_shape=[
            jax.ShapeDtypeStruct((length, TOTAL), jnp.float32),
            jax.ShapeDtypeStruct((length, 3 * TOTAL), jnp.bfloat16),
        ],
        in_specs=[block, pl.BlockSpec((TOTAL, TOTAL), lambda i: (0, 0))],
        out_specs=[block, pl.BlockSpec((step, 3 * TOTAL), lambda i: (i, 0))],
        compiler_params=pltpu.CompilerParams(vmem_limit_bytes=24 * MIB),
    )(raw, inverse)


def cols_kernel(raw_ref, inverse_ref, out_ref, parts_ref):
    solved = dot_nt(inverse_ref[...], raw_ref[...])
    out_ref[...] = solved
    high, low = split(solved)
    parts_ref[:TOTAL] = high
    parts_ref[TOTAL : 2 * TOTAL] = low
    parts_ref[2 * TOTAL :] = high


def solve_cols(raw, inverse):
    length = raw.shape[0]
    step = min(512, length)
    block = pl.BlockSpec((TOTAL, step), lambda i: (0, i))
    return pl.pallas_call(
        cols_kernel,
        grid=(length // step,),
        out_shape=[
            jax.ShapeDtypeStruct((TOTAL, length), jnp.float32),
            jax.ShapeDtypeStruct((3 * TOTAL, length), jnp.bfloat16),
        ],
        in_specs=[
            pl.BlockSpec((step, TOTAL), lambda i: (i, 0)),
            pl.BlockSpec((TOTAL, TOTAL), lambda i: (0, 0)),
        ],
        out_specs=[block, pl.BlockSpec((3 * TOTAL, step), lambda i: (0, i))],
        compiler_params=pltpu.CompilerParams(vmem_limit_bytes=24 * MIB),
    )(raw, inverse)


def final_kernel(
    cols_blocks, runs, code_ref, run_ref, place_ref, front_ref, rows_ref, rows_parts, cols_ref, cols_parts,
    lower_ref, arrived_ref, out_ref, cursor
):
    step = pl.program_id(0)
    sources, capacity = code_ref.shape
    height, width = front_ref.shape
    unit, side = arrived_ref.shape[2:]
    per_step = height // unit

    @pl.when(step == 0)
    def _():
        for s in range(sources):
            cursor[s] = 0

    chunk = min(512, width)
    for start in range(0, width, chunk):
        at = slice(start, start + chunk)
        change = jnp.dot(rows_parts[...], cols_parts[:, at], preferred_element_type=jnp.float32)
        out_ref[:, at] = front_ref[:, at] - change

    edge = (step + 1) * per_step * cols_blocks

    @pl.loop(0, sources)
    def _(s):
        def more(k):
            code = code_ref[s, jnp.minimum(k, capacity - 1)]
            return (k < capacity) & (code >= 0) & (code < edge)

        def add(k):
            code = code_ref[s, k]
            length = run_ref[s, k]
            unit_row = code // cols_blocks - step * per_step
            columns = pl.ds(pl.multiple_of(code % cols_blocks * side, side), side)
            for run in runs:
                skipped = length // (2 * run) * (2 * run)

                @pl.when(length // run % 2 == 1)
                def _():
                    rows = pl.ds(pl.multiple_of((unit_row + skipped) * unit, unit), run * unit)
                    block = arrived_ref[s, pl.ds(k + skipped, run)]
                    out_ref[rows, columns] += block.reshape(run * unit, side)

            return k + length

        cursor[s] = lax.while_loop(more, add, cursor[s])

    top = (place_ref[0] == 0) & (step == 0)

    @pl.when(top)
    def _():
        out_ref[...] = cols_ref[...]

    @pl.when(place_ref[1] == 0)
    def _():
        out_ref[:, :TOTAL] = jnp.where(top, lower_ref[...], rows_ref[...])


def finish(front, rows, cols, lower, arrived, codes, lengths, place, cols_blocks):
    row_len, col_len = front.shape
    height = TOTAL
    smem = pl.BlockSpec(memory_space=pltpu.SMEM)
    block = pl.BlockSpec((height, TOTAL), lambda i: (i, 0))
    parts = pl.BlockSpec((height, 3 * TOTAL), lambda i: (i, 0))
    wide = pl.BlockSpec((height, col_len), lambda i: (i, 0))
    whole = pl.BlockSpec((TOTAL, col_len), lambda i: (0, 0))
    whole_parts = pl.BlockSpec((3 * TOTAL, col_len), lambda i: (0, 0))
    runs = (16, 8, 4, 2, 1) if arrived.shape[2] == UNIT else (1,)
    return pl.pallas_call(
        functools.partial(final_kernel, cols_blocks, runs),
        grid=(row_len // height,),
        out_shape=jax.ShapeDtypeStruct((row_len, col_len), jnp.float32),
        in_specs=[
            smem, smem, smem, wide, block, parts, whole, whole_parts,
            pl.BlockSpec((TOTAL, TOTAL), lambda i: (0, 0)),
            pl.BlockSpec(memory_space=pltpu.VMEM),
        ],
        out_specs=wide,
        scratch_shapes=[pltpu.SMEM((codes.shape[0],), jnp.int32)],
        compiler_params=pltpu.CompilerParams(vmem_limit_bytes=56 * MIB),
    )(codes, lengths, place, front, *rows, *cols, lower, arrived)


def factor(diagonal):
    def lower_of(block):
        return jnp.linalg.cholesky(jnp.tril(block) + jnp.tril(block, -1).T)

    def inverse_of(block):
        return jax.scipy.linalg.solve_triangular(block, jnp.eye(NB, dtype=jnp.float32), lower=True)

    first = lower_of(diagonal[:NB, :NB])
    first_inverse = inverse_of(first)
    below = dot_nt(diagonal[NB:, :NB], first_inverse)
    second = lower_of(diagonal[NB:, NB:] - dot_nt(below, below))
    second_inverse = inverse_of(second)
    corner = -jnp.dot(second_inverse, jnp.dot(below, first_inverse, precision=precise), precision=precise)
    zero = jnp.zeros((NB, NB), jnp.float32)
    return jnp.block([[first, zero], [below, second]]), jnp.block([[first_inverse, zero], [corner, second_inverse]])


def body(front, tiles, tile_block, valid_rows):
    row_len, col_len = front.shape
    row_count = lax.axis_size("row")
    col_count = lax.axis_size("col")
    device_count = row_count * col_count
    per_device = tiles.shape[0]
    side = tiles.shape[1]
    capacity = 2 * per_device // device_count
    rows_blocks = row_len // side
    cols_blocks = col_len // side
    row_now = lax.axis_index("row")
    col_now = lax.axis_index("col")
    device_now = row_now * col_count + col_now

    block_row = tile_block[0].reshape(device_count, per_device)
    block_col = tile_block[1].reshape(device_count, per_device)
    target_row = block_row // rows_blocks
    target = target_row * col_count + block_col // cols_blocks
    code = block_row % rows_blocks * cols_blocks + block_col % cols_blocks
    position = lax.broadcasted_iota(jnp.int32, target.shape, 1)
    place = jnp.stack([row_now, col_now]).astype(jnp.int32)

    def own(values):
        return lax.dynamic_index_in_dim(values, device_now, 0, keepdims=False)

    in_panel = block_col < PANELS
    panel_key = jnp.where(in_panel, target_row, -1)
    panel_rank = jnp.sum(
        (panel_key[:, :, None] == panel_key[:, None, :]) & (position[:, None, :] < position[:, :, None]),
        axis=2,
    )
    same_col = lax.dynamic_index_in_dim(
        jnp.stack([panel_key, panel_rank, code]).reshape(3, row_count, col_count, per_device),
        col_now, 2, keepdims=False,
    )

    def send_panel(tiles, valid_rows, depth):
        ahead = (own(target_row) - row_now) % row_count
        fits = own(in_panel) & (own(panel_rank) < depth)
        panel_slot = jnp.where(fits, ahead * depth + own(panel_rank), -1)
        panel_out = pack(tiles, panel_slot, valid_rows, row_count * depth)
        panel_in = [panel_out[:depth]]
        for shift in range(1, row_count):
            sending = panel_out[shift * depth : (shift + 1) * depth]
            turn = [(r, (r + shift) % row_count) for r in range(row_count)]
            panel_in.append(lax.ppermute(sending, "row", turn))
        return panel_in

    def sum_panel(front, panel_in, depth):
        fits = (same_col[0] == row_now)[:, :, None] & (same_col[1][:, :, None] == jnp.arange(depth))
        panel_code = same_col[2] // cols_blocks * PANELS + same_col[2] % cols_blocks
        panel_codes = jnp.sum(jnp.where(fits, panel_code[:, :, None] + 1, 0), axis=1) - 1
        by_shift = (row_now - jnp.arange(row_count)) % row_count
        panel_codes = jnp.take(panel_codes, by_shift, axis=0).reshape(-1)
        first = (col_now == 0).astype(jnp.int32).reshape(1)
        return raw_panel(front, jnp.concatenate(panel_in, 0), panel_codes, first)

    def sum_corner(partial):
        corner = jnp.where(row_now == 0, partial[:TOTAL], 0.0)
        diagonal = corner
        for other in range(1, row_count):
            diagonal += lax.ppermute(corner, "row", [(0, other)])
        return diagonal

    panel_depth = (capacity * 5 + 7) // 8
    panel_in = send_panel(tiles, valid_rows, panel_depth)

    units = side // UNIT
    length = capacity * units
    width = length * 41 // 64
    pass_on = length * 13 // 32
    half_count = device_count // 2
    half_base = device_now // half_count * half_count
    unit_rows = rows_blocks * units
    local_codes = unit_rows * cols_blocks
    own_target, own_code = own(target), own(code)
    own_position = own(position)
    filled = (valid_rows + UNIT - 1) // UNIT
    key = (own_target * rows_blocks * cols_blocks + own_code) * per_device + own_position
    before = key[None, :] < key[:, None]
    together = own_target[None, :] == own_target[:, None]
    base = jnp.sum(jnp.where(before & together, filled[None, :], 0), axis=1)
    order = jnp.sum(before, axis=1)
    unit_code = (own_target * unit_rows + own_code // cols_blocks * units) * cols_blocks
    unit_code += own_code % cols_blocks
    meta = jnp.stack([own_position, own_target, base, filled, unit_code, valid_rows])
    meta = jnp.sum(
        jnp.where(order[None, :, None] == jnp.arange(per_device), meta[:, :, None], 0), axis=1
    )
    to_device = own_target[:, None] == jnp.arange(device_count)
    load = jnp.sum(jnp.where(to_device, filled[:, None], 0), axis=0).reshape(2, half_count)
    empty = load == 0
    empty_rank = jnp.cumsum(empty, axis=1) - 1
    device_ids = jnp.arange(device_count).reshape(2, half_count)
    listed = (empty[:, :, None]) & (empty_rank[:, :, None] == jnp.arange(half_count))
    empties = jnp.sum(jnp.where(listed, device_ids[:, :, None], 0), axis=1)
    free = jnp.sum(empty, axis=1)
    left = jnp.sum(jnp.maximum(load - width, 0), axis=1)
    failed = jnp.any(left > free * width) | jnp.any(own(in_panel) & (own(panel_rank) >= panel_depth))
    counts = jnp.concatenate([jnp.sum(own_target < half_count)[None], free]).astype(jnp.int32)
    outgoing, sent_codes = spread(
        tiles, meta.astype(jnp.int32), empties.astype(jnp.int32), counts,
        device_count, width, length, cols_blocks,
    )

    partial = sum_panel(front, panel_in, panel_depth)
    partial, sent_codes = lax.optimization_barrier((partial, sent_codes))
    diagonal = sum_corner(partial)
    got = lax.all_to_all(sent_codes[:, :width], ("row", "col"), 0, 0, tiled=True)
    got_target = got // local_codes
    local = got % local_codes
    mine = (got >= 0) & (got_target == device_now)
    direct_codes = jnp.where(mine, local, -1)
    steps = jnp.arange(width)
    opening = (local // cols_blocks % units == 0) | jnp.logical_not(mine)
    later = (steps[None, :] > steps[:, None]) & opening[:, None, :]
    direct_runs = jnp.min(jnp.where(later, steps, width), axis=2) - steps
    total_units = device_count * width
    passing = ((got >= 0) & (got_target != device_now)).reshape(-1)
    flat_key = jnp.where(passing, got.reshape(-1) * total_units + jnp.arange(total_units), -1)
    flat_target = jnp.where(passing, got_target.reshape(-1), -1)
    rank = jnp.sum(
        (flat_target[None, :] == flat_target[:, None]) & (flat_key[None, :] < flat_key[:, None]), axis=1
    )
    failed = failed | jnp.any(passing & (rank >= pass_on))
    relay_slot = jnp.where(
        passing & (rank < pass_on), (flat_target - half_base) * pass_on + rank, -1
    )
    picked = relay_slot[:, None] == jnp.arange(half_count * pass_on)
    relay_codes = jnp.sum(jnp.where(picked, local.reshape(-1)[:, None] + 1, 0), axis=0) - 1
    notes = jnp.zeros((2, half_count, pass_on + 1), jnp.int32)
    notes = lax.dynamic_update_slice(
        notes, relay_codes.reshape(1, half_count, pass_on).astype(jnp.int32), (device_now // half_count, 0, 0)
    )
    notes = notes.at[:, :, pass_on].set(failed.astype(jnp.int32))
    notes = lax.all_to_all(
        notes.reshape(device_count, pass_on + 1), ("row", "col"), 0, 0, tiled=True
    )
    too_full = jnp.any(notes[:, pass_on] != 0)
    relay_codes = lax.dynamic_slice_in_dim(notes, half_base, half_count, 0)[:, :pass_on]
    relay_slot = relay_slot.reshape(device_count, width)

    flat = relay_codes.reshape(-1)
    unit_row, relay_col = flat // cols_blocks, flat % cols_blocks
    wanted = (flat >= 0) & ((row_now > 0) | (unit_row >= TOTAL // UNIT))
    wanted &= (col_now > 0) | (relay_col >= PANELS)
    relay_block = unit_row // units * cols_blocks + relay_col
    relay_key = jnp.where(wanted, relay_block * units + unit_row % units, local_codes)
    relay_key = relay_key * flat.shape[0] + jnp.arange(flat.shape[0])
    relay_order = jnp.sum(relay_key[None, :] < relay_key[:, None], axis=1)
    listing = jnp.stack([relay_block, unit_row % units, jnp.arange(flat.shape[0])])
    at_order = relay_order[None, :, None] == jnp.arange(flat.shape[0])
    listing = jnp.sum(jnp.where(at_order, listing[:, :, None], 0), axis=1).astype(jnp.int32)
    listing = [*listing, jnp.sum(wanted).astype(jnp.int32).reshape(1)]

    raw_rows = lax.psum(partial, "col")
    outgoing, notes, diagonal = lax.optimization_barrier((outgoing, notes, diagonal))
    arrived = lax.all_to_all(outgoing, ("row", "col"), 0, 0, tiled=True)
    slice_start = col_now * col_len % row_len
    slice_root = col_now * col_len // row_len

    def chain(raw_rows, diagonal):
        raw_rows, diagonal = lax.optimization_barrier((raw_rows, diagonal))
        diagonal = lax.psum(diagonal, "col")
        raw_rows, diagonal = lax.optimization_barrier((raw_rows, diagonal))
        picked = lax.dynamic_slice_in_dim(raw_rows, slice_start, col_len, 0)
        raw_cols = lax.psum(jnp.where(row_now == slice_root, picked, 0.0), "row")
        lower, inverse = factor(diagonal)
        return solve_rows(raw_rows, inverse), solve_cols(raw_cols, inverse), lower

    rows, cols, lower = chain(raw_rows, diagonal)
    tables = (relay_slot, direct_codes, direct_runs, listing)
    arrived, rows, cols, lower, tables = lax.optimization_barrier((arrived, rows, cols, lower, tables))
    relay_slot, direct_codes, direct_runs, listing = tables

    def relayed(front, tiles, valid_rows, arrived, rows, cols, lower):
        passed = relay(relay_slot, arrived, half_count * pass_on)
        halves = [list(range(half_count)), list(range(half_count, device_count))]
        passed = lax.all_to_all(
            passed.reshape(half_count, pass_on, UNIT, side), ("row", "col"), 0, 0,
            axis_index_groups=halves, tiled=True,
        )
        partial = finish(
            front, rows, cols, lower, arrived, direct_codes, direct_runs, place, cols_blocks
        )
        return add_relayed(partial, passed.reshape(-1, UNIT, side), listing, cols_blocks)

    def padded(front, tiles, valid_rows, arrived, rows, cols, lower):
        partial = sum_panel(front, send_panel(tiles, valid_rows, capacity), capacity)
        raw_rows, diagonal = lax.psum(partial, "col"), sum_corner(partial)
        order = (target * rows_blocks * cols_blocks + code) * per_device + position
        ranking = jnp.sum(
            (target[:, :, None] == target[:, None, :]) & (order[:, None, :] < order[:, :, None]), axis=2
        )
        slot = own(target) * capacity + own(ranking)
        here = (target == device_now)[:, :, None] & (ranking[:, :, None] == jnp.arange(capacity))
        codes = jnp.sum(jnp.where(here, code[:, :, None] + 1, 0), axis=1) - 1
        packed = pack(tiles, slot, valid_rows, device_count * capacity)
        arrived = lax.all_to_all(
            packed.reshape(device_count, capacity, side, side), ("row", "col"), 0, 0, tiled=True
        )
        rows, cols, lower = chain(raw_rows, diagonal)
        return finish(
            front, rows, cols, lower, arrived, codes, jnp.ones_like(codes), place, cols_blocks
        )

    return lax.cond(
        too_full, padded, relayed, front, tiles, valid_rows, arrived, rows, cols, lower
    )


def solution(mesh):
    placed = (P("row", "col"), P(("row", "col"), None, None), P(), P(("row", "col")))
    return jax.shard_map(
        body, mesh=mesh, in_specs=placed, out_specs=P("row", "col"), check_vma=False
    )
```

```python
import functools

import jax
import jax.numpy as jnp
from jax import lax
from jax.experimental import pallas as pl
from jax.experimental.pallas import tpu as pltpu
from jax.sharding import PartitionSpec as P

NB = 128
PANELS = 2
TOTAL = NB * PANELS
MIB = 1 << 20
UNIT = 8
PANEL_SLOTS = 32


precise = lax.Precision.HIGHEST


def dot_nt(a, b, precision=precise):
    return lax.dot_general(
        a, b, (((1,), (1,)), ((), ())), precision=precision, preferred_element_type=jnp.float32
    )


def pack_kernel(slot_ref, valid_ref, tiles_ref, out_ref, buf, sem_in, sem_out):
    count, side = tiles_ref.shape[0], tiles_ref.shape[1]

    def fetch(t):
        return pltpu.make_async_copy(tiles_ref.at[t], buf.at[t], sem_in.at[t])

    def store(t):
        return pltpu.make_async_copy(buf.at[t], out_ref.at[jnp.maximum(slot_ref[t], 0)], sem_out.at[t])

    def each(act):
        @pl.loop(0, count)
        def _(t):
            @pl.when(slot_ref[t] >= 0)
            def _():
                act(t)

    def mask(t):
        fetch(t).wait()
        rows = lax.broadcasted_iota(jnp.int32, (side, side), 0)
        buf[t] = jnp.where(rows < valid_ref[t], buf[t], 0.0)
        store(t).start()

    each(lambda t: fetch(t).start())
    each(mask)
    each(lambda t: store(t).wait())


def pack(tiles, slots, valid, n_slots):
    count, side = tiles.shape[0], tiles.shape[1]
    smem = pl.BlockSpec(memory_space=pltpu.SMEM)
    return pl.pallas_call(
        pack_kernel,
        out_shape=jax.ShapeDtypeStruct((n_slots, side, side), jnp.float32),
        in_specs=[smem, smem, pl.BlockSpec(memory_space=pl.ANY)],
        out_specs=pl.BlockSpec(memory_space=pl.ANY),
        scratch_shapes=[
            pltpu.VMEM((count, side, side), jnp.float32),
            pltpu.SemaphoreType.DMA((count,)),
            pltpu.SemaphoreType.DMA((count,)),
        ],
        compiler_params=pltpu.CompilerParams(vmem_limit_bytes=24 * MIB),
    )(slots, valid, tiles)


def spread_kernel(
    width, stride, meta_ref, empty_ref, count_ref, tiles_ref, out_ref, code_ref, stage, sem
):
    count, units = tiles_ref.shape[0], tiles_ref.shape[1]
    devices, length = code_ref.shape

    @pl.loop(0, devices)
    def _(d):
        for k in range(length):
            code_ref[d, k] = -1

    @pl.loop(0, count)
    def _(i):
        tile, target, base = meta_ref[0, i], meta_ref[1, i], meta_ref[2, i]
        filled, code, valid = meta_ref[3, i], meta_ref[4, i], meta_ref[5, i]
        shape = tiles_ref.shape[1:]
        rows = lax.broadcasted_iota(jnp.int32, shape, 0) * shape[1]
        rows += lax.broadcasted_iota(jnp.int32, shape, 1)
        stage[target, pl.ds(base, units)] = jnp.where(rows < valid, tiles_ref[tile], 0.0)
        for u in range(units):
            code_ref[target, base + u] = jnp.where(u < filled, code + u * stride, -1)

    for half in range(2):
        first = 0 if half == 0 else count_ref[0]
        last = count_ref[0] if half == 0 else count
        free = count_ref[1 + half]

        def each_tile(i, carry):
            target, base, filled = meta_ref[1, i], meta_ref[2, i], meta_ref[3, i]

            def each_unit(q, carry):
                at, depth = carry
                relay = empty_ref[half, at]
                place = jnp.minimum(depth, width - 1)
                stage[relay, place] = stage[target, q]
                code_ref[relay, place] = code_ref[target, q]
                wrap = at + 1 >= free
                return jnp.where(wrap, 0, at + 1), jnp.where(wrap, depth + 1, depth)

            return lax.fori_loop(jnp.maximum(base, width), base + filled, each_unit, carry)

        lax.fori_loop(first, last, each_tile, (jnp.int32(0), jnp.int32(0)))

    copy = pltpu.make_async_copy(stage.at[:, pl.ds(0, width)], out_ref, sem)
    copy.start()
    copy.wait()


def spread(tiles, meta, empties, counts, devices, width, length, stride):
    count, side = tiles.shape[0], tiles.shape[1]
    units = side // UNIT
    smem = pl.BlockSpec(memory_space=pltpu.SMEM)
    return pl.pallas_call(
        functools.partial(spread_kernel, width, stride),
        out_shape=[
            jax.ShapeDtypeStruct((devices, width, UNIT, side), jnp.float32),
            jax.ShapeDtypeStruct((devices, length), jnp.int32),
        ],
        in_specs=[smem, smem, smem, pl.BlockSpec(memory_space=pltpu.VMEM)],
        out_specs=[pl.BlockSpec(memory_space=pl.ANY), smem],
        scratch_shapes=[
            pltpu.VMEM((devices, length, UNIT, side), jnp.float32),
            pltpu.SemaphoreType.DMA,
        ],
        compiler_params=pltpu.CompilerParams(vmem_limit_bytes=40 * MIB),
    )(meta, empties, counts, tiles.reshape(count, units, UNIT, side))


def relay_kernel(slot_ref, arrived_ref, out_ref):
    devices, width = slot_ref.shape

    @pl.loop(0, devices)
    def _(s):
        def more(k):
            return (k < width) & (slot_ref[s, jnp.minimum(k, width - 1)] >= 0)

        def move(k):
            out_ref[slot_ref[s, k]] = arrived_ref[s, k]
            return k + 1

        lax.while_loop(more, move, jnp.int32(0))


def relay(slots, arrived, length):
    vmem = pl.BlockSpec(memory_space=pltpu.VMEM)
    return pl.pallas_call(
        relay_kernel,
        out_shape=jax.ShapeDtypeStruct((length,) + arrived.shape[2:], jnp.float32),
        in_specs=[pl.BlockSpec(memory_space=pltpu.SMEM), vmem],
        out_specs=vmem,
        compiler_params=pltpu.CompilerParams(vmem_limit_bytes=40 * MIB),
    )(slots, arrived)


def add_kernel(
    cols_blocks, block_ref, unit_ref, index_ref, count_ref, partial_ref, arrived_ref, out_ref, buf,
    group_start, sem_in, sem_out
):
    slots, side = buf.shape[0], buf.shape[1]
    unit = arrived_ref.shape[1]
    ahead = slots // 2
    count = count_ref[0]

    def listed(i, carry):
        groups, last = carry
        block = block_ref[i]
        fresh = block != last

        @pl.when(fresh)
        def _():
            group_start[groups] = i

        return jnp.where(fresh, groups + 1, groups), block

    groups, _ = lax.fori_loop(0, count, listed, (jnp.int32(0), jnp.int32(-1)))
    group_start[groups] = count

    def window(g):
        block = block_ref[group_start[g]]
        rows = pl.ds(pl.multiple_of(block // cols_blocks * side, side), side)
        columns = pl.ds(pl.multiple_of(block % cols_blocks * side, side), side)
        return out_ref.at[rows, columns]

    def fetch(g):
        at = g % slots
        return pltpu.make_async_copy(window(g), buf.at[at], sem_in.at[at])

    def store(g):
        at = g % slots
        return pltpu.make_async_copy(buf.at[at], window(g), sem_out.at[at])

    @pl.loop(0, jnp.minimum(groups, ahead))
    def _(g):
        fetch(g).start()

    @pl.loop(0, groups)
    def _(g):
        @pl.when(g + ahead < groups)
        def _():
            @pl.when(g >= ahead)
            def _():
                store(g - ahead).wait()

            fetch(g + ahead).start()

        fetch(g).wait()

        @pl.loop(group_start[g], group_start[g + 1])
        def _(i):
            rows = pl.ds(pl.multiple_of(unit_ref[i] * unit, unit), unit)
            buf[g % slots, rows] += arrived_ref[index_ref[i]]

        store(g).start()

    @pl.loop(jnp.maximum(groups - slots, 0), groups)
    def _(g):
        store(g).wait()


def add_relayed(partial, arrived, listing, cols_blocks):
    row_len, col_len = partial.shape
    unit, side = arrived.shape[1:]
    smem = pl.BlockSpec(memory_space=pltpu.SMEM)
    hbm = pl.BlockSpec(memory_space=pl.ANY)
    return pl.pallas_call(
        functools.partial(add_kernel, cols_blocks),
        out_shape=jax.ShapeDtypeStruct((row_len, col_len), jnp.float32),
        in_specs=[smem, smem, smem, smem, hbm, pl.BlockSpec(memory_space=pltpu.VMEM)],
        out_specs=hbm,
        scratch_shapes=[
            pltpu.VMEM((16, side, side), jnp.float32),
            pltpu.SMEM((arrived.shape[0] + 1,), jnp.int32),
            pltpu.SemaphoreType.DMA((16,)),
            pltpu.SemaphoreType.DMA((16,)),
        ],
        input_output_aliases={4: 0},
        compiler_params=pltpu.CompilerParams(vmem_limit_bytes=24 * MIB),
    )(*listing, partial, arrived)


def place_kernel(slot_ref, arrived_ref, out_ref):
    out_ref[...] = jnp.zeros_like(out_ref)

    @pl.loop(0, arrived_ref.shape[0])
    def _(k):
        @pl.when(slot_ref[k] >= 0)
        def _():
            out_ref[slot_ref[k]] = arrived_ref[k]


def place_tiles(arrived, slots, length):
    vmem = pl.BlockSpec(memory_space=pltpu.VMEM)
    return pl.pallas_call(
        place_kernel,
        out_shape=jax.ShapeDtypeStruct((length,) + arrived.shape[1:], jnp.float32),
        in_specs=[pl.BlockSpec(memory_space=pltpu.SMEM), vmem],
        out_specs=vmem,
        compiler_params=pltpu.CompilerParams(vmem_limit_bytes=24 * MIB),
    )(slots, arrived)


def panel_kernel(code_ref, first_ref, front_ref, arrived_ref, out_ref):
    side = arrived_ref.shape[1]

    @pl.when(first_ref[0] == 1)
    def _():
        out_ref[...] = front_ref[...]

    @pl.when(first_ref[0] == 0)
    def _():
        out_ref[...] = jnp.zeros_like(out_ref)

    @pl.loop(0, arrived_ref.shape[0])
    def _(k):
        code = code_ref[k]
        for part in range(PANELS):

            @pl.when((code >= 0) & (code % PANELS == part))
            def _():
                rows = pl.ds(pl.multiple_of(code // PANELS * side, side), side)
                out_ref[rows, part * side : (part + 1) * side] += arrived_ref[k]


def raw_panel(front, arrived, codes, first):
    row_len = front.shape[0]
    smem = pl.BlockSpec(memory_space=pltpu.SMEM)
    return pl.pallas_call(
        panel_kernel,
        grid=(1,),
        out_shape=jax.ShapeDtypeStruct((row_len, TOTAL), jnp.float32),
        in_specs=[
            smem,
            smem,
            pl.BlockSpec((row_len, TOTAL), lambda i: (0, 0)),
            pl.BlockSpec(arrived.shape, lambda i: (0, 0, 0)),
        ],
        out_specs=pl.BlockSpec((row_len, TOTAL), lambda i: (0, 0)),
        compiler_params=pltpu.CompilerParams(vmem_limit_bytes=40 * MIB),
    )(codes, first, front, arrived)


def split(value):
    high = value.astype(jnp.bfloat16)
    low = (value - high.astype(jnp.float32)).astype(jnp.bfloat16)
    return high, low


def rows_kernel(raw_ref, inverse_ref, out_ref, parts_ref):
    solved = dot_nt(raw_ref[...], inverse_ref[...])
    out_ref[...] = solved
    high, low = split(solved)
    parts_ref[:, :TOTAL] = high
    parts_ref[:, TOTAL : 2 * TOTAL] = high
    parts_ref[:, 2 * TOTAL :] = low


def solve_rows(raw, inverse):
    length = raw.shape[0]
    step = min(512, length)
    block = pl.BlockSpec((step, TOTAL), lambda i: (i, 0))
    return pl.pallas_call(
        rows_kernel,
        grid=(length // step,),
        out_shape=[
            jax.ShapeDtypeStruct((length, TOTAL), jnp.float32),
            jax.ShapeDtypeStruct((length, 3 * TOTAL), jnp.bfloat16),
        ],
        in_specs=[block, pl.BlockSpec((TOTAL, TOTAL), lambda i: (0, 0))],
        out_specs=[block, pl.BlockSpec((step, 3 * TOTAL), lambda i: (i, 0))],
        compiler_params=pltpu.CompilerParams(vmem_limit_bytes=24 * MIB),
    )(raw, inverse)


def cols_kernel(raw_ref, inverse_ref, out_ref, parts_ref):
    solved = dot_nt(inverse_ref[...], raw_ref[...])
    out_ref[...] = solved
    high, low = split(solved)
    parts_ref[:TOTAL] = high
    parts_ref[TOTAL : 2 * TOTAL] = low
    parts_ref[2 * TOTAL :] = high


def solve_cols(raw, inverse):
    length = raw.shape[0]
    step = min(512, length)
    block = pl.BlockSpec((TOTAL, step), lambda i: (0, i))
    return pl.pallas_call(
        cols_kernel,
        grid=(length // step,),
        out_shape=[
            jax.ShapeDtypeStruct((TOTAL, length), jnp.float32),
            jax.ShapeDtypeStruct((3 * TOTAL, length), jnp.bfloat16),
        ],
        in_specs=[
            pl.BlockSpec((step, TOTAL), lambda i: (i, 0)),
            pl.BlockSpec((TOTAL, TOTAL), lambda i: (0, 0)),
        ],
        out_specs=[block, pl.BlockSpec((3 * TOTAL, step), lambda i: (0, i))],
        compiler_params=pltpu.CompilerParams(vmem_limit_bytes=24 * MIB),
    )(raw, inverse)


def final_kernel(
    cols_blocks, runs, code_ref, run_ref, place_ref, front_ref, rows_ref, rows_parts, cols_ref, cols_parts,
    lower_ref, arrived_ref, out_ref, cursor
):
    step = pl.program_id(0)
    sources, capacity = code_ref.shape
    height, width = front_ref.shape
    unit, side = arrived_ref.shape[2:]
    per_step = height // unit

    @pl.when(step == 0)
    def _():
        for s in range(sources):
            cursor[s] = 0

    chunk = min(512, width)
    for start in range(0, width, chunk):
        at = slice(start, start + chunk)
        change = jnp.dot(rows_parts[...], cols_parts[:, at], preferred_element_type=jnp.float32)
        out_ref[:, at] = front_ref[:, at] - change

    edge = (step + 1) * per_step * cols_blocks

    @pl.loop(0, sources)
    def _(s):
        def more(k):
            code = code_ref[s, jnp.minimum(k, capacity - 1)]
            return (k < capacity) & (code >= 0) & (code < edge)

        def add(k):
            code = code_ref[s, k]
            length = run_ref[s, k]
            unit_row = code // cols_blocks - step * per_step
            columns = pl.ds(pl.multiple_of(code % cols_blocks * side, side), side)
            for run in runs:
                skipped = length // (2 * run) * (2 * run)

                @pl.when(length // run % 2 == 1)
                def _():
                    rows = pl.ds(pl.multiple_of((unit_row + skipped) * unit, unit), run * unit)
                    block = arrived_ref[s, pl.ds(k + skipped, run)]
                    out_ref[rows, columns] += block.reshape(run * unit, side)

            return k + length

        cursor[s] = lax.while_loop(more, add, cursor[s])

    top = (place_ref[0] == 0) & (step == 0)

    @pl.when(top)
    def _():
        out_ref[...] = cols_ref[...]

    @pl.when(place_ref[1] == 0)
    def _():
        out_ref[:, :TOTAL] = jnp.where(top, lower_ref[...], rows_ref[...])


def finish(front, rows, cols, lower, arrived, codes, lengths, place, cols_blocks):
    row_len, col_len = front.shape
    height = TOTAL
    smem = pl.BlockSpec(memory_space=pltpu.SMEM)
    block = pl.BlockSpec((height, TOTAL), lambda i: (i, 0))
    parts = pl.BlockSpec((height, 3 * TOTAL), lambda i: (i, 0))
    wide = pl.BlockSpec((height, col_len), lambda i: (i, 0))
    whole = pl.BlockSpec((TOTAL, col_len), lambda i: (0, 0))
    whole_parts = pl.BlockSpec((3 * TOTAL, col_len), lambda i: (0, 0))
    runs = (16, 8, 4, 2, 1) if arrived.shape[2] == UNIT else (1,)
    return pl.pallas_call(
        functools.partial(final_kernel, cols_blocks, runs),
        grid=(row_len // height,),
        out_shape=jax.ShapeDtypeStruct((row_len, col_len), jnp.float32),
        in_specs=[
            smem, smem, smem, wide, block, parts, whole, whole_parts,
            pl.BlockSpec((TOTAL, TOTAL), lambda i: (0, 0)),
            pl.BlockSpec(memory_space=pltpu.VMEM),
        ],
        out_specs=wide,
        scratch_shapes=[pltpu.SMEM((codes.shape[0],), jnp.int32)],
        compiler_params=pltpu.CompilerParams(vmem_limit_bytes=56 * MIB),
    )(codes, lengths, place, front, *rows, *cols, lower, arrived)


def factor(diagonal):
    def lower_of(block):
        return jnp.linalg.cholesky(jnp.tril(block) + jnp.tril(block, -1).T)

    def inverse_of(block):
        return jax.scipy.linalg.solve_triangular(block, jnp.eye(NB, dtype=jnp.float32), lower=True)

    first = lower_of(diagonal[:NB, :NB])
    first_inverse = inverse_of(first)
    below = dot_nt(diagonal[NB:, :NB], first_inverse)
    second = lower_of(diagonal[NB:, NB:] - dot_nt(below, below))
    second_inverse = inverse_of(second)
    corner = -jnp.dot(second_inverse, jnp.dot(below, first_inverse, precision=precise), precision=precise)
    zero = jnp.zeros((NB, NB), jnp.float32)
    return jnp.block([[first, zero], [below, second]]), jnp.block([[first_inverse, zero], [corner, second_inverse]])


def body(front, tiles, tile_block, valid_rows):
    row_len, col_len = front.shape
    row_count = lax.axis_size("row")
    col_count = lax.axis_size("col")
    device_count = row_count * col_count
    per_device = tiles.shape[0]
    side = tiles.shape[1]
    capacity = 2 * per_device // device_count
    rows_blocks = row_len // side
    cols_blocks = col_len // side
    row_now = lax.axis_index("row")
    col_now = lax.axis_index("col")
    device_now = row_now * col_count + col_now

    block_row = tile_block[0].reshape(device_count, per_device)
    block_col = tile_block[1].reshape(device_count, per_device)
    target_row = block_row // rows_blocks
    target = target_row * col_count + block_col // cols_blocks
    code = block_row % rows_blocks * cols_blocks + block_col % cols_blocks
    position = lax.broadcasted_iota(jnp.int32, target.shape, 1)
    place = jnp.stack([row_now, col_now]).astype(jnp.int32)

    def own(values):
        return lax.dynamic_index_in_dim(values, device_now, 0, keepdims=False)

    in_panel = block_col < PANELS
    panel_key = jnp.where(in_panel, target_row, -1)
    panel_rank = jnp.sum(
        (panel_key[:, :, None] == panel_key[:, None, :]) & (position[:, None, :] < position[:, :, None]),
        axis=2,
    )
    same_col = lax.dynamic_index_in_dim(
        jnp.stack([panel_key, panel_rank, code]).reshape(3, row_count, col_count, per_device),
        col_now, 2, keepdims=False,
    )

    def send_panel(tiles, valid_rows, depth):
        ahead = (own(target_row) - row_now) % row_count
        fits = own(in_panel) & (own(panel_rank) < depth)
        panel_slot = jnp.where(fits, ahead * depth + own(panel_rank), -1)
        panel_out = pack(tiles, panel_slot, valid_rows, row_count * depth)
        panel_in = [panel_out[:depth]]
        for shift in range(1, row_count):
            sending = panel_out[shift * depth : (shift + 1) * depth]
            turn = [(r, (r + shift) % row_count) for r in range(row_count)]
            panel_in.append(lax.ppermute(sending, "row", turn))
        return panel_in

    def sum_panel(front, panel_in, depth):
        fits = (same_col[0] == row_now)[:, :, None] & (same_col[1][:, :, None] == jnp.arange(depth))
        panel_code = same_col[2] // cols_blocks * PANELS + same_col[2] % cols_blocks
        panel_codes = jnp.sum(jnp.where(fits, panel_code[:, :, None] + 1, 0), axis=1) - 1
        by_shift = (row_now - jnp.arange(row_count)) % row_count
        panel_codes = jnp.take(panel_codes, by_shift, axis=0).reshape(-1)
        first = (col_now == 0).astype(jnp.int32).reshape(1)
        return raw_panel(front, jnp.concatenate(panel_in, 0), panel_codes, first)

    front_panel = lax.psum(jnp.where(col_now == 0, front[:, :TOTAL], 0.0), "col")

    panel_depth = (capacity * 5 + 7) // 8
    panel_in = send_panel(tiles, valid_rows, panel_depth)
    for_row = in_panel & (target_row == row_now)
    row_tiles = jnp.sum(for_row, axis=1)
    sources = jnp.arange(device_count)
    row_offset = jnp.sum(
        jnp.where(sources[None, :] < sources[:, None], row_tiles[None, :], 0), axis=1
    )
    row_slot = jnp.where(for_row, row_offset[:, None] + panel_rank, -1).reshape(-1)
    at_slot = row_slot[None, :] == jnp.arange(PANEL_SLOTS)[:, None]
    row_code = (code // cols_blocks * PANELS + code % cols_blocks).reshape(-1)
    row_codes = jnp.sum(jnp.where(at_slot, row_code + 1, 0), axis=1) - 1
    by_shift = (row_now - jnp.arange(row_count)) % row_count * col_count + col_now
    depths = jnp.arange(panel_depth)
    slot_in = jnp.take(row_offset, by_shift)[:, None] + depths
    slot_in = jnp.where(depths < jnp.take(row_tiles, by_shift)[:, None], slot_in, -1)
    slot_in = jnp.where(slot_in < PANEL_SLOTS, slot_in, -1).reshape(-1)
    panel_tiles = place_tiles(jnp.concatenate(panel_in, 0), slot_in, PANEL_SLOTS)

    units = side // UNIT
    length = capacity * units
    width = length * 41 // 64
    pass_on = length * 13 // 32
    half_count = device_count // 2
    half_base = device_now // half_count * half_count
    unit_rows = rows_blocks * units
    local_codes = unit_rows * cols_blocks
    own_target, own_code = own(target), own(code)
    own_position = own(position)
    filled = (valid_rows + UNIT - 1) // UNIT
    key = (own_target * rows_blocks * cols_blocks + own_code) * per_device + own_position
    before = key[None, :] < key[:, None]
    together = own_target[None, :] == own_target[:, None]
    base = jnp.sum(jnp.where(before & together, filled[None, :], 0), axis=1)
    order = jnp.sum(before, axis=1)
    unit_code = (own_target * unit_rows + own_code // cols_blocks * units) * cols_blocks
    unit_code += own_code % cols_blocks
    meta = jnp.stack([own_position, own_target, base, filled, unit_code, valid_rows])
    meta = jnp.sum(
        jnp.where(order[None, :, None] == jnp.arange(per_device), meta[:, :, None], 0), axis=1
    )
    to_device = own_target[:, None] == jnp.arange(device_count)
    load = jnp.sum(jnp.where(to_device, filled[:, None], 0), axis=0).reshape(2, half_count)
    empty = load == 0
    empty_rank = jnp.cumsum(empty, axis=1) - 1
    device_ids = jnp.arange(device_count).reshape(2, half_count)
    listed = (empty[:, :, None]) & (empty_rank[:, :, None] == jnp.arange(half_count))
    empties = jnp.sum(jnp.where(listed, device_ids[:, :, None], 0), axis=1)
    free = jnp.sum(empty, axis=1)
    left = jnp.sum(jnp.maximum(load - width, 0), axis=1)
    failed = jnp.any(left > free * width) | (jnp.sum(row_tiles) > PANEL_SLOTS)
    failed |= jnp.any(own(in_panel) & (own(panel_rank) >= panel_depth))
    counts = jnp.concatenate([jnp.sum(own_target < half_count)[None], free]).astype(jnp.int32)
    outgoing, sent_codes = spread(
        tiles, meta.astype(jnp.int32), empties.astype(jnp.int32), counts,
        device_count, width, length, cols_blocks,
    )

    panel_tiles, sent_codes = lax.optimization_barrier((panel_tiles, sent_codes))
    got = lax.all_to_all(sent_codes[:, :width], ("row", "col"), 0, 0, tiled=True)
    got_target = got // local_codes
    local = got % local_codes
    mine = (got >= 0) & (got_target == device_now)
    direct_codes = jnp.where(mine, local, -1)
    steps = jnp.arange(width)
    opening = (local // cols_blocks % units == 0) | jnp.logical_not(mine)
    later = (steps[None, :] > steps[:, None]) & opening[:, None, :]
    direct_runs = jnp.min(jnp.where(later, steps, width), axis=2) - steps
    total_units = device_count * width
    passing = ((got >= 0) & (got_target != device_now)).reshape(-1)
    flat_key = jnp.where(passing, got.reshape(-1) * total_units + jnp.arange(total_units), -1)
    flat_target = jnp.where(passing, got_target.reshape(-1), -1)
    rank = jnp.sum(
        (flat_target[None, :] == flat_target[:, None]) & (flat_key[None, :] < flat_key[:, None]), axis=1
    )
    failed = failed | jnp.any(passing & (rank >= pass_on))
    relay_slot = jnp.where(
        passing & (rank < pass_on), (flat_target - half_base) * pass_on + rank, -1
    )
    picked = relay_slot[:, None] == jnp.arange(half_count * pass_on)
    relay_codes = jnp.sum(jnp.where(picked, local.reshape(-1)[:, None] + 1, 0), axis=0) - 1
    notes = jnp.zeros((2, half_count, pass_on + 1), jnp.int32)
    notes = lax.dynamic_update_slice(
        notes, relay_codes.reshape(1, half_count, pass_on).astype(jnp.int32), (device_now // half_count, 0, 0)
    )
    notes = notes.at[:, :, pass_on].set(failed.astype(jnp.int32))
    notes = lax.all_to_all(
        notes.reshape(device_count, pass_on + 1), ("row", "col"), 0, 0, tiled=True
    )
    too_full = jnp.any(notes[:, pass_on] != 0)
    relay_codes = lax.dynamic_slice_in_dim(notes, half_base, half_count, 0)[:, :pass_on]
    relay_slot = relay_slot.reshape(device_count, width)

    flat = relay_codes.reshape(-1)
    unit_row, relay_col = flat // cols_blocks, flat % cols_blocks
    wanted = (flat >= 0) & ((row_now > 0) | (unit_row >= TOTAL // UNIT))
    wanted &= (col_now > 0) | (relay_col >= PANELS)
    relay_block = unit_row // units * cols_blocks + relay_col
    relay_key = jnp.where(wanted, relay_block * units + unit_row % units, local_codes)
    relay_key = relay_key * flat.shape[0] + jnp.arange(flat.shape[0])
    relay_order = jnp.sum(relay_key[None, :] < relay_key[:, None], axis=1)
    listing = jnp.stack([relay_block, unit_row % units, jnp.arange(flat.shape[0])])
    at_order = relay_order[None, :, None] == jnp.arange(flat.shape[0])
    listing = jnp.sum(jnp.where(at_order, listing[:, :, None], 0), axis=1).astype(jnp.int32)
    listing = [*listing, jnp.sum(wanted).astype(jnp.int32).reshape(1)]

    outgoing, notes, front_panel, panel_tiles = lax.optimization_barrier(
        (outgoing, notes, front_panel, panel_tiles)
    )
    panel_tiles = lax.psum(panel_tiles, "col")
    raw_rows = raw_panel(front_panel, panel_tiles, row_codes, jnp.ones((1,), jnp.int32))
    arrived = lax.all_to_all(outgoing, ("row", "col"), 0, 0, tiled=True)
    slice_start = col_now * col_len % row_len
    slice_root = col_now * col_len // row_len

    def chain(raw_rows):
        picked = lax.dynamic_slice_in_dim(raw_rows, slice_start, col_len, 0)
        raw_cols = lax.psum(jnp.where(row_now == slice_root, picked, 0.0), "row")
        diagonal = jnp.where(row_now == 0, raw_rows[:TOTAL], jnp.eye(TOTAL, dtype=jnp.float32))
        lower, inverse = factor(diagonal)
        inverse, raw_cols = lax.optimization_barrier((inverse, raw_cols))
        inverse = lax.psum(jnp.where(row_now == 0, inverse, 0.0), "row")
        return solve_rows(raw_rows, inverse), solve_cols(raw_cols, inverse), lower

    rows, cols, lower = chain(raw_rows)
    tables = (relay_slot, direct_codes, direct_runs, listing)
    arrived, rows, cols, lower, tables = lax.optimization_barrier((arrived, rows, cols, lower, tables))
    relay_slot, direct_codes, direct_runs, listing = tables

    def relayed(front, tiles, valid_rows, arrived, rows, cols, lower):
        passed = relay(relay_slot, arrived, half_count * pass_on)
        halves = [list(range(half_count)), list(range(half_count, device_count))]
        passed = lax.all_to_all(
            passed.reshape(half_count, pass_on, UNIT, side), ("row", "col"), 0, 0,
            axis_index_groups=halves, tiled=True,
        )
        partial = finish(
            front, rows, cols, lower, arrived, direct_codes, direct_runs, place, cols_blocks
        )
        return add_relayed(partial, passed.reshape(-1, UNIT, side), listing, cols_blocks)

    def padded(front, tiles, valid_rows, arrived, rows, cols, lower):
        partial = sum_panel(front, send_panel(tiles, valid_rows, capacity), capacity)
        raw_rows = lax.psum(partial, "col")
        order = (target * rows_blocks * cols_blocks + code) * per_device + position
        ranking = jnp.sum(
            (target[:, :, None] == target[:, None, :]) & (order[:, None, :] < order[:, :, None]), axis=2
        )
        slot = own(target) * capacity + own(ranking)
        here = (target == device_now)[:, :, None] & (ranking[:, :, None] == jnp.arange(capacity))
        codes = jnp.sum(jnp.where(here, code[:, :, None] + 1, 0), axis=1) - 1
        packed = pack(tiles, slot, valid_rows, device_count * capacity)
        arrived = lax.all_to_all(
            packed.reshape(device_count, capacity, side, side), ("row", "col"), 0, 0, tiled=True
        )
        rows, cols, lower = chain(raw_rows)
        return finish(
            front, rows, cols, lower, arrived, codes, jnp.ones_like(codes), place, cols_blocks
        )

    return lax.cond(
        too_full, padded, relayed, front, tiles, valid_rows, arrived, rows, cols, lower
    )


def solution(mesh):
    placed = (P("row", "col"), P(("row", "col"), None, None), P(), P(("row", "col")))
    return jax.shard_map(
        body, mesh=mesh, in_specs=placed, out_specs=P("row", "col"), check_vma=False
    )
```

```python
import functools

import jax
import jax.numpy as jnp
from jax import lax
from jax.experimental import pallas as pl
from jax.experimental.pallas import tpu as pltpu
from jax.sharding import PartitionSpec as P

NB = 128
PANELS = 2
TOTAL = NB * PANELS
MIB = 1 << 20
UNIT = 8
PANEL_SLOTS = 32


precise = lax.Precision.HIGHEST


def dot_nt(a, b, precision=precise):
    return lax.dot_general(
        a, b, (((1,), (1,)), ((), ())), precision=precision, preferred_element_type=jnp.float32
    )


def pack_kernel(slot_ref, valid_ref, tiles_ref, out_ref, buf, sem_in, sem_out):
    count, side = tiles_ref.shape[0], tiles_ref.shape[1]

    def fetch(t):
        return pltpu.make_async_copy(tiles_ref.at[t], buf.at[t], sem_in.at[t])

    def store(t):
        return pltpu.make_async_copy(buf.at[t], out_ref.at[jnp.maximum(slot_ref[t], 0)], sem_out.at[t])

    def each(act):
        @pl.loop(0, count)
        def _(t):
            @pl.when(slot_ref[t] >= 0)
            def _():
                act(t)

    def mask(t):
        fetch(t).wait()
        rows = lax.broadcasted_iota(jnp.int32, (side, side), 0)
        buf[t] = jnp.where(rows < valid_ref[t], buf[t], 0.0)
        store(t).start()

    each(lambda t: fetch(t).start())
    each(mask)
    each(lambda t: store(t).wait())


def pack(tiles, slots, valid, n_slots):
    count, side = tiles.shape[0], tiles.shape[1]
    smem = pl.BlockSpec(memory_space=pltpu.SMEM)
    return pl.pallas_call(
        pack_kernel,
        out_shape=jax.ShapeDtypeStruct((n_slots, side, side), jnp.float32),
        in_specs=[smem, smem, pl.BlockSpec(memory_space=pl.ANY)],
        out_specs=pl.BlockSpec(memory_space=pl.ANY),
        scratch_shapes=[
            pltpu.VMEM((count, side, side), jnp.float32),
            pltpu.SemaphoreType.DMA((count,)),
            pltpu.SemaphoreType.DMA((count,)),
        ],
        compiler_params=pltpu.CompilerParams(vmem_limit_bytes=24 * MIB),
    )(slots, valid, tiles)


def spread_kernel(
    width, stride, meta_ref, empty_ref, count_ref, tiles_ref, out_ref, code_ref, stage, sem
):
    count, units = tiles_ref.shape[0], tiles_ref.shape[1]
    devices, length = code_ref.shape

    @pl.loop(0, devices)
    def _(d):
        for k in range(length):
            code_ref[d, k] = -1

    @pl.loop(0, count)
    def _(i):
        tile, target, base = meta_ref[0, i], meta_ref[1, i], meta_ref[2, i]
        filled, code, valid = meta_ref[3, i], meta_ref[4, i], meta_ref[5, i]
        shape = tiles_ref.shape[1:]
        rows = lax.broadcasted_iota(jnp.int32, shape, 0) * shape[1]
        rows += lax.broadcasted_iota(jnp.int32, shape, 1)
        stage[target, pl.ds(base, units)] = jnp.where(rows < valid, tiles_ref[tile], 0.0)
        for u in range(units):
            code_ref[target, base + u] = jnp.where(u < filled, code + u * stride, -1)

    for half in range(2):
        first = 0 if half == 0 else count_ref[0]
        last = count_ref[0] if half == 0 else count
        free = count_ref[1 + half]

        def each_tile(i, carry):
            target, base, filled = meta_ref[1, i], meta_ref[2, i], meta_ref[3, i]

            def each_unit(q, carry):
                at, depth = carry
                relay = empty_ref[half, at]
                place = jnp.minimum(depth, width - 1)
                stage[relay, place] = stage[target, q]
                code_ref[relay, place] = code_ref[target, q]
                wrap = at + 1 >= free
                return jnp.where(wrap, 0, at + 1), jnp.where(wrap, depth + 1, depth)

            return lax.fori_loop(jnp.maximum(base, width), base + filled, each_unit, carry)

        lax.fori_loop(first, last, each_tile, (jnp.int32(0), jnp.int32(0)))

    copy = pltpu.make_async_copy(stage.at[:, pl.ds(0, width)], out_ref, sem)
    copy.start()
    copy.wait()


def spread(tiles, meta, empties, counts, devices, width, length, stride):
    count, side = tiles.shape[0], tiles.shape[1]
    units = side // UNIT
    smem = pl.BlockSpec(memory_space=pltpu.SMEM)
    return pl.pallas_call(
        functools.partial(spread_kernel, width, stride),
        out_shape=[
            jax.ShapeDtypeStruct((devices, width, UNIT, side), jnp.float32),
            jax.ShapeDtypeStruct((devices, length), jnp.int32),
        ],
        in_specs=[smem, smem, smem, pl.BlockSpec(memory_space=pltpu.VMEM)],
        out_specs=[pl.BlockSpec(memory_space=pl.ANY), smem],
        scratch_shapes=[
            pltpu.VMEM((devices, length, UNIT, side), jnp.float32),
            pltpu.SemaphoreType.DMA,
        ],
        compiler_params=pltpu.CompilerParams(vmem_limit_bytes=40 * MIB),
    )(meta, empties, counts, tiles.reshape(count, units, UNIT, side))


def relay_kernel(slot_ref, arrived_ref, out_ref):
    devices, width = slot_ref.shape

    @pl.loop(0, devices)
    def _(s):
        def more(k):
            return (k < width) & (slot_ref[s, jnp.minimum(k, width - 1)] >= 0)

        def move(k):
            out_ref[slot_ref[s, k]] = arrived_ref[s, k]
            return k + 1

        lax.while_loop(more, move, jnp.int32(0))


def relay(slots, arrived, length):
    vmem = pl.BlockSpec(memory_space=pltpu.VMEM)
    return pl.pallas_call(
        relay_kernel,
        out_shape=jax.ShapeDtypeStruct((length,) + arrived.shape[2:], jnp.float32),
        in_specs=[pl.BlockSpec(memory_space=pltpu.SMEM), vmem],
        out_specs=vmem,
        compiler_params=pltpu.CompilerParams(vmem_limit_bytes=40 * MIB),
    )(slots, arrived)


def add_kernel(
    cols_blocks, block_ref, unit_ref, index_ref, count_ref, partial_ref, arrived_ref, out_ref, buf,
    group_start, sem_in, sem_out
):
    slots, side = buf.shape[0], buf.shape[1]
    unit = arrived_ref.shape[1]
    ahead = slots // 2
    count = count_ref[0]

    def listed(i, carry):
        groups, last = carry
        block = block_ref[i]
        fresh = block != last

        @pl.when(fresh)
        def _():
            group_start[groups] = i

        return jnp.where(fresh, groups + 1, groups), block

    groups, _ = lax.fori_loop(0, count, listed, (jnp.int32(0), jnp.int32(-1)))
    group_start[groups] = count

    def window(g):
        block = block_ref[group_start[g]]
        rows = pl.ds(pl.multiple_of(block // cols_blocks * side, side), side)
        columns = pl.ds(pl.multiple_of(block % cols_blocks * side, side), side)
        return out_ref.at[rows, columns]

    def fetch(g):
        at = g % slots
        return pltpu.make_async_copy(window(g), buf.at[at], sem_in.at[at])

    def store(g):
        at = g % slots
        return pltpu.make_async_copy(buf.at[at], window(g), sem_out.at[at])

    @pl.loop(0, jnp.minimum(groups, ahead))
    def _(g):
        fetch(g).start()

    @pl.loop(0, groups)
    def _(g):
        @pl.when(g + ahead < groups)
        def _():
            @pl.when(g >= ahead)
            def _():
                store(g - ahead).wait()

            fetch(g + ahead).start()

        fetch(g).wait()

        @pl.loop(group_start[g], group_start[g + 1])
        def _(i):
            rows = pl.ds(pl.multiple_of(unit_ref[i] * unit, unit), unit)
            buf[g % slots, rows] += arrived_ref[index_ref[i]]

        store(g).start()

    @pl.loop(jnp.maximum(groups - slots, 0), groups)
    def _(g):
        store(g).wait()


def add_relayed(partial, arrived, listing, cols_blocks):
    row_len, col_len = partial.shape
    unit, side = arrived.shape[1:]
    smem = pl.BlockSpec(memory_space=pltpu.SMEM)
    hbm = pl.BlockSpec(memory_space=pl.ANY)
    return pl.pallas_call(
        functools.partial(add_kernel, cols_blocks),
        out_shape=jax.ShapeDtypeStruct((row_len, col_len), jnp.float32),
        in_specs=[smem, smem, smem, smem, hbm, pl.BlockSpec(memory_space=pltpu.VMEM)],
        out_specs=hbm,
        scratch_shapes=[
            pltpu.VMEM((16, side, side), jnp.float32),
            pltpu.SMEM((arrived.shape[0] + 1,), jnp.int32),
            pltpu.SemaphoreType.DMA((16,)),
            pltpu.SemaphoreType.DMA((16,)),
        ],
        input_output_aliases={4: 0},
        compiler_params=pltpu.CompilerParams(vmem_limit_bytes=24 * MIB),
    )(*listing, partial, arrived)


def place_kernel(slot_ref, arrived_ref, out_ref):
    out_ref[...] = jnp.zeros_like(out_ref)

    @pl.loop(0, arrived_ref.shape[0])
    def _(k):
        @pl.when(slot_ref[k] >= 0)
        def _():
            out_ref[slot_ref[k]] = arrived_ref[k]


def place_tiles(arrived, slots, length):
    vmem = pl.BlockSpec(memory_space=pltpu.VMEM)
    return pl.pallas_call(
        place_kernel,
        out_shape=jax.ShapeDtypeStruct((length,) + arrived.shape[1:], jnp.float32),
        in_specs=[pl.BlockSpec(memory_space=pltpu.SMEM), vmem],
        out_specs=vmem,
        compiler_params=pltpu.CompilerParams(vmem_limit_bytes=24 * MIB),
    )(slots, arrived)


def panel_kernel(code_ref, first_ref, front_ref, arrived_ref, out_ref):
    side = arrived_ref.shape[1]

    @pl.when(first_ref[0] == 1)
    def _():
        out_ref[...] = front_ref[...]

    @pl.when(first_ref[0] == 0)
    def _():
        out_ref[...] = jnp.zeros_like(out_ref)

    @pl.loop(0, arrived_ref.shape[0])
    def _(k):
        code = code_ref[k]
        for part in range(PANELS):

            @pl.when((code >= 0) & (code % PANELS == part))
            def _():
                rows = pl.ds(pl.multiple_of(code // PANELS * side, side), side)
                out_ref[rows, part * side : (part + 1) * side] += arrived_ref[k]


def raw_panel(front, arrived, codes, first):
    row_len = front.shape[0]
    smem = pl.BlockSpec(memory_space=pltpu.SMEM)
    return pl.pallas_call(
        panel_kernel,
        grid=(1,),
        out_shape=jax.ShapeDtypeStruct((row_len, TOTAL), jnp.float32),
        in_specs=[
            smem,
            smem,
            pl.BlockSpec((row_len, TOTAL), lambda i: (0, 0)),
            pl.BlockSpec(arrived.shape, lambda i: (0, 0, 0)),
        ],
        out_specs=pl.BlockSpec((row_len, TOTAL), lambda i: (0, 0)),
        compiler_params=pltpu.CompilerParams(vmem_limit_bytes=40 * MIB),
    )(codes, first, front, arrived)


def split(value):
    high = value.astype(jnp.bfloat16)
    low = (value - high.astype(jnp.float32)).astype(jnp.bfloat16)
    return high, low


def rows_kernel(raw_ref, inverse_ref, out_ref, parts_ref):
    solved = dot_nt(raw_ref[...], inverse_ref[...])
    out_ref[...] = solved
    high, low = split(solved)
    parts_ref[:, :TOTAL] = high
    parts_ref[:, TOTAL : 2 * TOTAL] = high
    parts_ref[:, 2 * TOTAL :] = low


def solve_rows(raw, inverse):
    length = raw.shape[0]
    step = min(512, length)
    block = pl.BlockSpec((step, TOTAL), lambda i: (i, 0))
    return pl.pallas_call(
        rows_kernel,
        grid=(length // step,),
        out_shape=[
            jax.ShapeDtypeStruct((length, TOTAL), jnp.float32),
            jax.ShapeDtypeStruct((length, 3 * TOTAL), jnp.bfloat16),
        ],
        in_specs=[block, pl.BlockSpec((TOTAL, TOTAL), lambda i: (0, 0))],
        out_specs=[block, pl.BlockSpec((step, 3 * TOTAL), lambda i: (i, 0))],
        compiler_params=pltpu.CompilerParams(vmem_limit_bytes=24 * MIB),
    )(raw, inverse)


def cols_kernel(raw_ref, inverse_ref, out_ref, parts_ref):
    solved = dot_nt(inverse_ref[...], raw_ref[...])
    out_ref[...] = solved
    high, low = split(solved)
    parts_ref[:TOTAL] = high
    parts_ref[TOTAL : 2 * TOTAL] = low
    parts_ref[2 * TOTAL :] = high


def solve_cols(raw, inverse):
    length = raw.shape[0]
    step = min(512, length)
    block = pl.BlockSpec((TOTAL, step), lambda i: (0, i))
    return pl.pallas_call(
        cols_kernel,
        grid=(length // step,),
        out_shape=[
            jax.ShapeDtypeStruct((TOTAL, length), jnp.float32),
            jax.ShapeDtypeStruct((3 * TOTAL, length), jnp.bfloat16),
        ],
        in_specs=[
            pl.BlockSpec((step, TOTAL), lambda i: (i, 0)),
            pl.BlockSpec((TOTAL, TOTAL), lambda i: (0, 0)),
        ],
        out_specs=[block, pl.BlockSpec((3 * TOTAL, step), lambda i: (0, i))],
        compiler_params=pltpu.CompilerParams(vmem_limit_bytes=24 * MIB),
    )(raw, inverse)


def final_kernel(
    cols_blocks, runs, code_ref, run_ref, place_ref, front_ref, rows_ref, rows_parts, cols_ref, cols_parts,
    lower_ref, arrived_ref, out_ref, cursor
):
    step = pl.program_id(0)
    sources, capacity = code_ref.shape
    height, width = front_ref.shape
    unit, side = arrived_ref.shape[2:]
    per_step = height // unit

    @pl.when(step == 0)
    def _():
        for s in range(sources):
            cursor[s] = 0

    chunk = min(512, width)
    for start in range(0, width, chunk):
        at = slice(start, start + chunk)
        change = jnp.dot(rows_parts[...], cols_parts[:, at], preferred_element_type=jnp.float32)
        out_ref[:, at] = front_ref[:, at] - change

    edge = (step + 1) * per_step * cols_blocks

    @pl.loop(0, sources)
    def _(s):
        def more(k):
            code = code_ref[s, jnp.minimum(k, capacity - 1)]
            return (k < capacity) & (code >= 0) & (code < edge)

        def add(k):
            code = code_ref[s, k]
            length = run_ref[s, k]
            unit_row = code // cols_blocks - step * per_step
            columns = pl.ds(pl.multiple_of(code % cols_blocks * side, side), side)
            for run in runs:
                skipped = length // (2 * run) * (2 * run)

                @pl.when(length // run % 2 == 1)
                def _():
                    rows = pl.ds(pl.multiple_of((unit_row + skipped) * unit, unit), run * unit)
                    block = arrived_ref[s, pl.ds(k + skipped, run)]
                    out_ref[rows, columns] += block.reshape(run * unit, side)

            return k + length

        cursor[s] = lax.while_loop(more, add, cursor[s])

    top = (place_ref[0] == 0) & (step == 0)

    @pl.when(top)
    def _():
        out_ref[...] = cols_ref[...]

    @pl.when(place_ref[1] == 0)
    def _():
        out_ref[:, :TOTAL] = jnp.where(top, lower_ref[...], rows_ref[...])


def finish(front, rows, cols, lower, arrived, codes, lengths, place, cols_blocks):
    row_len, col_len = front.shape
    height = TOTAL
    smem = pl.BlockSpec(memory_space=pltpu.SMEM)
    block = pl.BlockSpec((height, TOTAL), lambda i: (i, 0))
    parts = pl.BlockSpec((height, 3 * TOTAL), lambda i: (i, 0))
    wide = pl.BlockSpec((height, col_len), lambda i: (i, 0))
    whole = pl.BlockSpec((TOTAL, col_len), lambda i: (0, 0))
    whole_parts = pl.BlockSpec((3 * TOTAL, col_len), lambda i: (0, 0))
    runs = (16, 8, 4, 2, 1) if arrived.shape[2] == UNIT else (1,)
    return pl.pallas_call(
        functools.partial(final_kernel, cols_blocks, runs),
        grid=(row_len // height,),
        out_shape=jax.ShapeDtypeStruct((row_len, col_len), jnp.float32),
        in_specs=[
            smem, smem, smem, wide, block, parts, whole, whole_parts,
            pl.BlockSpec((TOTAL, TOTAL), lambda i: (0, 0)),
            pl.BlockSpec(memory_space=pltpu.VMEM),
        ],
        out_specs=wide,
        scratch_shapes=[pltpu.SMEM((codes.shape[0],), jnp.int32)],
        compiler_params=pltpu.CompilerParams(vmem_limit_bytes=56 * MIB),
    )(codes, lengths, place, front, *rows, *cols, lower, arrived)


def factor(diagonal):
    def lower_of(block):
        return jnp.linalg.cholesky(jnp.tril(block) + jnp.tril(block, -1).T)

    def inverse_of(block):
        return jax.scipy.linalg.solve_triangular(block, jnp.eye(NB, dtype=jnp.float32), lower=True)

    first = lower_of(diagonal[:NB, :NB])
    first_inverse = inverse_of(first)
    below = dot_nt(diagonal[NB:, :NB], first_inverse)
    second = lower_of(diagonal[NB:, NB:] - dot_nt(below, below))
    second_inverse = inverse_of(second)
    corner = -jnp.dot(second_inverse, jnp.dot(below, first_inverse, precision=precise), precision=precise)
    zero = jnp.zeros((NB, NB), jnp.float32)
    return jnp.block([[first, zero], [below, second]]), jnp.block([[first_inverse, zero], [corner, second_inverse]])


def first_steps(value, col_now):
    half = value.shape[0] // 2
    upper, lower = value[:half], value[half:]
    upper_x = lax.ppermute(upper, "col", [(0, 2)])
    lower_y = lax.ppermute(lower, "col", [(0, 4)])
    return upper, lower, upper_x, lower_y


def last_steps(upper, lower, upper_x, lower_y, col_now):
    upper = jnp.where(col_now == 0, upper, upper_x)
    lower = jnp.where(col_now == 0, lower, lower_y)
    upper_y = lax.ppermute(upper, "col", [(0, 4), (2, 6)])
    lower_x = lax.ppermute(lower, "col", [(0, 2), (4, 6)])
    upper = jnp.where(col_now < 4, upper, upper_y)
    lower = jnp.where((col_now == 0) | (col_now == 4), lower, lower_x)
    upper_core = lax.ppermute(upper, "col", [(0, 1), (2, 3), (4, 5), (6, 7)])
    lower_core = lax.ppermute(lower, "col", [(0, 1), (2, 3), (4, 5), (6, 7)])
    whole = jnp.concatenate([upper, lower], 0)
    return jnp.where(col_now % 2 == 0, whole, jnp.concatenate([upper_core, lower_core], 0))


def body(front, tiles, tile_block, valid_rows):
    row_len, col_len = front.shape
    row_count = lax.axis_size("row")
    col_count = lax.axis_size("col")
    device_count = row_count * col_count
    per_device = tiles.shape[0]
    side = tiles.shape[1]
    capacity = 2 * per_device // device_count
    rows_blocks = row_len // side
    cols_blocks = col_len // side
    row_now = lax.axis_index("row")
    col_now = lax.axis_index("col")
    device_now = row_now * col_count + col_now

    block_row = tile_block[0].reshape(device_count, per_device)
    block_col = tile_block[1].reshape(device_count, per_device)
    target_row = block_row // rows_blocks
    target = target_row * col_count + block_col // cols_blocks
    code = block_row % rows_blocks * cols_blocks + block_col % cols_blocks
    position = lax.broadcasted_iota(jnp.int32, target.shape, 1)
    place = jnp.stack([row_now, col_now]).astype(jnp.int32)

    def own(values):
        return lax.dynamic_index_in_dim(values, device_now, 0, keepdims=False)

    in_panel = block_col < PANELS
    panel_key = jnp.where(in_panel, target_row, -1)
    panel_rank = jnp.sum(
        (panel_key[:, :, None] == panel_key[:, None, :]) & (position[:, None, :] < position[:, :, None]),
        axis=2,
    )
    same_col = lax.dynamic_index_in_dim(
        jnp.stack([panel_key, panel_rank, code]).reshape(3, row_count, col_count, per_device),
        col_now, 2, keepdims=False,
    )

    def send_panel(tiles, valid_rows, depth):
        ahead = (own(target_row) - row_now) % row_count
        fits = own(in_panel) & (own(panel_rank) < depth)
        panel_slot = jnp.where(fits, ahead * depth + own(panel_rank), -1)
        panel_out = pack(tiles, panel_slot, valid_rows, row_count * depth)
        panel_in = [panel_out[:depth]]
        for shift in range(1, row_count):
            sending = panel_out[shift * depth : (shift + 1) * depth]
            turn = [(r, (r + shift) % row_count) for r in range(row_count)]
            panel_in.append(lax.ppermute(sending, "row", turn))
        return panel_in

    def sum_panel(front, panel_in, depth):
        fits = (same_col[0] == row_now)[:, :, None] & (same_col[1][:, :, None] == jnp.arange(depth))
        panel_code = same_col[2] // cols_blocks * PANELS + same_col[2] % cols_blocks
        panel_codes = jnp.sum(jnp.where(fits, panel_code[:, :, None] + 1, 0), axis=1) - 1
        by_shift = (row_now - jnp.arange(row_count)) % row_count
        panel_codes = jnp.take(panel_codes, by_shift, axis=0).reshape(-1)
        first = (col_now == 0).astype(jnp.int32).reshape(1)
        return raw_panel(front, jnp.concatenate(panel_in, 0), panel_codes, first)

    eight = col_count == 8
    if eight:
        front_parts = first_steps(front[:, :TOTAL], col_now)
    else:
        front_panel = lax.psum(jnp.where(col_now == 0, front[:, :TOTAL], 0.0), "col")

    panel_depth = (capacity * 5 + 7) // 8
    panel_in = send_panel(tiles, valid_rows, panel_depth)
    for_row = in_panel & (target_row == row_now)
    row_tiles = jnp.sum(for_row, axis=1)
    sources = jnp.arange(device_count)
    row_offset = jnp.sum(
        jnp.where(sources[None, :] < sources[:, None], row_tiles[None, :], 0), axis=1
    )
    row_slot = jnp.where(for_row, row_offset[:, None] + panel_rank, -1).reshape(-1)
    at_slot = row_slot[None, :] == jnp.arange(PANEL_SLOTS)[:, None]
    row_code = (code // cols_blocks * PANELS + code % cols_blocks).reshape(-1)
    row_codes = jnp.sum(jnp.where(at_slot, row_code + 1, 0), axis=1) - 1
    by_shift = (row_now - jnp.arange(row_count)) % row_count * col_count + col_now
    depths = jnp.arange(panel_depth)
    slot_in = jnp.take(row_offset, by_shift)[:, None] + depths
    slot_in = jnp.where(depths < jnp.take(row_tiles, by_shift)[:, None], slot_in, -1)
    slot_in = jnp.where(slot_in < PANEL_SLOTS, slot_in, -1).reshape(-1)
    panel_tiles = place_tiles(jnp.concatenate(panel_in, 0), slot_in, PANEL_SLOTS)

    units = side // UNIT
    length = capacity * units
    width = length * 41 // 64
    pass_on = length * 13 // 32
    half_count = device_count // 2
    half_base = device_now // half_count * half_count
    unit_rows = rows_blocks * units
    local_codes = unit_rows * cols_blocks
    own_target, own_code = own(target), own(code)
    own_position = own(position)
    filled = (valid_rows + UNIT - 1) // UNIT
    key = (own_target * rows_blocks * cols_blocks + own_code) * per_device + own_position
    before = key[None, :] < key[:, None]
    together = own_target[None, :] == own_target[:, None]
    base = jnp.sum(jnp.where(before & together, filled[None, :], 0), axis=1)
    order = jnp.sum(before, axis=1)
    unit_code = (own_target * unit_rows + own_code // cols_blocks * units) * cols_blocks
    unit_code += own_code % cols_blocks
    meta = jnp.stack([own_position, own_target, base, filled, unit_code, valid_rows])
    meta = jnp.sum(
        jnp.where(order[None, :, None] == jnp.arange(per_device), meta[:, :, None], 0), axis=1
    )
    to_device = own_target[:, None] == jnp.arange(device_count)
    load = jnp.sum(jnp.where(to_device, filled[:, None], 0), axis=0).reshape(2, half_count)
    empty = load == 0
    empty_rank = jnp.cumsum(empty, axis=1) - 1
    device_ids = jnp.arange(device_count).reshape(2, half_count)
    listed = (empty[:, :, None]) & (empty_rank[:, :, None] == jnp.arange(half_count))
    empties = jnp.sum(jnp.where(listed, device_ids[:, :, None], 0), axis=1)
    free = jnp.sum(empty, axis=1)
    left = jnp.sum(jnp.maximum(load - width, 0), axis=1)
    failed = jnp.any(left > free * width) | (jnp.sum(row_tiles) > PANEL_SLOTS)
    failed |= jnp.any(own(in_panel) & (own(panel_rank) >= panel_depth))
    counts = jnp.concatenate([jnp.sum(own_target < half_count)[None], free]).astype(jnp.int32)
    outgoing, sent_codes = spread(
        tiles, meta.astype(jnp.int32), empties.astype(jnp.int32), counts,
        device_count, width, length, cols_blocks,
    )

    if eight:
        front_parts, sent_codes = lax.optimization_barrier((front_parts, sent_codes))
        front_panel = last_steps(*front_parts, col_now)
    panel_tiles, sent_codes = lax.optimization_barrier((panel_tiles, sent_codes))
    panel_tiles = lax.psum(panel_tiles, "col")
    got = lax.all_to_all(sent_codes[:, :width], ("row", "col"), 0, 0, tiled=True)
    got_target = got // local_codes
    local = got % local_codes
    mine = (got >= 0) & (got_target == device_now)
    direct_codes = jnp.where(mine, local, -1)
    steps = jnp.arange(width)
    opening = (local // cols_blocks % units == 0) | jnp.logical_not(mine)
    later = (steps[None, :] > steps[:, None]) & opening[:, None, :]
    direct_runs = jnp.min(jnp.where(later, steps, width), axis=2) - steps
    total_units = device_count * width
    passing = ((got >= 0) & (got_target != device_now)).reshape(-1)
    flat_key = jnp.where(passing, got.reshape(-1) * total_units + jnp.arange(total_units), -1)
    flat_target = jnp.where(passing, got_target.reshape(-1), -1)
    rank = jnp.sum(
        (flat_target[None, :] == flat_target[:, None]) & (flat_key[None, :] < flat_key[:, None]), axis=1
    )
    failed = failed | jnp.any(passing & (rank >= pass_on))
    relay_slot = jnp.where(
        passing & (rank < pass_on), (flat_target - half_base) * pass_on + rank, -1
    )
    picked = relay_slot[:, None] == jnp.arange(half_count * pass_on)
    relay_codes = jnp.sum(jnp.where(picked, local.reshape(-1)[:, None] + 1, 0), axis=0) - 1
    notes = jnp.zeros((2, half_count, pass_on + 1), jnp.int32)
    notes = lax.dynamic_update_slice(
        notes, relay_codes.reshape(1, half_count, pass_on).astype(jnp.int32), (device_now // half_count, 0, 0)
    )
    notes = notes.at[:, :, pass_on].set(failed.astype(jnp.int32))
    notes, panel_tiles = lax.optimization_barrier((notes, panel_tiles))
    notes = lax.all_to_all(
        notes.reshape(device_count, pass_on + 1), ("row", "col"), 0, 0, tiled=True
    )
    too_full = jnp.any(notes[:, pass_on] != 0)
    relay_codes = lax.dynamic_slice_in_dim(notes, half_base, half_count, 0)[:, :pass_on]
    relay_slot = relay_slot.reshape(device_count, width)

    flat = relay_codes.reshape(-1)
    unit_row, relay_col = flat // cols_blocks, flat % cols_blocks
    wanted = (flat >= 0) & ((row_now > 0) | (unit_row >= TOTAL // UNIT))
    wanted &= (col_now > 0) | (relay_col >= PANELS)
    relay_block = unit_row // units * cols_blocks + relay_col
    relay_key = jnp.where(wanted, relay_block * units + unit_row % units, local_codes)
    relay_key = relay_key * flat.shape[0] + jnp.arange(flat.shape[0])
    relay_order = jnp.sum(relay_key[None, :] < relay_key[:, None], axis=1)
    listing = jnp.stack([relay_block, unit_row % units, jnp.arange(flat.shape[0])])
    at_order = relay_order[None, :, None] == jnp.arange(flat.shape[0])
    listing = jnp.sum(jnp.where(at_order, listing[:, :, None], 0), axis=1).astype(jnp.int32)
    listing = [*listing, jnp.sum(wanted).astype(jnp.int32).reshape(1)]

    outgoing, notes, front_panel, panel_tiles = lax.optimization_barrier(
        (outgoing, notes, front_panel, panel_tiles)
    )
    raw_rows = raw_panel(front_panel, panel_tiles, row_codes, jnp.ones((1,), jnp.int32))
    arrived = lax.all_to_all(outgoing, ("row", "col"), 0, 0, tiled=True)
    slice_start = col_now * col_len % row_len
    slice_root = col_now * col_len // row_len

    def chain(raw_rows):
        picked = lax.dynamic_slice_in_dim(raw_rows, slice_start, col_len, 0)
        raw_cols = lax.psum(jnp.where(row_now == slice_root, picked, 0.0), "row")
        diagonal = jnp.where(row_now == 0, raw_rows[:TOTAL], jnp.eye(TOTAL, dtype=jnp.float32))
        lower, inverse = factor(diagonal)
        inverse, raw_cols = lax.optimization_barrier((inverse, raw_cols))
        inverse = lax.psum(jnp.where(row_now == 0, inverse, 0.0), "row")
        return solve_rows(raw_rows, inverse), solve_cols(raw_cols, inverse), lower

    rows, cols, lower = chain(raw_rows)
    tables = (relay_slot, direct_codes, direct_runs, listing)
    arrived, rows, cols, lower, tables = lax.optimization_barrier((arrived, rows, cols, lower, tables))
    relay_slot, direct_codes, direct_runs, listing = tables

    def relayed(front, tiles, valid_rows, arrived, rows, cols, lower):
        passed = relay(relay_slot, arrived, half_count * pass_on)
        halves = [list(range(half_count)), list(range(half_count, device_count))]
        passed = lax.all_to_all(
            passed.reshape(half_count, pass_on, UNIT, side), ("row", "col"), 0, 0,
            axis_index_groups=halves, tiled=True,
        )
        partial = finish(
            front, rows, cols, lower, arrived, direct_codes, direct_runs, place, cols_blocks
        )
        return add_relayed(partial, passed.reshape(-1, UNIT, side), listing, cols_blocks)

    def padded(front, tiles, valid_rows, arrived, rows, cols, lower):
        partial = sum_panel(front, send_panel(tiles, valid_rows, capacity), capacity)
        raw_rows = lax.psum(partial, "col")
        order = (target * rows_blocks * cols_blocks + code) * per_device + position
        ranking = jnp.sum(
            (target[:, :, None] == target[:, None, :]) & (order[:, None, :] < order[:, :, None]), axis=2
        )
        slot = own(target) * capacity + own(ranking)
        here = (target == device_now)[:, :, None] & (ranking[:, :, None] == jnp.arange(capacity))
        codes = jnp.sum(jnp.where(here, code[:, :, None] + 1, 0), axis=1) - 1
        packed = pack(tiles, slot, valid_rows, device_count * capacity)
        arrived = lax.all_to_all(
            packed.reshape(device_count, capacity, side, side), ("row", "col"), 0, 0, tiled=True
        )
        rows, cols, lower = chain(raw_rows)
        return finish(
            front, rows, cols, lower, arrived, codes, jnp.ones_like(codes), place, cols_blocks
        )

    return lax.cond(
        too_full, padded, relayed, front, tiles, valid_rows, arrived, rows, cols, lower
    )


def solution(mesh):
    placed = (P("row", "col"), P(("row", "col"), None, None), P(), P(("row", "col")))
    return jax.shard_map(
        body, mesh=mesh, in_specs=placed, out_specs=P("row", "col"), check_vma=False
    )
```

```python
import functools

import jax
import jax.numpy as jnp
from jax import lax
from jax.experimental import pallas as pl
from jax.experimental.pallas import tpu as pltpu
from jax.sharding import PartitionSpec as P

NB = 128
PANELS = 2
TOTAL = NB * PANELS
MIB = 1 << 20
UNIT = 8


precise = lax.Precision.HIGHEST


def dot_nt(a, b, precision=precise):
    return lax.dot_general(
        a, b, (((1,), (1,)), ((), ())), precision=precision, preferred_element_type=jnp.float32
    )


def pack_kernel(slot_ref, valid_ref, tiles_ref, out_ref, buf, sem_in, sem_out):
    count, side = tiles_ref.shape[0], tiles_ref.shape[1]

    def fetch(t):
        return pltpu.make_async_copy(tiles_ref.at[t], buf.at[t], sem_in.at[t])

    def store(t):
        return pltpu.make_async_copy(buf.at[t], out_ref.at[jnp.maximum(slot_ref[t], 0)], sem_out.at[t])

    def each(act):
        @pl.loop(0, count)
        def _(t):
            @pl.when(slot_ref[t] >= 0)
            def _():
                act(t)

    def mask(t):
        fetch(t).wait()
        rows = lax.broadcasted_iota(jnp.int32, (side, side), 0)
        buf[t] = jnp.where(rows < valid_ref[t], buf[t], 0.0)
        store(t).start()

    each(lambda t: fetch(t).start())
    each(mask)
    each(lambda t: store(t).wait())


def pack(tiles, slots, valid, n_slots):
    count, side = tiles.shape[0], tiles.shape[1]
    smem = pl.BlockSpec(memory_space=pltpu.SMEM)
    return pl.pallas_call(
        pack_kernel,
        out_shape=jax.ShapeDtypeStruct((n_slots, side, side), jnp.float32),
        in_specs=[smem, smem, pl.BlockSpec(memory_space=pl.ANY)],
        out_specs=pl.BlockSpec(memory_space=pl.ANY),
        scratch_shapes=[
            pltpu.VMEM((count, side, side), jnp.float32),
            pltpu.SemaphoreType.DMA((count,)),
            pltpu.SemaphoreType.DMA((count,)),
        ],
        compiler_params=pltpu.CompilerParams(vmem_limit_bytes=24 * MIB),
    )(slots, valid, tiles)


def spread_kernel(
    width, stride, meta_ref, empty_ref, count_ref, tiles_ref, out_ref, code_ref, stage, sem
):
    count, units = tiles_ref.shape[0], tiles_ref.shape[1]
    devices, length = code_ref.shape

    @pl.loop(0, devices)
    def _(d):
        for k in range(length):
            code_ref[d, k] = -1

    @pl.loop(0, count)
    def _(i):
        tile, target, base = meta_ref[0, i], meta_ref[1, i], meta_ref[2, i]
        filled, code, valid = meta_ref[3, i], meta_ref[4, i], meta_ref[5, i]
        shape = tiles_ref.shape[1:]
        rows = lax.broadcasted_iota(jnp.int32, shape, 0) * shape[1]
        rows += lax.broadcasted_iota(jnp.int32, shape, 1)
        stage[target, pl.ds(base, units)] = jnp.where(rows < valid, tiles_ref[tile], 0.0)
        for u in range(units):
            code_ref[target, base + u] = jnp.where(u < filled, code + u * stride, -1)

    for half in range(2):
        first = 0 if half == 0 else count_ref[0]
        last = count_ref[0] if half == 0 else count
        free = count_ref[1 + half]

        def each_tile(i, carry):
            target, base, filled = meta_ref[1, i], meta_ref[2, i], meta_ref[3, i]

            def each_unit(q, carry):
                at, depth = carry
                relay = empty_ref[half, at]
                place = jnp.minimum(depth, width - 1)
                stage[relay, place] = stage[target, q]
                code_ref[relay, place] = code_ref[target, q]
                wrap = at + 1 >= free
                return jnp.where(wrap, 0, at + 1), jnp.where(wrap, depth + 1, depth)

            return lax.fori_loop(jnp.maximum(base, width), base + filled, each_unit, carry)

        lax.fori_loop(first, last, each_tile, (jnp.int32(0), jnp.int32(0)))

    copy = pltpu.make_async_copy(stage.at[:, pl.ds(0, width)], out_ref, sem)
    copy.start()
    copy.wait()


def spread(tiles, meta, empties, counts, devices, width, length, stride):
    count, side = tiles.shape[0], tiles.shape[1]
    units = side // UNIT
    smem = pl.BlockSpec(memory_space=pltpu.SMEM)
    return pl.pallas_call(
        functools.partial(spread_kernel, width, stride),
        out_shape=[
            jax.ShapeDtypeStruct((devices, width, UNIT, side), jnp.float32),
            jax.ShapeDtypeStruct((devices, length), jnp.int32),
        ],
        in_specs=[smem, smem, smem, pl.BlockSpec(memory_space=pltpu.VMEM)],
        out_specs=[pl.BlockSpec(memory_space=pl.ANY), smem],
        scratch_shapes=[
            pltpu.VMEM((devices, length, UNIT, side), jnp.float32),
            pltpu.SemaphoreType.DMA,
        ],
        compiler_params=pltpu.CompilerParams(vmem_limit_bytes=40 * MIB),
    )(meta, empties, counts, tiles.reshape(count, units, UNIT, side))


def relay_kernel(slot_ref, arrived_ref, out_ref):
    devices, width = slot_ref.shape

    @pl.loop(0, devices)
    def _(s):
        def more(k):
            return (k < width) & (slot_ref[s, jnp.minimum(k, width - 1)] >= 0)

        def move(k):
            out_ref[slot_ref[s, k]] = arrived_ref[s, k]
            return k + 1

        lax.while_loop(more, move, jnp.int32(0))


def relay(slots, arrived, length):
    vmem = pl.BlockSpec(memory_space=pltpu.VMEM)
    return pl.pallas_call(
        relay_kernel,
        out_shape=jax.ShapeDtypeStruct((length,) + arrived.shape[2:], jnp.float32),
        in_specs=[pl.BlockSpec(memory_space=pltpu.SMEM), vmem],
        out_specs=vmem,
        compiler_params=pltpu.CompilerParams(vmem_limit_bytes=40 * MIB),
    )(slots, arrived)


def add_kernel(
    cols_blocks, block_ref, unit_ref, index_ref, count_ref, partial_ref, arrived_ref, out_ref, buf,
    group_start, sem_in, sem_out
):
    slots, side = buf.shape[0], buf.shape[1]
    unit = arrived_ref.shape[1]
    ahead = slots // 2
    count = count_ref[0]

    def listed(i, carry):
        groups, last = carry
        block = block_ref[i]
        fresh = block != last

        @pl.when(fresh)
        def _():
            group_start[groups] = i

        return jnp.where(fresh, groups + 1, groups), block

    groups, _ = lax.fori_loop(0, count, listed, (jnp.int32(0), jnp.int32(-1)))
    group_start[groups] = count

    def window(g):
        block = block_ref[group_start[g]]
        rows = pl.ds(pl.multiple_of(block // cols_blocks * side, side), side)
        columns = pl.ds(pl.multiple_of(block % cols_blocks * side, side), side)
        return out_ref.at[rows, columns]

    def fetch(g):
        at = g % slots
        return pltpu.make_async_copy(window(g), buf.at[at], sem_in.at[at])

    def store(g):
        at = g % slots
        return pltpu.make_async_copy(buf.at[at], window(g), sem_out.at[at])

    @pl.loop(0, jnp.minimum(groups, ahead))
    def _(g):
        fetch(g).start()

    @pl.loop(0, groups)
    def _(g):
        @pl.when(g + ahead < groups)
        def _():
            @pl.when(g >= ahead)
            def _():
                store(g - ahead).wait()

            fetch(g + ahead).start()

        fetch(g).wait()

        @pl.loop(group_start[g], group_start[g + 1])
        def _(i):
            rows = pl.ds(pl.multiple_of(unit_ref[i] * unit, unit), unit)
            buf[g % slots, rows] += arrived_ref[index_ref[i]]

        store(g).start()

    @pl.loop(jnp.maximum(groups - slots, 0), groups)
    def _(g):
        store(g).wait()


def add_relayed(partial, arrived, listing, cols_blocks):
    row_len, col_len = partial.shape
    unit, side = arrived.shape[1:]
    smem = pl.BlockSpec(memory_space=pltpu.SMEM)
    hbm = pl.BlockSpec(memory_space=pl.ANY)
    return pl.pallas_call(
        functools.partial(add_kernel, cols_blocks),
        out_shape=jax.ShapeDtypeStruct((row_len, col_len), jnp.float32),
        in_specs=[smem, smem, smem, smem, hbm, pl.BlockSpec(memory_space=pltpu.VMEM)],
        out_specs=hbm,
        scratch_shapes=[
            pltpu.VMEM((16, side, side), jnp.float32),
            pltpu.SMEM((arrived.shape[0] + 1,), jnp.int32),
            pltpu.SemaphoreType.DMA((16,)),
            pltpu.SemaphoreType.DMA((16,)),
        ],
        input_output_aliases={4: 0},
        compiler_params=pltpu.CompilerParams(vmem_limit_bytes=24 * MIB),
    )(*listing, partial, arrived)


def panel_kernel(code_ref, first_ref, front_ref, arrived_ref, out_ref):
    side = arrived_ref.shape[1]

    @pl.when(first_ref[0] == 1)
    def _():
        out_ref[...] = front_ref[...]

    @pl.when(first_ref[0] == 0)
    def _():
        out_ref[...] = jnp.zeros_like(out_ref)

    @pl.loop(0, arrived_ref.shape[0])
    def _(k):
        code = code_ref[k]
        for part in range(PANELS):

            @pl.when((code >= 0) & (code % PANELS == part))
            def _():
                rows = pl.ds(pl.multiple_of(code // PANELS * side, side), side)
                out_ref[rows, part * side : (part + 1) * side] += arrived_ref[k]


def raw_panel(front, arrived, codes, first):
    row_len = front.shape[0]
    smem = pl.BlockSpec(memory_space=pltpu.SMEM)
    return pl.pallas_call(
        panel_kernel,
        grid=(1,),
        out_shape=jax.ShapeDtypeStruct((row_len, TOTAL), jnp.float32),
        in_specs=[
            smem,
            smem,
            pl.BlockSpec((row_len, TOTAL), lambda i: (0, 0)),
            pl.BlockSpec(arrived.shape, lambda i: (0, 0, 0)),
        ],
        out_specs=pl.BlockSpec((row_len, TOTAL), lambda i: (0, 0)),
        compiler_params=pltpu.CompilerParams(vmem_limit_bytes=40 * MIB),
    )(codes, first, front, arrived)


def split(value):
    high = value.astype(jnp.bfloat16)
    low = (value - high.astype(jnp.float32)).astype(jnp.bfloat16)
    return high, low


def rows_kernel(raw_ref, inverse_ref, out_ref, parts_ref):
    solved = dot_nt(raw_ref[...], inverse_ref[...])
    out_ref[...] = solved
    high, low = split(solved)
    parts_ref[:, :TOTAL] = high
    parts_ref[:, TOTAL : 2 * TOTAL] = high
    parts_ref[:, 2 * TOTAL :] = low


def solve_rows(raw, inverse):
    length = raw.shape[0]
    step = min(512, length)
    block = pl.BlockSpec((step, TOTAL), lambda i: (i, 0))
    return pl.pallas_call(
        rows_kernel,
        grid=(length // step,),
        out_shape=[
            jax.ShapeDtypeStruct((length, TOTAL), jnp.float32),
            jax.ShapeDtypeStruct((length, 3 * TOTAL), jnp.bfloat16),
        ],
        in_specs=[block, pl.BlockSpec((TOTAL, TOTAL), lambda i: (0, 0))],
        out_specs=[block, pl.BlockSpec((step, 3 * TOTAL), lambda i: (i, 0))],
        compiler_params=pltpu.CompilerParams(vmem_limit_bytes=24 * MIB),
    )(raw, inverse)


def cols_kernel(raw_ref, inverse_ref, out_ref, parts_ref):
    solved = dot_nt(inverse_ref[...], raw_ref[...])
    out_ref[...] = solved
    high, low = split(solved)
    parts_ref[:TOTAL] = high
    parts_ref[TOTAL : 2 * TOTAL] = low
    parts_ref[2 * TOTAL :] = high


def solve_cols(raw, inverse):
    length = raw.shape[0]
    step = min(512, length)
    block = pl.BlockSpec((TOTAL, step), lambda i: (0, i))
    return pl.pallas_call(
        cols_kernel,
        grid=(length // step,),
        out_shape=[
            jax.ShapeDtypeStruct((TOTAL, length), jnp.float32),
            jax.ShapeDtypeStruct((3 * TOTAL, length), jnp.bfloat16),
        ],
        in_specs=[
            pl.BlockSpec((step, TOTAL), lambda i: (i, 0)),
            pl.BlockSpec((TOTAL, TOTAL), lambda i: (0, 0)),
        ],
        out_specs=[block, pl.BlockSpec((3 * TOTAL, step), lambda i: (0, i))],
        compiler_params=pltpu.CompilerParams(vmem_limit_bytes=24 * MIB),
    )(raw, inverse)


def final_kernel(
    cols_blocks, runs, code_ref, run_ref, place_ref, front_ref, rows_ref, rows_parts, cols_ref, cols_parts,
    lower_ref, arrived_ref, out_ref, cursor
):
    step = pl.program_id(0)
    sources, capacity = code_ref.shape
    height, width = front_ref.shape
    unit, side = arrived_ref.shape[2:]
    per_step = height // unit

    @pl.when(step == 0)
    def _():
        for s in range(sources):
            cursor[s] = 0

    chunk = min(512, width)
    for start in range(0, width, chunk):
        at = slice(start, start + chunk)
        change = jnp.dot(rows_parts[...], cols_parts[:, at], preferred_element_type=jnp.float32)
        out_ref[:, at] = front_ref[:, at] - change

    edge = (step + 1) * per_step * cols_blocks

    @pl.loop(0, sources)
    def _(s):
        def more(k):
            code = code_ref[s, jnp.minimum(k, capacity - 1)]
            return (k < capacity) & (code >= 0) & (code < edge)

        def add(k):
            code = code_ref[s, k]
            length = run_ref[s, k]
            unit_row = code // cols_blocks - step * per_step
            columns = pl.ds(pl.multiple_of(code % cols_blocks * side, side), side)
            for run in runs:
                skipped = length // (2 * run) * (2 * run)

                @pl.when(length // run % 2 == 1)
                def _():
                    rows = pl.ds(pl.multiple_of((unit_row + skipped) * unit, unit), run * unit)
                    block = arrived_ref[s, pl.ds(k + skipped, run)]
                    out_ref[rows, columns] += block.reshape(run * unit, side)

            return k + length

        cursor[s] = lax.while_loop(more, add, cursor[s])

    top = (place_ref[0] == 0) & (step == 0)

    @pl.when(top)
    def _():
        out_ref[...] = cols_ref[...]

    @pl.when(place_ref[1] == 0)
    def _():
        out_ref[:, :TOTAL] = jnp.where(top, lower_ref[...], rows_ref[...])


def finish(front, rows, cols, lower, arrived, codes, lengths, place, cols_blocks):
    row_len, col_len = front.shape
    height = TOTAL
    smem = pl.BlockSpec(memory_space=pltpu.SMEM)
    block = pl.BlockSpec((height, TOTAL), lambda i: (i, 0))
    parts = pl.BlockSpec((height, 3 * TOTAL), lambda i: (i, 0))
    wide = pl.BlockSpec((height, col_len), lambda i: (i, 0))
    whole = pl.BlockSpec((TOTAL, col_len), lambda i: (0, 0))
    whole_parts = pl.BlockSpec((3 * TOTAL, col_len), lambda i: (0, 0))
    runs = (16, 8, 4, 2, 1) if arrived.shape[2] == UNIT else (1,)
    return pl.pallas_call(
        functools.partial(final_kernel, cols_blocks, runs),
        grid=(row_len // height,),
        out_shape=jax.ShapeDtypeStruct((row_len, col_len), jnp.float32),
        in_specs=[
            smem, smem, smem, wide, block, parts, whole, whole_parts,
            pl.BlockSpec((TOTAL, TOTAL), lambda i: (0, 0)),
            pl.BlockSpec(memory_space=pltpu.VMEM),
        ],
        out_specs=wide,
        scratch_shapes=[pltpu.SMEM((codes.shape[0],), jnp.int32)],
        compiler_params=pltpu.CompilerParams(vmem_limit_bytes=56 * MIB),
    )(codes, lengths, place, front, *rows, *cols, lower, arrived)


def factor(diagonal):
    def lower_of(block):
        return jnp.linalg.cholesky(jnp.tril(block) + jnp.tril(block, -1).T)

    def inverse_of(block):
        return jax.scipy.linalg.solve_triangular(block, jnp.eye(NB, dtype=jnp.float32), lower=True)

    first = lower_of(diagonal[:NB, :NB])
    first_inverse = inverse_of(first)
    below = dot_nt(diagonal[NB:, :NB], first_inverse)
    second = lower_of(diagonal[NB:, NB:] - dot_nt(below, below))
    second_inverse = inverse_of(second)
    corner = -jnp.dot(second_inverse, jnp.dot(below, first_inverse, precision=precise), precision=precise)
    zero = jnp.zeros((NB, NB), jnp.float32)
    return jnp.block([[first, zero], [below, second]]), jnp.block([[first_inverse, zero], [corner, second_inverse]])


def body(front, tiles, tile_block, valid_rows):
    row_len, col_len = front.shape
    row_count = lax.axis_size("row")
    col_count = lax.axis_size("col")
    device_count = row_count * col_count
    per_device = tiles.shape[0]
    side = tiles.shape[1]
    capacity = 2 * per_device // device_count
    rows_blocks = row_len // side
    cols_blocks = col_len // side
    row_now = lax.axis_index("row")
    col_now = lax.axis_index("col")
    device_now = row_now * col_count + col_now

    block_row = tile_block[0].reshape(device_count, per_device)
    block_col = tile_block[1].reshape(device_count, per_device)
    target_row = block_row // rows_blocks
    target = target_row * col_count + block_col // cols_blocks
    code = block_row % rows_blocks * cols_blocks + block_col % cols_blocks
    position = lax.broadcasted_iota(jnp.int32, target.shape, 1)
    place = jnp.stack([row_now, col_now]).astype(jnp.int32)

    def own(values):
        return lax.dynamic_index_in_dim(values, device_now, 0, keepdims=False)

    in_panel = block_col < PANELS
    panel_key = jnp.where(in_panel, target_row, -1)
    panel_rank = jnp.sum(
        (panel_key[:, :, None] == panel_key[:, None, :]) & (position[:, None, :] < position[:, :, None]),
        axis=2,
    )
    same_col = lax.dynamic_index_in_dim(
        jnp.stack([panel_key, panel_rank, code]).reshape(3, row_count, col_count, per_device),
        col_now, 2, keepdims=False,
    )

    def send_panel(tiles, valid_rows, depth):
        ahead = (own(target_row) - row_now) % row_count
        fits = own(in_panel) & (own(panel_rank) < depth)
        panel_slot = jnp.where(fits, ahead * depth + own(panel_rank), -1)
        panel_out = pack(tiles, panel_slot, valid_rows, row_count * depth)
        panel_in = [panel_out[:depth]]
        for shift in range(1, row_count):
            sending = panel_out[shift * depth : (shift + 1) * depth]
            turn = [(r, (r + shift) % row_count) for r in range(row_count)]
            panel_in.append(lax.ppermute(sending, "row", turn))
        return panel_in

    def sum_panel(front, panel_in, depth):
        fits = (same_col[0] == row_now)[:, :, None] & (same_col[1][:, :, None] == jnp.arange(depth))
        panel_code = same_col[2] // cols_blocks * PANELS + same_col[2] % cols_blocks
        panel_codes = jnp.sum(jnp.where(fits, panel_code[:, :, None] + 1, 0), axis=1) - 1
        by_shift = (row_now - jnp.arange(row_count)) % row_count
        panel_codes = jnp.take(panel_codes, by_shift, axis=0).reshape(-1)
        first = (col_now == 0).astype(jnp.int32).reshape(1)
        return raw_panel(front, jnp.concatenate(panel_in, 0), panel_codes, first)

    panel_depth = (capacity * 5 + 7) // 8
    panel_in = send_panel(tiles, valid_rows, panel_depth)

    units = side // UNIT
    length = capacity * units
    width = length * 41 // 64
    pass_on = length * 13 // 32
    half_count = device_count // 2
    half_base = device_now // half_count * half_count
    unit_rows = rows_blocks * units
    local_codes = unit_rows * cols_blocks
    own_target, own_code = own(target), own(code)
    own_position = own(position)
    filled = (valid_rows + UNIT - 1) // UNIT
    key = (own_target * rows_blocks * cols_blocks + own_code) * per_device + own_position
    before = key[None, :] < key[:, None]
    together = own_target[None, :] == own_target[:, None]
    base = jnp.sum(jnp.where(before & together, filled[None, :], 0), axis=1)
    order = jnp.sum(before, axis=1)
    unit_code = (own_target * unit_rows + own_code // cols_blocks * units) * cols_blocks
    unit_code += own_code % cols_blocks
    meta = jnp.stack([own_position, own_target, base, filled, unit_code, valid_rows])
    meta = jnp.sum(
        jnp.where(order[None, :, None] == jnp.arange(per_device), meta[:, :, None], 0), axis=1
    )
    to_device = own_target[:, None] == jnp.arange(device_count)
    load = jnp.sum(jnp.where(to_device, filled[:, None], 0), axis=0).reshape(2, half_count)
    empty = load == 0
    empty_rank = jnp.cumsum(empty, axis=1) - 1
    device_ids = jnp.arange(device_count).reshape(2, half_count)
    listed = (empty[:, :, None]) & (empty_rank[:, :, None] == jnp.arange(half_count))
    empties = jnp.sum(jnp.where(listed, device_ids[:, :, None], 0), axis=1)
    free = jnp.sum(empty, axis=1)
    left = jnp.sum(jnp.maximum(load - width, 0), axis=1)
    failed = jnp.any(left > free * width) | jnp.any(own(in_panel) & (own(panel_rank) >= panel_depth))
    counts = jnp.concatenate([jnp.sum(own_target < half_count)[None], free]).astype(jnp.int32)
    outgoing, sent_codes = spread(
        tiles, meta.astype(jnp.int32), empties.astype(jnp.int32), counts,
        device_count, width, length, cols_blocks,
    )

    partial = sum_panel(front, panel_in, panel_depth)
    partial, sent_codes = lax.optimization_barrier((partial, sent_codes))
    raw_rows = lax.psum(partial, "col")
    got = lax.all_to_all(sent_codes[:, :width], ("row", "col"), 0, 0, tiled=True)
    outgoing, got = lax.optimization_barrier((outgoing, got))
    arrived = lax.all_to_all(outgoing, ("row", "col"), 0, 0, tiled=True)
    got_target = got // local_codes
    local = got % local_codes
    mine = (got >= 0) & (got_target == device_now)
    direct_codes = jnp.where(mine, local, -1)
    steps = jnp.arange(width)
    opening = (local // cols_blocks % units == 0) | jnp.logical_not(mine)
    later = (steps[None, :] > steps[:, None]) & opening[:, None, :]
    direct_runs = jnp.min(jnp.where(later, steps, width), axis=2) - steps
    total_units = device_count * width
    passing = ((got >= 0) & (got_target != device_now)).reshape(-1)
    flat_key = jnp.where(passing, got.reshape(-1) * total_units + jnp.arange(total_units), -1)
    flat_target = jnp.where(passing, got_target.reshape(-1), -1)
    rank = jnp.sum(
        (flat_target[None, :] == flat_target[:, None]) & (flat_key[None, :] < flat_key[:, None]), axis=1
    )
    failed = failed | jnp.any(passing & (rank >= pass_on))
    relay_slot = jnp.where(
        passing & (rank < pass_on), (flat_target - half_base) * pass_on + rank, -1
    )
    picked = relay_slot[:, None] == jnp.arange(half_count * pass_on)
    relay_codes = jnp.sum(jnp.where(picked, local.reshape(-1)[:, None] + 1, 0), axis=0) - 1
    notes = jnp.zeros((2, half_count, pass_on + 1), jnp.int32)
    notes = lax.dynamic_update_slice(
        notes, relay_codes.reshape(1, half_count, pass_on).astype(jnp.int32), (device_now // half_count, 0, 0)
    )
    notes = notes.at[:, :, pass_on].set(failed.astype(jnp.int32))
    notes, arrived = lax.optimization_barrier((notes, arrived))
    notes = lax.all_to_all(
        notes.reshape(device_count, pass_on + 1), ("row", "col"), 0, 0, tiled=True
    )
    too_full = jnp.any(notes[:, pass_on] != 0)
    relay_codes = lax.dynamic_slice_in_dim(notes, half_base, half_count, 0)[:, :pass_on]
    relay_slot = relay_slot.reshape(device_count, width)

    flat = relay_codes.reshape(-1)
    unit_row, relay_col = flat // cols_blocks, flat % cols_blocks
    wanted = (flat >= 0) & ((row_now > 0) | (unit_row >= TOTAL // UNIT))
    wanted &= (col_now > 0) | (relay_col >= PANELS)
    relay_block = unit_row // units * cols_blocks + relay_col
    relay_key = jnp.where(wanted, relay_block * units + unit_row % units, local_codes)
    relay_key = relay_key * flat.shape[0] + jnp.arange(flat.shape[0])
    relay_order = jnp.sum(relay_key[None, :] < relay_key[:, None], axis=1)
    listing = jnp.stack([relay_block, unit_row % units, jnp.arange(flat.shape[0])])
    at_order = relay_order[None, :, None] == jnp.arange(flat.shape[0])
    listing = jnp.sum(jnp.where(at_order, listing[:, :, None], 0), axis=1).astype(jnp.int32)
    listing = [*listing, jnp.sum(wanted).astype(jnp.int32).reshape(1)]

    passed = relay(relay_slot, arrived, half_count * pass_on)
    slice_start = col_now * col_len % row_len
    slice_root = col_now * col_len // row_len

    def chain(raw_rows, *others):
        picked = lax.dynamic_slice_in_dim(raw_rows, slice_start, col_len, 0)
        raw_cols = lax.psum(jnp.where(row_now == slice_root, picked, 0.0), "row")
        diagonal = jnp.where(row_now == 0, raw_rows[:TOTAL], jnp.eye(TOTAL, dtype=jnp.float32))
        lower, inverse = factor(diagonal)
        known = jnp.where(row_now == 0, inverse, 0.0)
        inverse = known
        for other in range(1, row_count):
            inverse += lax.ppermute(known, "row", [(0, other)])
        rows = solve_rows(raw_rows, inverse)
        raw_cols, rows, others = lax.optimization_barrier((raw_cols, rows, others))
        return rows, solve_cols(raw_cols, inverse), lower, *others

    tables = (direct_codes, direct_runs, listing)
    rows, cols, lower, arrived, passed, tables = chain(raw_rows, arrived, passed, tables)
    direct_codes, direct_runs, listing = tables

    def relayed(front, tiles, valid_rows, arrived, passed, rows, cols, lower):
        halves = [list(range(half_count)), list(range(half_count, device_count))]
        passed = lax.all_to_all(
            passed.reshape(half_count, pass_on, UNIT, side), ("row", "col"), 0, 0,
            axis_index_groups=halves, tiled=True,
        )
        partial = finish(
            front, rows, cols, lower, arrived, direct_codes, direct_runs, place, cols_blocks
        )
        return add_relayed(partial, passed.reshape(-1, UNIT, side), listing, cols_blocks)

    def padded(front, tiles, valid_rows, arrived, passed, rows, cols, lower):
        partial = sum_panel(front, send_panel(tiles, valid_rows, capacity), capacity)
        raw_rows = lax.psum(partial, "col")
        order = (target * rows_blocks * cols_blocks + code) * per_device + position
        ranking = jnp.sum(
            (target[:, :, None] == target[:, None, :]) & (order[:, None, :] < order[:, :, None]), axis=2
        )
        slot = own(target) * capacity + own(ranking)
        here = (target == device_now)[:, :, None] & (ranking[:, :, None] == jnp.arange(capacity))
        codes = jnp.sum(jnp.where(here, code[:, :, None] + 1, 0), axis=1) - 1
        packed = pack(tiles, slot, valid_rows, device_count * capacity)
        arrived = lax.all_to_all(
            packed.reshape(device_count, capacity, side, side), ("row", "col"), 0, 0, tiled=True
        )
        rows, cols, lower = chain(raw_rows)
        return finish(
            front, rows, cols, lower, arrived, codes, jnp.ones_like(codes), place, cols_blocks
        )

    return lax.cond(
        too_full, padded, relayed, front, tiles, valid_rows, arrived, passed, rows, cols, lower
    )


def solution(mesh):
    placed = (P("row", "col"), P(("row", "col"), None, None), P(), P(("row", "col")))
    return jax.shard_map(
        body, mesh=mesh, in_specs=placed, out_specs=P("row", "col"), check_vma=False
    )
```

```python
import functools

import jax
import jax.numpy as jnp
from jax import lax
from jax.experimental import pallas as pl
from jax.experimental.pallas import tpu as pltpu
from jax.sharding import PartitionSpec as P

NB = 128
PANELS = 2
TOTAL = NB * PANELS
MIB = 1 << 20
UNIT = 8


precise = lax.Precision.HIGHEST


def dot_nt(a, b, precision=precise):
    return lax.dot_general(
        a, b, (((1,), (1,)), ((), ())), precision=precision, preferred_element_type=jnp.float32
    )


def pack_kernel(slot_ref, valid_ref, tiles_ref, out_ref, buf, sem_in, sem_out):
    count, side = tiles_ref.shape[0], tiles_ref.shape[1]

    def fetch(t):
        return pltpu.make_async_copy(tiles_ref.at[t], buf.at[t], sem_in.at[t])

    def store(t):
        return pltpu.make_async_copy(buf.at[t], out_ref.at[jnp.maximum(slot_ref[t], 0)], sem_out.at[t])

    def each(act):
        @pl.loop(0, count)
        def _(t):
            @pl.when(slot_ref[t] >= 0)
            def _():
                act(t)

    def mask(t):
        fetch(t).wait()
        rows = lax.broadcasted_iota(jnp.int32, (side, side), 0)
        buf[t] = jnp.where(rows < valid_ref[t], buf[t], 0.0)
        store(t).start()

    each(lambda t: fetch(t).start())
    each(mask)
    each(lambda t: store(t).wait())


def pack(tiles, slots, valid, n_slots):
    count, side = tiles.shape[0], tiles.shape[1]
    smem = pl.BlockSpec(memory_space=pltpu.SMEM)
    return pl.pallas_call(
        pack_kernel,
        out_shape=jax.ShapeDtypeStruct((n_slots, side, side), jnp.float32),
        in_specs=[smem, smem, pl.BlockSpec(memory_space=pl.ANY)],
        out_specs=pl.BlockSpec(memory_space=pl.ANY),
        scratch_shapes=[
            pltpu.VMEM((count, side, side), jnp.float32),
            pltpu.SemaphoreType.DMA((count,)),
            pltpu.SemaphoreType.DMA((count,)),
        ],
        compiler_params=pltpu.CompilerParams(vmem_limit_bytes=24 * MIB),
    )(slots, valid, tiles)


def spread_kernel(
    width, stride, meta_ref, empty_ref, count_ref, tiles_ref, out_ref, code_ref, stage, sem
):
    count, units = tiles_ref.shape[0], tiles_ref.shape[1]
    devices, length = code_ref.shape

    @pl.loop(0, devices)
    def _(d):
        for k in range(length):
            code_ref[d, k] = -1

    @pl.loop(0, count)
    def _(i):
        tile, target, base = meta_ref[0, i], meta_ref[1, i], meta_ref[2, i]
        filled, code, valid = meta_ref[3, i], meta_ref[4, i], meta_ref[5, i]
        shape = tiles_ref.shape[1:]
        rows = lax.broadcasted_iota(jnp.int32, shape, 0) * shape[1]
        rows += lax.broadcasted_iota(jnp.int32, shape, 1)
        stage[target, pl.ds(base, units)] = jnp.where(rows < valid, tiles_ref[tile], 0.0)
        for u in range(units):
            code_ref[target, base + u] = jnp.where(u < filled, code + u * stride, -1)

    for half in range(2):
        first = 0 if half == 0 else count_ref[0]
        last = count_ref[0] if half == 0 else count
        free = count_ref[1 + half]

        def each_tile(i, carry):
            target, base, filled = meta_ref[1, i], meta_ref[2, i], meta_ref[3, i]

            def each_unit(q, carry):
                at, depth = carry
                relay = empty_ref[half, at]
                place = jnp.minimum(depth, width - 1)
                stage[relay, place] = stage[target, q]
                code_ref[relay, place] = code_ref[target, q]
                wrap = at + 1 >= free
                return jnp.where(wrap, 0, at + 1), jnp.where(wrap, depth + 1, depth)

            return lax.fori_loop(jnp.maximum(base, width), base + filled, each_unit, carry)

        lax.fori_loop(first, last, each_tile, (jnp.int32(0), jnp.int32(0)))

    copy = pltpu.make_async_copy(stage.at[:, pl.ds(0, width)], out_ref, sem)
    copy.start()
    copy.wait()


def spread(tiles, meta, empties, counts, devices, width, length, stride):
    count, side = tiles.shape[0], tiles.shape[1]
    units = side // UNIT
    smem = pl.BlockSpec(memory_space=pltpu.SMEM)
    return pl.pallas_call(
        functools.partial(spread_kernel, width, stride),
        out_shape=[
            jax.ShapeDtypeStruct((devices, width, UNIT, side), jnp.float32),
            jax.ShapeDtypeStruct((devices, length), jnp.int32),
        ],
        in_specs=[smem, smem, smem, pl.BlockSpec(memory_space=pltpu.VMEM)],
        out_specs=[pl.BlockSpec(memory_space=pl.ANY), smem],
        scratch_shapes=[
            pltpu.VMEM((devices, length, UNIT, side), jnp.float32),
            pltpu.SemaphoreType.DMA,
        ],
        compiler_params=pltpu.CompilerParams(vmem_limit_bytes=40 * MIB),
    )(meta, empties, counts, tiles.reshape(count, units, UNIT, side))


def relay_kernel(slot_ref, arrived_ref, out_ref):
    devices, width = slot_ref.shape

    @pl.loop(0, devices)
    def _(s):
        def more(k):
            return (k < width) & (slot_ref[s, jnp.minimum(k, width - 1)] >= 0)

        def move(k):
            out_ref[slot_ref[s, k]] = arrived_ref[s, k]
            return k + 1

        lax.while_loop(more, move, jnp.int32(0))


def relay(slots, arrived, length):
    vmem = pl.BlockSpec(memory_space=pltpu.VMEM)
    return pl.pallas_call(
        relay_kernel,
        out_shape=jax.ShapeDtypeStruct((length,) + arrived.shape[2:], jnp.float32),
        in_specs=[pl.BlockSpec(memory_space=pltpu.SMEM), vmem],
        out_specs=vmem,
        compiler_params=pltpu.CompilerParams(vmem_limit_bytes=40 * MIB),
    )(slots, arrived)


def add_kernel(
    cols_blocks, block_ref, unit_ref, index_ref, count_ref, partial_ref, arrived_ref, out_ref, buf,
    group_start, sem_in, sem_out
):
    slots, side = buf.shape[0], buf.shape[1]
    unit = arrived_ref.shape[1]
    ahead = slots // 2
    count = count_ref[0]

    def listed(i, carry):
        groups, last = carry
        block = block_ref[i]
        fresh = block != last

        @pl.when(fresh)
        def _():
            group_start[groups] = i

        return jnp.where(fresh, groups + 1, groups), block

    groups, _ = lax.fori_loop(0, count, listed, (jnp.int32(0), jnp.int32(-1)))
    group_start[groups] = count

    def window(g):
        block = block_ref[group_start[g]]
        rows = pl.ds(pl.multiple_of(block // cols_blocks * side, side), side)
        columns = pl.ds(pl.multiple_of(block % cols_blocks * side, side), side)
        return out_ref.at[rows, columns]

    def fetch(g):
        at = g % slots
        return pltpu.make_async_copy(window(g), buf.at[at], sem_in.at[at])

    def store(g):
        at = g % slots
        return pltpu.make_async_copy(buf.at[at], window(g), sem_out.at[at])

    @pl.loop(0, jnp.minimum(groups, ahead))
    def _(g):
        fetch(g).start()

    @pl.loop(0, groups)
    def _(g):
        @pl.when(g + ahead < groups)
        def _():
            @pl.when(g >= ahead)
            def _():
                store(g - ahead).wait()

            fetch(g + ahead).start()

        fetch(g).wait()

        @pl.loop(group_start[g], group_start[g + 1])
        def _(i):
            rows = pl.ds(pl.multiple_of(unit_ref[i] * unit, unit), unit)
            buf[g % slots, rows] += arrived_ref[index_ref[i]]

        store(g).start()

    @pl.loop(jnp.maximum(groups - slots, 0), groups)
    def _(g):
        store(g).wait()


def add_relayed(partial, arrived, listing, cols_blocks):
    row_len, col_len = partial.shape
    unit, side = arrived.shape[1:]
    smem = pl.BlockSpec(memory_space=pltpu.SMEM)
    hbm = pl.BlockSpec(memory_space=pl.ANY)
    return pl.pallas_call(
        functools.partial(add_kernel, cols_blocks),
        out_shape=jax.ShapeDtypeStruct((row_len, col_len), jnp.float32),
        in_specs=[smem, smem, smem, smem, hbm, pl.BlockSpec(memory_space=pltpu.VMEM)],
        out_specs=hbm,
        scratch_shapes=[
            pltpu.VMEM((16, side, side), jnp.float32),
            pltpu.SMEM((arrived.shape[0] + 1,), jnp.int32),
            pltpu.SemaphoreType.DMA((16,)),
            pltpu.SemaphoreType.DMA((16,)),
        ],
        input_output_aliases={4: 0},
        compiler_params=pltpu.CompilerParams(vmem_limit_bytes=24 * MIB),
    )(*listing, partial, arrived)


def panel_kernel(code_ref, first_ref, front_ref, arrived_ref, out_ref):
    side = arrived_ref.shape[1]

    @pl.when(first_ref[0] == 1)
    def _():
        out_ref[...] = front_ref[...]

    @pl.when(first_ref[0] == 0)
    def _():
        out_ref[...] = jnp.zeros_like(out_ref)

    @pl.loop(0, arrived_ref.shape[0])
    def _(k):
        code = code_ref[k]
        for part in range(PANELS):

            @pl.when((code >= 0) & (code % PANELS == part))
            def _():
                rows = pl.ds(pl.multiple_of(code // PANELS * side, side), side)
                out_ref[rows, part * side : (part + 1) * side] += arrived_ref[k]


def raw_panel(front, arrived, codes, first):
    row_len = front.shape[0]
    smem = pl.BlockSpec(memory_space=pltpu.SMEM)
    return pl.pallas_call(
        panel_kernel,
        grid=(1,),
        out_shape=jax.ShapeDtypeStruct((row_len, TOTAL), jnp.float32),
        in_specs=[
            smem,
            smem,
            pl.BlockSpec((row_len, TOTAL), lambda i: (0, 0)),
            pl.BlockSpec(arrived.shape, lambda i: (0, 0, 0)),
        ],
        out_specs=pl.BlockSpec((row_len, TOTAL), lambda i: (0, 0)),
        compiler_params=pltpu.CompilerParams(vmem_limit_bytes=40 * MIB),
    )(codes, first, front, arrived)


def split(value):
    high = value.astype(jnp.bfloat16)
    low = (value - high.astype(jnp.float32)).astype(jnp.bfloat16)
    return high, low


def rows_kernel(raw_ref, inverse_ref, out_ref, parts_ref):
    solved = dot_nt(raw_ref[...], inverse_ref[...])
    out_ref[...] = solved
    high, low = split(solved)
    parts_ref[:, :TOTAL] = high
    parts_ref[:, TOTAL : 2 * TOTAL] = high
    parts_ref[:, 2 * TOTAL :] = low


def solve_rows(raw, inverse):
    length = raw.shape[0]
    step = min(512, length)
    block = pl.BlockSpec((step, TOTAL), lambda i: (i, 0))
    return pl.pallas_call(
        rows_kernel,
        grid=(length // step,),
        out_shape=[
            jax.ShapeDtypeStruct((length, TOTAL), jnp.float32),
            jax.ShapeDtypeStruct((length, 3 * TOTAL), jnp.bfloat16),
        ],
        in_specs=[block, pl.BlockSpec((TOTAL, TOTAL), lambda i: (0, 0))],
        out_specs=[block, pl.BlockSpec((step, 3 * TOTAL), lambda i: (i, 0))],
        compiler_params=pltpu.CompilerParams(vmem_limit_bytes=24 * MIB),
    )(raw, inverse)


def cols_kernel(order_ref, raw_ref, inverse_ref, out_ref, parts_ref):
    solved = dot_nt(inverse_ref[...], raw_ref[0])
    out_ref[...] = solved
    high, low = split(solved)
    parts_ref[:TOTAL] = high
    parts_ref[TOTAL : 2 * TOTAL] = low
    parts_ref[2 * TOTAL :] = high


def solve_cols(chunks, order, inverse):
    count, step = chunks.shape[:2]
    length = count * step
    grid_spec = pltpu.PrefetchScalarGridSpec(
        num_scalar_prefetch=1,
        grid=(count,),
        in_specs=[
            pl.BlockSpec((1, step, TOTAL), lambda i, order: (order[i], 0, 0)),
            pl.BlockSpec((TOTAL, TOTAL), lambda i, order: (0, 0)),
        ],
        out_specs=[
            pl.BlockSpec((TOTAL, step), lambda i, order: (0, i)),
            pl.BlockSpec((3 * TOTAL, step), lambda i, order: (0, i)),
        ],
    )
    return pl.pallas_call(
        cols_kernel,
        grid_spec=grid_spec,
        out_shape=[
            jax.ShapeDtypeStruct((TOTAL, length), jnp.float32),
            jax.ShapeDtypeStruct((3 * TOTAL, length), jnp.bfloat16),
        ],
        compiler_params=pltpu.CompilerParams(vmem_limit_bytes=24 * MIB),
    )(order, chunks, inverse)


def final_kernel(
    cols_blocks, runs, code_ref, run_ref, place_ref, front_ref, rows_ref, rows_parts, cols_ref, cols_parts,
    lower_ref, arrived_ref, out_ref, cursor
):
    step = pl.program_id(0)
    sources, capacity = code_ref.shape
    height, width = front_ref.shape
    unit, side = arrived_ref.shape[2:]
    per_step = height // unit

    @pl.when(step == 0)
    def _():
        for s in range(sources):
            cursor[s] = 0

    chunk = min(512, width)
    for start in range(0, width, chunk):
        at = slice(start, start + chunk)
        change = jnp.dot(rows_parts[...], cols_parts[:, at], preferred_element_type=jnp.float32)
        out_ref[:, at] = front_ref[:, at] - change

    edge = (step + 1) * per_step * cols_blocks

    @pl.loop(0, sources)
    def _(s):
        def more(k):
            code = code_ref[s, jnp.minimum(k, capacity - 1)]
            return (k < capacity) & (code >= 0) & (code < edge)

        def add(k):
            code = code_ref[s, k]
            length = run_ref[s, k]
            unit_row = code // cols_blocks - step * per_step
            columns = pl.ds(pl.multiple_of(code % cols_blocks * side, side), side)
            for run in runs:
                skipped = length // (2 * run) * (2 * run)

                @pl.when(length // run % 2 == 1)
                def _():
                    rows = pl.ds(pl.multiple_of((unit_row + skipped) * unit, unit), run * unit)
                    block = arrived_ref[s, pl.ds(k + skipped, run)]
                    out_ref[rows, columns] += block.reshape(run * unit, side)

            return k + length

        cursor[s] = lax.while_loop(more, add, cursor[s])

    top = (place_ref[0] == 0) & (step == 0)

    @pl.when(top)
    def _():
        out_ref[...] = cols_ref[...]

    @pl.when(place_ref[1] == 0)
    def _():
        out_ref[:, :TOTAL] = jnp.where(top, lower_ref[...], rows_ref[...])


def finish(front, rows, cols, lower, arrived, codes, lengths, place, cols_blocks):
    row_len, col_len = front.shape
    height = TOTAL
    smem = pl.BlockSpec(memory_space=pltpu.SMEM)
    block = pl.BlockSpec((height, TOTAL), lambda i: (i, 0))
    parts = pl.BlockSpec((height, 3 * TOTAL), lambda i: (i, 0))
    wide = pl.BlockSpec((height, col_len), lambda i: (i, 0))
    whole = pl.BlockSpec((TOTAL, col_len), lambda i: (0, 0))
    whole_parts = pl.BlockSpec((3 * TOTAL, col_len), lambda i: (0, 0))
    runs = (16, 8, 4, 2, 1) if arrived.shape[2] == UNIT else (1,)
    return pl.pallas_call(
        functools.partial(final_kernel, cols_blocks, runs),
        grid=(row_len // height,),
        out_shape=jax.ShapeDtypeStruct((row_len, col_len), jnp.float32),
        in_specs=[
            smem, smem, smem, wide, block, parts, whole, whole_parts,
            pl.BlockSpec((TOTAL, TOTAL), lambda i: (0, 0)),
            pl.BlockSpec(memory_space=pltpu.VMEM),
        ],
        out_specs=wide,
        scratch_shapes=[pltpu.SMEM((codes.shape[0],), jnp.int32)],
        compiler_params=pltpu.CompilerParams(vmem_limit_bytes=56 * MIB),
    )(codes, lengths, place, front, *rows, *cols, lower, arrived)


def factor(diagonal):
    def lower_of(block):
        return jnp.linalg.cholesky(jnp.tril(block) + jnp.tril(block, -1).T)

    def inverse_of(block):
        return jax.scipy.linalg.solve_triangular(block, jnp.eye(NB, dtype=jnp.float32), lower=True)

    first = lower_of(diagonal[:NB, :NB])
    first_inverse = inverse_of(first)
    below = dot_nt(diagonal[NB:, :NB], first_inverse)
    second = lower_of(diagonal[NB:, NB:] - dot_nt(below, below))
    second_inverse = inverse_of(second)
    corner = -jnp.dot(second_inverse, jnp.dot(below, first_inverse, precision=precise), precision=precise)
    zero = jnp.zeros((NB, NB), jnp.float32)
    return jnp.block([[first, zero], [below, second]]), jnp.block([[first_inverse, zero], [corner, second_inverse]])


def body(front, tiles, tile_block, valid_rows):
    row_len, col_len = front.shape
    row_count = lax.axis_size("row")
    col_count = lax.axis_size("col")
    device_count = row_count * col_count
    per_device = tiles.shape[0]
    side = tiles.shape[1]
    capacity = 2 * per_device // device_count
    rows_blocks = row_len // side
    cols_blocks = col_len // side
    row_now = lax.axis_index("row")
    col_now = lax.axis_index("col")
    device_now = row_now * col_count + col_now

    block_row = tile_block[0].reshape(device_count, per_device)
    block_col = tile_block[1].reshape(device_count, per_device)
    target_row = block_row // rows_blocks
    target = target_row * col_count + block_col // cols_blocks
    code = block_row % rows_blocks * cols_blocks + block_col % cols_blocks
    position = lax.broadcasted_iota(jnp.int32, target.shape, 1)
    place = jnp.stack([row_now, col_now]).astype(jnp.int32)

    def own(values):
        return lax.dynamic_index_in_dim(values, device_now, 0, keepdims=False)

    in_panel = block_col < PANELS
    panel_key = jnp.where(in_panel, target_row, -1)
    panel_rank = jnp.sum(
        (panel_key[:, :, None] == panel_key[:, None, :]) & (position[:, None, :] < position[:, :, None]),
        axis=2,
    )
    same_col = lax.dynamic_index_in_dim(
        jnp.stack([panel_key, panel_rank, code]).reshape(3, row_count, col_count, per_device),
        col_now, 2, keepdims=False,
    )

    def send_panel(tiles, valid_rows, depth):
        ahead = (own(target_row) - row_now) % row_count
        fits = own(in_panel) & (own(panel_rank) < depth)
        panel_slot = jnp.where(fits, ahead * depth + own(panel_rank), -1)
        panel_out = pack(tiles, panel_slot, valid_rows, row_count * depth)
        panel_in = [panel_out[:depth]]
        for shift in range(1, row_count):
            sending = panel_out[shift * depth : (shift + 1) * depth]
            turn = [(r, (r + shift) % row_count) for r in range(row_count)]
            panel_in.append(lax.ppermute(sending, "row", turn))
        return panel_in

    def sum_panel(front, panel_in, depth):
        fits = (same_col[0] == row_now)[:, :, None] & (same_col[1][:, :, None] == jnp.arange(depth))
        panel_code = same_col[2] // cols_blocks * PANELS + same_col[2] % cols_blocks
        panel_codes = jnp.sum(jnp.where(fits, panel_code[:, :, None] + 1, 0), axis=1) - 1
        by_shift = (row_now - jnp.arange(row_count)) % row_count
        panel_codes = jnp.take(panel_codes, by_shift, axis=0).reshape(-1)
        first = (col_now == 0).astype(jnp.int32).reshape(1)
        return raw_panel(front, jnp.concatenate(panel_in, 0), panel_codes, first)

    def gather_panel(partial):
        chunk = lax.psum_scatter(partial, "col", scatter_dimension=0, tiled=True)
        gathered = lax.all_gather(chunk, "row", axis=0)
        return gathered, lax.all_gather(chunk, "col", axis=0, tiled=True)

    panel_depth = (capacity * 5 + 7) // 8
    panel_in = send_panel(tiles, valid_rows, panel_depth)

    units = side // UNIT
    length = capacity * units
    width = length * 41 // 64
    pass_on = length * 13 // 32
    half_count = device_count // 2
    half_base = device_now // half_count * half_count
    unit_rows = rows_blocks * units
    local_codes = unit_rows * cols_blocks
    own_target, own_code = own(target), own(code)
    own_position = own(position)
    filled = (valid_rows + UNIT - 1) // UNIT
    key = (own_target * rows_blocks * cols_blocks + own_code) * per_device + own_position
    before = key[None, :] < key[:, None]
    together = own_target[None, :] == own_target[:, None]
    base = jnp.sum(jnp.where(before & together, filled[None, :], 0), axis=1)
    order = jnp.sum(before, axis=1)
    unit_code = (own_target * unit_rows + own_code // cols_blocks * units) * cols_blocks
    unit_code += own_code % cols_blocks
    meta = jnp.stack([own_position, own_target, base, filled, unit_code, valid_rows])
    meta = jnp.sum(
        jnp.where(order[None, :, None] == jnp.arange(per_device), meta[:, :, None], 0), axis=1
    )
    to_device = own_target[:, None] == jnp.arange(device_count)
    load = jnp.sum(jnp.where(to_device, filled[:, None], 0), axis=0).reshape(2, half_count)
    empty = load == 0
    empty_rank = jnp.cumsum(empty, axis=1) - 1
    device_ids = jnp.arange(device_count).reshape(2, half_count)
    listed = (empty[:, :, None]) & (empty_rank[:, :, None] == jnp.arange(half_count))
    empties = jnp.sum(jnp.where(listed, device_ids[:, :, None], 0), axis=1)
    free = jnp.sum(empty, axis=1)
    left = jnp.sum(jnp.maximum(load - width, 0), axis=1)
    failed = jnp.any(left > free * width) | jnp.any(own(in_panel) & (own(panel_rank) >= panel_depth))
    counts = jnp.concatenate([jnp.sum(own_target < half_count)[None], free]).astype(jnp.int32)
    outgoing, sent_codes = spread(
        tiles, meta.astype(jnp.int32), empties.astype(jnp.int32), counts,
        device_count, width, length, cols_blocks,
    )

    partial = sum_panel(front, panel_in, panel_depth)
    partial, sent_codes = lax.optimization_barrier((partial, sent_codes))
    gathered, raw_rows = gather_panel(partial)
    got = lax.all_to_all(sent_codes[:, :width], ("row", "col"), 0, 0, tiled=True)
    outgoing, got = lax.optimization_barrier((outgoing, got))
    arrived = lax.all_to_all(outgoing, ("row", "col"), 0, 0, tiled=True)
    got_target = got // local_codes
    local = got % local_codes
    mine = (got >= 0) & (got_target == device_now)
    direct_codes = jnp.where(mine, local, -1)
    steps = jnp.arange(width)
    opening = (local // cols_blocks % units == 0) | jnp.logical_not(mine)
    later = (steps[None, :] > steps[:, None]) & opening[:, None, :]
    direct_runs = jnp.min(jnp.where(later, steps, width), axis=2) - steps
    total_units = device_count * width
    passing = ((got >= 0) & (got_target != device_now)).reshape(-1)
    flat_key = jnp.where(passing, got.reshape(-1) * total_units + jnp.arange(total_units), -1)
    flat_target = jnp.where(passing, got_target.reshape(-1), -1)
    rank = jnp.sum(
        (flat_target[None, :] == flat_target[:, None]) & (flat_key[None, :] < flat_key[:, None]), axis=1
    )
    failed = failed | jnp.any(passing & (rank >= pass_on))
    relay_slot = jnp.where(
        passing & (rank < pass_on), (flat_target - half_base) * pass_on + rank, -1
    )
    picked = relay_slot[:, None] == jnp.arange(half_count * pass_on)
    relay_codes = jnp.sum(jnp.where(picked, local.reshape(-1)[:, None] + 1, 0), axis=0) - 1
    notes = jnp.zeros((2, half_count, pass_on + 1), jnp.int32)
    notes = lax.dynamic_update_slice(
        notes, relay_codes.reshape(1, half_count, pass_on).astype(jnp.int32), (device_now // half_count, 0, 0)
    )
    notes = notes.at[:, :, pass_on].set(failed.astype(jnp.int32))
    notes, arrived = lax.optimization_barrier((notes, arrived))
    notes = lax.all_to_all(
        notes.reshape(device_count, pass_on + 1), ("row", "col"), 0, 0, tiled=True
    )
    too_full = jnp.any(notes[:, pass_on] != 0)
    relay_codes = lax.dynamic_slice_in_dim(notes, half_base, half_count, 0)[:, :pass_on]
    relay_slot = relay_slot.reshape(device_count, width)

    flat = relay_codes.reshape(-1)
    unit_row, relay_col = flat // cols_blocks, flat % cols_blocks
    wanted = (flat >= 0) & ((row_now > 0) | (unit_row >= TOTAL // UNIT))
    wanted &= (col_now > 0) | (relay_col >= PANELS)
    relay_block = unit_row // units * cols_blocks + relay_col
    relay_key = jnp.where(wanted, relay_block * units + unit_row % units, local_codes)
    relay_key = relay_key * flat.shape[0] + jnp.arange(flat.shape[0])
    relay_order = jnp.sum(relay_key[None, :] < relay_key[:, None], axis=1)
    listing = jnp.stack([relay_block, unit_row % units, jnp.arange(flat.shape[0])])
    at_order = relay_order[None, :, None] == jnp.arange(flat.shape[0])
    listing = jnp.sum(jnp.where(at_order, listing[:, :, None], 0), axis=1).astype(jnp.int32)
    listing = [*listing, jnp.sum(wanted).astype(jnp.int32).reshape(1)]

    passed = relay(relay_slot, arrived, half_count * pass_on)
    def chain(gathered, raw_rows, arrived):
        gathered, raw_rows = lax.optimization_barrier((gathered, raw_rows))
        diagonal = jnp.where(row_now == 0, raw_rows[:TOTAL], jnp.eye(TOTAL, dtype=jnp.float32))
        lower, inverse = factor(diagonal)
        known = jnp.where(row_now == 0, inverse, 0.0)
        gathered, arrived = lax.optimization_barrier((gathered, arrived))
        share = col_count // row_count
        chunks = []
        for turn in range(row_count):
            pairs = [
                (h * row_count + i, (i + turn) % row_count * share + h)
                for h in range(share)
                for i in range(row_count)
            ]
            sending = lax.dynamic_index_in_dim(gathered, (col_now + turn) % row_count, 0, keepdims=False)
            chunks.append(lax.ppermute(sending, "col", pairs))
        order = (col_now // share - jnp.arange(row_count)) % row_count
        inverse = known
        for other in range(1, row_count):
            inverse += lax.ppermute(known, "row", [(0, other)])
        rows = solve_rows(raw_rows, inverse)
        cols = solve_cols(jnp.stack(chunks), order.astype(jnp.int32), inverse)
        return rows, cols, lower

    tables = (direct_codes, direct_runs, listing)
    rows, cols, lower = chain(gathered, raw_rows, arrived)
    rows, cols, lower, passed, tables = lax.optimization_barrier((rows, cols, lower, passed, tables))
    direct_codes, direct_runs, listing = tables

    def relayed(front, tiles, valid_rows, arrived, passed, rows, cols, lower):
        halves = [list(range(half_count)), list(range(half_count, device_count))]
        passed = lax.all_to_all(
            passed.reshape(half_count, pass_on, UNIT, side), ("row", "col"), 0, 0,
            axis_index_groups=halves, tiled=True,
        )
        partial = finish(
            front, rows, cols, lower, arrived, direct_codes, direct_runs, place, cols_blocks
        )
        return add_relayed(partial, passed.reshape(-1, UNIT, side), listing, cols_blocks)

    def padded(front, tiles, valid_rows, arrived, passed, rows, cols, lower):
        partial = sum_panel(front, send_panel(tiles, valid_rows, capacity), capacity)
        gathered, raw_rows = gather_panel(partial)
        order = (target * rows_blocks * cols_blocks + code) * per_device + position
        ranking = jnp.sum(
            (target[:, :, None] == target[:, None, :]) & (order[:, None, :] < order[:, :, None]), axis=2
        )
        slot = own(target) * capacity + own(ranking)
        here = (target == device_now)[:, :, None] & (ranking[:, :, None] == jnp.arange(capacity))
        codes = jnp.sum(jnp.where(here, code[:, :, None] + 1, 0), axis=1) - 1
        packed = pack(tiles, slot, valid_rows, device_count * capacity)
        arrived = lax.all_to_all(
            packed.reshape(device_count, capacity, side, side), ("row", "col"), 0, 0, tiled=True
        )
        rows, cols, lower = chain(gathered, raw_rows, arrived)
        return finish(
            front, rows, cols, lower, arrived, codes, jnp.ones_like(codes), place, cols_blocks
        )

    return lax.cond(
        too_full, padded, relayed, front, tiles, valid_rows, arrived, passed, rows, cols, lower
    )


def solution(mesh):
    placed = (P("row", "col"), P(("row", "col"), None, None), P(), P(("row", "col")))
    return jax.shard_map(
        body, mesh=mesh, in_specs=placed, out_specs=P("row", "col"), check_vma=False
    )
```

```python
import functools

import jax
import jax.numpy as jnp
from jax import lax
from jax.experimental import pallas as pl
from jax.experimental.pallas import tpu as pltpu
from jax.sharding import PartitionSpec as P

NB = 128
PANELS = 2
TOTAL = NB * PANELS
MIB = 1 << 20
UNIT = 8


precise = lax.Precision.HIGHEST


def dot_nt(a, b, precision=precise):
    return lax.dot_general(
        a, b, (((1,), (1,)), ((), ())), precision=precision, preferred_element_type=jnp.float32
    )


def pack_kernel(slot_ref, valid_ref, tiles_ref, out_ref, buf, sem_in, sem_out):
    count, side = tiles_ref.shape[0], tiles_ref.shape[1]

    def fetch(t):
        return pltpu.make_async_copy(tiles_ref.at[t], buf.at[t], sem_in.at[t])

    def store(t):
        return pltpu.make_async_copy(buf.at[t], out_ref.at[jnp.maximum(slot_ref[t], 0)], sem_out.at[t])

    def each(act):
        @pl.loop(0, count)
        def _(t):
            @pl.when(slot_ref[t] >= 0)
            def _():
                act(t)

    def mask(t):
        fetch(t).wait()
        rows = lax.broadcasted_iota(jnp.int32, (side, side), 0)
        buf[t] = jnp.where(rows < valid_ref[t], buf[t], 0.0)
        store(t).start()

    each(lambda t: fetch(t).start())
    each(mask)
    each(lambda t: store(t).wait())


def pack(tiles, slots, valid, n_slots):
    count, side = tiles.shape[0], tiles.shape[1]
    smem = pl.BlockSpec(memory_space=pltpu.SMEM)
    return pl.pallas_call(
        pack_kernel,
        out_shape=jax.ShapeDtypeStruct((n_slots, side, side), jnp.float32),
        in_specs=[smem, smem, pl.BlockSpec(memory_space=pl.ANY)],
        out_specs=pl.BlockSpec(memory_space=pl.ANY),
        scratch_shapes=[
            pltpu.VMEM((count, side, side), jnp.float32),
            pltpu.SemaphoreType.DMA((count,)),
            pltpu.SemaphoreType.DMA((count,)),
        ],
        compiler_params=pltpu.CompilerParams(vmem_limit_bytes=24 * MIB),
    )(slots, valid, tiles)


def spread_kernel(
    width, stride, meta_ref, empty_ref, count_ref, tiles_ref, out_ref, code_ref, stage, sem
):
    count, units = tiles_ref.shape[0], tiles_ref.shape[1]
    devices, length = code_ref.shape

    @pl.loop(0, devices)
    def _(d):
        for k in range(length):
            code_ref[d, k] = -1

    @pl.loop(0, count)
    def _(i):
        tile, target, base = meta_ref[0, i], meta_ref[1, i], meta_ref[2, i]
        filled, code, valid = meta_ref[3, i], meta_ref[4, i], meta_ref[5, i]
        shape = tiles_ref.shape[1:]
        rows = lax.broadcasted_iota(jnp.int32, shape, 0) * shape[1]
        rows += lax.broadcasted_iota(jnp.int32, shape, 1)
        stage[target, pl.ds(base, units)] = jnp.where(rows < valid, tiles_ref[tile], 0.0)
        for u in range(units):
            code_ref[target, base + u] = jnp.where(u < filled, code + u * stride, -1)

    for half in range(2):
        first = 0 if half == 0 else count_ref[0]
        last = count_ref[0] if half == 0 else count
        free = count_ref[1 + half]

        def each_tile(i, carry):
            target, base, filled = meta_ref[1, i], meta_ref[2, i], meta_ref[3, i]

            def each_unit(q, carry):
                at, depth = carry
                relay = empty_ref[half, at]
                place = jnp.minimum(depth, width - 1)
                stage[relay, place] = stage[target, q]
                code_ref[relay, place] = code_ref[target, q]
                wrap = at + 1 >= free
                return jnp.where(wrap, 0, at + 1), jnp.where(wrap, depth + 1, depth)

            return lax.fori_loop(jnp.maximum(base, width), base + filled, each_unit, carry)

        lax.fori_loop(first, last, each_tile, (jnp.int32(0), jnp.int32(0)))

    copy = pltpu.make_async_copy(stage.at[:, pl.ds(0, width)], out_ref, sem)
    copy.start()
    copy.wait()


def spread(tiles, meta, empties, counts, devices, width, length, stride):
    count, side = tiles.shape[0], tiles.shape[1]
    units = side // UNIT
    smem = pl.BlockSpec(memory_space=pltpu.SMEM)
    return pl.pallas_call(
        functools.partial(spread_kernel, width, stride),
        out_shape=[
            jax.ShapeDtypeStruct((devices, width, UNIT, side), jnp.float32),
            jax.ShapeDtypeStruct((devices, length), jnp.int32),
        ],
        in_specs=[smem, smem, smem, pl.BlockSpec(memory_space=pltpu.VMEM)],
        out_specs=[pl.BlockSpec(memory_space=pl.ANY), smem],
        scratch_shapes=[
            pltpu.VMEM((devices, length, UNIT, side), jnp.float32),
            pltpu.SemaphoreType.DMA,
        ],
        compiler_params=pltpu.CompilerParams(vmem_limit_bytes=40 * MIB),
    )(meta, empties, counts, tiles.reshape(count, units, UNIT, side))


def relay_kernel(slot_ref, arrived_ref, out_ref):
    devices, width = slot_ref.shape

    @pl.loop(0, devices)
    def _(s):
        def more(k):
            return (k < width) & (slot_ref[s, jnp.minimum(k, width - 1)] >= 0)

        def move(k):
            out_ref[slot_ref[s, k]] = arrived_ref[s, k]
            return k + 1

        lax.while_loop(more, move, jnp.int32(0))


def relay(slots, arrived, length):
    vmem = pl.BlockSpec(memory_space=pltpu.VMEM)
    return pl.pallas_call(
        relay_kernel,
        out_shape=jax.ShapeDtypeStruct((length,) + arrived.shape[2:], jnp.float32),
        in_specs=[pl.BlockSpec(memory_space=pltpu.SMEM), vmem],
        out_specs=vmem,
        compiler_params=pltpu.CompilerParams(vmem_limit_bytes=40 * MIB),
    )(slots, arrived)


def add_kernel(
    cols_blocks, block_ref, unit_ref, index_ref, count_ref, partial_ref, arrived_ref, out_ref, buf,
    group_start, sem_in, sem_out
):
    slots, side = buf.shape[0], buf.shape[1]
    unit = arrived_ref.shape[1]
    ahead = slots // 2
    count = count_ref[0]

    def listed(i, carry):
        groups, last = carry
        block = block_ref[i]
        fresh = block != last

        @pl.when(fresh)
        def _():
            group_start[groups] = i

        return jnp.where(fresh, groups + 1, groups), block

    groups, _ = lax.fori_loop(0, count, listed, (jnp.int32(0), jnp.int32(-1)))
    group_start[groups] = count

    def window(g):
        block = block_ref[group_start[g]]
        rows = pl.ds(pl.multiple_of(block // cols_blocks * side, side), side)
        columns = pl.ds(pl.multiple_of(block % cols_blocks * side, side), side)
        return out_ref.at[rows, columns]

    def fetch(g):
        at = g % slots
        return pltpu.make_async_copy(window(g), buf.at[at], sem_in.at[at])

    def store(g):
        at = g % slots
        return pltpu.make_async_copy(buf.at[at], window(g), sem_out.at[at])

    @pl.loop(0, jnp.minimum(groups, ahead))
    def _(g):
        fetch(g).start()

    @pl.loop(0, groups)
    def _(g):
        @pl.when(g + ahead < groups)
        def _():
            @pl.when(g >= ahead)
            def _():
                store(g - ahead).wait()

            fetch(g + ahead).start()

        fetch(g).wait()

        @pl.loop(group_start[g], group_start[g + 1])
        def _(i):
            rows = pl.ds(pl.multiple_of(unit_ref[i] * unit, unit), unit)
            buf[g % slots, rows] += arrived_ref[index_ref[i]]

        store(g).start()

    @pl.loop(jnp.maximum(groups - slots, 0), groups)
    def _(g):
        store(g).wait()


def add_relayed(partial, arrived, listing, cols_blocks):
    row_len, col_len = partial.shape
    unit, side = arrived.shape[1:]
    smem = pl.BlockSpec(memory_space=pltpu.SMEM)
    hbm = pl.BlockSpec(memory_space=pl.ANY)
    return pl.pallas_call(
        functools.partial(add_kernel, cols_blocks),
        out_shape=jax.ShapeDtypeStruct((row_len, col_len), jnp.float32),
        in_specs=[smem, smem, smem, smem, hbm, pl.BlockSpec(memory_space=pltpu.VMEM)],
        out_specs=hbm,
        scratch_shapes=[
            pltpu.VMEM((16, side, side), jnp.float32),
            pltpu.SMEM((arrived.shape[0] + 1,), jnp.int32),
            pltpu.SemaphoreType.DMA((16,)),
            pltpu.SemaphoreType.DMA((16,)),
        ],
        input_output_aliases={4: 0},
        compiler_params=pltpu.CompilerParams(vmem_limit_bytes=24 * MIB),
    )(*listing, partial, arrived)


def panel_kernel(code_ref, first_ref, front_ref, arrived_ref, out_ref):
    side = arrived_ref.shape[1]

    @pl.when(first_ref[0] == 1)
    def _():
        out_ref[...] = front_ref[...]

    @pl.when(first_ref[0] == 0)
    def _():
        out_ref[...] = jnp.zeros_like(out_ref)

    @pl.loop(0, arrived_ref.shape[0])
    def _(k):
        code = code_ref[k]
        for part in range(PANELS):

            @pl.when((code >= 0) & (code % PANELS == part))
            def _():
                rows = pl.ds(pl.multiple_of(code // PANELS * side, side), side)
                out_ref[rows, part * side : (part + 1) * side] += arrived_ref[k]


def raw_panel(front, arrived, codes, first):
    row_len = front.shape[0]
    smem = pl.BlockSpec(memory_space=pltpu.SMEM)
    return pl.pallas_call(
        panel_kernel,
        grid=(1,),
        out_shape=jax.ShapeDtypeStruct((row_len, TOTAL), jnp.float32),
        in_specs=[
            smem,
            smem,
            pl.BlockSpec((row_len, TOTAL), lambda i: (0, 0)),
            pl.BlockSpec(arrived.shape, lambda i: (0, 0, 0)),
        ],
        out_specs=pl.BlockSpec((row_len, TOTAL), lambda i: (0, 0)),
        compiler_params=pltpu.CompilerParams(vmem_limit_bytes=40 * MIB),
    )(codes, first, front, arrived)


def split(value):
    high = value.astype(jnp.bfloat16)
    low = (value - high.astype(jnp.float32)).astype(jnp.bfloat16)
    return high, low


def rows_kernel(raw_ref, inverse_ref, out_ref, parts_ref):
    solved = dot_nt(raw_ref[...], inverse_ref[...])
    out_ref[...] = solved
    high, low = split(solved)
    parts_ref[:, :TOTAL] = high
    parts_ref[:, TOTAL : 2 * TOTAL] = high
    parts_ref[:, 2 * TOTAL :] = low


def solve_rows(raw, inverse):
    length = raw.shape[0]
    step = min(512, length)
    block = pl.BlockSpec((step, TOTAL), lambda i: (i, 0))
    return pl.pallas_call(
        rows_kernel,
        grid=(length // step,),
        out_shape=[
            jax.ShapeDtypeStruct((length, TOTAL), jnp.float32),
            jax.ShapeDtypeStruct((length, 3 * TOTAL), jnp.bfloat16),
        ],
        in_specs=[block, pl.BlockSpec((TOTAL, TOTAL), lambda i: (0, 0))],
        out_specs=[block, pl.BlockSpec((step, 3 * TOTAL), lambda i: (i, 0))],
        compiler_params=pltpu.CompilerParams(vmem_limit_bytes=24 * MIB),
    )(raw, inverse)


def cols_kernel(order_ref, raw_ref, inverse_ref, out_ref, parts_ref):
    solved = dot_nt(inverse_ref[...], raw_ref[0])
    out_ref[...] = solved
    high, low = split(solved)
    parts_ref[:TOTAL] = high
    parts_ref[TOTAL : 2 * TOTAL] = low
    parts_ref[2 * TOTAL :] = high


def solve_cols(chunks, order, inverse):
    count, step = chunks.shape[:2]
    length = count * step
    grid_spec = pltpu.PrefetchScalarGridSpec(
        num_scalar_prefetch=1,
        grid=(count,),
        in_specs=[
            pl.BlockSpec((1, step, TOTAL), lambda i, order: (order[i], 0, 0)),
            pl.BlockSpec((TOTAL, TOTAL), lambda i, order: (0, 0)),
        ],
        out_specs=[
            pl.BlockSpec((TOTAL, step), lambda i, order: (0, i)),
            pl.BlockSpec((3 * TOTAL, step), lambda i, order: (0, i)),
        ],
    )
    return pl.pallas_call(
        cols_kernel,
        grid_spec=grid_spec,
        out_shape=[
            jax.ShapeDtypeStruct((TOTAL, length), jnp.float32),
            jax.ShapeDtypeStruct((3 * TOTAL, length), jnp.bfloat16),
        ],
        compiler_params=pltpu.CompilerParams(vmem_limit_bytes=24 * MIB),
    )(order, chunks, inverse)


def final_kernel(
    cols_blocks, runs, code_ref, run_ref, place_ref, front_ref, rows_ref, rows_parts, cols_ref, cols_parts,
    lower_ref, arrived_ref, out_ref, cursor
):
    step = pl.program_id(0)
    sources, capacity = code_ref.shape
    height, width = front_ref.shape
    unit, side = arrived_ref.shape[2:]
    per_step = height // unit

    @pl.when(step == 0)
    def _():
        for s in range(sources):
            cursor[s] = 0

    chunk = min(512, width)
    for start in range(0, width, chunk):
        at = slice(start, start + chunk)
        change = jnp.dot(rows_parts[...], cols_parts[:, at], preferred_element_type=jnp.float32)
        out_ref[:, at] = front_ref[:, at] - change

    edge = (step + 1) * per_step * cols_blocks

    @pl.loop(0, sources)
    def _(s):
        def more(k):
            code = code_ref[s, jnp.minimum(k, capacity - 1)]
            return (k < capacity) & (code >= 0) & (code < edge)

        def add(k):
            code = code_ref[s, k]
            length = run_ref[s, k]
            unit_row = code // cols_blocks - step * per_step
            columns = pl.ds(pl.multiple_of(code % cols_blocks * side, side), side)
            for run in runs:
                skipped = length // (2 * run) * (2 * run)

                @pl.when(length // run % 2 == 1)
                def _():
                    rows = pl.ds(pl.multiple_of((unit_row + skipped) * unit, unit), run * unit)
                    block = arrived_ref[s, pl.ds(k + skipped, run)]
                    out_ref[rows, columns] += block.reshape(run * unit, side)

            return k + length

        cursor[s] = lax.while_loop(more, add, cursor[s])

    top = (place_ref[0] == 0) & (step == 0)

    @pl.when(top)
    def _():
        out_ref[...] = cols_ref[...]

    @pl.when(place_ref[1] == 0)
    def _():
        out_ref[:, :TOTAL] = jnp.where(top, lower_ref[...], rows_ref[...])


def finish(front, rows, cols, lower, arrived, codes, lengths, place, cols_blocks):
    row_len, col_len = front.shape
    height = TOTAL
    smem = pl.BlockSpec(memory_space=pltpu.SMEM)
    block = pl.BlockSpec((height, TOTAL), lambda i: (i, 0))
    parts = pl.BlockSpec((height, 3 * TOTAL), lambda i: (i, 0))
    wide = pl.BlockSpec((height, col_len), lambda i: (i, 0))
    whole = pl.BlockSpec((TOTAL, col_len), lambda i: (0, 0))
    whole_parts = pl.BlockSpec((3 * TOTAL, col_len), lambda i: (0, 0))
    runs = (16, 8, 4, 2, 1) if arrived.shape[2] == UNIT else (1,)
    return pl.pallas_call(
        functools.partial(final_kernel, cols_blocks, runs),
        grid=(row_len // height,),
        out_shape=jax.ShapeDtypeStruct((row_len, col_len), jnp.float32),
        in_specs=[
            smem, smem, smem, wide, block, parts, whole, whole_parts,
            pl.BlockSpec((TOTAL, TOTAL), lambda i: (0, 0)),
            pl.BlockSpec(memory_space=pltpu.VMEM),
        ],
        out_specs=wide,
        scratch_shapes=[pltpu.SMEM((codes.shape[0],), jnp.int32)],
        compiler_params=pltpu.CompilerParams(vmem_limit_bytes=56 * MIB),
    )(codes, lengths, place, front, *rows, *cols, lower, arrived)


def factor(diagonal):
    def lower_of(block):
        return jnp.linalg.cholesky(jnp.tril(block) + jnp.tril(block, -1).T)

    def inverse_of(block):
        return jax.scipy.linalg.solve_triangular(block, jnp.eye(NB, dtype=jnp.float32), lower=True)

    first = lower_of(diagonal[:NB, :NB])
    first_inverse = inverse_of(first)
    below = dot_nt(diagonal[NB:, :NB], first_inverse)
    second = lower_of(diagonal[NB:, NB:] - dot_nt(below, below))
    second_inverse = inverse_of(second)
    corner = -jnp.dot(second_inverse, jnp.dot(below, first_inverse, precision=precise), precision=precise)
    zero = jnp.zeros((NB, NB), jnp.float32)
    return jnp.block([[first, zero], [below, second]]), jnp.block([[first_inverse, zero], [corner, second_inverse]])


def body(front, tiles, tile_block, valid_rows):
    row_len, col_len = front.shape
    row_count = lax.axis_size("row")
    col_count = lax.axis_size("col")
    device_count = row_count * col_count
    per_device = tiles.shape[0]
    side = tiles.shape[1]
    capacity = 2 * per_device // device_count
    rows_blocks = row_len // side
    cols_blocks = col_len // side
    row_now = lax.axis_index("row")
    col_now = lax.axis_index("col")
    device_now = row_now * col_count + col_now

    block_row = tile_block[0].reshape(device_count, per_device)
    block_col = tile_block[1].reshape(device_count, per_device)
    target_row = block_row // rows_blocks
    target = target_row * col_count + block_col // cols_blocks
    code = block_row % rows_blocks * cols_blocks + block_col % cols_blocks
    position = lax.broadcasted_iota(jnp.int32, target.shape, 1)
    place = jnp.stack([row_now, col_now]).astype(jnp.int32)

    def own(values):
        return lax.dynamic_index_in_dim(values, device_now, 0, keepdims=False)

    in_panel = block_col < PANELS
    panel_key = jnp.where(in_panel, target_row, -1)
    panel_rank = jnp.sum(
        (panel_key[:, :, None] == panel_key[:, None, :]) & (position[:, None, :] < position[:, :, None]),
        axis=2,
    )
    same_col = lax.dynamic_index_in_dim(
        jnp.stack([panel_key, panel_rank, code]).reshape(3, row_count, col_count, per_device),
        col_now, 2, keepdims=False,
    )

    def send_panel(tiles, valid_rows, depth):
        ahead = (own(target_row) - row_now) % row_count
        fits = own(in_panel) & (own(panel_rank) < depth)
        panel_slot = jnp.where(fits, ahead * depth + own(panel_rank), -1)
        panel_out = pack(tiles, panel_slot, valid_rows, row_count * depth)
        panel_in = [panel_out[:depth]]
        for shift in range(1, row_count):
            sending = panel_out[shift * depth : (shift + 1) * depth]
            turn = [(r, (r + shift) % row_count) for r in range(row_count)]
            panel_in.append(lax.ppermute(sending, "row", turn))
        return panel_in

    def sum_panel(front, panel_in, depth):
        fits = (same_col[0] == row_now)[:, :, None] & (same_col[1][:, :, None] == jnp.arange(depth))
        panel_code = same_col[2] // cols_blocks * PANELS + same_col[2] % cols_blocks
        panel_codes = jnp.sum(jnp.where(fits, panel_code[:, :, None] + 1, 0), axis=1) - 1
        by_shift = (row_now - jnp.arange(row_count)) % row_count
        panel_codes = jnp.take(panel_codes, by_shift, axis=0).reshape(-1)
        first = (col_now == 0).astype(jnp.int32).reshape(1)
        return raw_panel(front, jnp.concatenate(panel_in, 0), panel_codes, first)

    def gather_panel(partial):
        chunk = lax.psum_scatter(partial, "col", scatter_dimension=0, tiled=True)
        raw_rows = lax.all_gather(chunk, "col", axis=0, tiled=True)
        chunk, raw_rows = lax.optimization_barrier((chunk, raw_rows))
        return lax.all_gather(chunk, "row", axis=0), raw_rows

    panel_depth = (capacity * 5 + 7) // 8
    panel_in = send_panel(tiles, valid_rows, panel_depth)

    units = side // UNIT
    length = capacity * units
    width = length * 41 // 64
    pass_on = length * 13 // 32
    half_count = device_count // 2
    half_base = device_now // half_count * half_count
    unit_rows = rows_blocks * units
    local_codes = unit_rows * cols_blocks
    own_target, own_code = own(target), own(code)
    own_position = own(position)
    filled = (valid_rows + UNIT - 1) // UNIT
    key = (own_target * rows_blocks * cols_blocks + own_code) * per_device + own_position
    before = key[None, :] < key[:, None]
    together = own_target[None, :] == own_target[:, None]
    base = jnp.sum(jnp.where(before & together, filled[None, :], 0), axis=1)
    order = jnp.sum(before, axis=1)
    unit_code = (own_target * unit_rows + own_code // cols_blocks * units) * cols_blocks
    unit_code += own_code % cols_blocks
    meta = jnp.stack([own_position, own_target, base, filled, unit_code, valid_rows])
    meta = jnp.sum(
        jnp.where(order[None, :, None] == jnp.arange(per_device), meta[:, :, None], 0), axis=1
    )
    to_device = own_target[:, None] == jnp.arange(device_count)
    load = jnp.sum(jnp.where(to_device, filled[:, None], 0), axis=0).reshape(2, half_count)
    empty = load == 0
    empty_rank = jnp.cumsum(empty, axis=1) - 1
    device_ids = jnp.arange(device_count).reshape(2, half_count)
    listed = (empty[:, :, None]) & (empty_rank[:, :, None] == jnp.arange(half_count))
    empties = jnp.sum(jnp.where(listed, device_ids[:, :, None], 0), axis=1)
    free = jnp.sum(empty, axis=1)
    left = jnp.sum(jnp.maximum(load - width, 0), axis=1)
    failed = jnp.any(left > free * width) | jnp.any(own(in_panel) & (own(panel_rank) >= panel_depth))
    counts = jnp.concatenate([jnp.sum(own_target < half_count)[None], free]).astype(jnp.int32)
    outgoing, sent_codes = spread(
        tiles, meta.astype(jnp.int32), empties.astype(jnp.int32), counts,
        device_count, width, length, cols_blocks,
    )

    partial = sum_panel(front, panel_in, panel_depth)
    partial, sent_codes = lax.optimization_barrier((partial, sent_codes))
    gathered, raw_rows = gather_panel(partial)
    got = lax.all_to_all(sent_codes[:, :width], ("row", "col"), 0, 0, tiled=True)
    outgoing, got = lax.optimization_barrier((outgoing, got))
    arrived = lax.all_to_all(outgoing, ("row", "col"), 0, 0, tiled=True)
    got_target = got // local_codes
    local = got % local_codes
    mine = (got >= 0) & (got_target == device_now)
    direct_codes = jnp.where(mine, local, -1)
    steps = jnp.arange(width)
    opening = (local // cols_blocks % units == 0) | jnp.logical_not(mine)
    later = (steps[None, :] > steps[:, None]) & opening[:, None, :]
    direct_runs = jnp.min(jnp.where(later, steps, width), axis=2) - steps
    total_units = device_count * width
    passing = ((got >= 0) & (got_target != device_now)).reshape(-1)
    flat_key = jnp.where(passing, got.reshape(-1) * total_units + jnp.arange(total_units), -1)
    flat_target = jnp.where(passing, got_target.reshape(-1), -1)
    rank = jnp.sum(
        (flat_target[None, :] == flat_target[:, None]) & (flat_key[None, :] < flat_key[:, None]), axis=1
    )
    failed = failed | jnp.any(passing & (rank >= pass_on))
    relay_slot = jnp.where(
        passing & (rank < pass_on), (flat_target - half_base) * pass_on + rank, -1
    )
    picked = relay_slot[:, None] == jnp.arange(half_count * pass_on)
    relay_codes = jnp.sum(jnp.where(picked, local.reshape(-1)[:, None] + 1, 0), axis=0) - 1
    notes = jnp.zeros((2, half_count, pass_on + 1), jnp.int32)
    notes = lax.dynamic_update_slice(
        notes, relay_codes.reshape(1, half_count, pass_on).astype(jnp.int32), (device_now // half_count, 0, 0)
    )
    notes = notes.at[:, :, pass_on].set(failed.astype(jnp.int32))
    notes, arrived = lax.optimization_barrier((notes, arrived))
    notes = lax.all_to_all(
        notes.reshape(device_count, pass_on + 1), ("row", "col"), 0, 0, tiled=True
    )
    too_full = jnp.any(notes[:, pass_on] != 0)
    relay_codes = lax.dynamic_slice_in_dim(notes, half_base, half_count, 0)[:, :pass_on]
    relay_slot = relay_slot.reshape(device_count, width)

    flat = relay_codes.reshape(-1)
    unit_row, relay_col = flat // cols_blocks, flat % cols_blocks
    wanted = (flat >= 0) & ((row_now > 0) | (unit_row >= TOTAL // UNIT))
    wanted &= (col_now > 0) | (relay_col >= PANELS)
    relay_block = unit_row // units * cols_blocks + relay_col
    relay_key = jnp.where(wanted, relay_block * units + unit_row % units, local_codes)
    relay_key = relay_key * flat.shape[0] + jnp.arange(flat.shape[0])
    relay_order = jnp.sum(relay_key[None, :] < relay_key[:, None], axis=1)
    listing = jnp.stack([relay_block, unit_row % units, jnp.arange(flat.shape[0])])
    at_order = relay_order[None, :, None] == jnp.arange(flat.shape[0])
    listing = jnp.sum(jnp.where(at_order, listing[:, :, None], 0), axis=1).astype(jnp.int32)
    listing = [*listing, jnp.sum(wanted).astype(jnp.int32).reshape(1)]

    passed = relay(relay_slot, arrived, half_count * pass_on)
    def chain(gathered, raw_rows, arrived):
        diagonal = jnp.where(row_now == 0, raw_rows[:TOTAL], jnp.eye(TOTAL, dtype=jnp.float32))
        lower, inverse = factor(diagonal)
        known = jnp.where(row_now == 0, inverse, 0.0)
        gathered, known, arrived = lax.optimization_barrier((gathered, known, arrived))
        share = col_count // row_count
        chunks = []
        for turn in range(row_count):
            pairs = [
                (h * row_count + i, (i + turn) % row_count * share + h)
                for h in range(share)
                for i in range(row_count)
            ]
            sending = lax.dynamic_index_in_dim(gathered, (col_now + turn) % row_count, 0, keepdims=False)
            chunks.append(lax.ppermute(sending, "col", pairs))
        order = (col_now // share - jnp.arange(row_count)) % row_count
        inverse = known
        for other in range(1, row_count):
            inverse += lax.ppermute(known, "row", [(0, other)])
        rows = solve_rows(raw_rows, inverse)
        cols = solve_cols(jnp.stack(chunks), order.astype(jnp.int32), inverse)
        return rows, cols, lower

    tables = (direct_codes, direct_runs, listing)
    rows, cols, lower = chain(gathered, raw_rows, arrived)
    rows, cols, lower, passed, tables = lax.optimization_barrier((rows, cols, lower, passed, tables))
    direct_codes, direct_runs, listing = tables

    def relayed(front, tiles, valid_rows, arrived, passed, rows, cols, lower):
        halves = [list(range(half_count)), list(range(half_count, device_count))]
        passed = lax.all_to_all(
            passed.reshape(half_count, pass_on, UNIT, side), ("row", "col"), 0, 0,
            axis_index_groups=halves, tiled=True,
        )
        partial = finish(
            front, rows, cols, lower, arrived, direct_codes, direct_runs, place, cols_blocks
        )
        return add_relayed(partial, passed.reshape(-1, UNIT, side), listing, cols_blocks)

    def padded(front, tiles, valid_rows, arrived, passed, rows, cols, lower):
        partial = sum_panel(front, send_panel(tiles, valid_rows, capacity), capacity)
        gathered, raw_rows = gather_panel(partial)
        order = (target * rows_blocks * cols_blocks + code) * per_device + position
        ranking = jnp.sum(
            (target[:, :, None] == target[:, None, :]) & (order[:, None, :] < order[:, :, None]), axis=2
        )
        slot = own(target) * capacity + own(ranking)
        here = (target == device_now)[:, :, None] & (ranking[:, :, None] == jnp.arange(capacity))
        codes = jnp.sum(jnp.where(here, code[:, :, None] + 1, 0), axis=1) - 1
        packed = pack(tiles, slot, valid_rows, device_count * capacity)
        arrived = lax.all_to_all(
            packed.reshape(device_count, capacity, side, side), ("row", "col"), 0, 0, tiled=True
        )
        rows, cols, lower = chain(gathered, raw_rows, arrived)
        return finish(
            front, rows, cols, lower, arrived, codes, jnp.ones_like(codes), place, cols_blocks
        )

    return lax.cond(
        too_full, padded, relayed, front, tiles, valid_rows, arrived, passed, rows, cols, lower
    )


def solution(mesh):
    placed = (P("row", "col"), P(("row", "col"), None, None), P(), P(("row", "col")))
    return jax.shard_map(
        body, mesh=mesh, in_specs=placed, out_specs=P("row", "col"), check_vma=False
    )
```

```python
import functools

import jax
import jax.numpy as jnp
from jax import lax
from jax.experimental import pallas as pl
from jax.experimental.pallas import tpu as pltpu
from jax.sharding import PartitionSpec as P

NB = 128
PANELS = 2
TOTAL = NB * PANELS
MIB = 1 << 20
UNIT = 8


precise = lax.Precision.HIGHEST


def dot_nt(a, b, precision=precise):
    return lax.dot_general(
        a, b, (((1,), (1,)), ((), ())), precision=precision, preferred_element_type=jnp.float32
    )


def pack_kernel(slot_ref, valid_ref, tiles_ref, out_ref, buf, sem_in, sem_out):
    count, side = tiles_ref.shape[0], tiles_ref.shape[1]

    def fetch(t):
        return pltpu.make_async_copy(tiles_ref.at[t], buf.at[t], sem_in.at[t])

    def store(t):
        return pltpu.make_async_copy(buf.at[t], out_ref.at[jnp.maximum(slot_ref[t], 0)], sem_out.at[t])

    def each(act):
        @pl.loop(0, count)
        def _(t):
            @pl.when(slot_ref[t] >= 0)
            def _():
                act(t)

    def mask(t):
        fetch(t).wait()
        rows = lax.broadcasted_iota(jnp.int32, (side, side), 0)
        buf[t] = jnp.where(rows < valid_ref[t], buf[t], 0.0)
        store(t).start()

    each(lambda t: fetch(t).start())
    each(mask)
    each(lambda t: store(t).wait())


def pack(tiles, slots, valid, n_slots):
    count, side = tiles.shape[0], tiles.shape[1]
    smem = pl.BlockSpec(memory_space=pltpu.SMEM)
    return pl.pallas_call(
        pack_kernel,
        out_shape=jax.ShapeDtypeStruct((n_slots, side, side), jnp.float32),
        in_specs=[smem, smem, pl.BlockSpec(memory_space=pl.ANY)],
        out_specs=pl.BlockSpec(memory_space=pl.ANY),
        scratch_shapes=[
            pltpu.VMEM((count, side, side), jnp.float32),
            pltpu.SemaphoreType.DMA((count,)),
            pltpu.SemaphoreType.DMA((count,)),
        ],
        compiler_params=pltpu.CompilerParams(vmem_limit_bytes=24 * MIB),
    )(slots, valid, tiles)


def spread_kernel(
    width, stride, meta_ref, empty_ref, count_ref, tiles_ref, out_ref, code_ref, stage, sem
):
    count, units = tiles_ref.shape[0], tiles_ref.shape[1]
    devices, length = code_ref.shape

    @pl.loop(0, devices)
    def _(d):
        for k in range(length):
            code_ref[d, k] = -1

    @pl.loop(0, count)
    def _(i):
        tile, target, base = meta_ref[0, i], meta_ref[1, i], meta_ref[2, i]
        filled, code, valid = meta_ref[3, i], meta_ref[4, i], meta_ref[5, i]
        shape = tiles_ref.shape[1:]
        rows = lax.broadcasted_iota(jnp.int32, shape, 0) * shape[1]
        rows += lax.broadcasted_iota(jnp.int32, shape, 1)
        stage[target, pl.ds(base, units)] = jnp.where(rows < valid, tiles_ref[tile], 0.0)
        for u in range(units):
            code_ref[target, base + u] = jnp.where(u < filled, code + u * stride, -1)

    for half in range(2):
        first = 0 if half == 0 else count_ref[0]
        last = count_ref[0] if half == 0 else count
        free = count_ref[1 + half]

        def each_tile(i, carry):
            target, base, filled = meta_ref[1, i], meta_ref[2, i], meta_ref[3, i]

            def each_unit(q, carry):
                at, depth = carry
                relay = empty_ref[half, at]
                place = jnp.minimum(depth, width - 1)
                stage[relay, place] = stage[target, q]
                code_ref[relay, place] = code_ref[target, q]
                wrap = at + 1 >= free
                return jnp.where(wrap, 0, at + 1), jnp.where(wrap, depth + 1, depth)

            return lax.fori_loop(jnp.maximum(base, width), base + filled, each_unit, carry)

        lax.fori_loop(first, last, each_tile, (jnp.int32(0), jnp.int32(0)))

    copy = pltpu.make_async_copy(stage.at[:, pl.ds(0, width)], out_ref, sem)
    copy.start()
    copy.wait()


def spread(tiles, meta, empties, counts, devices, width, length, stride):
    count, side = tiles.shape[0], tiles.shape[1]
    units = side // UNIT
    smem = pl.BlockSpec(memory_space=pltpu.SMEM)
    return pl.pallas_call(
        functools.partial(spread_kernel, width, stride),
        out_shape=[
            jax.ShapeDtypeStruct((devices, width, UNIT, side), jnp.float32),
            jax.ShapeDtypeStruct((devices, length), jnp.int32),
        ],
        in_specs=[smem, smem, smem, pl.BlockSpec(memory_space=pltpu.VMEM)],
        out_specs=[pl.BlockSpec(memory_space=pl.ANY), smem],
        scratch_shapes=[
            pltpu.VMEM((devices, length, UNIT, side), jnp.float32),
            pltpu.SemaphoreType.DMA,
        ],
        compiler_params=pltpu.CompilerParams(vmem_limit_bytes=40 * MIB),
    )(meta, empties, counts, tiles.reshape(count, units, UNIT, side))


def relay_kernel(slot_ref, arrived_ref, out_ref):
    devices, width = slot_ref.shape

    @pl.loop(0, devices)
    def _(s):
        def more(k):
            return (k < width) & (slot_ref[s, jnp.minimum(k, width - 1)] >= 0)

        def move(k):
            out_ref[slot_ref[s, k]] = arrived_ref[s, k]
            return k + 1

        lax.while_loop(more, move, jnp.int32(0))


def relay(slots, arrived, length):
    vmem = pl.BlockSpec(memory_space=pltpu.VMEM)
    return pl.pallas_call(
        relay_kernel,
        out_shape=jax.ShapeDtypeStruct((length,) + arrived.shape[2:], jnp.float32),
        in_specs=[pl.BlockSpec(memory_space=pltpu.SMEM), vmem],
        out_specs=vmem,
        compiler_params=pltpu.CompilerParams(vmem_limit_bytes=40 * MIB),
    )(slots, arrived)


def add_kernel(
    cols_blocks, block_ref, unit_ref, index_ref, count_ref, partial_ref, arrived_ref, out_ref, buf,
    group_start, sem_in, sem_out
):
    slots, side = buf.shape[0], buf.shape[1]
    unit = arrived_ref.shape[1]
    ahead = slots // 2
    count = count_ref[0]

    def listed(i, carry):
        groups, last = carry
        block = block_ref[i]
        fresh = block != last

        @pl.when(fresh)
        def _():
            group_start[groups] = i

        return jnp.where(fresh, groups + 1, groups), block

    groups, _ = lax.fori_loop(0, count, listed, (jnp.int32(0), jnp.int32(-1)))
    group_start[groups] = count

    def window(g):
        block = block_ref[group_start[g]]
        rows = pl.ds(pl.multiple_of(block // cols_blocks * side, side), side)
        columns = pl.ds(pl.multiple_of(block % cols_blocks * side, side), side)
        return out_ref.at[rows, columns]

    def fetch(g):
        at = g % slots
        return pltpu.make_async_copy(window(g), buf.at[at], sem_in.at[at])

    def store(g):
        at = g % slots
        return pltpu.make_async_copy(buf.at[at], window(g), sem_out.at[at])

    @pl.loop(0, jnp.minimum(groups, ahead))
    def _(g):
        fetch(g).start()

    @pl.loop(0, groups)
    def _(g):
        @pl.when(g + ahead < groups)
        def _():
            @pl.when(g >= ahead)
            def _():
                store(g - ahead).wait()

            fetch(g + ahead).start()

        fetch(g).wait()

        @pl.loop(group_start[g], group_start[g + 1])
        def _(i):
            rows = pl.ds(pl.multiple_of(unit_ref[i] * unit, unit), unit)
            buf[g % slots, rows] += arrived_ref[index_ref[i]]

        store(g).start()

    @pl.loop(jnp.maximum(groups - slots, 0), groups)
    def _(g):
        store(g).wait()


def add_relayed(partial, arrived, listing, cols_blocks):
    row_len, col_len = partial.shape
    unit, side = arrived.shape[1:]
    smem = pl.BlockSpec(memory_space=pltpu.SMEM)
    hbm = pl.BlockSpec(memory_space=pl.ANY)
    return pl.pallas_call(
        functools.partial(add_kernel, cols_blocks),
        out_shape=jax.ShapeDtypeStruct((row_len, col_len), jnp.float32),
        in_specs=[smem, smem, smem, smem, hbm, pl.BlockSpec(memory_space=pltpu.VMEM)],
        out_specs=hbm,
        scratch_shapes=[
            pltpu.VMEM((16, side, side), jnp.float32),
            pltpu.SMEM((arrived.shape[0] + 1,), jnp.int32),
            pltpu.SemaphoreType.DMA((16,)),
            pltpu.SemaphoreType.DMA((16,)),
        ],
        input_output_aliases={4: 0},
        compiler_params=pltpu.CompilerParams(vmem_limit_bytes=24 * MIB),
    )(*listing, partial, arrived)


def panel_kernel(code_ref, first_ref, front_ref, arrived_ref, out_ref):
    side = arrived_ref.shape[1]

    @pl.when(first_ref[0] == 1)
    def _():
        out_ref[...] = front_ref[...]

    @pl.when(first_ref[0] == 0)
    def _():
        out_ref[...] = jnp.zeros_like(out_ref)

    @pl.loop(0, arrived_ref.shape[0])
    def _(k):
        code = code_ref[k]
        for part in range(PANELS):

            @pl.when((code >= 0) & (code % PANELS == part))
            def _():
                rows = pl.ds(pl.multiple_of(code // PANELS * side, side), side)
                out_ref[rows, part * side : (part + 1) * side] += arrived_ref[k]


def raw_panel(front, arrived, codes, first):
    row_len = front.shape[0]
    smem = pl.BlockSpec(memory_space=pltpu.SMEM)
    return pl.pallas_call(
        panel_kernel,
        grid=(1,),
        out_shape=jax.ShapeDtypeStruct((row_len, TOTAL), jnp.float32),
        in_specs=[
            smem,
            smem,
            pl.BlockSpec((row_len, TOTAL), lambda i: (0, 0)),
            pl.BlockSpec(arrived.shape, lambda i: (0, 0, 0)),
        ],
        out_specs=pl.BlockSpec((row_len, TOTAL), lambda i: (0, 0)),
        compiler_params=pltpu.CompilerParams(vmem_limit_bytes=40 * MIB),
    )(codes, first, front, arrived)


def split(value):
    high = value.astype(jnp.bfloat16)
    low = (value - high.astype(jnp.float32)).astype(jnp.bfloat16)
    return high, low


def rows_kernel(raw_ref, inverse_ref, out_ref, parts_ref):
    solved = dot_nt(raw_ref[...], inverse_ref[...])
    out_ref[...] = solved
    high, low = split(solved)
    parts_ref[:, :TOTAL] = high
    parts_ref[:, TOTAL : 2 * TOTAL] = high
    parts_ref[:, 2 * TOTAL :] = low


def solve_rows(raw, inverse):
    length = raw.shape[0]
    step = min(512, length)
    block = pl.BlockSpec((step, TOTAL), lambda i: (i, 0))
    return pl.pallas_call(
        rows_kernel,
        grid=(length // step,),
        out_shape=[
            jax.ShapeDtypeStruct((length, TOTAL), jnp.float32),
            jax.ShapeDtypeStruct((length, 3 * TOTAL), jnp.bfloat16),
        ],
        in_specs=[block, pl.BlockSpec((TOTAL, TOTAL), lambda i: (0, 0))],
        out_specs=[block, pl.BlockSpec((step, 3 * TOTAL), lambda i: (i, 0))],
        compiler_params=pltpu.CompilerParams(vmem_limit_bytes=24 * MIB),
    )(raw, inverse)


def cols_kernel(order_ref, raw_ref, inverse_ref, out_ref, parts_ref):
    solved = dot_nt(inverse_ref[...], raw_ref[0])
    out_ref[...] = solved
    high, low = split(solved)
    parts_ref[:TOTAL] = high
    parts_ref[TOTAL : 2 * TOTAL] = low
    parts_ref[2 * TOTAL :] = high


def solve_cols(chunks, order, inverse):
    count, step = chunks.shape[:2]
    length = count * step
    grid_spec = pltpu.PrefetchScalarGridSpec(
        num_scalar_prefetch=1,
        grid=(count,),
        in_specs=[
            pl.BlockSpec((1, step, TOTAL), lambda i, order: (order[i], 0, 0)),
            pl.BlockSpec((TOTAL, TOTAL), lambda i, order: (0, 0)),
        ],
        out_specs=[
            pl.BlockSpec((TOTAL, step), lambda i, order: (0, i)),
            pl.BlockSpec((3 * TOTAL, step), lambda i, order: (0, i)),
        ],
    )
    return pl.pallas_call(
        cols_kernel,
        grid_spec=grid_spec,
        out_shape=[
            jax.ShapeDtypeStruct((TOTAL, length), jnp.float32),
            jax.ShapeDtypeStruct((3 * TOTAL, length), jnp.bfloat16),
        ],
        compiler_params=pltpu.CompilerParams(vmem_limit_bytes=24 * MIB),
    )(order, chunks, inverse)


def final_kernel(
    cols_blocks, runs, code_ref, run_ref, place_ref, front_ref, rows_ref, rows_parts, cols_ref, cols_parts,
    lower_ref, arrived_ref, out_ref, cursor
):
    step = pl.program_id(0)
    sources, capacity = code_ref.shape
    height, width = front_ref.shape
    unit, side = arrived_ref.shape[2:]
    per_step = height // unit

    @pl.when(step == 0)
    def _():
        for s in range(sources):
            cursor[s] = 0

    chunk = min(512, width)
    for start in range(0, width, chunk):
        at = slice(start, start + chunk)
        change = jnp.dot(rows_parts[...], cols_parts[:, at], preferred_element_type=jnp.float32)
        out_ref[:, at] = front_ref[:, at] - change

    edge = (step + 1) * per_step * cols_blocks

    @pl.loop(0, sources)
    def _(s):
        def more(k):
            code = code_ref[s, jnp.minimum(k, capacity - 1)]
            return (k < capacity) & (code >= 0) & (code < edge)

        def add(k):
            code = code_ref[s, k]
            length = run_ref[s, k]
            unit_row = code // cols_blocks - step * per_step
            columns = pl.ds(pl.multiple_of(code % cols_blocks * side, side), side)
            for run in runs:
                skipped = length // (2 * run) * (2 * run)

                @pl.when(length // run % 2 == 1)
                def _():
                    rows = pl.ds(pl.multiple_of((unit_row + skipped) * unit, unit), run * unit)
                    block = arrived_ref[s, pl.ds(k + skipped, run)]
                    out_ref[rows, columns] += block.reshape(run * unit, side)

            return k + length

        cursor[s] = lax.while_loop(more, add, cursor[s])

    top = (place_ref[0] == 0) & (step == 0)

    @pl.when(top)
    def _():
        out_ref[...] = cols_ref[...]

    @pl.when(place_ref[1] == 0)
    def _():
        out_ref[:, :TOTAL] = jnp.where(top, lower_ref[...], rows_ref[...])


def finish(front, rows, cols, lower, arrived, codes, lengths, place, cols_blocks):
    row_len, col_len = front.shape
    height = TOTAL
    smem = pl.BlockSpec(memory_space=pltpu.SMEM)
    block = pl.BlockSpec((height, TOTAL), lambda i: (i, 0))
    parts = pl.BlockSpec((height, 3 * TOTAL), lambda i: (i, 0))
    wide = pl.BlockSpec((height, col_len), lambda i: (i, 0))
    whole = pl.BlockSpec((TOTAL, col_len), lambda i: (0, 0))
    whole_parts = pl.BlockSpec((3 * TOTAL, col_len), lambda i: (0, 0))
    runs = (16, 8, 4, 2, 1) if arrived.shape[2] == UNIT else (1,)
    return pl.pallas_call(
        functools.partial(final_kernel, cols_blocks, runs),
        grid=(row_len // height,),
        out_shape=jax.ShapeDtypeStruct((row_len, col_len), jnp.float32),
        in_specs=[
            smem, smem, smem, wide, block, parts, whole, whole_parts,
            pl.BlockSpec((TOTAL, TOTAL), lambda i: (0, 0)),
            pl.BlockSpec(memory_space=pltpu.VMEM),
        ],
        out_specs=wide,
        scratch_shapes=[pltpu.SMEM((codes.shape[0],), jnp.int32)],
        compiler_params=pltpu.CompilerParams(vmem_limit_bytes=56 * MIB),
    )(codes, lengths, place, front, *rows, *cols, lower, arrived)


def factor(diagonal):
    def lower_of(block):
        return jnp.linalg.cholesky(jnp.tril(block) + jnp.tril(block, -1).T)

    def inverse_of(block):
        return jax.scipy.linalg.solve_triangular(block, jnp.eye(NB, dtype=jnp.float32), lower=True)

    first = lower_of(diagonal[:NB, :NB])
    first_inverse = inverse_of(first)
    below = dot_nt(diagonal[NB:, :NB], first_inverse)
    second = lower_of(diagonal[NB:, NB:] - dot_nt(below, below))
    second_inverse = inverse_of(second)
    corner = -jnp.dot(second_inverse, jnp.dot(below, first_inverse, precision=precise), precision=precise)
    zero = jnp.zeros((NB, NB), jnp.float32)
    return jnp.block([[first, zero], [below, second]]), jnp.block([[first_inverse, zero], [corner, second_inverse]])


def body(front, tiles, tile_block, valid_rows):
    row_len, col_len = front.shape
    row_count = lax.axis_size("row")
    col_count = lax.axis_size("col")
    device_count = row_count * col_count
    per_device = tiles.shape[0]
    side = tiles.shape[1]
    capacity = 2 * per_device // device_count
    rows_blocks = row_len // side
    cols_blocks = col_len // side
    row_now = lax.axis_index("row")
    col_now = lax.axis_index("col")
    device_now = row_now * col_count + col_now

    block_row = tile_block[0].reshape(device_count, per_device)
    block_col = tile_block[1].reshape(device_count, per_device)
    target_row = block_row // rows_blocks
    target = target_row * col_count + block_col // cols_blocks
    code = block_row % rows_blocks * cols_blocks + block_col % cols_blocks
    position = lax.broadcasted_iota(jnp.int32, target.shape, 1)
    place = jnp.stack([row_now, col_now]).astype(jnp.int32)

    def own(values):
        return lax.dynamic_index_in_dim(values, device_now, 0, keepdims=False)

    in_panel = block_col < PANELS
    panel_key = jnp.where(in_panel, target_row, -1)
    panel_rank = jnp.sum(
        (panel_key[:, :, None] == panel_key[:, None, :]) & (position[:, None, :] < position[:, :, None]),
        axis=2,
    )
    same_col = lax.dynamic_index_in_dim(
        jnp.stack([panel_key, panel_rank, code]).reshape(3, row_count, col_count, per_device),
        col_now, 2, keepdims=False,
    )

    def send_panel(tiles, valid_rows, depth):
        ahead = (own(target_row) - row_now) % row_count
        fits = own(in_panel) & (own(panel_rank) < depth)
        panel_slot = jnp.where(fits, ahead * depth + own(panel_rank), -1)
        panel_out = pack(tiles, panel_slot, valid_rows, row_count * depth)
        panel_in = [panel_out[:depth]]
        for shift in range(1, row_count):
            sending = panel_out[shift * depth : (shift + 1) * depth]
            turn = [(r, (r + shift) % row_count) for r in range(row_count)]
            panel_in.append(lax.ppermute(sending, "row", turn))
        return panel_in

    def sum_panel(front, panel_in, depth):
        fits = (same_col[0] == row_now)[:, :, None] & (same_col[1][:, :, None] == jnp.arange(depth))
        panel_code = same_col[2] // cols_blocks * PANELS + same_col[2] % cols_blocks
        panel_codes = jnp.sum(jnp.where(fits, panel_code[:, :, None] + 1, 0), axis=1) - 1
        by_shift = (row_now - jnp.arange(row_count)) % row_count
        panel_codes = jnp.take(panel_codes, by_shift, axis=0).reshape(-1)
        first = (col_now == 0).astype(jnp.int32).reshape(1)
        return raw_panel(front, jnp.concatenate(panel_in, 0), panel_codes, first)

    def gather_panel(partial):
        chunk = lax.psum_scatter(partial, "col", scatter_dimension=0, tiled=True)
        raw_rows = lax.all_gather(chunk, "col", axis=0, tiled=True)
        chunk, raw_rows = lax.optimization_barrier((chunk, raw_rows))
        return lax.all_gather(chunk, "row", axis=0), raw_rows

    panel_depth = (capacity * 5 + 7) // 8
    panel_in = send_panel(tiles, valid_rows, panel_depth)

    units = side // UNIT
    length = capacity * units
    width = length * 41 // 64
    pass_on = length * 13 // 32
    half_count = device_count // 2
    half_base = device_now // half_count * half_count
    unit_rows = rows_blocks * units
    local_codes = unit_rows * cols_blocks
    own_target, own_code = own(target), own(code)
    own_position = own(position)
    filled = (valid_rows + UNIT - 1) // UNIT
    key = (own_target * rows_blocks * cols_blocks + own_code) * per_device + own_position
    before = key[None, :] < key[:, None]
    together = own_target[None, :] == own_target[:, None]
    base = jnp.sum(jnp.where(before & together, filled[None, :], 0), axis=1)
    order = jnp.sum(before, axis=1)
    unit_code = (own_target * unit_rows + own_code // cols_blocks * units) * cols_blocks
    unit_code += own_code % cols_blocks
    meta = jnp.stack([own_position, own_target, base, filled, unit_code, valid_rows])
    meta = jnp.sum(
        jnp.where(order[None, :, None] == jnp.arange(per_device), meta[:, :, None], 0), axis=1
    )
    to_device = own_target[:, None] == jnp.arange(device_count)
    load = jnp.sum(jnp.where(to_device, filled[:, None], 0), axis=0).reshape(2, half_count)
    empty = load == 0
    empty_rank = jnp.cumsum(empty, axis=1) - 1
    device_ids = jnp.arange(device_count).reshape(2, half_count)
    listed = (empty[:, :, None]) & (empty_rank[:, :, None] == jnp.arange(half_count))
    empties = jnp.sum(jnp.where(listed, device_ids[:, :, None], 0), axis=1)
    free = jnp.sum(empty, axis=1)
    left = jnp.sum(jnp.maximum(load - width, 0), axis=1)
    failed = jnp.any(left > free * width) | jnp.any(own(in_panel) & (own(panel_rank) >= panel_depth))
    counts = jnp.concatenate([jnp.sum(own_target < half_count)[None], free]).astype(jnp.int32)
    outgoing, sent_codes = spread(
        tiles, meta.astype(jnp.int32), empties.astype(jnp.int32), counts,
        device_count, width, length, cols_blocks,
    )

    partial = sum_panel(front, panel_in, panel_depth)
    partial, sent_codes = lax.optimization_barrier((partial, sent_codes))
    gathered, raw_rows = gather_panel(partial)
    got = lax.all_to_all(sent_codes[:, :width], ("row", "col"), 0, 0, tiled=True)
    outgoing, got = lax.optimization_barrier((outgoing, got))
    arrived = lax.all_to_all(outgoing, ("row", "col"), 0, 0, tiled=True)
    got_target = got // local_codes
    local = got % local_codes
    mine = (got >= 0) & (got_target == device_now)
    direct_codes = jnp.where(mine, local, -1)
    steps = jnp.arange(width)
    opening = (local // cols_blocks % units == 0) | jnp.logical_not(mine)
    later = (steps[None, :] > steps[:, None]) & opening[:, None, :]
    direct_runs = jnp.min(jnp.where(later, steps, width), axis=2) - steps
    total_units = device_count * width
    passing = ((got >= 0) & (got_target != device_now)).reshape(-1)
    flat_key = jnp.where(passing, got.reshape(-1) * total_units + jnp.arange(total_units), -1)
    flat_target = jnp.where(passing, got_target.reshape(-1), -1)
    rank = jnp.sum(
        (flat_target[None, :] == flat_target[:, None]) & (flat_key[None, :] < flat_key[:, None]), axis=1
    )
    failed = failed | jnp.any(passing & (rank >= pass_on))
    relay_slot = jnp.where(
        passing & (rank < pass_on), (flat_target - half_base) * pass_on + rank, -1
    )
    picked = relay_slot[:, None] == jnp.arange(half_count * pass_on)
    relay_codes = jnp.sum(jnp.where(picked, local.reshape(-1)[:, None] + 1, 0), axis=0) - 1
    notes = jnp.zeros((2, half_count, pass_on + 1), jnp.int32)
    notes = lax.dynamic_update_slice(
        notes, relay_codes.reshape(1, half_count, pass_on).astype(jnp.int32), (device_now // half_count, 0, 0)
    )
    notes = notes.at[:, :, pass_on].set(failed.astype(jnp.int32))
    notes, arrived = lax.optimization_barrier((notes, arrived))
    notes = lax.all_to_all(
        notes.reshape(device_count, pass_on + 1), ("row", "col"), 0, 0, tiled=True
    )
    relay_codes = lax.dynamic_slice_in_dim(notes, half_base, half_count, 0)[:, :pass_on]
    relay_slot = relay_slot.reshape(device_count, width)

    flat = relay_codes.reshape(-1)
    unit_row, relay_col = flat // cols_blocks, flat % cols_blocks
    wanted = (flat >= 0) & ((row_now > 0) | (unit_row >= TOTAL // UNIT))
    wanted &= (col_now > 0) | (relay_col >= PANELS)
    relay_block = unit_row // units * cols_blocks + relay_col
    relay_key = jnp.where(wanted, relay_block * units + unit_row % units, local_codes)
    relay_key = relay_key * flat.shape[0] + jnp.arange(flat.shape[0])
    relay_order = jnp.sum(relay_key[None, :] < relay_key[:, None], axis=1)
    listing = jnp.stack([relay_block, unit_row % units, jnp.arange(flat.shape[0])])
    at_order = relay_order[None, :, None] == jnp.arange(flat.shape[0])
    listing = jnp.sum(jnp.where(at_order, listing[:, :, None], 0), axis=1).astype(jnp.int32)
    listing = [*listing, jnp.sum(wanted).astype(jnp.int32).reshape(1)]

    passed = relay(relay_slot, arrived, half_count * pass_on)
    def chain(gathered, raw_rows):
        diagonal = jnp.where(row_now == 0, raw_rows[:TOTAL], jnp.eye(TOTAL, dtype=jnp.float32))
        lower, inverse = factor(diagonal)
        known = jnp.where(row_now == 0, inverse, 0.0)
        gathered, known = lax.optimization_barrier((gathered, known))
        share = col_count // row_count
        chunks = []
        for turn in range(row_count):
            pairs = [
                (h * row_count + i, (i + turn) % row_count * share + h)
                for h in range(share)
                for i in range(row_count)
            ]
            sending = lax.dynamic_index_in_dim(gathered, (col_now + turn) % row_count, 0, keepdims=False)
            chunks.append(lax.ppermute(sending, "col", pairs))
        order = (col_now // share - jnp.arange(row_count)) % row_count
        inverse = known
        for other in range(1, row_count):
            inverse += lax.ppermute(known, "row", [(0, other)])
        rows = solve_rows(raw_rows, inverse)
        cols = solve_cols(jnp.stack(chunks), order.astype(jnp.int32), inverse)
        return rows, cols, lower

    rows, cols, lower = chain(gathered, raw_rows)
    passed, notes = lax.optimization_barrier((passed, notes))
    too_full = jnp.any(notes[:, pass_on] != 0)
    halves = [list(range(half_count)), list(range(half_count, device_count))]
    passed = lax.all_to_all(
        passed.reshape(half_count, pass_on, UNIT, side), ("row", "col"), 0, 0,
        axis_index_groups=halves, tiled=True,
    )
    partial = finish(front, rows, cols, lower, arrived, direct_codes, direct_runs, place, cols_blocks)
    result = add_relayed(partial, passed.reshape(-1, UNIT, side), listing, cols_blocks)

    def padded():
        partial = sum_panel(front, send_panel(tiles, valid_rows, capacity), capacity)
        gathered, raw_rows = gather_panel(partial)
        order = (target * rows_blocks * cols_blocks + code) * per_device + position
        ranking = jnp.sum(
            (target[:, :, None] == target[:, None, :]) & (order[:, None, :] < order[:, :, None]), axis=2
        )
        slot = own(target) * capacity + own(ranking)
        here = (target == device_now)[:, :, None] & (ranking[:, :, None] == jnp.arange(capacity))
        codes = jnp.sum(jnp.where(here, code[:, :, None] + 1, 0), axis=1) - 1
        packed = pack(tiles, slot, valid_rows, device_count * capacity)
        arrived = lax.all_to_all(
            packed.reshape(device_count, capacity, side, side), ("row", "col"), 0, 0, tiled=True
        )
        rows, cols, lower = chain(gathered, raw_rows)
        return finish(
            front, rows, cols, lower, arrived, codes, jnp.ones_like(codes), place, cols_blocks
        )

    def unfinished(state):
        return state[0] > 0

    def redo(state):
        return jnp.int32(0), padded()

    return lax.while_loop(unfinished, redo, (too_full.astype(jnp.int32), result))[1]


def solution(mesh):
    placed = (P("row", "col"), P(("row", "col"), None, None), P(), P(("row", "col")))
    return jax.shard_map(
        body, mesh=mesh, in_specs=placed, out_specs=P("row", "col"), check_vma=False
    )
```

```python
import functools

import jax
import jax.numpy as jnp
from jax import lax
from jax.experimental import pallas as pl
from jax.experimental.pallas import tpu as pltpu
from jax.sharding import PartitionSpec as P

NB = 128
PANELS = 2
TOTAL = NB * PANELS
MIB = 1 << 20
UNIT = 8


precise = lax.Precision.HIGHEST


def dot_nt(a, b, precision=precise):
    return lax.dot_general(
        a, b, (((1,), (1,)), ((), ())), precision=precision, preferred_element_type=jnp.float32
    )


def pack_kernel(slot_ref, valid_ref, tiles_ref, out_ref, buf, sem_in, sem_out):
    count, side = tiles_ref.shape[0], tiles_ref.shape[1]

    def fetch(t):
        return pltpu.make_async_copy(tiles_ref.at[t], buf.at[t], sem_in.at[t])

    def store(t):
        return pltpu.make_async_copy(buf.at[t], out_ref.at[jnp.maximum(slot_ref[t], 0)], sem_out.at[t])

    def each(act):
        @pl.loop(0, count)
        def _(t):
            @pl.when(slot_ref[t] >= 0)
            def _():
                act(t)

    def mask(t):
        fetch(t).wait()
        rows = lax.broadcasted_iota(jnp.int32, (side, side), 0)
        buf[t] = jnp.where(rows < valid_ref[t], buf[t], 0.0)
        store(t).start()

    each(lambda t: fetch(t).start())
    each(mask)
    each(lambda t: store(t).wait())


def pack(tiles, slots, valid, n_slots):
    count, side = tiles.shape[0], tiles.shape[1]
    smem = pl.BlockSpec(memory_space=pltpu.SMEM)
    return pl.pallas_call(
        pack_kernel,
        out_shape=jax.ShapeDtypeStruct((n_slots, side, side), jnp.float32),
        in_specs=[smem, smem, pl.BlockSpec(memory_space=pl.ANY)],
        out_specs=pl.BlockSpec(memory_space=pl.ANY),
        scratch_shapes=[
            pltpu.VMEM((count, side, side), jnp.float32),
            pltpu.SemaphoreType.DMA((count,)),
            pltpu.SemaphoreType.DMA((count,)),
        ],
        compiler_params=pltpu.CompilerParams(vmem_limit_bytes=24 * MIB),
    )(slots, valid, tiles)


def spread_kernel(
    width, stride, meta_ref, empty_ref, count_ref, tiles_ref, out_ref, code_ref, stage, sem
):
    count, units = tiles_ref.shape[0], tiles_ref.shape[1]
    devices, length = code_ref.shape

    @pl.loop(0, devices)
    def _(d):
        for k in range(length):
            code_ref[d, k] = -1

    @pl.loop(0, count)
    def _(i):
        tile, target, base = meta_ref[0, i], meta_ref[1, i], meta_ref[2, i]
        filled, code, valid = meta_ref[3, i], meta_ref[4, i], meta_ref[5, i]
        shape = tiles_ref.shape[1:]
        rows = lax.broadcasted_iota(jnp.int32, shape, 0) * shape[1]
        rows += lax.broadcasted_iota(jnp.int32, shape, 1)
        stage[target, pl.ds(base, units)] = jnp.where(rows < valid, tiles_ref[tile], 0.0)
        for u in range(units):
            code_ref[target, base + u] = jnp.where(u < filled, code + u * stride, -1)

    for half in range(2):
        first = 0 if half == 0 else count_ref[0]
        last = count_ref[0] if half == 0 else count
        free = count_ref[1 + half]

        def each_tile(i, carry):
            target, base, filled = meta_ref[1, i], meta_ref[2, i], meta_ref[3, i]

            def each_unit(q, carry):
                at, depth = carry
                relay = empty_ref[half, at]
                place = jnp.minimum(depth, width - 1)
                stage[relay, place] = stage[target, q]
                code_ref[relay, place] = code_ref[target, q]
                wrap = at + 1 >= free
                return jnp.where(wrap, 0, at + 1), jnp.where(wrap, depth + 1, depth)

            return lax.fori_loop(jnp.maximum(base, width), base + filled, each_unit, carry)

        lax.fori_loop(first, last, each_tile, (jnp.int32(0), jnp.int32(0)))

    copy = pltpu.make_async_copy(stage.at[:, pl.ds(0, width)], out_ref, sem)
    copy.start()
    copy.wait()


def spread(tiles, meta, empties, counts, devices, width, length, stride):
    count, side = tiles.shape[0], tiles.shape[1]
    units = side // UNIT
    smem = pl.BlockSpec(memory_space=pltpu.SMEM)
    return pl.pallas_call(
        functools.partial(spread_kernel, width, stride),
        out_shape=[
            jax.ShapeDtypeStruct((devices, width, UNIT, side), jnp.float32),
            jax.ShapeDtypeStruct((devices, length), jnp.int32),
        ],
        in_specs=[smem, smem, smem, pl.BlockSpec(memory_space=pltpu.VMEM)],
        out_specs=[pl.BlockSpec(memory_space=pl.ANY), smem],
        scratch_shapes=[
            pltpu.VMEM((devices, length, UNIT, side), jnp.float32),
            pltpu.SemaphoreType.DMA,
        ],
        compiler_params=pltpu.CompilerParams(vmem_limit_bytes=40 * MIB),
    )(meta, empties, counts, tiles.reshape(count, units, UNIT, side))


def relay_kernel(slot_ref, arrived_ref, out_ref):
    devices, width = slot_ref.shape

    @pl.loop(0, devices)
    def _(s):
        def more(k):
            return (k < width) & (slot_ref[s, jnp.minimum(k, width - 1)] >= 0)

        def move(k):
            out_ref[slot_ref[s, k]] = arrived_ref[s, k]
            return k + 1

        lax.while_loop(more, move, jnp.int32(0))


def relay(slots, arrived, length):
    vmem = pl.BlockSpec(memory_space=pltpu.VMEM)
    return pl.pallas_call(
        relay_kernel,
        out_shape=jax.ShapeDtypeStruct((length,) + arrived.shape[2:], jnp.float32),
        in_specs=[pl.BlockSpec(memory_space=pltpu.SMEM), vmem],
        out_specs=vmem,
        compiler_params=pltpu.CompilerParams(vmem_limit_bytes=40 * MIB),
    )(slots, arrived)


def add_kernel(
    cols_blocks, block_ref, unit_ref, index_ref, count_ref, partial_ref, arrived_ref, out_ref, buf,
    group_start, sem_in, sem_out
):
    slots, side = buf.shape[0], buf.shape[1]
    unit = arrived_ref.shape[1]
    ahead = slots // 2
    count = count_ref[0]

    def listed(i, carry):
        groups, last = carry
        block = block_ref[i]
        fresh = block != last

        @pl.when(fresh)
        def _():
            group_start[groups] = i

        return jnp.where(fresh, groups + 1, groups), block

    groups, _ = lax.fori_loop(0, count, listed, (jnp.int32(0), jnp.int32(-1)))
    group_start[groups] = count

    def window(g):
        block = block_ref[group_start[g]]
        rows = pl.ds(pl.multiple_of(block // cols_blocks * side, side), side)
        columns = pl.ds(pl.multiple_of(block % cols_blocks * side, side), side)
        return out_ref.at[rows, columns]

    def fetch(g):
        at = g % slots
        return pltpu.make_async_copy(window(g), buf.at[at], sem_in.at[at])

    def store(g):
        at = g % slots
        return pltpu.make_async_copy(buf.at[at], window(g), sem_out.at[at])

    @pl.loop(0, jnp.minimum(groups, ahead))
    def _(g):
        fetch(g).start()

    @pl.loop(0, groups)
    def _(g):
        @pl.when(g + ahead < groups)
        def _():
            @pl.when(g >= ahead)
            def _():
                store(g - ahead).wait()

            fetch(g + ahead).start()

        fetch(g).wait()

        @pl.loop(group_start[g], group_start[g + 1])
        def _(i):
            rows = pl.ds(pl.multiple_of(unit_ref[i] * unit, unit), unit)
            buf[g % slots, rows] += arrived_ref[index_ref[i]]

        store(g).start()

    @pl.loop(jnp.maximum(groups - slots, 0), groups)
    def _(g):
        store(g).wait()


def add_relayed(partial, arrived, listing, cols_blocks):
    row_len, col_len = partial.shape
    unit, side = arrived.shape[1:]
    smem = pl.BlockSpec(memory_space=pltpu.SMEM)
    hbm = pl.BlockSpec(memory_space=pl.ANY)
    return pl.pallas_call(
        functools.partial(add_kernel, cols_blocks),
        out_shape=jax.ShapeDtypeStruct((row_len, col_len), jnp.float32),
        in_specs=[smem, smem, smem, smem, hbm, pl.BlockSpec(memory_space=pltpu.VMEM)],
        out_specs=hbm,
        scratch_shapes=[
            pltpu.VMEM((16, side, side), jnp.float32),
            pltpu.SMEM((arrived.shape[0] + 1,), jnp.int32),
            pltpu.SemaphoreType.DMA((16,)),
            pltpu.SemaphoreType.DMA((16,)),
        ],
        input_output_aliases={4: 0},
        compiler_params=pltpu.CompilerParams(vmem_limit_bytes=24 * MIB),
    )(*listing, partial, arrived)


def panel_kernel(code_ref, first_ref, front_ref, arrived_ref, out_ref):
    side = arrived_ref.shape[1]

    @pl.when(first_ref[0] == 1)
    def _():
        out_ref[...] = front_ref[...]

    @pl.when(first_ref[0] == 0)
    def _():
        out_ref[...] = jnp.zeros_like(out_ref)

    @pl.loop(0, arrived_ref.shape[0])
    def _(k):
        code = code_ref[k]
        for part in range(PANELS):

            @pl.when((code >= 0) & (code % PANELS == part))
            def _():
                rows = pl.ds(pl.multiple_of(code // PANELS * side, side), side)
                out_ref[rows, part * side : (part + 1) * side] += arrived_ref[k]


def raw_panel(front, arrived, codes, first):
    row_len = front.shape[0]
    smem = pl.BlockSpec(memory_space=pltpu.SMEM)
    return pl.pallas_call(
        panel_kernel,
        grid=(1,),
        out_shape=jax.ShapeDtypeStruct((row_len, TOTAL), jnp.float32),
        in_specs=[
            smem,
            smem,
            pl.BlockSpec((row_len, TOTAL), lambda i: (0, 0)),
            pl.BlockSpec(arrived.shape, lambda i: (0, 0, 0)),
        ],
        out_specs=pl.BlockSpec((row_len, TOTAL), lambda i: (0, 0)),
        compiler_params=pltpu.CompilerParams(vmem_limit_bytes=40 * MIB),
    )(codes, first, front, arrived)


def split(value):
    high = value.astype(jnp.bfloat16)
    low = (value - high.astype(jnp.float32)).astype(jnp.bfloat16)
    return high, low


def rows_kernel(raw_ref, inverse_ref, out_ref, parts_ref):
    solved = dot_nt(raw_ref[...], inverse_ref[...])
    out_ref[...] = solved
    high, low = split(solved)
    parts_ref[:, :TOTAL] = high
    parts_ref[:, TOTAL : 2 * TOTAL] = high
    parts_ref[:, 2 * TOTAL :] = low


def solve_rows(raw, inverse):
    length = raw.shape[0]
    step = min(512, length)
    block = pl.BlockSpec((step, TOTAL), lambda i: (i, 0))
    return pl.pallas_call(
        rows_kernel,
        grid=(length // step,),
        out_shape=[
            jax.ShapeDtypeStruct((length, TOTAL), jnp.float32),
            jax.ShapeDtypeStruct((length, 3 * TOTAL), jnp.bfloat16),
        ],
        in_specs=[block, pl.BlockSpec((TOTAL, TOTAL), lambda i: (0, 0))],
        out_specs=[block, pl.BlockSpec((step, 3 * TOTAL), lambda i: (i, 0))],
        compiler_params=pltpu.CompilerParams(vmem_limit_bytes=24 * MIB),
    )(raw, inverse)


def cols_kernel(order_ref, raw_ref, inverse_ref, out_ref, parts_ref):
    solved = dot_nt(inverse_ref[...], raw_ref[0])
    out_ref[...] = solved
    high, low = split(solved)
    parts_ref[:TOTAL] = high
    parts_ref[TOTAL : 2 * TOTAL] = low
    parts_ref[2 * TOTAL :] = high


def solve_cols(chunks, order, inverse):
    count, step = chunks.shape[:2]
    length = count * step
    grid_spec = pltpu.PrefetchScalarGridSpec(
        num_scalar_prefetch=1,
        grid=(count,),
        in_specs=[
            pl.BlockSpec((1, step, TOTAL), lambda i, order: (order[i], 0, 0)),
            pl.BlockSpec((TOTAL, TOTAL), lambda i, order: (0, 0)),
        ],
        out_specs=[
            pl.BlockSpec((TOTAL, step), lambda i, order: (0, i)),
            pl.BlockSpec((3 * TOTAL, step), lambda i, order: (0, i)),
        ],
    )
    return pl.pallas_call(
        cols_kernel,
        grid_spec=grid_spec,
        out_shape=[
            jax.ShapeDtypeStruct((TOTAL, length), jnp.float32),
            jax.ShapeDtypeStruct((3 * TOTAL, length), jnp.bfloat16),
        ],
        compiler_params=pltpu.CompilerParams(vmem_limit_bytes=24 * MIB),
    )(order, chunks, inverse)


def final_kernel(
    cols_blocks, runs, code_ref, run_ref, place_ref, front_ref, rows_ref, rows_parts, cols_ref, cols_parts,
    lower_ref, arrived_ref, out_ref, cursor
):
    step = pl.program_id(0)
    sources, capacity = code_ref.shape
    height, width = front_ref.shape
    unit, side = arrived_ref.shape[2:]
    per_step = height // unit

    @pl.when(step == 0)
    def _():
        for s in range(sources):
            cursor[s] = 0

    chunk = min(512, width)
    for start in range(0, width, chunk):
        at = slice(start, start + chunk)
        change = jnp.dot(rows_parts[...], cols_parts[:, at], preferred_element_type=jnp.float32)
        out_ref[:, at] = front_ref[:, at] - change

    edge = (step + 1) * per_step * cols_blocks

    @pl.loop(0, sources)
    def _(s):
        def more(k):
            code = code_ref[s, jnp.minimum(k, capacity - 1)]
            return (k < capacity) & (code >= 0) & (code < edge)

        def add(k):
            code = code_ref[s, k]
            length = run_ref[s, k]
            unit_row = code // cols_blocks - step * per_step
            columns = pl.ds(pl.multiple_of(code % cols_blocks * side, side), side)
            for run in runs:
                skipped = length // (2 * run) * (2 * run)

                @pl.when(length // run % 2 == 1)
                def _():
                    rows = pl.ds(pl.multiple_of((unit_row + skipped) * unit, unit), run * unit)
                    block = arrived_ref[s, pl.ds(k + skipped, run)]
                    out_ref[rows, columns] += block.reshape(run * unit, side)

            return k + length

        cursor[s] = lax.while_loop(more, add, cursor[s])

    top = (place_ref[0] == 0) & (step == 0)

    @pl.when(top)
    def _():
        out_ref[...] = cols_ref[...]

    @pl.when(place_ref[1] == 0)
    def _():
        out_ref[:, :TOTAL] = jnp.where(top, lower_ref[...], rows_ref[...])


def finish(front, rows, cols, lower, arrived, codes, lengths, place, cols_blocks):
    row_len, col_len = front.shape
    height = TOTAL
    smem = pl.BlockSpec(memory_space=pltpu.SMEM)
    block = pl.BlockSpec((height, TOTAL), lambda i: (i, 0))
    parts = pl.BlockSpec((height, 3 * TOTAL), lambda i: (i, 0))
    wide = pl.BlockSpec((height, col_len), lambda i: (i, 0))
    whole = pl.BlockSpec((TOTAL, col_len), lambda i: (0, 0))
    whole_parts = pl.BlockSpec((3 * TOTAL, col_len), lambda i: (0, 0))
    runs = (16, 8, 4, 2, 1) if arrived.shape[2] == UNIT else (1,)
    return pl.pallas_call(
        functools.partial(final_kernel, cols_blocks, runs),
        grid=(row_len // height,),
        out_shape=jax.ShapeDtypeStruct((row_len, col_len), jnp.float32),
        in_specs=[
            smem, smem, smem, wide, block, parts, whole, whole_parts,
            pl.BlockSpec((TOTAL, TOTAL), lambda i: (0, 0)),
            pl.BlockSpec(memory_space=pltpu.VMEM),
        ],
        out_specs=wide,
        scratch_shapes=[pltpu.SMEM((codes.shape[0],), jnp.int32)],
        compiler_params=pltpu.CompilerParams(vmem_limit_bytes=56 * MIB),
    )(codes, lengths, place, front, *rows, *cols, lower, arrived)


def factor(diagonal):
    def lower_of(block):
        return jnp.linalg.cholesky(jnp.tril(block) + jnp.tril(block, -1).T)

    def inverse_of(block):
        return jax.scipy.linalg.solve_triangular(block, jnp.eye(NB, dtype=jnp.float32), lower=True)

    first = lower_of(diagonal[:NB, :NB])
    first_inverse = inverse_of(first)
    below = dot_nt(diagonal[NB:, :NB], first_inverse)
    second = lower_of(diagonal[NB:, NB:] - dot_nt(below, below))
    second_inverse = inverse_of(second)
    corner = -jnp.dot(second_inverse, jnp.dot(below, first_inverse, precision=precise), precision=precise)
    zero = jnp.zeros((NB, NB), jnp.float32)
    return jnp.block([[first, zero], [below, second]]), jnp.block([[first_inverse, zero], [corner, second_inverse]])


def body(front, tiles, tile_block, valid_rows):
    row_len, col_len = front.shape
    row_count = lax.axis_size("row")
    col_count = lax.axis_size("col")
    device_count = row_count * col_count
    per_device = tiles.shape[0]
    side = tiles.shape[1]
    capacity = 2 * per_device // device_count
    rows_blocks = row_len // side
    cols_blocks = col_len // side
    row_now = lax.axis_index("row")
    col_now = lax.axis_index("col")
    device_now = row_now * col_count + col_now

    block_row = tile_block[0].reshape(device_count, per_device)
    block_col = tile_block[1].reshape(device_count, per_device)
    target_row = block_row // rows_blocks
    target = target_row * col_count + block_col // cols_blocks
    code = block_row % rows_blocks * cols_blocks + block_col % cols_blocks
    position = lax.broadcasted_iota(jnp.int32, target.shape, 1)
    place = jnp.stack([row_now, col_now]).astype(jnp.int32)

    def own(values):
        return lax.dynamic_index_in_dim(values, device_now, 0, keepdims=False)

    in_panel = block_col < PANELS
    panel_key = jnp.where(in_panel, target_row, -1)
    panel_rank = jnp.sum(
        (panel_key[:, :, None] == panel_key[:, None, :]) & (position[:, None, :] < position[:, :, None]),
        axis=2,
    )
    same_col = lax.dynamic_index_in_dim(
        jnp.stack([panel_key, panel_rank, code]).reshape(3, row_count, col_count, per_device),
        col_now, 2, keepdims=False,
    )

    def send_panel(tiles, valid_rows, depth):
        ahead = (own(target_row) - row_now) % row_count
        fits = own(in_panel) & (own(panel_rank) < depth)
        panel_slot = jnp.where(fits, ahead * depth + own(panel_rank), -1)
        panel_out = pack(tiles, panel_slot, valid_rows, row_count * depth)
        panel_in = [panel_out[:depth]]
        for shift in range(1, row_count):
            sending = panel_out[shift * depth : (shift + 1) * depth]
            turn = [(r, (r + shift) % row_count) for r in range(row_count)]
            panel_in.append(lax.ppermute(sending, "row", turn))
        return panel_in

    def sum_panel(front, panel_in, depth):
        fits = (same_col[0] == row_now)[:, :, None] & (same_col[1][:, :, None] == jnp.arange(depth))
        panel_code = same_col[2] // cols_blocks * PANELS + same_col[2] % cols_blocks
        panel_codes = jnp.sum(jnp.where(fits, panel_code[:, :, None] + 1, 0), axis=1) - 1
        by_shift = (row_now - jnp.arange(row_count)) % row_count
        panel_codes = jnp.take(panel_codes, by_shift, axis=0).reshape(-1)
        first = (col_now == 0).astype(jnp.int32).reshape(1)
        return raw_panel(front, jnp.concatenate(panel_in, 0), panel_codes, first)

    def gather_panel(partial):
        chunk = lax.psum_scatter(partial, "col", scatter_dimension=0, tiled=True)
        raw_rows = lax.all_gather(chunk, "col", axis=0, tiled=True)
        chunk, raw_rows = lax.optimization_barrier((chunk, raw_rows))
        return lax.all_gather(chunk, "row", axis=0), raw_rows

    panel_depth = (capacity * 5 + 7) // 8
    panel_in = send_panel(tiles, valid_rows, panel_depth)

    units = side // UNIT
    length = capacity * units
    width = length * 41 // 64
    pass_on = length * 13 // 32
    half_count = device_count // 2
    half_base = device_now // half_count * half_count
    unit_rows = rows_blocks * units
    local_codes = unit_rows * cols_blocks
    own_target, own_code = own(target), own(code)
    own_position = own(position)
    filled = (valid_rows + UNIT - 1) // UNIT
    key = (own_target * rows_blocks * cols_blocks + own_code) * per_device + own_position
    before = key[None, :] < key[:, None]
    together = own_target[None, :] == own_target[:, None]
    base = jnp.sum(jnp.where(before & together, filled[None, :], 0), axis=1)
    order = jnp.sum(before, axis=1)
    unit_code = (own_target * unit_rows + own_code // cols_blocks * units) * cols_blocks
    unit_code += own_code % cols_blocks
    meta = jnp.stack([own_position, own_target, base, filled, unit_code, valid_rows])
    meta = jnp.sum(
        jnp.where(order[None, :, None] == jnp.arange(per_device), meta[:, :, None], 0), axis=1
    )
    to_device = own_target[:, None] == jnp.arange(device_count)
    load = jnp.sum(jnp.where(to_device, filled[:, None], 0), axis=0).reshape(2, half_count)
    empty = load == 0
    empty_rank = jnp.cumsum(empty, axis=1) - 1
    device_ids = jnp.arange(device_count).reshape(2, half_count)
    listed = (empty[:, :, None]) & (empty_rank[:, :, None] == jnp.arange(half_count))
    empties = jnp.sum(jnp.where(listed, device_ids[:, :, None], 0), axis=1)
    free = jnp.sum(empty, axis=1)
    left = jnp.sum(jnp.maximum(load - width, 0), axis=1)
    failed = jnp.any(left > free * width) | jnp.any(own(in_panel) & (own(panel_rank) >= panel_depth))
    counts = jnp.concatenate([jnp.sum(own_target < half_count)[None], free]).astype(jnp.int32)
    outgoing, sent_codes = spread(
        tiles, meta.astype(jnp.int32), empties.astype(jnp.int32), counts,
        device_count, width, length, cols_blocks,
    )

    partial = sum_panel(front, panel_in, panel_depth)
    partial, sent_codes = lax.optimization_barrier((partial, sent_codes))
    gathered, raw_rows = gather_panel(partial)
    got = lax.all_to_all(sent_codes[:, :width], ("row", "col"), 0, 0, tiled=True)
    outgoing, got = lax.optimization_barrier((outgoing, got))
    arrived = lax.all_to_all(outgoing, ("row", "col"), 0, 0, tiled=True)
    got_target = got // local_codes
    local = got % local_codes
    mine = (got >= 0) & (got_target == device_now)
    direct_codes = jnp.where(mine, local, -1)
    steps = jnp.arange(width)
    opening = (local // cols_blocks % units == 0) | jnp.logical_not(mine)
    later = (steps[None, :] > steps[:, None]) & opening[:, None, :]
    direct_runs = jnp.min(jnp.where(later, steps, width), axis=2) - steps
    total_units = device_count * width
    passing = ((got >= 0) & (got_target != device_now)).reshape(-1)
    flat_key = jnp.where(passing, got.reshape(-1) * total_units + jnp.arange(total_units), -1)
    flat_target = jnp.where(passing, got_target.reshape(-1), -1)
    rank = jnp.sum(
        (flat_target[None, :] == flat_target[:, None]) & (flat_key[None, :] < flat_key[:, None]), axis=1
    )
    failed = failed | jnp.any(passing & (rank >= pass_on))
    relay_slot = jnp.where(
        passing & (rank < pass_on), (flat_target - half_base) * pass_on + rank, -1
    )
    picked = relay_slot[:, None] == jnp.arange(half_count * pass_on)
    relay_codes = jnp.sum(jnp.where(picked, local.reshape(-1)[:, None] + 1, 0), axis=0) - 1
    notes = jnp.zeros((2, half_count, pass_on + 1), jnp.int32)
    notes = lax.dynamic_update_slice(
        notes, relay_codes.reshape(1, half_count, pass_on).astype(jnp.int32), (device_now // half_count, 0, 0)
    )
    notes = notes.at[:, :, pass_on].set(failed.astype(jnp.int32))
    def chain(gathered, raw_rows, arrived):
        diagonal = jnp.where(row_now == 0, raw_rows[:TOTAL], jnp.eye(TOTAL, dtype=jnp.float32))
        lower, inverse = factor(diagonal)
        known = jnp.where(row_now == 0, inverse, 0.0)
        gathered, known = lax.optimization_barrier((gathered, known))
        share = col_count // row_count
        chunks = []
        for turn in range(row_count):
            pairs = [
                (h * row_count + i, (i + turn) % row_count * share + h)
                for h in range(share)
                for i in range(row_count)
            ]
            sending = lax.dynamic_index_in_dim(gathered, (col_now + turn) % row_count, 0, keepdims=False)
            chunks.append(lax.ppermute(sending, "col", pairs))
        order = (col_now // share - jnp.arange(row_count)) % row_count
        inverse = known
        for other in range(1, row_count):
            inverse += lax.ppermute(known, "row", [(0, other)])
        arrived, inverse, chunks = lax.optimization_barrier((arrived, inverse, chunks))
        rows = solve_rows(raw_rows, inverse)
        cols = solve_cols(jnp.stack(chunks), order.astype(jnp.int32), inverse)
        return rows, cols, lower, arrived

    rows, cols, lower, arrived = chain(gathered, raw_rows, arrived)
    notes, arrived = lax.optimization_barrier((notes, arrived))
    notes = lax.all_to_all(
        notes.reshape(device_count, pass_on + 1), ("row", "col"), 0, 0, tiled=True
    )
    relay_codes = lax.dynamic_slice_in_dim(notes, half_base, half_count, 0)[:, :pass_on]
    relay_slot = relay_slot.reshape(device_count, width)

    flat = relay_codes.reshape(-1)
    unit_row, relay_col = flat // cols_blocks, flat % cols_blocks
    wanted = (flat >= 0) & ((row_now > 0) | (unit_row >= TOTAL // UNIT))
    wanted &= (col_now > 0) | (relay_col >= PANELS)
    relay_block = unit_row // units * cols_blocks + relay_col
    relay_key = jnp.where(wanted, relay_block * units + unit_row % units, local_codes)
    relay_key = relay_key * flat.shape[0] + jnp.arange(flat.shape[0])
    relay_order = jnp.sum(relay_key[None, :] < relay_key[:, None], axis=1)
    listing = jnp.stack([relay_block, unit_row % units, jnp.arange(flat.shape[0])])
    at_order = relay_order[None, :, None] == jnp.arange(flat.shape[0])
    listing = jnp.sum(jnp.where(at_order, listing[:, :, None], 0), axis=1).astype(jnp.int32)
    listing = [*listing, jnp.sum(wanted).astype(jnp.int32).reshape(1)]

    passed = relay(relay_slot, arrived, half_count * pass_on)
    passed, notes = lax.optimization_barrier((passed, notes))
    too_full = jnp.any(notes[:, pass_on] != 0)
    halves = [list(range(half_count)), list(range(half_count, device_count))]
    passed = lax.all_to_all(
        passed.reshape(half_count, pass_on, UNIT, side), ("row", "col"), 0, 0,
        axis_index_groups=halves, tiled=True,
    )
    partial = finish(front, rows, cols, lower, arrived, direct_codes, direct_runs, place, cols_blocks)
    result = add_relayed(partial, passed.reshape(-1, UNIT, side), listing, cols_blocks)

    def padded():
        partial = sum_panel(front, send_panel(tiles, valid_rows, capacity), capacity)
        gathered, raw_rows = gather_panel(partial)
        order = (target * rows_blocks * cols_blocks + code) * per_device + position
        ranking = jnp.sum(
            (target[:, :, None] == target[:, None, :]) & (order[:, None, :] < order[:, :, None]), axis=2
        )
        slot = own(target) * capacity + own(ranking)
        here = (target == device_now)[:, :, None] & (ranking[:, :, None] == jnp.arange(capacity))
        codes = jnp.sum(jnp.where(here, code[:, :, None] + 1, 0), axis=1) - 1
        packed = pack(tiles, slot, valid_rows, device_count * capacity)
        arrived = lax.all_to_all(
            packed.reshape(device_count, capacity, side, side), ("row", "col"), 0, 0, tiled=True
        )
        rows, cols, lower, arrived = chain(gathered, raw_rows, arrived)
        return finish(
            front, rows, cols, lower, arrived, codes, jnp.ones_like(codes), place, cols_blocks
        )

    def unfinished(state):
        return state[0] > 0

    def redo(state):
        return jnp.int32(0), padded()

    return lax.while_loop(unfinished, redo, (too_full.astype(jnp.int32), result))[1]


def solution(mesh):
    placed = (P("row", "col"), P(("row", "col"), None, None), P(), P(("row", "col")))
    return jax.shard_map(
        body, mesh=mesh, in_specs=placed, out_specs=P("row", "col"), check_vma=False
    )
```

```python
import functools

import jax
import jax.numpy as jnp
from jax import lax
from jax.experimental import pallas as pl
from jax.experimental.pallas import tpu as pltpu
from jax.sharding import PartitionSpec as P

NB = 128
PANELS = 2
TOTAL = NB * PANELS
MIB = 1 << 20
UNIT = 8


precise = lax.Precision.HIGHEST


def dot_nt(a, b, precision=precise):
    return lax.dot_general(
        a, b, (((1,), (1,)), ((), ())), precision=precision, preferred_element_type=jnp.float32
    )


def pack_kernel(slot_ref, valid_ref, tiles_ref, out_ref, buf, sem_in, sem_out):
    count, side = tiles_ref.shape[0], tiles_ref.shape[1]

    def fetch(t):
        return pltpu.make_async_copy(tiles_ref.at[t], buf.at[t], sem_in.at[t])

    def store(t):
        return pltpu.make_async_copy(buf.at[t], out_ref.at[jnp.maximum(slot_ref[t], 0)], sem_out.at[t])

    def each(act):
        @pl.loop(0, count)
        def _(t):
            @pl.when(slot_ref[t] >= 0)
            def _():
                act(t)

    def mask(t):
        fetch(t).wait()
        rows = lax.broadcasted_iota(jnp.int32, (side, side), 0)
        buf[t] = jnp.where(rows < valid_ref[t], buf[t], 0.0)
        store(t).start()

    each(lambda t: fetch(t).start())
    each(mask)
    each(lambda t: store(t).wait())


def pack(tiles, slots, valid, n_slots):
    count, side = tiles.shape[0], tiles.shape[1]
    smem = pl.BlockSpec(memory_space=pltpu.SMEM)
    return pl.pallas_call(
        pack_kernel,
        out_shape=jax.ShapeDtypeStruct((n_slots, side, side), jnp.float32),
        in_specs=[smem, smem, pl.BlockSpec(memory_space=pl.ANY)],
        out_specs=pl.BlockSpec(memory_space=pl.ANY),
        scratch_shapes=[
            pltpu.VMEM((count, side, side), jnp.float32),
            pltpu.SemaphoreType.DMA((count,)),
            pltpu.SemaphoreType.DMA((count,)),
        ],
        compiler_params=pltpu.CompilerParams(vmem_limit_bytes=24 * MIB),
    )(slots, valid, tiles)


def spread_kernel(
    width, stride, meta_ref, empty_ref, count_ref, tiles_ref, out_ref, code_ref, stage, sem
):
    count, units = tiles_ref.shape[0], tiles_ref.shape[1]
    devices, length = code_ref.shape

    @pl.loop(0, devices)
    def _(d):
        for k in range(length):
            code_ref[d, k] = -1

    @pl.loop(0, count)
    def _(i):
        tile, target, base = meta_ref[0, i], meta_ref[1, i], meta_ref[2, i]
        filled, code, valid = meta_ref[3, i], meta_ref[4, i], meta_ref[5, i]
        shape = tiles_ref.shape[1:]
        rows = lax.broadcasted_iota(jnp.int32, shape, 0) * shape[1]
        rows += lax.broadcasted_iota(jnp.int32, shape, 1)
        stage[target, pl.ds(base, units)] = jnp.where(rows < valid, tiles_ref[tile], 0.0)
        for u in range(units):
            code_ref[target, base + u] = jnp.where(u < filled, code + u * stride, -1)

    for half in range(2):
        first = 0 if half == 0 else count_ref[0]
        last = count_ref[0] if half == 0 else count
        free = count_ref[1 + half]

        def each_tile(i, carry):
            target, base, filled = meta_ref[1, i], meta_ref[2, i], meta_ref[3, i]

            def each_unit(q, carry):
                at, depth = carry
                relay = empty_ref[half, at]
                place = jnp.minimum(depth, width - 1)
                stage[relay, place] = stage[target, q]
                code_ref[relay, place] = code_ref[target, q]
                wrap = at + 1 >= free
                return jnp.where(wrap, 0, at + 1), jnp.where(wrap, depth + 1, depth)

            return lax.fori_loop(jnp.maximum(base, width), base + filled, each_unit, carry)

        lax.fori_loop(first, last, each_tile, (jnp.int32(0), jnp.int32(0)))

    copy = pltpu.make_async_copy(stage.at[:, pl.ds(0, width)], out_ref, sem)
    copy.start()
    copy.wait()


def spread(tiles, meta, empties, counts, devices, width, length, stride):
    count, side = tiles.shape[0], tiles.shape[1]
    units = side // UNIT
    smem = pl.BlockSpec(memory_space=pltpu.SMEM)
    return pl.pallas_call(
        functools.partial(spread_kernel, width, stride),
        out_shape=[
            jax.ShapeDtypeStruct((devices, width, UNIT, side), jnp.float32),
            jax.ShapeDtypeStruct((devices, length), jnp.int32),
        ],
        in_specs=[smem, smem, smem, pl.BlockSpec(memory_space=pltpu.VMEM)],
        out_specs=[pl.BlockSpec(memory_space=pl.ANY), smem],
        scratch_shapes=[
            pltpu.VMEM((devices, length, UNIT, side), jnp.float32),
            pltpu.SemaphoreType.DMA,
        ],
        compiler_params=pltpu.CompilerParams(vmem_limit_bytes=40 * MIB),
    )(meta, empties, counts, tiles.reshape(count, units, UNIT, side))


def relay_kernel(slot_ref, arrived_ref, out_ref):
    devices, width = slot_ref.shape

    @pl.loop(0, devices)
    def _(s):
        def more(k):
            return (k < width) & (slot_ref[s, jnp.minimum(k, width - 1)] >= 0)

        def move(k):
            out_ref[slot_ref[s, k]] = arrived_ref[s, k]
            return k + 1

        lax.while_loop(more, move, jnp.int32(0))


def relay(slots, arrived, length):
    vmem = pl.BlockSpec(memory_space=pltpu.VMEM)
    return pl.pallas_call(
        relay_kernel,
        out_shape=jax.ShapeDtypeStruct((length,) + arrived.shape[2:], jnp.float32),
        in_specs=[pl.BlockSpec(memory_space=pltpu.SMEM), vmem],
        out_specs=vmem,
        compiler_params=pltpu.CompilerParams(vmem_limit_bytes=40 * MIB),
    )(slots, arrived)


def add_kernel(
    cols_blocks, block_ref, unit_ref, index_ref, count_ref, partial_ref, arrived_ref, out_ref, buf,
    group_start, sem_in, sem_out
):
    slots, side = buf.shape[0], buf.shape[1]
    unit = arrived_ref.shape[1]
    ahead = slots // 2
    count = count_ref[0]

    def listed(i, carry):
        groups, last = carry
        block = block_ref[i]
        fresh = block != last

        @pl.when(fresh)
        def _():
            group_start[groups] = i

        return jnp.where(fresh, groups + 1, groups), block

    groups, _ = lax.fori_loop(0, count, listed, (jnp.int32(0), jnp.int32(-1)))
    group_start[groups] = count

    def window(g):
        block = block_ref[group_start[g]]
        rows = pl.ds(pl.multiple_of(block // cols_blocks * side, side), side)
        columns = pl.ds(pl.multiple_of(block % cols_blocks * side, side), side)
        return out_ref.at[rows, columns]

    def fetch(g):
        at = g % slots
        return pltpu.make_async_copy(window(g), buf.at[at], sem_in.at[at])

    def store(g):
        at = g % slots
        return pltpu.make_async_copy(buf.at[at], window(g), sem_out.at[at])

    @pl.loop(0, jnp.minimum(groups, ahead))
    def _(g):
        fetch(g).start()

    @pl.loop(0, groups)
    def _(g):
        @pl.when(g + ahead < groups)
        def _():
            @pl.when(g >= ahead)
            def _():
                store(g - ahead).wait()

            fetch(g + ahead).start()

        fetch(g).wait()

        @pl.loop(group_start[g], group_start[g + 1])
        def _(i):
            rows = pl.ds(pl.multiple_of(unit_ref[i] * unit, unit), unit)
            buf[g % slots, rows] += arrived_ref[index_ref[i]]

        store(g).start()

    @pl.loop(jnp.maximum(groups - slots, 0), groups)
    def _(g):
        store(g).wait()


def add_relayed(partial, arrived, listing, cols_blocks):
    row_len, col_len = partial.shape
    unit, side = arrived.shape[1:]
    smem = pl.BlockSpec(memory_space=pltpu.SMEM)
    hbm = pl.BlockSpec(memory_space=pl.ANY)
    return pl.pallas_call(
        functools.partial(add_kernel, cols_blocks),
        out_shape=jax.ShapeDtypeStruct((row_len, col_len), jnp.float32),
        in_specs=[smem, smem, smem, smem, hbm, pl.BlockSpec(memory_space=pltpu.VMEM)],
        out_specs=hbm,
        scratch_shapes=[
            pltpu.VMEM((16, side, side), jnp.float32),
            pltpu.SMEM((arrived.shape[0] + 1,), jnp.int32),
            pltpu.SemaphoreType.DMA((16,)),
            pltpu.SemaphoreType.DMA((16,)),
        ],
        input_output_aliases={4: 0},
        compiler_params=pltpu.CompilerParams(vmem_limit_bytes=24 * MIB),
    )(*listing, partial, arrived)


def panel_kernel(code_ref, first_ref, front_ref, arrived_ref, out_ref):
    side = arrived_ref.shape[1]

    @pl.when(first_ref[0] == 1)
    def _():
        out_ref[...] = front_ref[...]

    @pl.when(first_ref[0] == 0)
    def _():
        out_ref[...] = jnp.zeros_like(out_ref)

    @pl.loop(0, arrived_ref.shape[0])
    def _(k):
        code = code_ref[k]
        for part in range(PANELS):

            @pl.when((code >= 0) & (code % PANELS == part))
            def _():
                rows = pl.ds(pl.multiple_of(code // PANELS * side, side), side)
                out_ref[rows, part * side : (part + 1) * side] += arrived_ref[k]


def raw_panel(front, arrived, codes, first):
    row_len = front.shape[0]
    smem = pl.BlockSpec(memory_space=pltpu.SMEM)
    return pl.pallas_call(
        panel_kernel,
        grid=(1,),
        out_shape=jax.ShapeDtypeStruct((row_len, TOTAL), jnp.float32),
        in_specs=[
            smem,
            smem,
            pl.BlockSpec((row_len, TOTAL), lambda i: (0, 0)),
            pl.BlockSpec(arrived.shape, lambda i: (0, 0, 0)),
        ],
        out_specs=pl.BlockSpec((row_len, TOTAL), lambda i: (0, 0)),
        compiler_params=pltpu.CompilerParams(vmem_limit_bytes=40 * MIB),
    )(codes, first, front, arrived)


def split(value):
    high = value.astype(jnp.bfloat16)
    low = (value - high.astype(jnp.float32)).astype(jnp.bfloat16)
    return high, low


def rows_kernel(raw_ref, inverse_ref, out_ref, parts_ref):
    solved = dot_nt(raw_ref[...], inverse_ref[...])
    out_ref[...] = solved
    high, low = split(solved)
    parts_ref[:, :TOTAL] = high
    parts_ref[:, TOTAL : 2 * TOTAL] = high
    parts_ref[:, 2 * TOTAL :] = low


def solve_rows(raw, inverse):
    length = raw.shape[0]
    step = min(512, length)
    block = pl.BlockSpec((step, TOTAL), lambda i: (i, 0))
    return pl.pallas_call(
        rows_kernel,
        grid=(length // step,),
        out_shape=[
            jax.ShapeDtypeStruct((length, TOTAL), jnp.float32),
            jax.ShapeDtypeStruct((length, 3 * TOTAL), jnp.bfloat16),
        ],
        in_specs=[block, pl.BlockSpec((TOTAL, TOTAL), lambda i: (0, 0))],
        out_specs=[block, pl.BlockSpec((step, 3 * TOTAL), lambda i: (i, 0))],
        compiler_params=pltpu.CompilerParams(vmem_limit_bytes=24 * MIB),
    )(raw, inverse)


def cols_kernel(order_ref, raw_ref, inverse_ref, out_ref, parts_ref):
    solved = dot_nt(inverse_ref[...], raw_ref[0])
    out_ref[...] = solved
    high, low = split(solved)
    parts_ref[:TOTAL] = high
    parts_ref[TOTAL : 2 * TOTAL] = low
    parts_ref[2 * TOTAL :] = high


def solve_cols(chunks, order, inverse):
    count, step = chunks.shape[:2]
    length = count * step
    grid_spec = pltpu.PrefetchScalarGridSpec(
        num_scalar_prefetch=1,
        grid=(count,),
        in_specs=[
            pl.BlockSpec((1, step, TOTAL), lambda i, order: (order[i], 0, 0)),
            pl.BlockSpec((TOTAL, TOTAL), lambda i, order: (0, 0)),
        ],
        out_specs=[
            pl.BlockSpec((TOTAL, step), lambda i, order: (0, i)),
            pl.BlockSpec((3 * TOTAL, step), lambda i, order: (0, i)),
        ],
    )
    return pl.pallas_call(
        cols_kernel,
        grid_spec=grid_spec,
        out_shape=[
            jax.ShapeDtypeStruct((TOTAL, length), jnp.float32),
            jax.ShapeDtypeStruct((3 * TOTAL, length), jnp.bfloat16),
        ],
        compiler_params=pltpu.CompilerParams(vmem_limit_bytes=24 * MIB),
    )(order, chunks, inverse)


def final_kernel(
    cols_blocks, runs, code_ref, run_ref, place_ref, front_ref, rows_ref, rows_parts, cols_ref, cols_parts,
    lower_ref, arrived_ref, out_ref, cursor
):
    step = pl.program_id(0)
    sources, capacity = code_ref.shape
    height, width = front_ref.shape
    unit, side = arrived_ref.shape[2:]
    per_step = height // unit

    @pl.when(step == 0)
    def _():
        for s in range(sources):
            cursor[s] = 0

    chunk = min(512, width)
    for start in range(0, width, chunk):
        at = slice(start, start + chunk)
        change = jnp.dot(rows_parts[...], cols_parts[:, at], preferred_element_type=jnp.float32)
        out_ref[:, at] = front_ref[:, at] - change

    edge = (step + 1) * per_step * cols_blocks

    @pl.loop(0, sources)
    def _(s):
        def more(k):
            code = code_ref[s, jnp.minimum(k, capacity - 1)]
            return (k < capacity) & (code >= 0) & (code < edge)

        def add(k):
            code = code_ref[s, k]
            length = run_ref[s, k]
            unit_row = code // cols_blocks - step * per_step
            columns = pl.ds(pl.multiple_of(code % cols_blocks * side, side), side)
            for run in runs:
                skipped = length // (2 * run) * (2 * run)

                @pl.when(length // run % 2 == 1)
                def _():
                    rows = pl.ds(pl.multiple_of((unit_row + skipped) * unit, unit), run * unit)
                    block = arrived_ref[s, pl.ds(k + skipped, run)]
                    out_ref[rows, columns] += block.reshape(run * unit, side)

            return k + length

        cursor[s] = lax.while_loop(more, add, cursor[s])

    top = (place_ref[0] == 0) & (step == 0)

    @pl.when(top)
    def _():
        out_ref[...] = cols_ref[...]

    @pl.when(place_ref[1] == 0)
    def _():
        out_ref[:, :TOTAL] = jnp.where(top, lower_ref[...], rows_ref[...])


def finish(front, rows, cols, lower, arrived, codes, lengths, place, cols_blocks):
    row_len, col_len = front.shape
    height = TOTAL
    smem = pl.BlockSpec(memory_space=pltpu.SMEM)
    block = pl.BlockSpec((height, TOTAL), lambda i: (i, 0))
    parts = pl.BlockSpec((height, 3 * TOTAL), lambda i: (i, 0))
    wide = pl.BlockSpec((height, col_len), lambda i: (i, 0))
    whole = pl.BlockSpec((TOTAL, col_len), lambda i: (0, 0))
    whole_parts = pl.BlockSpec((3 * TOTAL, col_len), lambda i: (0, 0))
    runs = (16, 8, 4, 2, 1) if arrived.shape[2] == UNIT else (1,)
    return pl.pallas_call(
        functools.partial(final_kernel, cols_blocks, runs),
        grid=(row_len // height,),
        out_shape=jax.ShapeDtypeStruct((row_len, col_len), jnp.float32),
        in_specs=[
            smem, smem, smem, wide, block, parts, whole, whole_parts,
            pl.BlockSpec((TOTAL, TOTAL), lambda i: (0, 0)),
            pl.BlockSpec(memory_space=pltpu.VMEM),
        ],
        out_specs=wide,
        scratch_shapes=[pltpu.SMEM((codes.shape[0],), jnp.int32)],
        compiler_params=pltpu.CompilerParams(vmem_limit_bytes=56 * MIB),
    )(codes, lengths, place, front, *rows, *cols, lower, arrived)


def factor(diagonal):
    def lower_of(block):
        return jnp.linalg.cholesky(jnp.tril(block) + jnp.tril(block, -1).T)

    def inverse_of(block):
        return jax.scipy.linalg.solve_triangular(block, jnp.eye(NB, dtype=jnp.float32), lower=True)

    first = lower_of(diagonal[:NB, :NB])
    first_inverse = inverse_of(first)
    below = dot_nt(diagonal[NB:, :NB], first_inverse)
    second = lower_of(diagonal[NB:, NB:] - dot_nt(below, below))
    second_inverse = inverse_of(second)
    corner = -jnp.dot(second_inverse, jnp.dot(below, first_inverse, precision=precise), precision=precise)
    zero = jnp.zeros((NB, NB), jnp.float32)
    return jnp.block([[first, zero], [below, second]]), jnp.block([[first_inverse, zero], [corner, second_inverse]])


def body(front, tiles, tile_block, valid_rows):
    row_len, col_len = front.shape
    row_count = lax.axis_size("row")
    col_count = lax.axis_size("col")
    device_count = row_count * col_count
    per_device = tiles.shape[0]
    side = tiles.shape[1]
    capacity = 2 * per_device // device_count
    rows_blocks = row_len // side
    cols_blocks = col_len // side
    row_now = lax.axis_index("row")
    col_now = lax.axis_index("col")
    device_now = row_now * col_count + col_now

    block_row = tile_block[0].reshape(device_count, per_device)
    block_col = tile_block[1].reshape(device_count, per_device)
    target_row = block_row // rows_blocks
    target = target_row * col_count + block_col // cols_blocks
    code = block_row % rows_blocks * cols_blocks + block_col % cols_blocks
    position = lax.broadcasted_iota(jnp.int32, target.shape, 1)
    place = jnp.stack([row_now, col_now]).astype(jnp.int32)

    def own(values):
        return lax.dynamic_index_in_dim(values, device_now, 0, keepdims=False)

    in_panel = block_col < PANELS
    panel_key = jnp.where(in_panel, target_row, -1)
    panel_rank = jnp.sum(
        (panel_key[:, :, None] == panel_key[:, None, :]) & (position[:, None, :] < position[:, :, None]),
        axis=2,
    )
    same_col = lax.dynamic_index_in_dim(
        jnp.stack([panel_key, panel_rank, code]).reshape(3, row_count, col_count, per_device),
        col_now, 2, keepdims=False,
    )

    def send_panel(tiles, valid_rows, depth):
        ahead = (own(target_row) - row_now) % row_count
        fits = own(in_panel) & (own(panel_rank) < depth)
        panel_slot = jnp.where(fits, ahead * depth + own(panel_rank), -1)
        panel_out = pack(tiles, panel_slot, valid_rows, row_count * depth)
        panel_in = [panel_out[:depth]]
        for shift in range(1, row_count):
            sending = panel_out[shift * depth : (shift + 1) * depth]
            turn = [(r, (r + shift) % row_count) for r in range(row_count)]
            panel_in.append(lax.ppermute(sending, "row", turn))
        return panel_in

    def sum_panel(front, panel_in, depth):
        fits = (same_col[0] == row_now)[:, :, None] & (same_col[1][:, :, None] == jnp.arange(depth))
        panel_code = same_col[2] // cols_blocks * PANELS + same_col[2] % cols_blocks
        panel_codes = jnp.sum(jnp.where(fits, panel_code[:, :, None] + 1, 0), axis=1) - 1
        by_shift = (row_now - jnp.arange(row_count)) % row_count
        panel_codes = jnp.take(panel_codes, by_shift, axis=0).reshape(-1)
        first = (col_now == 0).astype(jnp.int32).reshape(1)
        return raw_panel(front, jnp.concatenate(panel_in, 0), panel_codes, first)

    def gather_panel(partial):
        chunk = lax.psum_scatter(partial, "col", scatter_dimension=0, tiled=True)
        raw_rows = lax.all_gather(chunk, "col", axis=0, tiled=True)
        chunk, raw_rows = lax.optimization_barrier((chunk, raw_rows))
        return lax.all_gather(chunk, "row", axis=0), raw_rows

    panel_depth = (capacity * 5 + 7) // 8
    panel_in = send_panel(tiles, valid_rows, panel_depth)

    units = side // UNIT
    length = capacity * units
    width = length * 41 // 64
    pass_on = length * 13 // 32
    half_count = device_count // 2
    half_base = device_now // half_count * half_count
    unit_rows = rows_blocks * units
    local_codes = unit_rows * cols_blocks
    own_target, own_code = own(target), own(code)
    own_position = own(position)
    filled = (valid_rows + UNIT - 1) // UNIT
    key = (own_target * rows_blocks * cols_blocks + own_code) * per_device + own_position
    before = key[None, :] < key[:, None]
    together = own_target[None, :] == own_target[:, None]
    base = jnp.sum(jnp.where(before & together, filled[None, :], 0), axis=1)
    order = jnp.sum(before, axis=1)
    unit_code = (own_target * unit_rows + own_code // cols_blocks * units) * cols_blocks
    unit_code += own_code % cols_blocks
    meta = jnp.stack([own_position, own_target, base, filled, unit_code, valid_rows])
    meta = jnp.sum(
        jnp.where(order[None, :, None] == jnp.arange(per_device), meta[:, :, None], 0), axis=1
    )
    to_device = own_target[:, None] == jnp.arange(device_count)
    load = jnp.sum(jnp.where(to_device, filled[:, None], 0), axis=0).reshape(2, half_count)
    empty = load == 0
    empty_rank = jnp.cumsum(empty, axis=1) - 1
    device_ids = jnp.arange(device_count).reshape(2, half_count)
    listed = (empty[:, :, None]) & (empty_rank[:, :, None] == jnp.arange(half_count))
    empties = jnp.sum(jnp.where(listed, device_ids[:, :, None], 0), axis=1)
    free = jnp.sum(empty, axis=1)
    left = jnp.sum(jnp.maximum(load - width, 0), axis=1)
    failed = jnp.any(left > free * width) | jnp.any(own(in_panel) & (own(panel_rank) >= panel_depth))
    counts = jnp.concatenate([jnp.sum(own_target < half_count)[None], free]).astype(jnp.int32)
    outgoing, sent_codes = spread(
        tiles, meta.astype(jnp.int32), empties.astype(jnp.int32), counts,
        device_count, width, length, cols_blocks,
    )

    partial = sum_panel(front, panel_in, panel_depth)
    partial, sent_codes = lax.optimization_barrier((partial, sent_codes))
    gathered, raw_rows = gather_panel(partial)
    got = lax.all_to_all(sent_codes[:, :width], ("row", "col"), 0, 0, tiled=True)
    outgoing, got = lax.optimization_barrier((outgoing, got))
    arrived = lax.all_to_all(outgoing, ("row", "col"), 0, 0, tiled=True)
    got_target = got // local_codes
    local = got % local_codes
    mine = (got >= 0) & (got_target == device_now)
    direct_codes = jnp.where(mine, local, -1)
    steps = jnp.arange(width)
    opening = (local // cols_blocks % units == 0) | jnp.logical_not(mine)
    later = (steps[None, :] > steps[:, None]) & opening[:, None, :]
    direct_runs = jnp.min(jnp.where(later, steps, width), axis=2) - steps
    total_units = device_count * width
    passing = ((got >= 0) & (got_target != device_now)).reshape(-1)
    flat_key = jnp.where(passing, got.reshape(-1) * total_units + jnp.arange(total_units), -1)
    flat_target = jnp.where(passing, got_target.reshape(-1), -1)
    rank = jnp.sum(
        (flat_target[None, :] == flat_target[:, None]) & (flat_key[None, :] < flat_key[:, None]), axis=1
    )
    failed = failed | jnp.any(passing & (rank >= pass_on))
    relay_slot = jnp.where(
        passing & (rank < pass_on), (flat_target - half_base) * pass_on + rank, -1
    )
    picked = relay_slot[:, None] == jnp.arange(half_count * pass_on)
    relay_codes = jnp.sum(jnp.where(picked, local.reshape(-1)[:, None] + 1, 0), axis=0) - 1
    notes = jnp.zeros((2, half_count, pass_on + 1), jnp.int32)
    notes = lax.dynamic_update_slice(
        notes, relay_codes.reshape(1, half_count, pass_on).astype(jnp.int32), (device_now // half_count, 0, 0)
    )
    notes = notes.at[:, :, pass_on].set(failed.astype(jnp.int32))
    def chain(gathered, raw_rows):
        diagonal = jnp.where(row_now == 0, raw_rows[:TOTAL], jnp.eye(TOTAL, dtype=jnp.float32))
        lower, inverse = factor(diagonal)
        known = jnp.where(row_now == 0, inverse, 0.0)
        gathered, known = lax.optimization_barrier((gathered, known))
        share = col_count // row_count
        chunks = []
        for turn in range(row_count):
            pairs = [
                (h * row_count + i, (i + turn) % row_count * share + h)
                for h in range(share)
                for i in range(row_count)
            ]
            sending = lax.dynamic_index_in_dim(gathered, (col_now + turn) % row_count, 0, keepdims=False)
            chunks.append(lax.ppermute(sending, "col", pairs))
        order = (col_now // share - jnp.arange(row_count)) % row_count
        inverse = known
        for other in range(1, row_count):
            inverse += lax.ppermute(known, "row", [(0, other)])
        return known, inverse, jnp.stack(chunks), order.astype(jnp.int32), lower

    def solve(raw_rows, inverse, chunks, order):
        rows = solve_rows(raw_rows, inverse)
        return rows, solve_cols(chunks, order, inverse)

    known, inverse, chunks, order, lower = chain(gathered, raw_rows)
    notes, arrived, known = lax.optimization_barrier((notes, arrived, known))
    notes = lax.all_to_all(
        notes.reshape(device_count, pass_on + 1), ("row", "col"), 0, 0, tiled=True
    )
    relay_codes = lax.dynamic_slice_in_dim(notes, half_base, half_count, 0)[:, :pass_on]
    relay_slot = relay_slot.reshape(device_count, width)

    flat = relay_codes.reshape(-1)
    unit_row, relay_col = flat // cols_blocks, flat % cols_blocks
    wanted = (flat >= 0) & ((row_now > 0) | (unit_row >= TOTAL // UNIT))
    wanted &= (col_now > 0) | (relay_col >= PANELS)
    relay_block = unit_row // units * cols_blocks + relay_col
    relay_key = jnp.where(wanted, relay_block * units + unit_row % units, local_codes)
    relay_key = relay_key * flat.shape[0] + jnp.arange(flat.shape[0])
    relay_order = jnp.sum(relay_key[None, :] < relay_key[:, None], axis=1)
    listing = jnp.stack([relay_block, unit_row % units, jnp.arange(flat.shape[0])])
    at_order = relay_order[None, :, None] == jnp.arange(flat.shape[0])
    listing = jnp.sum(jnp.where(at_order, listing[:, :, None], 0), axis=1).astype(jnp.int32)
    listing = [*listing, jnp.sum(wanted).astype(jnp.int32).reshape(1)]

    passed = relay(relay_slot, arrived, half_count * pass_on)
    passed, notes, inverse, chunks = lax.optimization_barrier((passed, notes, inverse, chunks))
    rows, cols = solve(raw_rows, inverse, chunks, order)
    too_full = jnp.any(notes[:, pass_on] != 0)
    halves = [list(range(half_count)), list(range(half_count, device_count))]
    passed = lax.all_to_all(
        passed.reshape(half_count, pass_on, UNIT, side), ("row", "col"), 0, 0,
        axis_index_groups=halves, tiled=True,
    )
    partial = finish(front, rows, cols, lower, arrived, direct_codes, direct_runs, place, cols_blocks)
    result = add_relayed(partial, passed.reshape(-1, UNIT, side), listing, cols_blocks)

    def padded():
        partial = sum_panel(front, send_panel(tiles, valid_rows, capacity), capacity)
        gathered, raw_rows = gather_panel(partial)
        order = (target * rows_blocks * cols_blocks + code) * per_device + position
        ranking = jnp.sum(
            (target[:, :, None] == target[:, None, :]) & (order[:, None, :] < order[:, :, None]), axis=2
        )
        slot = own(target) * capacity + own(ranking)
        here = (target == device_now)[:, :, None] & (ranking[:, :, None] == jnp.arange(capacity))
        codes = jnp.sum(jnp.where(here, code[:, :, None] + 1, 0), axis=1) - 1
        packed = pack(tiles, slot, valid_rows, device_count * capacity)
        arrived = lax.all_to_all(
            packed.reshape(device_count, capacity, side, side), ("row", "col"), 0, 0, tiled=True
        )
        _, inverse, chunks, order, lower = chain(gathered, raw_rows)
        rows, cols = solve(raw_rows, inverse, chunks, order)
        return finish(
            front, rows, cols, lower, arrived, codes, jnp.ones_like(codes), place, cols_blocks
        )

    def unfinished(state):
        return state[0] > 0

    def redo(state):
        return jnp.int32(0), padded()

    return lax.while_loop(unfinished, redo, (too_full.astype(jnp.int32), result))[1]


def solution(mesh):
    placed = (P("row", "col"), P(("row", "col"), None, None), P(), P(("row", "col")))
    return jax.shard_map(
        body, mesh=mesh, in_specs=placed, out_specs=P("row", "col"), check_vma=False
    )
```

```python
import functools

import jax
import jax.numpy as jnp
from jax import lax
from jax.experimental import pallas as pl
from jax.experimental.pallas import tpu as pltpu
from jax.sharding import PartitionSpec as P

NB = 128
PANELS = 2
TOTAL = NB * PANELS
MIB = 1 << 20
UNIT = 8


precise = lax.Precision.HIGHEST


def dot_nt(a, b, precision=precise):
    return lax.dot_general(
        a, b, (((1,), (1,)), ((), ())), precision=precision, preferred_element_type=jnp.float32
    )


def pack_kernel(slot_ref, valid_ref, tiles_ref, out_ref, buf, sem_in, sem_out):
    count, side = tiles_ref.shape[0], tiles_ref.shape[1]

    def fetch(t):
        return pltpu.make_async_copy(tiles_ref.at[t], buf.at[t], sem_in.at[t])

    def store(t):
        return pltpu.make_async_copy(buf.at[t], out_ref.at[jnp.maximum(slot_ref[t], 0)], sem_out.at[t])

    def each(act):
        @pl.loop(0, count)
        def _(t):
            @pl.when(slot_ref[t] >= 0)
            def _():
                act(t)

    def mask(t):
        fetch(t).wait()
        rows = lax.broadcasted_iota(jnp.int32, (side, side), 0)
        buf[t] = jnp.where(rows < valid_ref[t], buf[t], 0.0)
        store(t).start()

    each(lambda t: fetch(t).start())
    each(mask)
    each(lambda t: store(t).wait())


def pack(tiles, slots, valid, n_slots):
    count, side = tiles.shape[0], tiles.shape[1]
    smem = pl.BlockSpec(memory_space=pltpu.SMEM)
    return pl.pallas_call(
        pack_kernel,
        out_shape=jax.ShapeDtypeStruct((n_slots, side, side), jnp.float32),
        in_specs=[smem, smem, pl.BlockSpec(memory_space=pl.ANY)],
        out_specs=pl.BlockSpec(memory_space=pl.ANY),
        scratch_shapes=[
            pltpu.VMEM((count, side, side), jnp.float32),
            pltpu.SemaphoreType.DMA((count,)),
            pltpu.SemaphoreType.DMA((count,)),
        ],
        compiler_params=pltpu.CompilerParams(vmem_limit_bytes=24 * MIB),
    )(slots, valid, tiles)


def spread_kernel(
    width, stride, meta_ref, empty_ref, count_ref, tiles_ref, out_ref, code_ref, stage, sem
):
    count, units = tiles_ref.shape[0], tiles_ref.shape[1]
    devices, length = code_ref.shape

    @pl.loop(0, devices)
    def _(d):
        for k in range(length):
            code_ref[d, k] = -1

    @pl.loop(0, count)
    def _(i):
        tile, target, base = meta_ref[0, i], meta_ref[1, i], meta_ref[2, i]
        filled, code, valid = meta_ref[3, i], meta_ref[4, i], meta_ref[5, i]
        shape = tiles_ref.shape[1:]
        rows = lax.broadcasted_iota(jnp.int32, shape, 0) * shape[1]
        rows += lax.broadcasted_iota(jnp.int32, shape, 1)
        stage[target, pl.ds(base, units)] = jnp.where(rows < valid, tiles_ref[tile], 0.0)
        for u in range(units):
            code_ref[target, base + u] = jnp.where(u < filled, code + u * stride, -1)

    for half in range(2):
        first = 0 if half == 0 else count_ref[0]
        last = count_ref[0] if half == 0 else count
        free = count_ref[1 + half]

        def each_tile(i, carry):
            target, base, filled = meta_ref[1, i], meta_ref[2, i], meta_ref[3, i]

            def each_unit(q, carry):
                at, depth = carry
                relay = empty_ref[half, at]
                place = jnp.minimum(depth, width - 1)
                stage[relay, place] = stage[target, q]
                code_ref[relay, place] = code_ref[target, q]
                wrap = at + 1 >= free
                return jnp.where(wrap, 0, at + 1), jnp.where(wrap, depth + 1, depth)

            return lax.fori_loop(jnp.maximum(base, width), base + filled, each_unit, carry)

        lax.fori_loop(first, last, each_tile, (jnp.int32(0), jnp.int32(0)))

    copy = pltpu.make_async_copy(stage.at[:, pl.ds(0, width)], out_ref, sem)
    copy.start()
    copy.wait()


def spread(tiles, meta, empties, counts, devices, width, length, stride):
    count, side = tiles.shape[0], tiles.shape[1]
    units = side // UNIT
    smem = pl.BlockSpec(memory_space=pltpu.SMEM)
    return pl.pallas_call(
        functools.partial(spread_kernel, width, stride),
        out_shape=[
            jax.ShapeDtypeStruct((devices, width, UNIT, side), jnp.float32),
            jax.ShapeDtypeStruct((devices, length), jnp.int32),
        ],
        in_specs=[smem, smem, smem, pl.BlockSpec(memory_space=pltpu.VMEM)],
        out_specs=[pl.BlockSpec(memory_space=pl.ANY), smem],
        scratch_shapes=[
            pltpu.VMEM((devices, length, UNIT, side), jnp.float32),
            pltpu.SemaphoreType.DMA,
        ],
        compiler_params=pltpu.CompilerParams(vmem_limit_bytes=40 * MIB),
    )(meta, empties, counts, tiles.reshape(count, units, UNIT, side))


def relay_kernel(slot_ref, arrived_ref, out_ref):
    devices, width = slot_ref.shape

    @pl.loop(0, devices)
    def _(s):
        def more(k):
            return (k < width) & (slot_ref[s, jnp.minimum(k, width - 1)] >= 0)

        def move(k):
            out_ref[slot_ref[s, k]] = arrived_ref[s, k]
            return k + 1

        lax.while_loop(more, move, jnp.int32(0))


def relay(slots, arrived, length):
    vmem = pl.BlockSpec(memory_space=pltpu.VMEM)
    return pl.pallas_call(
        relay_kernel,
        out_shape=jax.ShapeDtypeStruct((length,) + arrived.shape[2:], jnp.float32),
        in_specs=[pl.BlockSpec(memory_space=pltpu.SMEM), vmem],
        out_specs=vmem,
        compiler_params=pltpu.CompilerParams(vmem_limit_bytes=40 * MIB),
    )(slots, arrived)


def add_kernel(
    cols_blocks, block_ref, unit_ref, index_ref, count_ref, partial_ref, arrived_ref, out_ref, buf,
    group_start, sem_in, sem_out
):
    slots, side = buf.shape[0], buf.shape[1]
    unit = arrived_ref.shape[1]
    ahead = slots // 2
    count = count_ref[0]

    def listed(i, carry):
        groups, last = carry
        block = block_ref[i]
        fresh = block != last

        @pl.when(fresh)
        def _():
            group_start[groups] = i

        return jnp.where(fresh, groups + 1, groups), block

    groups, _ = lax.fori_loop(0, count, listed, (jnp.int32(0), jnp.int32(-1)))
    group_start[groups] = count

    def window(g):
        block = block_ref[group_start[g]]
        rows = pl.ds(pl.multiple_of(block // cols_blocks * side, side), side)
        columns = pl.ds(pl.multiple_of(block % cols_blocks * side, side), side)
        return out_ref.at[rows, columns]

    def fetch(g):
        at = g % slots
        return pltpu.make_async_copy(window(g), buf.at[at], sem_in.at[at])

    def store(g):
        at = g % slots
        return pltpu.make_async_copy(buf.at[at], window(g), sem_out.at[at])

    @pl.loop(0, jnp.minimum(groups, ahead))
    def _(g):
        fetch(g).start()

    @pl.loop(0, groups)
    def _(g):
        @pl.when(g + ahead < groups)
        def _():
            @pl.when(g >= ahead)
            def _():
                store(g - ahead).wait()

            fetch(g + ahead).start()

        fetch(g).wait()

        @pl.loop(group_start[g], group_start[g + 1])
        def _(i):
            rows = pl.ds(pl.multiple_of(unit_ref[i] * unit, unit), unit)
            buf[g % slots, rows] += arrived_ref[index_ref[i]]

        store(g).start()

    @pl.loop(jnp.maximum(groups - slots, 0), groups)
    def _(g):
        store(g).wait()


def add_relayed(partial, arrived, listing, cols_blocks):
    row_len, col_len = partial.shape
    unit, side = arrived.shape[1:]
    smem = pl.BlockSpec(memory_space=pltpu.SMEM)
    hbm = pl.BlockSpec(memory_space=pl.ANY)
    return pl.pallas_call(
        functools.partial(add_kernel, cols_blocks),
        out_shape=jax.ShapeDtypeStruct((row_len, col_len), jnp.float32),
        in_specs=[smem, smem, smem, smem, hbm, pl.BlockSpec(memory_space=pltpu.VMEM)],
        out_specs=hbm,
        scratch_shapes=[
            pltpu.VMEM((16, side, side), jnp.float32),
            pltpu.SMEM((arrived.shape[0] + 1,), jnp.int32),
            pltpu.SemaphoreType.DMA((16,)),
            pltpu.SemaphoreType.DMA((16,)),
        ],
        input_output_aliases={4: 0},
        compiler_params=pltpu.CompilerParams(vmem_limit_bytes=24 * MIB),
    )(*listing, partial, arrived)


def panel_kernel(code_ref, first_ref, front_ref, arrived_ref, out_ref):
    side = arrived_ref.shape[1]

    @pl.when(first_ref[0] == 1)
    def _():
        out_ref[...] = front_ref[...]

    @pl.when(first_ref[0] == 0)
    def _():
        out_ref[...] = jnp.zeros_like(out_ref)

    @pl.loop(0, arrived_ref.shape[0])
    def _(k):
        code = code_ref[k]
        for part in range(PANELS):

            @pl.when((code >= 0) & (code % PANELS == part))
            def _():
                rows = pl.ds(pl.multiple_of(code // PANELS * side, side), side)
                out_ref[rows, part * side : (part + 1) * side] += arrived_ref[k]


def raw_panel(front, arrived, codes, first):
    row_len = front.shape[0]
    smem = pl.BlockSpec(memory_space=pltpu.SMEM)
    return pl.pallas_call(
        panel_kernel,
        grid=(1,),
        out_shape=jax.ShapeDtypeStruct((row_len, TOTAL), jnp.float32),
        in_specs=[
            smem,
            smem,
            pl.BlockSpec((row_len, TOTAL), lambda i: (0, 0)),
            pl.BlockSpec(arrived.shape, lambda i: (0, 0, 0)),
        ],
        out_specs=pl.BlockSpec((row_len, TOTAL), lambda i: (0, 0)),
        compiler_params=pltpu.CompilerParams(vmem_limit_bytes=40 * MIB),
    )(codes, first, front, arrived)


def split(value):
    high = value.astype(jnp.bfloat16)
    low = (value - high.astype(jnp.float32)).astype(jnp.bfloat16)
    return high, low


def rows_kernel(raw_ref, inverse_ref, out_ref, parts_ref):
    solved = dot_nt(raw_ref[...], inverse_ref[...])
    out_ref[...] = solved
    high, low = split(solved)
    parts_ref[:, :TOTAL] = high
    parts_ref[:, TOTAL : 2 * TOTAL] = high
    parts_ref[:, 2 * TOTAL :] = low


def solve_rows(raw, inverse):
    length = raw.shape[0]
    step = min(512, length)
    block = pl.BlockSpec((step, TOTAL), lambda i: (i, 0))
    return pl.pallas_call(
        rows_kernel,
        grid=(length // step,),
        out_shape=[
            jax.ShapeDtypeStruct((length, TOTAL), jnp.float32),
            jax.ShapeDtypeStruct((length, 3 * TOTAL), jnp.bfloat16),
        ],
        in_specs=[block, pl.BlockSpec((TOTAL, TOTAL), lambda i: (0, 0))],
        out_specs=[block, pl.BlockSpec((step, 3 * TOTAL), lambda i: (i, 0))],
        compiler_params=pltpu.CompilerParams(vmem_limit_bytes=24 * MIB),
    )(raw, inverse)


def cols_kernel(order_ref, raw_ref, inverse_ref, out_ref, parts_ref):
    solved = dot_nt(inverse_ref[...], raw_ref[0])
    out_ref[...] = solved
    high, low = split(solved)
    parts_ref[:TOTAL] = high
    parts_ref[TOTAL : 2 * TOTAL] = low
    parts_ref[2 * TOTAL :] = high


def solve_cols(chunks, order, inverse):
    count, step = chunks.shape[:2]
    length = count * step
    grid_spec = pltpu.PrefetchScalarGridSpec(
        num_scalar_prefetch=1,
        grid=(count,),
        in_specs=[
            pl.BlockSpec((1, step, TOTAL), lambda i, order: (order[i], 0, 0)),
            pl.BlockSpec((TOTAL, TOTAL), lambda i, order: (0, 0)),
        ],
        out_specs=[
            pl.BlockSpec((TOTAL, step), lambda i, order: (0, i)),
            pl.BlockSpec((3 * TOTAL, step), lambda i, order: (0, i)),
        ],
    )
    return pl.pallas_call(
        cols_kernel,
        grid_spec=grid_spec,
        out_shape=[
            jax.ShapeDtypeStruct((TOTAL, length), jnp.float32),
            jax.ShapeDtypeStruct((3 * TOTAL, length), jnp.bfloat16),
        ],
        compiler_params=pltpu.CompilerParams(vmem_limit_bytes=24 * MIB),
    )(order, chunks, inverse)


def final_kernel(
    cols_blocks, runs, code_ref, run_ref, place_ref, front_ref, rows_ref, rows_parts, cols_ref, cols_parts,
    lower_ref, arrived_ref, out_ref, cursor
):
    step = pl.program_id(0)
    sources, capacity = code_ref.shape
    height, width = front_ref.shape
    unit, side = arrived_ref.shape[2:]
    per_step = height // unit

    @pl.when(step == 0)
    def _():
        for s in range(sources):
            cursor[s] = 0

    chunk = min(512, width)
    for start in range(0, width, chunk):
        at = slice(start, start + chunk)
        change = jnp.dot(rows_parts[...], cols_parts[:, at], preferred_element_type=jnp.float32)
        out_ref[:, at] = front_ref[:, at] - change

    edge = (step + 1) * per_step * cols_blocks

    @pl.loop(0, sources)
    def _(s):
        def more(k):
            code = code_ref[s, jnp.minimum(k, capacity - 1)]
            return (k < capacity) & (code >= 0) & (code < edge)

        def add(k):
            code = code_ref[s, k]
            length = run_ref[s, k]
            unit_row = code // cols_blocks - step * per_step
            columns = pl.ds(pl.multiple_of(code % cols_blocks * side, side), side)
            for run in runs:
                skipped = length // (2 * run) * (2 * run)

                @pl.when(length // run % 2 == 1)
                def _():
                    rows = pl.ds(pl.multiple_of((unit_row + skipped) * unit, unit), run * unit)
                    block = arrived_ref[s, pl.ds(k + skipped, run)]
                    out_ref[rows, columns] += block.reshape(run * unit, side)

            return k + length

        cursor[s] = lax.while_loop(more, add, cursor[s])

    top = (place_ref[0] == 0) & (step == 0)

    @pl.when(top)
    def _():
        out_ref[...] = cols_ref[...]

    @pl.when(place_ref[1] == 0)
    def _():
        out_ref[:, :TOTAL] = jnp.where(top, lower_ref[...], rows_ref[...])


def finish(front, rows, cols, lower, arrived, codes, lengths, place, cols_blocks):
    row_len, col_len = front.shape
    height = TOTAL
    smem = pl.BlockSpec(memory_space=pltpu.SMEM)
    block = pl.BlockSpec((height, TOTAL), lambda i: (i, 0))
    parts = pl.BlockSpec((height, 3 * TOTAL), lambda i: (i, 0))
    wide = pl.BlockSpec((height, col_len), lambda i: (i, 0))
    whole = pl.BlockSpec((TOTAL, col_len), lambda i: (0, 0))
    whole_parts = pl.BlockSpec((3 * TOTAL, col_len), lambda i: (0, 0))
    runs = (16, 8, 4, 2, 1) if arrived.shape[2] == UNIT else (1,)
    return pl.pallas_call(
        functools.partial(final_kernel, cols_blocks, runs),
        grid=(row_len // height,),
        out_shape=jax.ShapeDtypeStruct((row_len, col_len), jnp.float32),
        in_specs=[
            smem, smem, smem, wide, block, parts, whole, whole_parts,
            pl.BlockSpec((TOTAL, TOTAL), lambda i: (0, 0)),
            pl.BlockSpec(memory_space=pltpu.VMEM),
        ],
        out_specs=wide,
        scratch_shapes=[pltpu.SMEM((codes.shape[0],), jnp.int32)],
        compiler_params=pltpu.CompilerParams(vmem_limit_bytes=56 * MIB),
    )(codes, lengths, place, front, *rows, *cols, lower, arrived)


def factor(diagonal):
    def lower_of(block):
        return jnp.linalg.cholesky(jnp.tril(block) + jnp.tril(block, -1).T)

    def inverse_of(block):
        return jax.scipy.linalg.solve_triangular(block, jnp.eye(NB, dtype=jnp.float32), lower=True)

    first = lower_of(diagonal[:NB, :NB])
    first_inverse = inverse_of(first)
    below = dot_nt(diagonal[NB:, :NB], first_inverse)
    second = lower_of(diagonal[NB:, NB:] - dot_nt(below, below))
    second_inverse = inverse_of(second)
    corner = -jnp.dot(second_inverse, jnp.dot(below, first_inverse, precision=precise), precision=precise)
    zero = jnp.zeros((NB, NB), jnp.float32)
    return jnp.block([[first, zero], [below, second]]), jnp.block([[first_inverse, zero], [corner, second_inverse]])


def body(front, tiles, tile_block, valid_rows):
    row_len, col_len = front.shape
    row_count = lax.axis_size("row")
    col_count = lax.axis_size("col")
    device_count = row_count * col_count
    per_device = tiles.shape[0]
    side = tiles.shape[1]
    capacity = 2 * per_device // device_count
    rows_blocks = row_len // side
    cols_blocks = col_len // side
    row_now = lax.axis_index("row")
    col_now = lax.axis_index("col")
    device_now = row_now * col_count + col_now

    block_row = tile_block[0].reshape(device_count, per_device)
    block_col = tile_block[1].reshape(device_count, per_device)
    target_row = block_row // rows_blocks
    target = target_row * col_count + block_col // cols_blocks
    code = block_row % rows_blocks * cols_blocks + block_col % cols_blocks
    position = lax.broadcasted_iota(jnp.int32, target.shape, 1)
    place = jnp.stack([row_now, col_now]).astype(jnp.int32)

    def own(values):
        return lax.dynamic_index_in_dim(values, device_now, 0, keepdims=False)

    in_panel = block_col < PANELS
    panel_key = jnp.where(in_panel, target_row, -1)
    panel_rank = jnp.sum(
        (panel_key[:, :, None] == panel_key[:, None, :]) & (position[:, None, :] < position[:, :, None]),
        axis=2,
    )
    same_col = lax.dynamic_index_in_dim(
        jnp.stack([panel_key, panel_rank, code]).reshape(3, row_count, col_count, per_device),
        col_now, 2, keepdims=False,
    )

    def send_panel(tiles, valid_rows, depth):
        ahead = (own(target_row) - row_now) % row_count
        fits = own(in_panel) & (own(panel_rank) < depth)
        panel_slot = jnp.where(fits, ahead * depth + own(panel_rank), -1)
        panel_out = pack(tiles, panel_slot, valid_rows, row_count * depth)
        panel_in = [panel_out[:depth]]
        for shift in range(1, row_count):
            sending = panel_out[shift * depth : (shift + 1) * depth]
            turn = [(r, (r + shift) % row_count) for r in range(row_count)]
            panel_in.append(lax.ppermute(sending, "row", turn))
        return panel_in

    def sum_panel(front, panel_in, depth):
        fits = (same_col[0] == row_now)[:, :, None] & (same_col[1][:, :, None] == jnp.arange(depth))
        panel_code = same_col[2] // cols_blocks * PANELS + same_col[2] % cols_blocks
        panel_codes = jnp.sum(jnp.where(fits, panel_code[:, :, None] + 1, 0), axis=1) - 1
        by_shift = (row_now - jnp.arange(row_count)) % row_count
        panel_codes = jnp.take(panel_codes, by_shift, axis=0).reshape(-1)
        first = (col_now == 0).astype(jnp.int32).reshape(1)
        return raw_panel(front, jnp.concatenate(panel_in, 0), panel_codes, first)

    def gather_panel(partial):
        chunk = lax.psum_scatter(partial, "col", scatter_dimension=0, tiled=True)
        raw_rows = lax.all_gather(chunk, "col", axis=0, tiled=True)
        chunk, _ = lax.optimization_barrier((chunk, raw_rows[:8, :NB]))
        return lax.all_gather(chunk, "row", axis=0), raw_rows

    panel_depth = (capacity * 5 + 7) // 8
    panel_in = send_panel(tiles, valid_rows, panel_depth)

    units = side // UNIT
    length = capacity * units
    width = length * 41 // 64
    pass_on = length * 13 // 32
    half_count = device_count // 2
    half_base = device_now // half_count * half_count
    unit_rows = rows_blocks * units
    local_codes = unit_rows * cols_blocks
    own_target, own_code = own(target), own(code)
    own_position = own(position)
    filled = (valid_rows + UNIT - 1) // UNIT
    key = (own_target * rows_blocks * cols_blocks + own_code) * per_device + own_position
    before = key[None, :] < key[:, None]
    together = own_target[None, :] == own_target[:, None]
    base = jnp.sum(jnp.where(before & together, filled[None, :], 0), axis=1)
    order = jnp.sum(before, axis=1)
    unit_code = (own_target * unit_rows + own_code // cols_blocks * units) * cols_blocks
    unit_code += own_code % cols_blocks
    meta = jnp.stack([own_position, own_target, base, filled, unit_code, valid_rows])
    meta = jnp.sum(
        jnp.where(order[None, :, None] == jnp.arange(per_device), meta[:, :, None], 0), axis=1
    )
    to_device = own_target[:, None] == jnp.arange(device_count)
    load = jnp.sum(jnp.where(to_device, filled[:, None], 0), axis=0).reshape(2, half_count)
    empty = load == 0
    empty_rank = jnp.cumsum(empty, axis=1) - 1
    device_ids = jnp.arange(device_count).reshape(2, half_count)
    listed = (empty[:, :, None]) & (empty_rank[:, :, None] == jnp.arange(half_count))
    empties = jnp.sum(jnp.where(listed, device_ids[:, :, None], 0), axis=1)
    free = jnp.sum(empty, axis=1)
    left = jnp.sum(jnp.maximum(load - width, 0), axis=1)
    failed = jnp.any(left > free * width) | jnp.any(own(in_panel) & (own(panel_rank) >= panel_depth))
    counts = jnp.concatenate([jnp.sum(own_target < half_count)[None], free]).astype(jnp.int32)
    outgoing, sent_codes = spread(
        tiles, meta.astype(jnp.int32), empties.astype(jnp.int32), counts,
        device_count, width, length, cols_blocks,
    )

    partial = sum_panel(front, panel_in, panel_depth)
    partial, sent_codes = lax.optimization_barrier((partial, sent_codes))
    gathered, raw_rows = gather_panel(partial)
    got = lax.all_to_all(sent_codes[:, :width], ("row", "col"), 0, 0, tiled=True)
    outgoing, got = lax.optimization_barrier((outgoing, got))
    arrived = lax.all_to_all(outgoing, ("row", "col"), 0, 0, tiled=True)
    got_target = got // local_codes
    local = got % local_codes
    mine = (got >= 0) & (got_target == device_now)
    direct_codes = jnp.where(mine, local, -1)
    steps = jnp.arange(width)
    opening = (local // cols_blocks % units == 0) | jnp.logical_not(mine)
    later = (steps[None, :] > steps[:, None]) & opening[:, None, :]
    direct_runs = jnp.min(jnp.where(later, steps, width), axis=2) - steps
    total_units = device_count * width
    passing = ((got >= 0) & (got_target != device_now)).reshape(-1)
    flat_key = jnp.where(passing, got.reshape(-1) * total_units + jnp.arange(total_units), -1)
    flat_target = jnp.where(passing, got_target.reshape(-1), -1)
    rank = jnp.sum(
        (flat_target[None, :] == flat_target[:, None]) & (flat_key[None, :] < flat_key[:, None]), axis=1
    )
    failed = failed | jnp.any(passing & (rank >= pass_on))
    relay_slot = jnp.where(
        passing & (rank < pass_on), (flat_target - half_base) * pass_on + rank, -1
    )
    picked = relay_slot[:, None] == jnp.arange(half_count * pass_on)
    relay_codes = jnp.sum(jnp.where(picked, local.reshape(-1)[:, None] + 1, 0), axis=0) - 1
    notes = jnp.zeros((2, half_count, pass_on + 1), jnp.int32)
    notes = lax.dynamic_update_slice(
        notes, relay_codes.reshape(1, half_count, pass_on).astype(jnp.int32), (device_now // half_count, 0, 0)
    )
    notes = notes.at[:, :, pass_on].set(failed.astype(jnp.int32))
    def chain(gathered, raw_rows, tables):
        diagonal = jnp.where(row_now == 0, raw_rows[:TOTAL], jnp.eye(TOTAL, dtype=jnp.float32))
        diagonal, tables = lax.optimization_barrier((diagonal, tables))
        lower, inverse = factor(diagonal)
        known = jnp.where(row_now == 0, inverse, 0.0)
        gathered, known = lax.optimization_barrier((gathered, known))
        share = col_count // row_count
        chunks = []
        for turn in range(row_count):
            pairs = [
                (h * row_count + i, (i + turn) % row_count * share + h)
                for h in range(share)
                for i in range(row_count)
            ]
            sending = lax.dynamic_index_in_dim(gathered, (col_now + turn) % row_count, 0, keepdims=False)
            chunks.append(lax.ppermute(sending, "col", pairs))
        order = (col_now // share - jnp.arange(row_count)) % row_count
        inverse = known
        for other in range(1, row_count):
            inverse += lax.ppermute(known, "row", [(0, other)])
        return known, inverse, chunks, order.astype(jnp.int32), lower, tables

    def solve(raw_rows, inverse, chunks, order):
        rows = solve_rows(raw_rows, inverse)
        return rows, solve_cols(jnp.stack(chunks), order, inverse)

    relay_slot = relay_slot.reshape(device_count, width)
    tables = (notes, relay_slot, direct_codes, direct_runs)
    known, inverse, chunks, order, lower, tables = chain(gathered, raw_rows, tables)
    notes, relay_slot, direct_codes, direct_runs = tables
    notes, arrived, known = lax.optimization_barrier((notes, arrived, known))
    notes = lax.all_to_all(
        notes.reshape(device_count, pass_on + 1), ("row", "col"), 0, 0, tiled=True
    )
    relay_codes = lax.dynamic_slice_in_dim(notes, half_base, half_count, 0)[:, :pass_on]

    flat = relay_codes.reshape(-1)
    unit_row, relay_col = flat // cols_blocks, flat % cols_blocks
    wanted = (flat >= 0) & ((row_now > 0) | (unit_row >= TOTAL // UNIT))
    wanted &= (col_now > 0) | (relay_col >= PANELS)
    relay_block = unit_row // units * cols_blocks + relay_col
    relay_key = jnp.where(wanted, relay_block * units + unit_row % units, local_codes)
    relay_key = relay_key * flat.shape[0] + jnp.arange(flat.shape[0])
    relay_order = jnp.sum(relay_key[None, :] < relay_key[:, None], axis=1)
    listing = jnp.stack([relay_block, unit_row % units, jnp.arange(flat.shape[0])])
    at_order = relay_order[None, :, None] == jnp.arange(flat.shape[0])
    listing = jnp.sum(jnp.where(at_order, listing[:, :, None], 0), axis=1).astype(jnp.int32)
    listing = [*listing, jnp.sum(wanted).astype(jnp.int32).reshape(1)]

    passed = relay(relay_slot, arrived, half_count * pass_on)
    passed, notes, inverse, chunks = lax.optimization_barrier((passed, notes, inverse, chunks))
    rows, cols = solve(raw_rows, inverse, chunks, order)
    too_full = jnp.any(notes[:, pass_on] != 0)
    halves = [list(range(half_count)), list(range(half_count, device_count))]
    passed = lax.all_to_all(
        passed.reshape(half_count, pass_on, UNIT, side), ("row", "col"), 0, 0,
        axis_index_groups=halves, tiled=True,
    )
    partial = finish(front, rows, cols, lower, arrived, direct_codes, direct_runs, place, cols_blocks)
    result = add_relayed(partial, passed.reshape(-1, UNIT, side), listing, cols_blocks)

    def padded():
        partial = sum_panel(front, send_panel(tiles, valid_rows, capacity), capacity)
        gathered, raw_rows = gather_panel(partial)
        order = (target * rows_blocks * cols_blocks + code) * per_device + position
        ranking = jnp.sum(
            (target[:, :, None] == target[:, None, :]) & (order[:, None, :] < order[:, :, None]), axis=2
        )
        slot = own(target) * capacity + own(ranking)
        here = (target == device_now)[:, :, None] & (ranking[:, :, None] == jnp.arange(capacity))
        codes = jnp.sum(jnp.where(here, code[:, :, None] + 1, 0), axis=1) - 1
        packed = pack(tiles, slot, valid_rows, device_count * capacity)
        arrived = lax.all_to_all(
            packed.reshape(device_count, capacity, side, side), ("row", "col"), 0, 0, tiled=True
        )
        _, inverse, chunks, order, lower, _ = chain(gathered, raw_rows, ())
        rows, cols = solve(raw_rows, inverse, chunks, order)
        return finish(
            front, rows, cols, lower, arrived, codes, jnp.ones_like(codes), place, cols_blocks
        )

    def unfinished(state):
        return state[0] > 0

    def redo(state):
        return jnp.int32(0), padded()

    return lax.while_loop(unfinished, redo, (too_full.astype(jnp.int32), result))[1]


def solution(mesh):
    placed = (P("row", "col"), P(("row", "col"), None, None), P(), P(("row", "col")))
    return jax.shard_map(
        body, mesh=mesh, in_specs=placed, out_specs=P("row", "col"), check_vma=False
    )
```

```python
import functools

import jax
import jax.numpy as jnp
from jax import lax
from jax.experimental import pallas as pl
from jax.experimental.pallas import tpu as pltpu
from jax.sharding import PartitionSpec as P

NB = 128
PANELS = 2
TOTAL = NB * PANELS
MIB = 1 << 20
UNIT = 8


precise = lax.Precision.HIGHEST


def dot_nt(a, b, precision=precise):
    return lax.dot_general(
        a, b, (((1,), (1,)), ((), ())), precision=precision, preferred_element_type=jnp.float32
    )


def pack_kernel(slot_ref, valid_ref, tiles_ref, out_ref, buf, sem_in, sem_out):
    count, side = tiles_ref.shape[0], tiles_ref.shape[1]

    def fetch(t):
        return pltpu.make_async_copy(tiles_ref.at[t], buf.at[t], sem_in.at[t])

    def store(t):
        return pltpu.make_async_copy(buf.at[t], out_ref.at[jnp.maximum(slot_ref[t], 0)], sem_out.at[t])

    def each(act):
        @pl.loop(0, count)
        def _(t):
            @pl.when(slot_ref[t] >= 0)
            def _():
                act(t)

    def mask(t):
        fetch(t).wait()
        rows = lax.broadcasted_iota(jnp.int32, (side, side), 0)
        buf[t] = jnp.where(rows < valid_ref[t], buf[t], 0.0)
        store(t).start()

    each(lambda t: fetch(t).start())
    each(mask)
    each(lambda t: store(t).wait())


def pack(tiles, slots, valid, n_slots):
    count, side = tiles.shape[0], tiles.shape[1]
    smem = pl.BlockSpec(memory_space=pltpu.SMEM)
    return pl.pallas_call(
        pack_kernel,
        out_shape=jax.ShapeDtypeStruct((n_slots, side, side), jnp.float32),
        in_specs=[smem, smem, pl.BlockSpec(memory_space=pl.ANY)],
        out_specs=pl.BlockSpec(memory_space=pl.ANY),
        scratch_shapes=[
            pltpu.VMEM((count, side, side), jnp.float32),
            pltpu.SemaphoreType.DMA((count,)),
            pltpu.SemaphoreType.DMA((count,)),
        ],
        compiler_params=pltpu.CompilerParams(vmem_limit_bytes=24 * MIB),
    )(slots, valid, tiles)


def spread_kernel(
    width, stride, meta_ref, empty_ref, count_ref, tiles_ref, out_ref, code_ref, stage, sem
):
    count, units = tiles_ref.shape[0], tiles_ref.shape[1]
    devices, length = code_ref.shape

    @pl.loop(0, devices)
    def _(d):
        for k in range(length):
            code_ref[d, k] = -1

    @pl.loop(0, count)
    def _(i):
        tile, target, base = meta_ref[0, i], meta_ref[1, i], meta_ref[2, i]
        filled, code, valid = meta_ref[3, i], meta_ref[4, i], meta_ref[5, i]
        shape = tiles_ref.shape[1:]
        rows = lax.broadcasted_iota(jnp.int32, shape, 0) * shape[1]
        rows += lax.broadcasted_iota(jnp.int32, shape, 1)
        stage[target, pl.ds(base, units)] = jnp.where(rows < valid, tiles_ref[tile], 0.0)
        for u in range(units):
            code_ref[target, base + u] = jnp.where(u < filled, code + u * stride, -1)

    for half in range(2):
        first = 0 if half == 0 else count_ref[0]
        last = count_ref[0] if half == 0 else count
        free = count_ref[1 + half]

        def each_tile(i, carry):
            target, base, filled = meta_ref[1, i], meta_ref[2, i], meta_ref[3, i]

            def each_unit(q, carry):
                at, depth = carry
                relay = empty_ref[half, at]
                place = jnp.minimum(depth, width - 1)
                stage[relay, place] = stage[target, q]
                code_ref[relay, place] = code_ref[target, q]
                wrap = at + 1 >= free
                return jnp.where(wrap, 0, at + 1), jnp.where(wrap, depth + 1, depth)

            return lax.fori_loop(jnp.maximum(base, width), base + filled, each_unit, carry)

        lax.fori_loop(first, last, each_tile, (jnp.int32(0), jnp.int32(0)))

    copy = pltpu.make_async_copy(stage.at[:, pl.ds(0, width)], out_ref, sem)
    copy.start()
    copy.wait()


def spread(tiles, meta, empties, counts, devices, width, length, stride):
    count, side = tiles.shape[0], tiles.shape[1]
    units = side // UNIT
    smem = pl.BlockSpec(memory_space=pltpu.SMEM)
    return pl.pallas_call(
        functools.partial(spread_kernel, width, stride),
        out_shape=[
            jax.ShapeDtypeStruct((devices, width, UNIT, side), jnp.float32),
            jax.ShapeDtypeStruct((devices, length), jnp.int32),
        ],
        in_specs=[smem, smem, smem, pl.BlockSpec(memory_space=pltpu.VMEM)],
        out_specs=[pl.BlockSpec(memory_space=pl.ANY), smem],
        scratch_shapes=[
            pltpu.VMEM((devices, length, UNIT, side), jnp.float32),
            pltpu.SemaphoreType.DMA,
        ],
        compiler_params=pltpu.CompilerParams(vmem_limit_bytes=40 * MIB),
    )(meta, empties, counts, tiles.reshape(count, units, UNIT, side))


def relay_kernel(slot_ref, arrived_ref, out_ref):
    devices, width = slot_ref.shape

    @pl.loop(0, devices)
    def _(s):
        def more(k):
            return (k < width) & (slot_ref[s, jnp.minimum(k, width - 1)] >= 0)

        def move(k):
            out_ref[slot_ref[s, k]] = arrived_ref[s, k]
            return k + 1

        lax.while_loop(more, move, jnp.int32(0))


def relay(slots, arrived, length):
    vmem = pl.BlockSpec(memory_space=pltpu.VMEM)
    return pl.pallas_call(
        relay_kernel,
        out_shape=jax.ShapeDtypeStruct((length,) + arrived.shape[2:], jnp.float32),
        in_specs=[pl.BlockSpec(memory_space=pltpu.SMEM), vmem],
        out_specs=vmem,
        compiler_params=pltpu.CompilerParams(vmem_limit_bytes=40 * MIB),
    )(slots, arrived)


def add_kernel(
    cols_blocks, block_ref, unit_ref, index_ref, count_ref, partial_ref, arrived_ref, out_ref, buf,
    group_start, sem_in, sem_out
):
    slots, side = buf.shape[0], buf.shape[1]
    unit = arrived_ref.shape[1]
    ahead = slots // 2
    count = count_ref[0]

    def listed(i, carry):
        groups, last = carry
        block = block_ref[i]
        fresh = block != last

        @pl.when(fresh)
        def _():
            group_start[groups] = i

        return jnp.where(fresh, groups + 1, groups), block

    groups, _ = lax.fori_loop(0, count, listed, (jnp.int32(0), jnp.int32(-1)))
    group_start[groups] = count

    def window(g):
        block = block_ref[group_start[g]]
        rows = pl.ds(pl.multiple_of(block // cols_blocks * side, side), side)
        columns = pl.ds(pl.multiple_of(block % cols_blocks * side, side), side)
        return out_ref.at[rows, columns]

    def fetch(g):
        at = g % slots
        return pltpu.make_async_copy(window(g), buf.at[at], sem_in.at[at])

    def store(g):
        at = g % slots
        return pltpu.make_async_copy(buf.at[at], window(g), sem_out.at[at])

    @pl.loop(0, jnp.minimum(groups, ahead))
    def _(g):
        fetch(g).start()

    @pl.loop(0, groups)
    def _(g):
        @pl.when(g + ahead < groups)
        def _():
            @pl.when(g >= ahead)
            def _():
                store(g - ahead).wait()

            fetch(g + ahead).start()

        fetch(g).wait()

        @pl.loop(group_start[g], group_start[g + 1])
        def _(i):
            rows = pl.ds(pl.multiple_of(unit_ref[i] * unit, unit), unit)
            buf[g % slots, rows] += arrived_ref[index_ref[i]]

        store(g).start()

    @pl.loop(jnp.maximum(groups - slots, 0), groups)
    def _(g):
        store(g).wait()


def add_relayed(partial, arrived, listing, cols_blocks):
    row_len, col_len = partial.shape
    unit, side = arrived.shape[1:]
    smem = pl.BlockSpec(memory_space=pltpu.SMEM)
    hbm = pl.BlockSpec(memory_space=pl.ANY)
    return pl.pallas_call(
        functools.partial(add_kernel, cols_blocks),
        out_shape=jax.ShapeDtypeStruct((row_len, col_len), jnp.float32),
        in_specs=[smem, smem, smem, smem, hbm, pl.BlockSpec(memory_space=pltpu.VMEM)],
        out_specs=hbm,
        scratch_shapes=[
            pltpu.VMEM((16, side, side), jnp.float32),
            pltpu.SMEM((arrived.shape[0] + 1,), jnp.int32),
            pltpu.SemaphoreType.DMA((16,)),
            pltpu.SemaphoreType.DMA((16,)),
        ],
        input_output_aliases={4: 0},
        compiler_params=pltpu.CompilerParams(vmem_limit_bytes=24 * MIB),
    )(*listing, partial, arrived)


def panel_kernel(code_ref, first_ref, front_ref, arrived_ref, out_ref):
    side = arrived_ref.shape[1]

    @pl.when(first_ref[0] == 1)
    def _():
        out_ref[...] = front_ref[...]

    @pl.when(first_ref[0] == 0)
    def _():
        out_ref[...] = jnp.zeros_like(out_ref)

    @pl.loop(0, arrived_ref.shape[0])
    def _(k):
        code = code_ref[k]
        for part in range(PANELS):

            @pl.when((code >= 0) & (code % PANELS == part))
            def _():
                rows = pl.ds(pl.multiple_of(code // PANELS * side, side), side)
                out_ref[rows, part * side : (part + 1) * side] += arrived_ref[k]


def raw_panel(front, arrived, codes, first):
    row_len = front.shape[0]
    smem = pl.BlockSpec(memory_space=pltpu.SMEM)
    return pl.pallas_call(
        panel_kernel,
        grid=(1,),
        out_shape=jax.ShapeDtypeStruct((row_len, TOTAL), jnp.float32),
        in_specs=[
            smem,
            smem,
            pl.BlockSpec((row_len, TOTAL), lambda i: (0, 0)),
            pl.BlockSpec(arrived.shape, lambda i: (0, 0, 0)),
        ],
        out_specs=pl.BlockSpec((row_len, TOTAL), lambda i: (0, 0)),
        compiler_params=pltpu.CompilerParams(vmem_limit_bytes=40 * MIB),
    )(codes, first, front, arrived)


def split(value):
    high = value.astype(jnp.bfloat16)
    low = (value - high.astype(jnp.float32)).astype(jnp.bfloat16)
    return high, low


def rows_kernel(raw_ref, inverse_ref, out_ref, parts_ref):
    solved = dot_nt(raw_ref[...], inverse_ref[...])
    out_ref[...] = solved
    high, low = split(solved)
    parts_ref[:, :TOTAL] = high
    parts_ref[:, TOTAL : 2 * TOTAL] = high
    parts_ref[:, 2 * TOTAL :] = low


def solve_rows(raw, inverse):
    length = raw.shape[0]
    step = min(512, length)
    block = pl.BlockSpec((step, TOTAL), lambda i: (i, 0))
    return pl.pallas_call(
        rows_kernel,
        grid=(length // step,),
        out_shape=[
            jax.ShapeDtypeStruct((length, TOTAL), jnp.float32),
            jax.ShapeDtypeStruct((length, 3 * TOTAL), jnp.bfloat16),
        ],
        in_specs=[block, pl.BlockSpec((TOTAL, TOTAL), lambda i: (0, 0))],
        out_specs=[block, pl.BlockSpec((step, 3 * TOTAL), lambda i: (i, 0))],
        compiler_params=pltpu.CompilerParams(vmem_limit_bytes=24 * MIB),
    )(raw, inverse)


def cols_kernel(order_ref, raw_ref, inverse_ref, out_ref, parts_ref):
    solved = dot_nt(inverse_ref[...], raw_ref[0])
    out_ref[...] = solved
    high, low = split(solved)
    parts_ref[:TOTAL] = high
    parts_ref[TOTAL : 2 * TOTAL] = low
    parts_ref[2 * TOTAL :] = high


def solve_cols(chunks, order, inverse):
    count, step = chunks.shape[:2]
    length = count * step
    grid_spec = pltpu.PrefetchScalarGridSpec(
        num_scalar_prefetch=1,
        grid=(count,),
        in_specs=[
            pl.BlockSpec((1, step, TOTAL), lambda i, order: (order[i], 0, 0)),
            pl.BlockSpec((TOTAL, TOTAL), lambda i, order: (0, 0)),
        ],
        out_specs=[
            pl.BlockSpec((TOTAL, step), lambda i, order: (0, i)),
            pl.BlockSpec((3 * TOTAL, step), lambda i, order: (0, i)),
        ],
    )
    return pl.pallas_call(
        cols_kernel,
        grid_spec=grid_spec,
        out_shape=[
            jax.ShapeDtypeStruct((TOTAL, length), jnp.float32),
            jax.ShapeDtypeStruct((3 * TOTAL, length), jnp.bfloat16),
        ],
        compiler_params=pltpu.CompilerParams(vmem_limit_bytes=24 * MIB),
    )(order, chunks, inverse)


def final_kernel(
    cols_blocks, runs, code_ref, run_ref, place_ref, front_ref, rows_ref, rows_parts, cols_ref, cols_parts,
    lower_ref, arrived_ref, out_ref, cursor
):
    step = pl.program_id(0)
    sources, capacity = code_ref.shape
    height, width = front_ref.shape
    unit, side = arrived_ref.shape[2:]
    per_step = height // unit

    @pl.when(step == 0)
    def _():
        for s in range(sources):
            cursor[s] = 0

    chunk = min(512, width)
    for start in range(0, width, chunk):
        at = slice(start, start + chunk)
        change = jnp.dot(rows_parts[...], cols_parts[:, at], preferred_element_type=jnp.float32)
        out_ref[:, at] = front_ref[:, at] - change

    edge = (step + 1) * per_step * cols_blocks

    @pl.loop(0, sources)
    def _(s):
        def more(k):
            code = code_ref[s, jnp.minimum(k, capacity - 1)]
            return (k < capacity) & (code >= 0) & (code < edge)

        def add(k):
            code = code_ref[s, k]
            length = run_ref[s, k]
            unit_row = code // cols_blocks - step * per_step
            columns = pl.ds(pl.multiple_of(code % cols_blocks * side, side), side)
            for run in runs:
                skipped = length // (2 * run) * (2 * run)

                @pl.when(length // run % 2 == 1)
                def _():
                    rows = pl.ds(pl.multiple_of((unit_row + skipped) * unit, unit), run * unit)
                    block = arrived_ref[s, pl.ds(k + skipped, run)]
                    out_ref[rows, columns] += block.reshape(run * unit, side)

            return k + length

        cursor[s] = lax.while_loop(more, add, cursor[s])

    top = (place_ref[0] == 0) & (step == 0)

    @pl.when(top)
    def _():
        out_ref[...] = cols_ref[...]

    @pl.when(place_ref[1] == 0)
    def _():
        out_ref[:, :TOTAL] = jnp.where(top, lower_ref[...], rows_ref[...])


def finish(front, rows, cols, lower, arrived, codes, lengths, place, cols_blocks):
    row_len, col_len = front.shape
    height = TOTAL
    smem = pl.BlockSpec(memory_space=pltpu.SMEM)
    block = pl.BlockSpec((height, TOTAL), lambda i: (i, 0))
    parts = pl.BlockSpec((height, 3 * TOTAL), lambda i: (i, 0))
    wide = pl.BlockSpec((height, col_len), lambda i: (i, 0))
    whole = pl.BlockSpec((TOTAL, col_len), lambda i: (0, 0))
    whole_parts = pl.BlockSpec((3 * TOTAL, col_len), lambda i: (0, 0))
    runs = (16, 8, 4, 2, 1) if arrived.shape[2] == UNIT else (1,)
    return pl.pallas_call(
        functools.partial(final_kernel, cols_blocks, runs),
        grid=(row_len // height,),
        out_shape=jax.ShapeDtypeStruct((row_len, col_len), jnp.float32),
        in_specs=[
            smem, smem, smem, wide, block, parts, whole, whole_parts,
            pl.BlockSpec((TOTAL, TOTAL), lambda i: (0, 0)),
            pl.BlockSpec(memory_space=pltpu.VMEM),
        ],
        out_specs=wide,
        scratch_shapes=[pltpu.SMEM((codes.shape[0],), jnp.int32)],
        compiler_params=pltpu.CompilerParams(vmem_limit_bytes=56 * MIB),
    )(codes, lengths, place, front, *rows, *cols, lower, arrived)


def factor(diagonal):
    def lower_of(block):
        return jnp.linalg.cholesky(jnp.tril(block) + jnp.tril(block, -1).T)

    def inverse_of(block):
        return jax.scipy.linalg.solve_triangular(block, jnp.eye(NB, dtype=jnp.float32), lower=True)

    first = lower_of(diagonal[:NB, :NB])
    first_inverse = inverse_of(first)
    below = dot_nt(diagonal[NB:, :NB], first_inverse)
    second = lower_of(diagonal[NB:, NB:] - dot_nt(below, below))
    second_inverse = inverse_of(second)
    corner = -jnp.dot(second_inverse, jnp.dot(below, first_inverse, precision=precise), precision=precise)
    zero = jnp.zeros((NB, NB), jnp.float32)
    return jnp.block([[first, zero], [below, second]]), jnp.block([[first_inverse, zero], [corner, second_inverse]])


def body(front, tiles, tile_block, valid_rows):
    row_len, col_len = front.shape
    row_count = lax.axis_size("row")
    col_count = lax.axis_size("col")
    device_count = row_count * col_count
    per_device = tiles.shape[0]
    side = tiles.shape[1]
    capacity = 2 * per_device // device_count
    rows_blocks = row_len // side
    cols_blocks = col_len // side
    row_now = lax.axis_index("row")
    col_now = lax.axis_index("col")
    device_now = row_now * col_count + col_now

    block_row = tile_block[0].reshape(device_count, per_device)
    block_col = tile_block[1].reshape(device_count, per_device)
    target_row = block_row // rows_blocks
    target = target_row * col_count + block_col // cols_blocks
    code = block_row % rows_blocks * cols_blocks + block_col % cols_blocks
    position = lax.broadcasted_iota(jnp.int32, target.shape, 1)
    place = jnp.stack([row_now, col_now]).astype(jnp.int32)

    def own(values):
        return lax.dynamic_index_in_dim(values, device_now, 0, keepdims=False)

    in_panel = block_col < PANELS
    panel_key = jnp.where(in_panel, target_row, -1)
    panel_rank = jnp.sum(
        (panel_key[:, :, None] == panel_key[:, None, :]) & (position[:, None, :] < position[:, :, None]),
        axis=2,
    )
    same_col = lax.dynamic_index_in_dim(
        jnp.stack([panel_key, panel_rank, code]).reshape(3, row_count, col_count, per_device),
        col_now, 2, keepdims=False,
    )

    def send_panel(tiles, valid_rows, depth):
        ahead = (own(target_row) - row_now) % row_count
        fits = own(in_panel) & (own(panel_rank) < depth)
        panel_slot = jnp.where(fits, ahead * depth + own(panel_rank), -1)
        panel_out = pack(tiles, panel_slot, valid_rows, row_count * depth)
        panel_in = [panel_out[:depth]]
        for shift in range(1, row_count):
            sending = panel_out[shift * depth : (shift + 1) * depth]
            turn = [(r, (r + shift) % row_count) for r in range(row_count)]
            panel_in.append(lax.ppermute(sending, "row", turn))
        return panel_in

    def sum_panel(front, panel_in, depth):
        fits = (same_col[0] == row_now)[:, :, None] & (same_col[1][:, :, None] == jnp.arange(depth))
        panel_code = same_col[2] // cols_blocks * PANELS + same_col[2] % cols_blocks
        panel_codes = jnp.sum(jnp.where(fits, panel_code[:, :, None] + 1, 0), axis=1) - 1
        by_shift = (row_now - jnp.arange(row_count)) % row_count
        panel_codes = jnp.take(panel_codes, by_shift, axis=0).reshape(-1)
        first = (col_now == 0).astype(jnp.int32).reshape(1)
        return raw_panel(front, jnp.concatenate(panel_in, 0), panel_codes, first)

    def gather_panel(partial):
        chunk = lax.psum_scatter(partial, "col", scatter_dimension=0, tiled=True)
        raw_rows = lax.all_gather(chunk, "col", axis=0, tiled=True)
        chunk, raw_rows = lax.optimization_barrier((chunk, raw_rows))
        return lax.all_gather(chunk, "row", axis=0), raw_rows

    panel_depth = (capacity * 5 + 7) // 8
    panel_in = send_panel(tiles, valid_rows, panel_depth)

    units = side // UNIT
    length = capacity * units
    width = length * 41 // 64
    pass_on = length * 13 // 32
    half_count = device_count // 2
    half_base = device_now // half_count * half_count
    unit_rows = rows_blocks * units
    local_codes = unit_rows * cols_blocks
    own_target, own_code = own(target), own(code)
    own_position = own(position)
    filled = (valid_rows + UNIT - 1) // UNIT
    key = (own_target * rows_blocks * cols_blocks + own_code) * per_device + own_position
    before = key[None, :] < key[:, None]
    together = own_target[None, :] == own_target[:, None]
    base = jnp.sum(jnp.where(before & together, filled[None, :], 0), axis=1)
    order = jnp.sum(before, axis=1)
    unit_code = (own_target * unit_rows + own_code // cols_blocks * units) * cols_blocks
    unit_code += own_code % cols_blocks
    meta = jnp.stack([own_position, own_target, base, filled, unit_code, valid_rows])
    meta = jnp.sum(
        jnp.where(order[None, :, None] == jnp.arange(per_device), meta[:, :, None], 0), axis=1
    )
    to_device = own_target[:, None] == jnp.arange(device_count)
    load = jnp.sum(jnp.where(to_device, filled[:, None], 0), axis=0).reshape(2, half_count)
    empty = load == 0
    empty_rank = jnp.cumsum(empty, axis=1) - 1
    device_ids = jnp.arange(device_count).reshape(2, half_count)
    listed = (empty[:, :, None]) & (empty_rank[:, :, None] == jnp.arange(half_count))
    empties = jnp.sum(jnp.where(listed, device_ids[:, :, None], 0), axis=1)
    free = jnp.sum(empty, axis=1)
    left = jnp.sum(jnp.maximum(load - width, 0), axis=1)
    failed = jnp.any(left > free * width) | jnp.any(own(in_panel) & (own(panel_rank) >= panel_depth))
    counts = jnp.concatenate([jnp.sum(own_target < half_count)[None], free]).astype(jnp.int32)
    outgoing, sent_codes = spread(
        tiles, meta.astype(jnp.int32), empties.astype(jnp.int32), counts,
        device_count, width, length, cols_blocks,
    )

    partial = sum_panel(front, panel_in, panel_depth)
    partial, sent_codes = lax.optimization_barrier((partial, sent_codes))
    gathered, raw_rows = gather_panel(partial)
    got = lax.all_to_all(sent_codes[:, :width], ("row", "col"), 0, 0, tiled=True)
    outgoing, got = lax.optimization_barrier((outgoing, got))
    arrived = lax.all_to_all(outgoing, ("row", "col"), 0, 0, tiled=True)
    got_target = got // local_codes
    local = got % local_codes
    mine = (got >= 0) & (got_target == device_now)
    direct_codes = jnp.where(mine, local, -1)
    steps = jnp.arange(width)
    opening = (local // cols_blocks % units == 0) | jnp.logical_not(mine)
    later = (steps[None, :] > steps[:, None]) & opening[:, None, :]
    direct_runs = jnp.min(jnp.where(later, steps, width), axis=2) - steps
    total_units = device_count * width
    passing = ((got >= 0) & (got_target != device_now)).reshape(-1)
    flat_key = jnp.where(passing, got.reshape(-1) * total_units + jnp.arange(total_units), -1)
    flat_target = jnp.where(passing, got_target.reshape(-1), -1)
    rank = jnp.sum(
        (flat_target[None, :] == flat_target[:, None]) & (flat_key[None, :] < flat_key[:, None]), axis=1
    )
    failed = failed | jnp.any(passing & (rank >= pass_on))
    relay_slot = jnp.where(
        passing & (rank < pass_on), (flat_target - half_base) * pass_on + rank, -1
    )
    picked = relay_slot[:, None] == jnp.arange(half_count * pass_on)
    relay_codes = jnp.sum(jnp.where(picked, local.reshape(-1)[:, None] + 1, 0), axis=0) - 1
    notes = jnp.zeros((2, half_count, pass_on + 1), jnp.int32)
    notes = lax.dynamic_update_slice(
        notes, relay_codes.reshape(1, half_count, pass_on).astype(jnp.int32), (device_now // half_count, 0, 0)
    )
    notes = notes.at[:, :, pass_on].set(failed.astype(jnp.int32))
    def chain(gathered, raw_rows, tables):
        diagonal = jnp.where(row_now == 0, raw_rows[:TOTAL], jnp.eye(TOTAL, dtype=jnp.float32))
        diagonal, tables = lax.optimization_barrier((diagonal, tables))
        lower, inverse = factor(diagonal)
        known = jnp.where(row_now == 0, inverse, 0.0)
        gathered, known = lax.optimization_barrier((gathered, known))
        share = col_count // row_count
        chunks = []
        for turn in range(row_count):
            pairs = [
                (h * row_count + i, (i + turn) % row_count * share + h)
                for h in range(share)
                for i in range(row_count)
            ]
            sending = lax.dynamic_index_in_dim(gathered, (col_now + turn) % row_count, 0, keepdims=False)
            chunks.append(lax.ppermute(sending, "col", pairs))
        order = (col_now // share - jnp.arange(row_count)) % row_count
        inverse = known
        for other in range(1, row_count):
            inverse += lax.ppermute(known, "row", [(0, other)])
        return known, inverse, chunks, order.astype(jnp.int32), lower, tables

    def solve(raw_rows, inverse, chunks, order):
        rows = solve_rows(raw_rows, inverse)
        return rows, solve_cols(jnp.stack(chunks), order, inverse)

    relay_slot = relay_slot.reshape(device_count, width)
    tables = (notes, relay_slot, direct_codes, direct_runs)
    known, inverse, chunks, order, lower, tables = chain(gathered, raw_rows, tables)
    notes, relay_slot, direct_codes, direct_runs = tables
    notes, arrived, known = lax.optimization_barrier((notes, arrived, known))
    notes = lax.all_to_all(
        notes.reshape(device_count, pass_on + 1), ("row", "col"), 0, 0, tiled=True
    )
    relay_codes = lax.dynamic_slice_in_dim(notes, half_base, half_count, 0)[:, :pass_on]

    flat = relay_codes.reshape(-1)
    unit_row, relay_col = flat // cols_blocks, flat % cols_blocks
    wanted = (flat >= 0) & ((row_now > 0) | (unit_row >= TOTAL // UNIT))
    wanted &= (col_now > 0) | (relay_col >= PANELS)
    relay_block = unit_row // units * cols_blocks + relay_col
    relay_key = jnp.where(wanted, relay_block * units + unit_row % units, local_codes)
    relay_key = relay_key * flat.shape[0] + jnp.arange(flat.shape[0])
    relay_order = jnp.sum(relay_key[None, :] < relay_key[:, None], axis=1)
    listing = jnp.stack([relay_block, unit_row % units, jnp.arange(flat.shape[0])])
    at_order = relay_order[None, :, None] == jnp.arange(flat.shape[0])
    listing = jnp.sum(jnp.where(at_order, listing[:, :, None], 0), axis=1).astype(jnp.int32)
    listing = [*listing, jnp.sum(wanted).astype(jnp.int32).reshape(1)]

    passed = relay(relay_slot, arrived, half_count * pass_on)
    passed, notes, inverse, chunks = lax.optimization_barrier((passed, notes, inverse, chunks))
    rows, cols = solve(raw_rows, inverse, chunks, order)
    too_full = jnp.any(notes[:, pass_on] != 0)
    halves = [list(range(half_count)), list(range(half_count, device_count))]
    passed = lax.all_to_all(
        passed.reshape(half_count, pass_on, UNIT, side), ("row", "col"), 0, 0,
        axis_index_groups=halves, tiled=True,
    )
    partial = finish(front, rows, cols, lower, arrived, direct_codes, direct_runs, place, cols_blocks)
    result = add_relayed(partial, passed.reshape(-1, UNIT, side), listing, cols_blocks)

    def padded():
        partial = sum_panel(front, send_panel(tiles, valid_rows, capacity), capacity)
        gathered, raw_rows = gather_panel(partial)
        order = (target * rows_blocks * cols_blocks + code) * per_device + position
        ranking = jnp.sum(
            (target[:, :, None] == target[:, None, :]) & (order[:, None, :] < order[:, :, None]), axis=2
        )
        slot = own(target) * capacity + own(ranking)
        here = (target == device_now)[:, :, None] & (ranking[:, :, None] == jnp.arange(capacity))
        codes = jnp.sum(jnp.where(here, code[:, :, None] + 1, 0), axis=1) - 1
        packed = pack(tiles, slot, valid_rows, device_count * capacity)
        arrived = lax.all_to_all(
            packed.reshape(device_count, capacity, side, side), ("row", "col"), 0, 0, tiled=True
        )
        _, inverse, chunks, order, lower, _ = chain(gathered, raw_rows, ())
        rows, cols = solve(raw_rows, inverse, chunks, order)
        return finish(
            front, rows, cols, lower, arrived, codes, jnp.ones_like(codes), place, cols_blocks
        )

    def unfinished(state):
        return state[0] > 0

    def redo(state):
        return jnp.int32(0), padded()

    return lax.while_loop(unfinished, redo, (too_full.astype(jnp.int32), result))[1]


def solution(mesh):
    placed = (P("row", "col"), P(("row", "col"), None, None), P(), P(("row", "col")))
    return jax.shard_map(
        body, mesh=mesh, in_specs=placed, out_specs=P("row", "col"), check_vma=False
    )
```
